32 devices in a mesh: group: 2 (over x), shard: 16 (over z, y, core).
Axes of the slice: x: 2, y: 2, z: 4, core: 2. Of those that a mesh axis runs over, the one named last changes fastest.
Arguments:
- hidden_in: float32 [2, 32, 512, 1536], P(None, ('group', 'shard')), may hold values from -6 to 6
- lengths: int32 [2, 32], P(None, ('group', 'shard')), may hold values from 128 to 512, as said below
- pre_gain: bfloat16 [1536], P('shard'), may hold values from 0.5 to 1.5
- in_proj: bfloat16 [1536, 6448], P('shard'), may hold values from -0.15625 to 0.15625
- conv_weight: bfloat16 [4, 3328], P(None, 'shard'), may hold values from -3 to 3
- conv_bias: bfloat16 [3328], P('shard'), may hold values from -3 to 3
- head_params: float32 [3, 48], replicated, may hold values from -8.5 to 6, as said below
- gate_gain: bfloat16 [3072], P('shard'), may hold values from 0.5 to 1.5
- out_proj: bfloat16 [3072, 1536], P('shard'), may hold values from -0.109375 to 0.109375
- cotangent: float32 [2, 32, 512, 1536], P(None, ('group', 'shard')), may hold values from -6 to 6
Outputs:
- layer_out: float32 [2, 32, 512, 1536], P(None, ('group', 'shard'))
- grad_input: float32 [2, 32, 512, 1536], P(None, ('group', 'shard'))
- grad_pre_gain: float32 [1536], P('shard')
- grad_in_proj: float32 [1536, 6448], P('shard')
- grad_conv_weight: float32 [4, 3328], P(None, 'shard')
- grad_conv_bias: float32 [3328], P('shard')
- grad_head_params: float32 [3, 48], replicated
- grad_gate_gain: float32 [3072], P('shard')
- grad_out_proj: float32 [3072, 1536], P('shard')
The draws below stay inside these ranges and needn't reach their ends.
Inputs may be any that keep to these rules, and one draw needn't show every extreme that they name: `lengths`: in each micro-batch at least one sequence fills its whole slot of 512 rows. `head_params`: row 0 holds the time-step biases, row 1 the logarithms of the decay rates, row 2 the skip gains.
All inputs are finite; a program needn't handle non-finite values.
Results may differ from the reference program's by a relative error of at most 0.0067.
Values may be sent and summed in bfloat16 or wider, within the bound.
No kernel may reach another device: no remote copies, remote signals or barrier semaphores. Data moves between devices by JAX's collectives and lax.ppermute only.
A program may use at most 384 MiB of HBM per device.

```python
import math
import jax
import jax.numpy as jnp
from jax import lax

D = 1536
INNER = 3072
HEADDIM = 64
STATE = 128
CONV = 4
STRETCH = 256
SLOT = 512
MICRO = 2
HEADS = 48
CONVDIM = 3328
PROJ = 6448
SEQS = 32


def draw_lengths(key, part):
    key = jax.random.fold_in(key, 11)
    first_key, second_key = jax.random.split(key)
    drawn_lengths = jax.random.randint(first_key, (MICRO, SEQS), SLOT // 4, SLOT + 1)
    chosen = jax.random.randint(second_key, (MICRO, 1), 0, SEQS)
    columns = jnp.arange(SEQS)[None, :]
    return jnp.where(columns == chosen, SLOT, drawn_lengths).astype(jnp.int32)


def draw_head_params(key, part):
    key = jax.random.fold_in(key, 23)
    bias_key, rate_key, skip_key = jax.random.split(key, 3)
    dt_biases = jax.random.uniform(bias_key, (HEADS,), jnp.float32, -7.0, -4.0)
    log_rates = jax.random.uniform(rate_key, (HEADS,), jnp.float32, 0.0, 1.386)
    skip_gains = jax.random.uniform(skip_key, (HEADS,), jnp.float32, 2.0, 6.0)
    return jnp.stack([dt_biases, log_rates, skip_gains], axis=0)


def spiked(values, stream_key, source, target, blocks, factor):
    owner, partner = [(jnp.arange(values.shape[dim]) // (values.shape[dim] // blocks)).reshape([-1 if axis == dim else 1 for axis in range(values.ndim)]) for dim in (source, target)]
    chosen = jax.random.permutation(stream_key, blocks)[partner]
    strong = (owner == chosen) | (owner == (partner + blocks // 2) % blocks)
    return jnp.where(strong, factor * values, values)


def block_scale(stream_key, dims, shards, low, top_value):
    gain, own = 1.0, jax.random.fold_in(stream_key, 6)
    for position, parts in shards:
        heights = jnp.exp(jax.random.uniform(jax.random.fold_in(own, position), (parts,), jnp.float32, low / len(shards), top_value / len(shards)))
        gain = gain * jnp.repeat(heights, dims[position] // parts).reshape([-1 if axis == position else 1 for axis in range(len(dims))])
    return gain


def normal_values(key, shape, deviation, limit, cuts=(), kind=jnp.bfloat16):
    loudness = block_scale(key, shape, cuts, -0.22, 0.18) if cuts else 1.0
    values = jax.random.normal(key, shape, jnp.float32) * deviation * loudness
    return jnp.minimum(jnp.maximum(values, -limit), limit).astype(kind)


def gaussian_with(own_key, dims, spread, limit, shards, heavy, held_as=jnp.bfloat16):
    entries = spread * jax.random.normal(own_key, dims, jnp.float32)
    if shards:
        entries = entries * block_scale(own_key, dims, shards, -0.22, 0.18)
    return jnp.clip(spiked(entries, jax.random.fold_in(own_key, 3), *heavy), -limit, limit).astype(held_as)


def setup_inputs(seed: int = 0) -> dict:
    arg_keys = jax.random.split(jax.random.key(seed), 11)
    return {
        "hidden_in": gaussian_with(arg_keys[0], (MICRO, SEQS, SLOT, D), 1.0, 6.0, ((1, 32),), (1, 3, 32, 2.75), jnp.float32),
        "lengths": draw_lengths(jax.random.fold_in(arg_keys[10], 71), 0),
        "pre_gain": jnp.clip(1.0 + 0.1 * jax.random.normal(arg_keys[2], (D,), jnp.float32), 0.5, 1.5).astype(jnp.bfloat16),
        "in_proj": normal_values(arg_keys[3], (D, PROJ), D ** -0.5, 0.15625, ((0, 16),)),
        "conv_weight": normal_values(arg_keys[4], (CONV, CONVDIM), CONV ** -0.5, 3.0, ((1, 16),)),
        "conv_bias": normal_values(arg_keys[5], (CONVDIM,), 0.5, 3.0, ((0, 16),)),
        "head_params": draw_head_params(jax.random.fold_in(arg_keys[10], 71), 0),
        "gate_gain": jnp.clip(1.0 + 0.1 * jax.random.normal(arg_keys[7], (INNER,), jnp.float32), 0.5, 1.5).astype(jnp.bfloat16),
        "out_proj": normal_values(arg_keys[8], (INNER, D), INNER ** -0.5, 0.109375, ((0, 16),)),
        "cotangent": normal_values(arg_keys[9], (MICRO, SEQS, SLOT, D), 1.0, 6.0, ((1, 32),), jnp.float32),
    }


@jax.custom_vjp
def low(v):
    return lax.optimization_barrier(v.astype(jnp.bfloat16)).astype(jnp.float32)

@jax.custom_vjp
def low_back(v):
    return v

def low_keep(v):
    return (low(v), None)

def low_pass(kept, grad):
    return (grad,)

def back_keep(v):
    return (v, None)

def back_low(kept, grad):
    return (low(grad),)
low.defvjp(low_keep, low_pass)
low_back.defvjp(back_keep, back_low)
EPS = 1e-05
HIGHEST = lax.Precision.HIGHEST

def product(left, right):
    return jnp.dot(left, right, precision=HIGHEST)

def causal_conv(values, taps_weight, bias_row):
    tap_count = taps_weight.shape[0]
    length = values.shape[0]
    padded = jnp.pad(values, ((tap_count - 1, 0), (0, 0)))
    running = bias_row[None, :]
    for offset in range(tap_count):
        running = running + taps_weight[offset][None, :] * padded[offset:offset + length]
    return running

def block_step(carry_state, pieces, a_rate, skip_gain):
    x_low, b_low, c_low, dt_rows = pieces
    span_rows = dt_rows.shape[0]
    cum_rate = jnp.cumsum(dt_rows * a_rate[None, :], axis=0)
    causal = jnp.arange(span_rows)[:, None] >= jnp.arange(span_rows)[None, :]
    cb_full = low_back(product(c_low, b_low.T))
    cum_heads = cum_rate.T
    decay_mat = jnp.exp(jnp.where(causal[None], cum_heads[:, :, None] - cum_heads[:, None, :], -10000.0))
    mixing = low(cb_full[None] * decay_mat * dt_rows.T[:, None, :])
    intra_part = low_back(jnp.einsum('hts,shp->thp', mixing, x_low, precision=HIGHEST))
    inter_part = low_back(jnp.einsum('tn,hpn->thp', c_low, low(carry_state), precision=HIGHEST))
    core_out = intra_part + jnp.exp(cum_rate)[:, :, None] * inter_part
    last_cum = cum_rate[-1]
    scaled = low(x_low * (jnp.exp(last_cum[None, :] - cum_rate) * dt_rows)[:, :, None])
    update = low_back(jnp.einsum('thp,tn->hpn', scaled, b_low, precision=HIGHEST))
    new_state = jnp.exp(last_cum)[:, None, None] * carry_state + update
    return (new_state, core_out + skip_gain[None, :, None] * x_low)

def sequence(row_in, row_mask, pre_gain, in_proj, conv_weight, conv_bias, head_params, gate_gain, out_proj):
    length = row_in.shape[0]
    inv_first = lax.rsqrt(lax.optimization_barrier(jnp.mean(row_in * row_in, axis=-1, keepdims=True)) + EPS)
    normed = low(row_in * inv_first * pre_gain[None, :])
    projected = low_back(product(normed, in_proj))
    z_part = projected[:, :INNER]
    conv_in = projected[:, INNER:2 * INNER + 2 * STATE]
    dt_raw = projected[:, 2 * INNER + 2 * STATE:]
    active = jax.nn.silu(causal_conv(conv_in, conv_weight, conv_bias))
    x_low = low(active[:, :INNER]).reshape(length, HEADS, HEADDIM)
    b_low = low(active[:, INNER:INNER + STATE])
    c_low = low(active[:, INNER + STATE:])
    dt_rows = jax.nn.softplus(dt_raw + head_params[0][None, :])
    a_rate = -jnp.exp(head_params[1])
    blocks = length // STRETCH

    def split_blocks(values):
        return values.reshape((blocks, STRETCH) + values.shape[1:])

    def block_body(carry_state, pieces):
        return block_step(carry_state, pieces, a_rate, head_params[2])
    zero_state = jnp.zeros((HEADS, HEADDIM, STATE), jnp.float32)
    _, outputs = lax.scan(jax.checkpoint(block_body), zero_state, (split_blocks(x_low), split_blocks(b_low), split_blocks(c_low), split_blocks(dt_rows)))
    y_rows = outputs.reshape(length, INNER)
    gated_rows = y_rows * jax.nn.silu(z_part)
    inv_second = lax.rsqrt(lax.optimization_barrier(jnp.mean(gated_rows * gated_rows, axis=-1, keepdims=True)) + EPS)
    gate_low = low(gated_rows * inv_second * gate_gain[None, :])
    branch = low_back(product(gate_low, out_proj))
    return row_mask[:, None] * (row_in + branch)

def reference(hidden_in, lengths, pre_gain, in_proj, conv_weight, conv_bias, head_params, gate_gain, out_proj, cotangent):
    params = tuple((weight_arg.astype(jnp.float32) for weight_arg in (pre_gain, in_proj, conv_weight, conv_bias, head_params, gate_gain, out_proj)))
    total_seqs = MICRO * SEQS
    batched = math.gcd(max(4096 // SLOT, 1), total_seqs)
    block_count = total_seqs // batched
    block_in = hidden_in.reshape(block_count, batched, SLOT, D)
    block_cot = cotangent.reshape(block_count, batched, SLOT, D)
    block_len = lengths.reshape(block_count, batched).astype(jnp.int32)
    positions = jnp.arange(SLOT, dtype=jnp.int32)

    def one_block(grad_sums, block_items):
        rows_in, rows_len, rows_cot = block_items
        row_masks = (positions[None, :] < rows_len[:, None]).astype(jnp.float32)

        def forward(inputs_now, *weights):

            def single(row_in, row_mask):
                return sequence(row_in, row_mask, *weights)
            return jax.vmap(single)(inputs_now, row_masks)
        outputs, pullback = jax.vjp(forward, rows_in, *params)
        pulled = pullback(rows_cot)
        grad_sums = tuple((running + grad_part for running, grad_part in zip(grad_sums, pulled[1:])))
        return (grad_sums, (outputs, pulled[0]))
    zero_sums = tuple((jnp.zeros_like(weight_arg) for weight_arg in params))
    grad_sums, (outputs, grad_rows) = lax.scan(one_block, zero_sums, (block_in, block_len, block_cot))
    layer_out = outputs.reshape(MICRO, SEQS, SLOT, D)
    grad_input = grad_rows.reshape(MICRO, SEQS, SLOT, D)
    return (layer_out, grad_input, grad_sums[0], grad_sums[1], grad_sums[2], grad_sums[3], grad_sums[4], grad_sums[5], grad_sums[6])
```

```python
import functools

import jax
import jax.numpy as jnp
from jax import lax
from jax.experimental import pallas as pl
from jax.experimental.pallas import tpu as pltpu
from jax.sharding import PartitionSpec as P

STRETCH = 256
HALF = 128
LANES = 128
GROUP_HEADS = 4
EPS = 1e-05
BF = jnp.bfloat16
F32 = jnp.float32
VMEM_BYTES = 56 * 1024 * 1024


def params(**kwargs):
    return pltpu.CompilerParams(vmem_limit_bytes=VMEM_BYTES, **kwargs)


def dot_nn(left, right):
    return lax.dot_general(left, right, (((1,), (0,)), ((), ())), preferred_element_type=F32)


def dot_nt(left, right):
    return lax.dot_general(left, right, (((1,), (1,)), ((), ())), preferred_element_type=F32)


def dot_tn(left, right):
    return lax.dot_general(left, right, (((0,), (0,)), ((), ())), preferred_element_type=F32)


def sigmoid(values):
    return 1.0 / (1.0 + jnp.exp(-values))


def row_index(values):
    return lax.broadcasted_iota(jnp.int32, (values.shape[0], 1), 0)


def shift_down(values, count):
    rolled = pltpu.roll(values, count, 0)
    return jnp.where(row_index(values) >= count, rolled, 0.0)


def shift_up(values, count):
    rows = values.shape[0]
    rolled = pltpu.roll(values, rows - count, 0)
    return jnp.where(row_index(values) < rows - count, rolled, 0.0)


def conv_parts(values, taps_ref):
    shifted = [shift_down(values, 3), shift_down(values, 2), shift_down(values, 1), values]
    pre = taps_ref[4:5, :]
    for k in range(4):
        pre = pre + taps_ref[k : k + 1, :] * shifted[k]
    return shifted, pre


def conv_back(grad_pre, taps_ref):
    total = taps_ref[3:4, :] * grad_pre
    for k in range(3):
        total = total + taps_ref[k : k + 1, :] * shift_up(grad_pre, 3 - k)
    return total


def column_sum(values):
    return jnp.sum(values, axis=0, keepdims=True)


def prepare_kernel(raw_ref, taps_ref, heads_ref, b_ref, c_ref, bt_ref, ct_ref, dt_ref, cum_ref, cumt_ref):
    _, pre = conv_parts(raw_ref[:, : 2 * LANES], taps_ref)
    active = pre * sigmoid(pre)
    b_part, c_part = active[:, :LANES], active[:, LANES:]
    b_ref[...] = b_part.astype(BF)
    c_ref[...] = c_part.astype(BF)
    bt_ref[...] = b_part.T.astype(BF)
    ct_ref[...] = c_part.T.astype(BF)
    raw = raw_ref[:, 2 * LANES :] + heads_ref[0:1, :]
    dt = jnp.maximum(raw, 0.0) + jnp.log1p(jnp.exp(-jnp.abs(raw)))
    cum = dt * heads_ref[1:2, :]
    place = row_index(cum) % STRETCH
    step = 1
    while step < STRETCH:
        cum = cum + jnp.where(place >= step, pltpu.roll(cum, step, 0), 0.0)
        step *= 2
    dt_ref[...] = dt
    cum_ref[...] = cum
    cumt_ref[...] = cum.T


def prepare(raw, taps, heads, slot):
    rows = raw.shape[0]
    tall = pl.BlockSpec((slot, LANES), lambda q: (q, 0))
    wide = pl.BlockSpec((LANES, slot), lambda q: (0, q))
    return pl.pallas_call(
        prepare_kernel,
        grid=(rows // slot,),
        in_specs=[
            pl.BlockSpec((slot, 3 * LANES), lambda q: (q, 0)),
            pl.BlockSpec((8, 2 * LANES), lambda q: (0, 0)),
            pl.BlockSpec((8, LANES), lambda q: (0, 0)),
        ],
        out_specs=[tall, tall, wide, wide, tall, tall, wide],
        out_shape=[
            jax.ShapeDtypeStruct((rows, LANES), BF),
            jax.ShapeDtypeStruct((rows, LANES), BF),
            jax.ShapeDtypeStruct((LANES, rows), BF),
            jax.ShapeDtypeStruct((LANES, rows), BF),
            jax.ShapeDtypeStruct((rows, LANES), F32),
            jax.ShapeDtypeStruct((rows, LANES), F32),
            jax.ShapeDtypeStruct((LANES, rows), F32),
        ],
        compiler_params=params(),
        name="prepare",
    )(raw, taps, heads)


def head_tables(cum_ref, dt_ref, first_head):
    shift = lax.rem(LANES - first_head, LANES)
    cum = pltpu.roll(cum_ref[...], shift, 1)
    dt = pltpu.roll(dt_ref[...], shift, 1)
    rows = cum.shape[0]
    cum_wide = [jnp.broadcast_to(cum[:, i : i + 1], (rows, LANES)) for i in range(GROUP_HEADS)]
    dt_wide = [jnp.broadcast_to(dt[:, i : i + 1], (rows, LANES)) for i in range(GROUP_HEADS)]
    left = lax.broadcasted_iota(jnp.int32, (1, LANES), 1) < LANES // 2

    def spread(wide):
        return jnp.concatenate(
            [jnp.where(left, wide[i], wide[i + 1]) for i in range(0, GROUP_HEADS, 2)], axis=1
        )

    return cum_wide, spread(cum_wide), spread(dt_wide), left


def decay_tiles(cum_wide, cumt_row, block, lower):
    begin = block * STRETCH
    top = cum_wide[begin : begin + HALF]
    low = cum_wide[begin + HALF : begin + STRETCH]
    row_left = cumt_row[:, begin : begin + HALF]
    row_right = cumt_row[:, begin + HALF : begin + STRETCH]
    first = jnp.where(lower, jnp.exp(top - row_left), 0.0)
    second = jnp.exp(low - row_left)
    third = jnp.where(lower, jnp.exp(low - row_right), 0.0)
    return first, jnp.concatenate([second, third], axis=1)


def join_tiles(first, below):
    return jnp.concatenate(
        [jnp.concatenate([first, jnp.zeros_like(first)], axis=1), below], axis=0
    )


def lower_mask():
    return lax.broadcasted_iota(jnp.int32, (HALF, HALF), 0) >= lax.broadcasted_iota(
        jnp.int32, (HALF, HALF), 1
    )


def forward_kernel(x_ref, taps_ref, b_ref, c_ref, bt_ref, dt_ref, cum_ref, cumt_ref, y_ref):
    first_head = pl.program_id(1) * GROUP_HEADS
    _, pre = conv_parts(x_ref[...], taps_ref)
    x_low = (pre * sigmoid(pre)).astype(BF).astype(F32)
    cum_wide, cum_x, dt_x, left = head_tables(cum_ref, dt_ref, first_head)
    x_dt = (x_low * dt_x).astype(BF)
    skipped = taps_ref[5:6, :] * x_low
    fade = jnp.exp(cum_x[STRETCH - 1 : STRETCH] - cum_x[:STRETCH])
    scaled = (x_low[:STRETCH] * (fade * dt_x[:STRETCH])).astype(BF)
    state = dot_nn(bt_ref[:, :STRETCH], scaled).astype(BF)
    inter = jnp.exp(cum_x[STRETCH:]) * dot_nn(c_ref[STRETCH:, :], state)
    lower = lower_mask()
    zero = jnp.zeros((STRETCH, LANES), BF)
    for block in range(2):
        rows = slice(block * STRETCH, (block + 1) * STRETCH)
        cb = dot_nt(c_ref[rows, :], b_ref[rows, :])
        for pair in range(GROUP_HEADS // 2):
            lanes = slice(pair * LANES, (pair + 1) * LANES)
            x_pair = x_dt[rows, lanes]
            total = skipped[rows, lanes]
            if block == 1:
                total = total + inter[:, lanes]
            for side in range(2):
                head = 2 * pair + side
                row = cumt_ref[pl.ds(first_head + head, 1), :]
                first, below = decay_tiles(cum_wide[head], row, block, lower)
                mixing = join_tiles(
                    (cb[:HALF, :HALF] * first).astype(BF), (cb[HALF:, :] * below).astype(BF)
                )
                keep = left if side == 0 else jnp.logical_not(left)
                total = total + dot_nn(mixing, jnp.where(keep, x_pair, zero))
            y_ref[rows, lanes] = total


def scan_forward(px, taps, prep, slot):
    b_low, c_low, b_t, _, dt, cum, cum_t = prep
    rows, inner = px.shape
    width = GROUP_HEADS * 64
    tall = pl.BlockSpec((slot, LANES), lambda q, h: (q, 0))
    wide = pl.BlockSpec((LANES, slot), lambda q, h: (0, q))
    tile = pl.BlockSpec((slot, width), lambda q, h: (q, h))
    return pl.pallas_call(
        forward_kernel,
        grid=(rows // slot, inner // width),
        in_specs=[
            tile,
            pl.BlockSpec((8, width), lambda q, h: (0, h)),
            tall,
            tall,
            wide,
            tall,
            tall,
            wide,
        ],
        out_specs=tile,
        out_shape=jax.ShapeDtypeStruct((rows, inner), F32),
        compiler_params=params(),
        cost_estimate=pl.CostEstimate(
            flops=60 * rows * inner * 512, bytes_accessed=8 * rows * inner, transcendentals=0
        ),
        name="scan_forward",
    )(px, taps, b_low, c_low, b_t, dt, cum, cum_t)


def gate_kernel(y_ref, z_ref, gain_ref, gate_ref, inv_ref):
    z = z_ref[...]
    gated = y_ref[...] * (z * sigmoid(z))
    mean = jnp.sum(gated * gated, axis=1, keepdims=True) * (1.0 / gated.shape[1])
    inv = lax.rsqrt(mean + EPS)
    gate_ref[...] = (gated * inv * gain_ref[...]).astype(BF)
    inv_ref[...] = jnp.broadcast_to(inv, inv_ref.shape)


def gate_forward(y_rows, pz, gain):
    rows, inner = y_rows.shape
    size = 128
    tile = pl.BlockSpec((size, inner), lambda t: (t, 0))
    return pl.pallas_call(
        gate_kernel,
        grid=(rows // size,),
        in_specs=[tile, tile, pl.BlockSpec((1, inner), lambda t: (0, 0))],
        out_specs=[tile, pl.BlockSpec((size, LANES), lambda t: (t, 0))],
        out_shape=[
            jax.ShapeDtypeStruct((rows, inner), BF),
            jax.ShapeDtypeStruct((rows, LANES), F32),
        ],
        compiler_params=params(),
        cost_estimate=pl.CostEstimate(
            flops=20 * rows * inner, bytes_accessed=10 * rows * inner, transcendentals=0
        ),
        name="gate_forward",
    )(y_rows, pz, gain)


def gate_back_kernel(y_ref, z_ref, grad_ref, inv_ref, gain_ref, gy_ref, gz_ref, gain_sum_ref):
    y = y_ref[...]
    z = z_ref[...]
    grad = grad_ref[...]
    inv = inv_ref[:, 0:1]
    sig = sigmoid(z)
    silu = z * sig
    normal = y * silu * inv
    grad_normal = grad * gain_ref[...]
    mean = jnp.sum(grad_normal * normal, axis=1, keepdims=True) * (1.0 / y.shape[1])
    gated = inv * (grad_normal - normal * mean)
    gy_ref[...] = (gated * silu).astype(BF)
    gz_ref[...] = (gated * y * (sig + silu * (1.0 - sig))).astype(BF)
    part = grad * normal
    folded = part[0:8]
    for start in range(8, part.shape[0], 8):
        folded = folded + part[start : start + 8]

    @pl.when(pl.program_id(0) == 0)
    def _():
        gain_sum_ref[...] = folded

    @pl.when(pl.program_id(0) > 0)
    def _():
        gain_sum_ref[...] += folded


def gate_backward(y_rows, pz, grad_gate, inv, gain):
    rows, inner = y_rows.shape
    size = 128
    tile = pl.BlockSpec((size, inner), lambda t: (t, 0))
    return pl.pallas_call(
        gate_back_kernel,
        grid=(rows // size,),
        in_specs=[
            tile,
            tile,
            tile,
            pl.BlockSpec((size, LANES), lambda t: (t, 0)),
            pl.BlockSpec((1, inner), lambda t: (0, 0)),
        ],
        out_specs=[tile, tile, pl.BlockSpec((8, inner), lambda t: (0, 0))],
        out_shape=[
            jax.ShapeDtypeStruct((rows, inner), BF),
            jax.ShapeDtypeStruct((rows, inner), BF),
            jax.ShapeDtypeStruct((8, inner), F32),
        ],
        compiler_params=params(),
        cost_estimate=pl.CostEstimate(
            flops=30 * rows * inner, bytes_accessed=16 * rows * inner, transcendentals=0
        ),
        name="gate_backward",
    )(y_rows, pz, grad_gate, inv, gain)


def add_heads(total_ref, product, spread):
    high = product.astype(BF)
    low = (product - high.astype(F32)).astype(BF)
    total_ref[...] += dot_nn(high, spread) + dot_nn(low, spread)


def backward_kernel(
    group_start,
    x_ref,
    taps_ref,
    y_ref,
    gy_ref,
    b_ref,
    c_ref,
    bt_ref,
    ct_ref,
    dt_ref,
    cum_ref,
    cumt_ref,
    gx_ref,
    sums_ref,
    gb_ref,
    gc_ref,
    one_ref,
    two_ref,
    cb_ref,
):
    first_head = (pl.program_id(1) + group_start) * GROUP_HEADS

    @pl.when(pl.program_id(1) == 0)
    def _():
        gb_ref[...] = jnp.zeros_like(gb_ref)
        gc_ref[...] = jnp.zeros_like(gc_ref)
        one_ref[...] = jnp.zeros_like(one_ref)
        two_ref[...] = jnp.zeros_like(two_ref)
        cb_ref[...] = jnp.zeros_like(cb_ref)

    shifted, pre = conv_parts(x_ref[...], taps_ref)
    sig = sigmoid(pre)
    active = pre * sig
    slope = sig + active * (1.0 - sig)
    x_low = active.astype(BF).astype(F32)
    gy_low = gy_ref[...]
    gy = gy_low.astype(F32)
    cum_wide, cum_x, dt_x, left = head_tables(cum_ref, dt_ref, first_head)
    x_dt = (x_low * dt_x).astype(BF)
    skip = taps_ref[5:6, :]

    grad_inter = (gy[STRETCH:] * jnp.exp(cum_x[STRETCH:])).astype(BF)
    fade = jnp.exp(cum_x[STRETCH - 1 : STRETCH] - cum_x[:STRETCH])
    scaled = (x_low[:STRETCH] * (fade * dt_x[:STRETCH])).astype(BF)
    state = dot_nn(bt_ref[:, :STRETCH], scaled)
    gc_ref[STRETCH:, :] += dot_nt(grad_inter, state.astype(BF))
    grad_state = dot_nn(ct_ref[:, STRETCH:], grad_inter).astype(BF)
    gb_ref[:STRETCH, :] += dot_nt(scaled, grad_state)
    grad_scaled = dot_nn(b_ref[:STRETCH, :], grad_state)
    last_sum = column_sum(grad_state.astype(F32) * state)

    lower = lower_mask()
    zero = jnp.zeros((STRETCH, LANES), BF)
    rest = []
    for block in range(2):
        rows = slice(block * STRETCH, (block + 1) * STRETCH)
        cb = dot_nt(c_ref[rows, :], b_ref[rows, :])
        cb_first = cb_below = None
        parts = []
        for pair in range(GROUP_HEADS // 2):
            lanes = slice(pair * LANES, (pair + 1) * LANES)
            x_pair = x_dt[rows, lanes]
            gy_pair = gy_low[rows, lanes]
            total = None
            for side in range(2):
                head = 2 * pair + side
                row = cumt_ref[pl.ds(first_head + head, 1), :]
                first, below = decay_tiles(cum_wide[head], row, block, lower)
                mixing = join_tiles(
                    (cb[:HALF, :HALF] * first).astype(BF), (cb[HALF:, :] * below).astype(BF)
                )
                keep = left if side == 0 else jnp.logical_not(left)
                gy_head = jnp.where(keep, gy_pair, zero)
                mix_first = dot_nt(gy_head[:HALF], x_pair[:HALF]) * first
                mix_below = dot_nt(gy_head[HALF:], x_pair) * below
                cb_first = mix_first if cb_first is None else cb_first + mix_first
                cb_below = mix_below if cb_below is None else cb_below + mix_below
                now = dot_tn(mixing, gy_head)
                total = now if total is None else total + now
            parts.append(total)
        cb_ref[0, block, :HALF, :HALF] += cb_first
        cb_ref[0, block, HALF:, :] += cb_below
        rest.append(jnp.concatenate(parts, axis=1))
    moved = x_dt.astype(F32) * jnp.concatenate(rest, axis=0)
    moved = jnp.concatenate(
        [moved[:STRETCH] + scaled.astype(F32) * grad_scaled, moved[STRETCH:]], axis=0
    )
    rest[0] = rest[0] + fade * grad_scaled
    grad_pull = jnp.concatenate(rest, axis=0)

    width = x_low.shape[1]
    spread = (
        lax.broadcasted_iota(jnp.int32, (width, LANES), 1)
        == first_head + lax.broadcasted_iota(jnp.int32, (width, LANES), 0) // 64
    ).astype(F32).astype(BF)
    add_heads(one_ref, gy * (y_ref[...] - skip * x_low) - moved, spread)
    add_heads(two_ref, x_low * grad_pull, spread)

    grad_pre = (skip * gy + dt_x * grad_pull) * slope
    gx_ref[...] = conv_back(grad_pre, taps_ref).astype(BF)
    lines = [column_sum(grad_pre * shifted[k]) for k in range(4)]
    lines += [column_sum(grad_pre), column_sum(gy * x_low), last_sum, jnp.zeros_like(last_sum)]
    sums_ref[0] = jnp.concatenate(lines, axis=0)


def scan_backward(px, taps, y_rows, grad_y, prep, slot, start, count):
    b_low, c_low, b_t, c_t, dt, cum, cum_t = prep
    rows, inner = px.shape
    width = GROUP_HEADS * 64
    seqs = rows // slot
    tall = pl.BlockSpec((slot, LANES), lambda q, h: (q, 0))
    wide = pl.BlockSpec((LANES, slot), lambda q, h: (0, q))
    tile = pl.BlockSpec((slot, width), lambda q, h: (q, h + start))
    return pl.pallas_call(
        functools.partial(backward_kernel, start),
        grid=(seqs, count),
        in_specs=[
            tile,
            pl.BlockSpec((8, width), lambda q, h: (0, h + start)),
            tile,
            tile,
            tall,
            tall,
            wide,
            wide,
            tall,
            tall,
            wide,
        ],
        out_specs=[
            pl.BlockSpec((slot, width), lambda q, h: (q, h)),
            pl.BlockSpec((1, 8, width), lambda q, h: (q, 0, h)),
            tall,
            tall,
            tall,
            tall,
            pl.BlockSpec((1, 2, STRETCH, STRETCH), lambda q, h: (q, 0, 0, 0)),
        ],
        out_shape=[
            jax.ShapeDtypeStruct((rows, count * width), BF),
            jax.ShapeDtypeStruct((seqs, 8, count * width), F32),
            jax.ShapeDtypeStruct((rows, LANES), F32),
            jax.ShapeDtypeStruct((rows, LANES), F32),
            jax.ShapeDtypeStruct((rows, LANES), F32),
            jax.ShapeDtypeStruct((rows, LANES), F32),
            jax.ShapeDtypeStruct((seqs, 2, STRETCH, STRETCH), F32),
        ],
        compiler_params=params(),
        cost_estimate=pl.CostEstimate(
            flops=120 * rows * count * width * 512,
            bytes_accessed=14 * rows * count * width,
            transcendentals=0,
        ),
        name="scan_backward",
    )(px, taps, y_rows, grad_y, b_low, c_low, b_t, c_t, dt, cum, cum_t)


def finish_kernel(
    raw_ref,
    taps_ref,
    heads_ref,
    b_ref,
    c_ref,
    dt_ref,
    gb_ref,
    gc_ref,
    one_ref,
    two_ref,
    cb_ref,
    last_ref,
    out_ref,
    sums_ref,
    head_sums_ref,
):
    shifted, pre = conv_parts(raw_ref[:, : 2 * LANES], taps_ref)
    sig = sigmoid(pre)
    slope = sig + pre * sig * (1.0 - sig)
    grad_b, grad_c = [], []
    for block in range(2):
        rows = slice(block * STRETCH, (block + 1) * STRETCH)
        cb = cb_ref[0, block].astype(BF)
        grad_c.append(gc_ref[rows, :] + dot_nn(cb, b_ref[rows, :]))
        grad_b.append(gb_ref[rows, :] + dot_tn(cb, c_ref[rows, :]))
    grad_active = jnp.concatenate(
        [jnp.concatenate(grad_b, axis=0), jnp.concatenate(grad_c, axis=0)], axis=1
    )
    grad_pre = grad_active * slope
    lines = [column_sum(grad_pre * shifted[k]) for k in range(4)] + [column_sum(grad_pre)]
    lines.append(jnp.zeros((3, 2 * LANES), F32))
    sums_ref[0] = jnp.concatenate(lines, axis=0)

    dt = dt_ref[...]
    two = two_ref[...]
    rate = heads_ref[1:2, :]
    place = row_index(dt)
    grad_cum = one_ref[...]
    grad_cum = grad_cum + jnp.where(place == STRETCH - 1, last_ref[0, 0:1, :], 0.0)
    inside = place % STRETCH
    step = 1
    while step < STRETCH:
        moved = pltpu.roll(grad_cum, grad_cum.shape[0] - step, 0)
        grad_cum = grad_cum + jnp.where(inside < STRETCH - step, moved, 0.0)
        step *= 2
    grad_dt = grad_cum * rate + two
    grad_raw = grad_dt * sigmoid(raw_ref[:, 2 * LANES :] + heads_ref[0:1, :])
    head_sums_ref[0] = jnp.concatenate(
        [column_sum(grad_raw), column_sum(grad_cum * dt) * rate, jnp.zeros((6, LANES), F32)], axis=0
    )
    out_ref[:, : 2 * LANES] = conv_back(grad_pre, taps_ref).astype(BF)
    out_ref[:, 2 * LANES :] = grad_raw.astype(BF)


def finish(raw, taps, heads, prep, gb, gc, one, two, cb, last, slot):
    b_low, c_low, _, _, dt, _, _ = prep
    rows = raw.shape[0]
    seqs = rows // slot
    tall = pl.BlockSpec((slot, LANES), lambda q: (q, 0))
    return pl.pallas_call(
        finish_kernel,
        grid=(seqs,),
        in_specs=[
            pl.BlockSpec((slot, 3 * LANES), lambda q: (q, 0)),
            pl.BlockSpec((8, 2 * LANES), lambda q: (0, 0)),
            pl.BlockSpec((8, LANES), lambda q: (0, 0)),
            tall,
            tall,
            tall,
            tall,
            tall,
            tall,
            tall,
            pl.BlockSpec((1, 2, STRETCH, STRETCH), lambda q: (q, 0, 0, 0)),
            pl.BlockSpec((1, 8, LANES), lambda q: (q, 0, 0)),
        ],
        out_specs=[
            pl.BlockSpec((slot, 3 * LANES), lambda q: (q, 0)),
            pl.BlockSpec((1, 8, 2 * LANES), lambda q: (q, 0, 0)),
            pl.BlockSpec((1, 8, LANES), lambda q: (q, 0, 0)),
        ],
        out_shape=[
            jax.ShapeDtypeStruct((rows, 3 * LANES), BF),
            jax.ShapeDtypeStruct((seqs, 8, 2 * LANES), F32),
            jax.ShapeDtypeStruct((seqs, 8, LANES), F32),
        ],
        compiler_params=params(),
        name="finish",
    )(raw, taps, heads, b_low, c_low, dt, gb, gc, one, two, cb, last)


def halving_sum(grad, order, shards, groups):
    bits = shards.bit_length() - 1
    part = grad.shape[0] // shards
    place = lax.axis_index("shard")
    now = grad.reshape((2,) * bits + (part, grad.shape[1]))
    live = list(range(bits - 1, -1, -1))
    for bit in order:
        axis = live.index(bit)
        mine = (place >> bit) & 1
        keep = lax.dynamic_index_in_dim(now, mine, axis, keepdims=False)
        give = lax.dynamic_index_in_dim(now, 1 - mine, axis, keepdims=False)
        got = lax.ppermute(give, "shard", [(i, i ^ (1 << bit)) for i in range(shards)])
        now = (keep.astype(F32) + got.astype(F32)).astype(BF)
        live.remove(bit)
    total = now.astype(F32)
    for step in range(1, groups):
        got = lax.ppermute(now, "group", [(i, (i + step) % groups) for i in range(groups)])
        total = total + got.astype(F32)
    return total


def local(
    shards,
    groups,
    hidden_in,
    lengths,
    pre_gain,
    in_proj,
    conv_weight,
    conv_bias,
    head_params,
    gate_gain,
    out_proj,
    cotangent,
):
    micro, own, slot, width = hidden_in.shape
    rows = micro * own * slot
    inner = out_proj.shape[0] * shards
    channels = conv_bias.shape[0] * shards
    heads = head_params.shape[1]
    state = (channels - inner) // 2
    tail = 2 * state + heads
    part = in_proj.shape[0]
    taps = conv_weight.shape[0]
    hidden = hidden_in.reshape(rows, width)
    cot = cotangent.reshape(rows, width)

    small = jnp.concatenate(
        [pre_gain, gate_gain, conv_bias, conv_weight.reshape(-1)], axis=0
    )
    extra = -(-small.shape[0] // part)
    small = jnp.pad(small, (0, extra * part - small.shape[0])).reshape(part, extra)
    narrow = jnp.concatenate([in_proj[:, inner + inner :], small], axis=1)
    narrow_all = lax.all_gather(narrow, "shard", axis=0, tiled=True)
    w_x = lax.all_gather(in_proj[:, inner : 2 * inner], "shard", axis=0, tiled=True)
    w_z = lax.all_gather(in_proj[:, :inner], "shard", axis=0, tiled=True)
    w_out = lax.all_gather(out_proj, "shard", axis=0, tiled=True)

    w_tail = jnp.pad(narrow_all[:, :tail], ((0, 0), (0, 3 * LANES - tail)))
    packed = narrow_all[:, tail:].reshape(shards, extra * part)
    sizes = (part, out_proj.shape[0], conv_bias.shape[0], taps * conv_bias.shape[0])
    ends = [sum(sizes[: i + 1]) for i in range(4)]
    pre_all = packed[:, : ends[0]].reshape(1, width).astype(F32)
    gate_all = packed[:, ends[0] : ends[1]].reshape(1, inner).astype(F32)
    bias_all = packed[:, ends[1] : ends[2]].reshape(1, channels).astype(F32)
    taps_all = packed[:, ends[2] : ends[3]].reshape(shards, taps, -1)
    taps_all = jnp.swapaxes(taps_all, 0, 1).reshape(taps, channels).astype(F32)
    skip_row = jnp.pad(jnp.repeat(head_params[2], inner // heads), (0, channels - inner))
    table = jnp.concatenate(
        [taps_all, bias_all, skip_row[None, :], jnp.zeros((2, channels), F32)], axis=0
    )
    table_x, table_bc = table[:, :inner], table[:, inner:]
    rate = -jnp.exp(head_params[1])
    head_rows = jnp.pad(
        jnp.stack([head_params[0], rate], axis=0), ((0, 6), (0, LANES - heads))
    )

    inv_first = lax.rsqrt(jnp.mean(hidden * hidden, axis=-1, keepdims=True) + EPS)
    normed = (hidden * inv_first * pre_all).astype(BF)
    raw = dot_nn(normed, w_tail)
    px = dot_nn(normed, w_x)
    pz = dot_nn(normed, w_z)
    prep = prepare(raw, table_bc, head_rows, slot)
    y_rows = scan_forward(px, table_x, prep, slot)
    gate_low, inv = gate_forward(y_rows, pz, gate_all)

    positions = jnp.arange(slot, dtype=jnp.int32)
    mask = (positions[None, :] < lengths.reshape(-1)[:, None]).astype(F32).reshape(rows, 1)
    grad_branch = mask * cot
    grad_low = grad_branch.astype(BF)
    order = list(range(shards.bit_length() - 1))
    g_out = dot_tn(gate_low, grad_low).astype(BF)
    sum_out = halving_sum(g_out, order, shards, groups)
    grad_gate = dot_nt(grad_low, w_out)
    grad_y, grad_z, gain_sum = gate_backward(y_rows, pz, grad_gate, inv, gate_all)
    g_z = dot_tn(normed, grad_z).astype(BF)
    sum_z = halving_sum(g_z, order, shards, groups)

    total_groups = inner // (GROUP_HEADS * 64)
    cuts = [(0, total_groups // 2), (total_groups // 2, total_groups - total_groups // 2)]
    grad_xs, sums_x, line_parts, extras = [], [], [], None
    for start, count in cuts:
        outs = scan_backward(px, table_x, y_rows, grad_y, prep, slot, start, count)
        grad_xs.append(outs[0])
        line_parts.append(jnp.sum(outs[1], axis=0))
        last = outs[1][:, 6].reshape(micro * own, -1, inner // heads).sum(axis=2)
        last = jnp.pad(
            last,
            (
                (0, 0),
                (start * GROUP_HEADS, LANES - (start + count) * GROUP_HEADS),
            ),
        )
        now = outs[2:] + [last] if isinstance(outs, list) else tuple(outs[2:]) + (last,)
        extras = now if extras is None else tuple(a + b for a, b in zip(extras, now))
        g_x = dot_tn(normed, outs[0]).astype(BF)
        sums_x.append(halving_sum(g_x, order, shards, groups))
    gb, gc, one, two, cb, last = extras
    last = jnp.pad(last[:, None, :], ((0, 0), (0, 7), (0, 0)))
    grad_tail, lines_bc, head_sums = finish(
        raw, table_bc, head_rows, prep, gb, gc, one, two, cb, last, slot
    )
    g_tail = dot_tn(normed, grad_tail)[:, :tail].astype(BF)
    sum_tail = halving_sum(g_tail, order, shards, groups)

    grad_normed = dot_nt(grad_z, w_z) + dot_nt(grad_tail, w_tail)
    span = inner // len(cuts)
    for i, grad_x in enumerate(grad_xs):
        grad_normed = grad_normed + dot_nt(grad_x, w_x[:, i * span : (i + 1) * span])
    rows_norm = hidden * inv_first
    g_pre = jnp.sum(grad_normed * rows_norm, axis=0)
    scaled_grad = grad_normed * pre_all
    inside = jnp.mean(scaled_grad * rows_norm, axis=-1, keepdims=True)
    grad_input = inv_first * (scaled_grad - rows_norm * inside) + grad_branch
    layer_out = mask * (hidden + dot_nn(gate_low, w_out))

    lines = jnp.concatenate(line_parts + [jnp.sum(lines_bc, axis=0)], axis=1)
    head_sum = jnp.sum(head_sums, axis=0)
    skip_sum = lines[5, :inner].reshape(heads, -1).sum(axis=1)
    vector = jnp.concatenate(
        [
            g_pre,
            jnp.sum(gain_sum, axis=0),
            lines[:5].reshape(-1),
            head_sum[0, :heads],
            head_sum[1, :heads],
            skip_sum,
        ]
    )
    vector = lax.psum(vector, ("group", "shard"))
    place = lax.axis_index("shard")
    at = 0
    g_pre = lax.dynamic_slice_in_dim(vector, at + place * part, part)
    at += width
    g_gate = lax.dynamic_slice_in_dim(vector, at + place * sizes[1], sizes[1])
    at += inner
    g_lines = vector[at : at + 5 * channels].reshape(5, channels)
    g_lines = lax.dynamic_slice_in_dim(g_lines, place * sizes[2], sizes[2], axis=1)
    at += 5 * channels
    g_heads = vector[at : at + 3 * heads].reshape(3, heads)

    g_in = jnp.concatenate([sum_z] + sums_x + [sum_tail], axis=1)
    return (
        layer_out.reshape(hidden_in.shape),
        grad_input.reshape(hidden_in.shape),
        g_pre,
        g_in,
        g_lines[:4],
        g_lines[4],
        g_heads,
        g_gate,
        sum_out,
    )


def solution(mesh):
    rows = P(None, ("group", "shard"), None, None)
    in_specs = (
        rows,
        P(None, ("group", "shard")),
        P("shard"),
        P("shard", None),
        P(None, "shard"),
        P("shard"),
        P(),
        P("shard"),
        P("shard", None),
        rows,
    )
    out_specs = (
        rows,
        rows,
        P("shard"),
        P("shard", None),
        P(None, "shard"),
        P("shard"),
        P(),
        P("shard"),
        P("shard", None),
    )
    body = functools.partial(local, mesh.shape["shard"], mesh.shape["group"])
    return jax.shard_map(body, mesh=mesh, in_specs=in_specs, out_specs=out_specs, check_vma=False)
```

```python
import functools

import jax
import jax.numpy as jnp
from jax import lax
from jax.experimental import pallas as pl
from jax.experimental.pallas import tpu as pltpu
from jax.sharding import PartitionSpec as P

STRETCH = 256
HALF = 128
LANES = 128
GROUP_HEADS = 4
EPS = 1e-05
BF = jnp.bfloat16
F32 = jnp.float32
VMEM_BYTES = 56 * 1024 * 1024


def params(**kwargs):
    return pltpu.CompilerParams(vmem_limit_bytes=VMEM_BYTES, **kwargs)


def cost(seconds):
    return pl.CostEstimate(
        flops=int(seconds * 2.0e13), bytes_accessed=int(seconds * 6.0e10), transcendentals=0
    )


def dot_nn(left, right):
    return lax.dot_general(left, right, (((1,), (0,)), ((), ())), preferred_element_type=F32)


def dot_nt(left, right):
    return lax.dot_general(left, right, (((1,), (1,)), ((), ())), preferred_element_type=F32)


def dot_tn(left, right):
    return lax.dot_general(left, right, (((0,), (0,)), ((), ())), preferred_element_type=F32)


def sigmoid(values):
    return 1.0 / (1.0 + jnp.exp(-values))


def row_index(values):
    return lax.broadcasted_iota(jnp.int32, (values.shape[0], 1), 0)


def shift_down(values, count):
    rolled = pltpu.roll(values, count, 0)
    return jnp.where(row_index(values) >= count, rolled, 0.0)


def shift_up(values, count):
    rows = values.shape[0]
    rolled = pltpu.roll(values, rows - count, 0)
    return jnp.where(row_index(values) < rows - count, rolled, 0.0)


def conv_parts(values, taps_ref):
    shifted = [shift_down(values, 3), shift_down(values, 2), shift_down(values, 1), values]
    pre = taps_ref[4:5, :]
    for k in range(4):
        pre = pre + taps_ref[k : k + 1, :] * shifted[k]
    return shifted, pre


def conv_back(grad_pre, taps_ref):
    total = taps_ref[3:4, :] * grad_pre
    for k in range(3):
        total = total + taps_ref[k : k + 1, :] * shift_up(grad_pre, 3 - k)
    return total


def column_sum(values):
    return jnp.sum(values, axis=0, keepdims=True)


def prepare_kernel(raw_ref, taps_ref, heads_ref, b_ref, c_ref, bt_ref, ct_ref, dt_ref, cum_ref, cumt_ref):
    _, pre = conv_parts(raw_ref[:, : 2 * LANES], taps_ref)
    active = pre * sigmoid(pre)
    b_part, c_part = active[:, :LANES], active[:, LANES:]
    b_ref[...] = b_part.astype(BF)
    c_ref[...] = c_part.astype(BF)
    bt_ref[...] = b_part.T.astype(BF)
    ct_ref[...] = c_part.T.astype(BF)
    raw = raw_ref[:, 2 * LANES :] + heads_ref[0:1, :]
    dt = jnp.maximum(raw, 0.0) + jnp.log1p(jnp.exp(-jnp.abs(raw)))
    cum = dt * heads_ref[1:2, :]
    place = row_index(cum) % STRETCH
    step = 1
    while step < STRETCH:
        cum = cum + jnp.where(place >= step, pltpu.roll(cum, step, 0), 0.0)
        step *= 2
    dt_ref[...] = dt
    cum_ref[...] = cum
    cumt_ref[...] = cum.T


def prepare(raw, taps, heads, slot):
    rows = raw.shape[0]
    tall = pl.BlockSpec((slot, LANES), lambda q: (q, 0))
    wide = pl.BlockSpec((LANES, slot), lambda q: (0, q))
    return pl.pallas_call(
        prepare_kernel,
        grid=(rows // slot,),
        in_specs=[
            pl.BlockSpec((slot, 3 * LANES), lambda q: (q, 0)),
            pl.BlockSpec((8, 2 * LANES), lambda q: (0, 0)),
            pl.BlockSpec((8, LANES), lambda q: (0, 0)),
        ],
        out_specs=[tall, tall, wide, wide, tall, tall, wide],
        out_shape=[
            jax.ShapeDtypeStruct((rows, LANES), BF),
            jax.ShapeDtypeStruct((rows, LANES), BF),
            jax.ShapeDtypeStruct((LANES, rows), BF),
            jax.ShapeDtypeStruct((LANES, rows), BF),
            jax.ShapeDtypeStruct((rows, LANES), F32),
            jax.ShapeDtypeStruct((rows, LANES), F32),
            jax.ShapeDtypeStruct((LANES, rows), F32),
        ],
        compiler_params=params(),
        name="prepare",
    )(raw, taps, heads)


def head_tables(cum_ref, dt_ref, first_head):
    shift = lax.rem(LANES - first_head, LANES)
    cum = pltpu.roll(cum_ref[...], shift, 1)
    dt = pltpu.roll(dt_ref[...], shift, 1)
    rows = cum.shape[0]
    cum_wide = [jnp.broadcast_to(cum[:, i : i + 1], (rows, LANES)) for i in range(GROUP_HEADS)]
    dt_wide = [jnp.broadcast_to(dt[:, i : i + 1], (rows, LANES)) for i in range(GROUP_HEADS)]
    left = lax.broadcasted_iota(jnp.int32, (1, LANES), 1) < LANES // 2

    def spread(wide):
        return jnp.concatenate(
            [jnp.where(left, wide[i], wide[i + 1]) for i in range(0, GROUP_HEADS, 2)], axis=1
        )

    return cum_wide, spread(cum_wide), spread(dt_wide), left


def decay_tiles(cum_wide, cumt_row, block, lower):
    begin = block * STRETCH
    top = cum_wide[begin : begin + HALF]
    low = cum_wide[begin + HALF : begin + STRETCH]
    row_left = cumt_row[:, begin : begin + HALF]
    row_right = cumt_row[:, begin + HALF : begin + STRETCH]
    first = jnp.where(lower, jnp.exp(top - row_left), 0.0)
    second = jnp.exp(low - row_left)
    third = jnp.where(lower, jnp.exp(low - row_right), 0.0)
    return first, jnp.concatenate([second, third], axis=1)


def join_tiles(first, below):
    return jnp.concatenate(
        [jnp.concatenate([first, jnp.zeros_like(first)], axis=1), below], axis=0
    )


def lower_mask():
    return lax.broadcasted_iota(jnp.int32, (HALF, HALF), 0) >= lax.broadcasted_iota(
        jnp.int32, (HALF, HALF), 1
    )


def forward_kernel(
    group_start, x_ref, taps_ref, b_ref, c_ref, bt_ref, dt_ref, cum_ref, cumt_ref, y_ref
):
    first_head = (pl.program_id(1) + group_start) * GROUP_HEADS
    _, pre = conv_parts(x_ref[...], taps_ref)
    x_low = (pre * sigmoid(pre)).astype(BF).astype(F32)
    cum_wide, cum_x, dt_x, left = head_tables(cum_ref, dt_ref, first_head)
    x_dt = (x_low * dt_x).astype(BF)
    skipped = taps_ref[5:6, :] * x_low
    fade = jnp.exp(cum_x[STRETCH - 1 : STRETCH] - cum_x[:STRETCH])
    scaled = (x_low[:STRETCH] * (fade * dt_x[:STRETCH])).astype(BF)
    state = dot_nn(bt_ref[:, :STRETCH], scaled).astype(BF)
    inter = jnp.exp(cum_x[STRETCH:]) * dot_nn(c_ref[STRETCH:, :], state)
    lower = lower_mask()
    zero = jnp.zeros((STRETCH, LANES), BF)
    for block in range(2):
        rows = slice(block * STRETCH, (block + 1) * STRETCH)
        cb = dot_nt(c_ref[rows, :], b_ref[rows, :])
        for pair in range(GROUP_HEADS // 2):
            lanes = slice(pair * LANES, (pair + 1) * LANES)
            x_pair = x_dt[rows, lanes]
            total = skipped[rows, lanes]
            if block == 1:
                total = total + inter[:, lanes]
            for side in range(2):
                head = 2 * pair + side
                row = cumt_ref[pl.ds(first_head + head, 1), :]
                first, below = decay_tiles(cum_wide[head], row, block, lower)
                mixing = join_tiles(
                    (cb[:HALF, :HALF] * first).astype(BF), (cb[HALF:, :] * below).astype(BF)
                )
                keep = left if side == 0 else jnp.logical_not(left)
                total = total + dot_nn(mixing, jnp.where(keep, x_pair, zero))
            y_ref[rows, lanes] = total


def scan_forward(px, offset, taps, prep, slot, start, count):
    b_low, c_low, b_t, _, dt, cum, cum_t = prep
    rows = px.shape[0]
    width = GROUP_HEADS * 64
    tall = pl.BlockSpec((slot, LANES), lambda q, h: (q, 0))
    wide = pl.BlockSpec((LANES, slot), lambda q, h: (0, q))
    tile = pl.BlockSpec((slot, width), lambda q, h: (q, h))
    return pl.pallas_call(
        functools.partial(forward_kernel, start),
        grid=(rows // slot, count),
        in_specs=[
            pl.BlockSpec((slot, width), lambda q, h: (q, h + offset)),
            pl.BlockSpec((8, width), lambda q, h: (0, h + start)),
            tall,
            tall,
            wide,
            tall,
            tall,
            wide,
        ],
        out_specs=tile,
        out_shape=jax.ShapeDtypeStruct((rows, count * width), F32),
        compiler_params=params(),
        cost_estimate=cost(3.3e-6 * count),
        name="scan_forward",
    )(px, taps, b_low, c_low, b_t, dt, cum, cum_t)


def gate_kernel(count, *refs):
    y_refs = refs[:count]
    z_ref, gain_ref, gate_ref, inv_ref = refs[count:]
    y = jnp.concatenate([ref[...] for ref in y_refs], axis=1)
    z = z_ref[...]
    gated = y * (z * sigmoid(z))
    mean = jnp.sum(gated * gated, axis=1, keepdims=True) * (1.0 / gated.shape[1])
    inv = lax.rsqrt(mean + EPS)
    gate_ref[...] = (gated * inv * gain_ref[...]).astype(BF)
    inv_ref[...] = jnp.broadcast_to(inv, inv_ref.shape)


def row_tile(size, array):
    return pl.BlockSpec((size, array.shape[1]), lambda t: (t, 0))


def gate_forward(y_parts, pz, gain):
    rows, inner = pz.shape
    size = 128
    tile = pl.BlockSpec((size, inner), lambda t: (t, 0))
    return pl.pallas_call(
        functools.partial(gate_kernel, len(y_parts)),
        grid=(rows // size,),
        in_specs=[row_tile(size, y) for y in y_parts]
        + [tile, pl.BlockSpec((1, inner), lambda t: (0, 0))],
        out_specs=[tile, pl.BlockSpec((size, LANES), lambda t: (t, 0))],
        out_shape=[
            jax.ShapeDtypeStruct((rows, inner), BF),
            jax.ShapeDtypeStruct((rows, LANES), F32),
        ],
        compiler_params=params(),
        cost_estimate=cost(15e-6),
        name="gate_forward",
    )(*y_parts, pz, gain)


def gate_back_kernel(count, *refs):
    y_refs = refs[:count]
    z_ref, grad_ref, inv_ref, gain_ref, gy_ref, gz_ref, gain_sum_ref = refs[count:]
    y = jnp.concatenate([ref[...] for ref in y_refs], axis=1)
    z = z_ref[...]
    grad = grad_ref[...]
    inv = inv_ref[:, 0:1]
    sig = sigmoid(z)
    silu = z * sig
    normal = y * silu * inv
    grad_normal = grad * gain_ref[...]
    mean = jnp.sum(grad_normal * normal, axis=1, keepdims=True) * (1.0 / y.shape[1])
    gated = inv * (grad_normal - normal * mean)
    gy_ref[...] = (gated * silu).astype(BF)
    gz_ref[...] = (gated * y * (sig + silu * (1.0 - sig))).astype(BF)
    part = grad * normal
    folded = part[0:8]
    for start in range(8, part.shape[0], 8):
        folded = folded + part[start : start + 8]

    @pl.when(pl.program_id(0) == 0)
    def _():
        gain_sum_ref[...] = folded

    @pl.when(pl.program_id(0) > 0)
    def _():
        gain_sum_ref[...] += folded


def gate_backward(y_parts, pz, grad_gate, inv, gain):
    rows, inner = pz.shape
    size = 128
    tile = pl.BlockSpec((size, inner), lambda t: (t, 0))
    return pl.pallas_call(
        functools.partial(gate_back_kernel, len(y_parts)),
        grid=(rows // size,),
        in_specs=[row_tile(size, y) for y in y_parts]
        + [
            tile,
            tile,
            pl.BlockSpec((size, LANES), lambda t: (t, 0)),
            pl.BlockSpec((1, inner), lambda t: (0, 0)),
        ],
        out_specs=[tile, tile, pl.BlockSpec((8, inner), lambda t: (0, 0))],
        out_shape=[
            jax.ShapeDtypeStruct((rows, inner), BF),
            jax.ShapeDtypeStruct((rows, inner), BF),
            jax.ShapeDtypeStruct((8, inner), F32),
        ],
        compiler_params=params(),
        cost_estimate=cost(24e-6),
        name="gate_backward",
    )(*y_parts, pz, grad_gate, inv, gain)


def head_sums(product, spread):
    high = product.astype(BF)
    low = (product - high.astype(F32)).astype(BF)
    return dot_nn(high, spread) + dot_nn(low, spread)


def backward_kernel(group_start, *refs):
    x_ref, taps_ref, y_ref, gy_ref, b_ref, c_ref, bt_ref, ct_ref = refs[:8]
    dt_ref, cum_ref, cumt_ref = refs[8:11]
    gx_ref, lines_ref, *totals = refs[-8:]
    gb_ref, gc_ref, one_ref, two_ref, cb_ref, heads_ref = totals
    befores = refs[12:-8]
    first_head = (pl.program_id(0) + group_start) * GROUP_HEADS
    seq = pl.program_id(1)
    slot = x_ref.shape[0]

    @pl.when((pl.program_id(0) == 0) & (seq == 0))
    def _():
        for i, total in enumerate(totals):
            total[...] = befores[i][...] if befores else jnp.zeros_like(total)

    at = pl.multiple_of(seq * slot, slot)
    whole_rows = pl.ds(at, slot)
    early_rows = pl.ds(at, STRETCH)
    late_rows = pl.ds(pl.multiple_of(at + STRETCH, STRETCH), STRETCH)
    shifted, pre = conv_parts(x_ref[...], taps_ref)
    sig = sigmoid(pre)
    active = pre * sig
    slope = sig + active * (1.0 - sig)
    x_low = active.astype(BF).astype(F32)
    gy_low = gy_ref[...]
    gy = gy_low.astype(F32)
    cum_wide, cum_x, dt_x, left = head_tables(cum_ref, dt_ref, first_head)
    x_dt = (x_low * dt_x).astype(BF)
    skip = taps_ref[5:6, :]

    grad_inter = (gy[STRETCH:] * jnp.exp(cum_x[STRETCH:])).astype(BF)
    fade = jnp.exp(cum_x[STRETCH - 1 : STRETCH] - cum_x[:STRETCH])
    scaled = (x_low[:STRETCH] * (fade * dt_x[:STRETCH])).astype(BF)
    state = dot_nn(bt_ref[:, :STRETCH], scaled)
    gc_ref[late_rows, :] += dot_nt(grad_inter, state.astype(BF))
    grad_state = dot_nn(ct_ref[:, STRETCH:], grad_inter).astype(BF)
    gb_ref[early_rows, :] += dot_nt(scaled, grad_state)
    grad_scaled = dot_nn(b_ref[:STRETCH, :], grad_state)
    last_sum = column_sum(grad_state.astype(F32) * state)

    lower = lower_mask()
    zero = jnp.zeros((STRETCH, LANES), BF)
    rest = []
    for block in range(2):
        rows = slice(block * STRETCH, (block + 1) * STRETCH)
        cb = dot_nt(c_ref[rows, :], b_ref[rows, :])
        cb_first = cb_below = None
        parts = []
        for pair in range(GROUP_HEADS // 2):
            lanes = slice(pair * LANES, (pair + 1) * LANES)
            x_pair = x_dt[rows, lanes]
            gy_pair = gy_low[rows, lanes]
            total = None
            for side in range(2):
                head = 2 * pair + side
                row = cumt_ref[pl.ds(first_head + head, 1), :]
                first, below = decay_tiles(cum_wide[head], row, block, lower)
                mixing = join_tiles(
                    (cb[:HALF, :HALF] * first).astype(BF), (cb[HALF:, :] * below).astype(BF)
                )
                keep = left if side == 0 else jnp.logical_not(left)
                gy_head = jnp.where(keep, gy_pair, zero)
                mix_first = dot_nt(gy_head[:HALF], x_pair[:HALF]) * first
                mix_below = dot_nt(gy_head[HALF:], x_pair) * below
                cb_first = mix_first if cb_first is None else cb_first + mix_first
                cb_below = mix_below if cb_below is None else cb_below + mix_below
                now = dot_tn(mixing, gy_head)
                total = now if total is None else total + now
            parts.append(total)
        cb_ref[seq, block, :HALF, :HALF] += cb_first
        cb_ref[seq, block, HALF:, :] += cb_below
        rest.append(jnp.concatenate(parts, axis=1))
    moved = x_dt.astype(F32) * jnp.concatenate(rest, axis=0)
    moved = jnp.concatenate(
        [moved[:STRETCH] + scaled.astype(F32) * grad_scaled, moved[STRETCH:]], axis=0
    )
    rest[0] = rest[0] + fade * grad_scaled
    grad_pull = jnp.concatenate(rest, axis=0)

    width = x_low.shape[1]
    spread = (
        lax.broadcasted_iota(jnp.int32, (width, LANES), 1)
        == first_head + lax.broadcasted_iota(jnp.int32, (width, LANES), 0) // 64
    ).astype(F32).astype(BF)
    moved = gy * (y_ref[...] - skip * x_low) - moved
    edge = lax.broadcasted_iota(jnp.int32, (8, 1), 0) == 7
    moved = jnp.concatenate(
        [
            moved[: STRETCH - 8],
            moved[STRETCH - 8 : STRETCH] + jnp.where(edge, last_sum, 0.0),
            moved[STRETCH:],
        ],
        axis=0,
    )
    one_ref[whole_rows, :] += head_sums(moved, spread)
    two_ref[whole_rows, :] += head_sums(x_low * grad_pull, spread)
    third = lax.broadcasted_iota(jnp.int32, (8, 1), 0) == 2
    skip_line = jnp.where(third, column_sum(gy * x_low), 0.0)
    heads_ref[...] += head_sums(skip_line, spread)

    grad_pre = (skip * gy + dt_x * grad_pull) * slope
    gx_ref[...] = conv_back(grad_pre, taps_ref).astype(BF)
    lines = [column_sum(grad_pre * shifted[k]) for k in range(4)] + [column_sum(grad_pre)]
    lines = jnp.concatenate(lines + [jnp.zeros((3, width), F32)], axis=0)

    @pl.when(seq == 0)
    def _():
        lines_ref[...] = lines

    @pl.when(seq > 0)
    def _():
        lines_ref[...] += lines


def scan_backward(px, at, taps, y_rows, y_at, grad_y, prep, slot, start, count, before=None):
    b_low, c_low, b_t, c_t, dt, cum, cum_t = prep
    rows = px.shape[0]
    width = GROUP_HEADS * 64
    seqs = rows // slot
    tall = pl.BlockSpec((slot, LANES), lambda h, q: (q, 0))
    wide = pl.BlockSpec((LANES, slot), lambda h, q: (0, q))
    tile = pl.BlockSpec((slot, width), lambda h, q: (q, h + at))
    flat = jax.ShapeDtypeStruct((rows, LANES), F32)
    whole = pl.BlockSpec((rows, LANES), lambda h, q: (0, 0))
    totals = [whole] * 4 + [
        pl.BlockSpec((seqs, 2, STRETCH, STRETCH), lambda h, q: (0, 0, 0, 0)),
        pl.BlockSpec((8, LANES), lambda h, q: (0, 0)),
    ]
    extra, extra_specs, aliases = [jnp.zeros((8, LANES), BF)], [pl.BlockSpec(memory_space=pl.ANY)], {}
    if before is not None:
        if before[0].shape == px.shape:
            extra = [before[0]]
            aliases[11] = 0
        extra = extra + list(before[2:])
        extra_specs = extra_specs + totals
        aliases.update({12 + i: 2 + i for i in range(6)})
    return pl.pallas_call(
        functools.partial(backward_kernel, start),
        grid=(count, seqs),
        in_specs=[
            tile,
            pl.BlockSpec((8, width), lambda h, q: (0, h + start)),
            pl.BlockSpec((slot, width), lambda h, q: (q, h + y_at)),
            pl.BlockSpec((slot, width), lambda h, q: (q, h + start)),
            tall,
            tall,
            wide,
            wide,
            tall,
            tall,
            wide,
        ]
        + extra_specs,
        out_specs=[tile, pl.BlockSpec((8, width), lambda h, q: (0, h))] + totals,
        out_shape=[
            jax.ShapeDtypeStruct(px.shape, BF),
            jax.ShapeDtypeStruct((8, count * width), F32),
            flat,
            flat,
            flat,
            flat,
            jax.ShapeDtypeStruct((seqs, 2, STRETCH, STRETCH), F32),
            jax.ShapeDtypeStruct((8, LANES), F32),
        ],
        input_output_aliases=aliases,
        compiler_params=params(),
        cost_estimate=cost(3.3e-6 * count),
        name="scan_backward",
    )(px, taps, y_rows, grad_y, b_low, c_low, b_t, c_t, dt, cum, cum_t, *extra)


def finish_kernel(
    raw_ref,
    taps_ref,
    heads_ref,
    b_ref,
    c_ref,
    dt_ref,
    gb_ref,
    gc_ref,
    one_ref,
    two_ref,
    cb_ref,
    head_before_ref,
    before_ref,
    out_ref,
    lines_ref,
    head_total_ref,
):
    @pl.when(pl.program_id(0) == 0)
    def _():
        lines_ref[...] = jnp.zeros_like(lines_ref)
        head_total_ref[...] = head_before_ref[...]

    shifted, pre = conv_parts(raw_ref[:, : 2 * LANES], taps_ref)
    sig = sigmoid(pre)
    slope = sig + pre * sig * (1.0 - sig)
    grad_b, grad_c = [], []
    for block in range(2):
        rows = slice(block * STRETCH, (block + 1) * STRETCH)
        cb = cb_ref[0, block].astype(BF)
        grad_c.append(gc_ref[rows, :] + dot_nn(cb, b_ref[rows, :]))
        grad_b.append(gb_ref[rows, :] + dot_tn(cb, c_ref[rows, :]))
    grad_active = jnp.concatenate(
        [jnp.concatenate(grad_b, axis=0), jnp.concatenate(grad_c, axis=0)], axis=1
    )
    grad_pre = grad_active * slope
    lines = [column_sum(grad_pre * shifted[k]) for k in range(4)] + [column_sum(grad_pre)]
    lines.append(jnp.zeros((3, 2 * LANES), F32))
    lines_ref[...] += jnp.concatenate(lines, axis=0)

    dt = dt_ref[...]
    two = two_ref[...]
    rate = heads_ref[1:2, :]
    place = row_index(dt)
    grad_cum = one_ref[...]
    inside = place % STRETCH
    step = 1
    while step < STRETCH:
        moved = pltpu.roll(grad_cum, grad_cum.shape[0] - step, 0)
        grad_cum = grad_cum + jnp.where(inside < STRETCH - step, moved, 0.0)
        step *= 2
    grad_dt = grad_cum * rate + two
    grad_raw = grad_dt * sigmoid(raw_ref[:, 2 * LANES : 3 * LANES] + heads_ref[0:1, :])
    head_total_ref[...] += jnp.concatenate(
        [column_sum(grad_raw), column_sum(grad_cum * dt) * rate, jnp.zeros((6, LANES), F32)], axis=0
    )
    out_ref[:, : 2 * LANES] = conv_back(grad_pre, taps_ref).astype(BF)
    out_ref[:, 2 * LANES : 3 * LANES] = grad_raw.astype(BF)
    out_ref[:, 3 * LANES :] = jnp.zeros_like(out_ref[:, 3 * LANES :])


def finish(raw, taps, heads, prep, totals, grads, narrow, slot):
    b_low, c_low, _, _, dt, _, _ = prep
    rows = raw.shape[0]
    seqs = rows // slot
    tall = pl.BlockSpec((slot, LANES), lambda q: (q, 0))
    return pl.pallas_call(
        finish_kernel,
        grid=(seqs,),
        in_specs=[
            pl.BlockSpec((slot, 3 * LANES), lambda q: (q, 0)),
            pl.BlockSpec((8, 2 * LANES), lambda q: (0, 0)),
            pl.BlockSpec((8, LANES), lambda q: (0, 0)),
            tall,
            tall,
            tall,
            tall,
            tall,
            tall,
            tall,
            pl.BlockSpec((1, 2, STRETCH, STRETCH), lambda q: (q, 0, 0, 0)),
            pl.BlockSpec((8, LANES), lambda q: (0, 0)),
            pl.BlockSpec(memory_space=pl.ANY),
        ],
        out_specs=[
            pl.BlockSpec((slot, narrow), lambda q: (q, 0)),
            pl.BlockSpec((8, 2 * LANES), lambda q: (0, 0)),
            pl.BlockSpec((8, LANES), lambda q: (0, 0)),
        ],
        out_shape=[
            jax.ShapeDtypeStruct(grads.shape, BF),
            jax.ShapeDtypeStruct((8, 2 * LANES), F32),
            jax.ShapeDtypeStruct((8, LANES), F32),
        ],
        input_output_aliases={12: 0},
        compiler_params=params(),
        cost_estimate=cost(3e-6),
        name="finish",
    )(raw, taps, heads, b_low, c_low, dt, *totals, grads)


def project_kernel(mine_ref, other_ref, w_mine_ref, w_other_ref, out_ref):
    out_ref[...] = dot_tn(mine_ref[...], w_mine_ref[...]) + dot_tn(
        other_ref[...], w_other_ref[...]
    )


def project(mine, other, w_mine, w_other, size):
    depth, rows = mine.shape
    columns = w_mine.shape[1]
    whole = pl.BlockSpec((depth, rows), lambda j: (0, 0))
    tile = pl.BlockSpec((depth, size), lambda j: (0, j))
    return pl.pallas_call(
        project_kernel,
        grid=(columns // size,),
        in_specs=[whole, whole, tile, tile],
        out_specs=pl.BlockSpec((rows, size), lambda j: (0, j)),
        out_shape=jax.ShapeDtypeStruct((rows, columns), F32),
        compiler_params=params(),
        cost_estimate=cost(4 * depth * rows * columns / 6.5e14),
        name="project",
    )(mine, other, w_mine, w_other)


def pair_kernel(mine_ref, other_ref, grad_ref, keep_ref, give_ref):
    grad = grad_ref[...]
    give_ref[...] = dot_nn(other_ref[...], grad).astype(give_ref.dtype)
    keep_ref[...] = dot_nn(mine_ref[...], grad).astype(keep_ref.dtype)


def weight_grads(mine, other, grad, size, dtype):
    depth, rows = mine.shape
    columns = grad.shape[1]
    whole = pl.BlockSpec((depth, rows), lambda j: (0, 0))
    tile = pl.BlockSpec((depth, size), lambda j: (0, j))
    shape = jax.ShapeDtypeStruct((depth, columns), dtype)
    return pl.pallas_call(
        pair_kernel,
        grid=(columns // size,),
        in_specs=[whole, whole, pl.BlockSpec((rows, size), lambda j: (0, j))],
        out_specs=[tile, tile],
        out_shape=[shape, shape],
        compiler_params=params(),
        cost_estimate=cost(4 * depth * rows * columns / 6.5e14),
        name="weight_grads",
    )(mine, other, grad)


def out_grads_kernel(part, core_ref, gate_ref, grad_ref, keep_ref, give_ref):
    product = dot_tn(gate_ref[...], grad_ref[...]).astype(BF)
    chips = keep_ref.shape[0]
    for chip in range(chips):
        first = product[2 * chip * part : (2 * chip + 1) * part]
        second = product[(2 * chip + 1) * part : (2 * chip + 2) * part]

        @pl.when(core_ref[0] == 0)
        def _():
            keep_ref[chip] = first
            give_ref[chip] = second

        @pl.when(core_ref[0] == 1)
        def _():
            keep_ref[chip] = second
            give_ref[chip] = first


def out_grads(core, gate_low, grad_low, part):
    rows, inner = gate_low.shape
    width = grad_low.shape[1]
    chips = inner // (2 * part)
    each = 1
    while each * 2 * part % LANES:
        each *= 2
    tile = pl.BlockSpec((each, part, width), lambda j: (j, 0, 0))
    shape = jax.ShapeDtypeStruct((chips, part, width), BF)
    return pl.pallas_call(
        functools.partial(out_grads_kernel, part),
        grid=(chips // each,),
        in_specs=[
            pl.BlockSpec(memory_space=pltpu.SMEM),
            pl.BlockSpec((rows, each * 2 * part), lambda j: (0, j)),
            pl.BlockSpec((rows, width), lambda j: (0, 0)),
        ],
        out_specs=[tile, tile],
        out_shape=[shape, shape],
        compiler_params=params(),
        cost_estimate=cost(15e-6),
        name="out_grads",
    )(core, gate_low, grad_low)


def interleave(weight_ref, mine_ref, other_ref, core_ref, part):
    for at in range(mine_ref.shape[0] // part):
        rows = slice(at * part, (at + 1) * part)
        low = slice(2 * at * part, (2 * at + 1) * part)
        high = slice((2 * at + 1) * part, (2 * at + 2) * part)

        @pl.when(core_ref[0] == 0)
        def _():
            weight_ref[low, :] = mine_ref[rows, :]
            weight_ref[high, :] = other_ref[rows, :]

        @pl.when(core_ref[0] == 1)
        def _():
            weight_ref[low, :] = other_ref[rows, :]
            weight_ref[high, :] = mine_ref[rows, :]


def input_grads_kernel(sizes, part, first_refs, final, core_ref, *refs):
    count = len(sizes)
    triples = [refs[3 * i : 3 * i + 3] for i in range(count)]
    refs = refs[3 * count :]
    steps = sum(sizes)
    step = pl.program_id(0)
    if first_refs:
        before_ref, refs = refs[0], refs[1:]
    if final:
        hidden_ref, inv_ref, gain_ref, mask_ref, cot_ref, out_ref, line_ref, total, weight = refs
    else:
        total, weight = refs
    begin = 0
    for (grad_ref, mine_ref, other_ref), size in zip(triples, sizes):

        @pl.when((step >= begin) & (step < begin + size))
        def _():
            interleave(weight, mine_ref, other_ref, core_ref, part)

        begin += size
    begin = 0
    for (grad_ref, mine_ref, other_ref), size in zip(triples, sizes):

        @pl.when((step >= begin) & (step < begin + size))
        def _(begin=begin, grad_ref=grad_ref):
            now = dot_nt(grad_ref[...], weight[...])
            if begin == 0:

                @pl.when(step == 0)
                def _():
                    total[...] = now + before_ref[...] if first_refs else now

                @pl.when(step > 0)
                def _():
                    total[...] += now

            else:
                total[...] += now

        begin += size
    if final:

        @pl.when(step == 0)
        def _():
            line_ref[...] = jnp.zeros_like(line_ref)

        @pl.when(step >= steps)
        def _():
            tile = hidden_ref.shape[0]
            grad = total[pl.ds(pl.multiple_of((step - steps) * tile, tile), tile), :]
            inv = inv_ref[...]
            normal = hidden_ref[...] * inv
            product = grad * normal
            folded = product[0:8]
            for start in range(8, tile, 8):
                folded = folded + product[start : start + 8]
            line_ref[...] += folded
            inside = jnp.sum(product * gain_ref[...], axis=1, keepdims=True) * (1.0 / grad.shape[1])
            out_ref[...] = inv * (grad * gain_ref[...] - normal * inside) + mask_ref[...] * cot_ref[...]


def input_grads(core, grads, mines, others, part, before=None, final=None):
    rows = grads[0].shape[0]
    depth = mines[0].shape[0]
    width = 2 * depth
    size, tile = 512, 128
    sizes = [g.shape[1] // size for g in grads]
    steps = sum(sizes)
    in_specs, args, begin = [pl.BlockSpec(memory_space=pltpu.SMEM)], [core], 0
    for grad, mine, other, count in zip(grads, mines, others, sizes):

        def place(k, begin=begin, count=count):
            return (0, jnp.clip(k - begin, 0, count - 1))

        in_specs += [pl.BlockSpec((rows, size), place)] + [pl.BlockSpec((depth, size), place)] * 2
        args += [grad, mine, other]
        begin += count
    if before is not None:
        in_specs.append(pl.BlockSpec((rows, width), lambda k: (0, 0), pipeline_mode=pl.Buffered(1)))
        args.append(before)
    scratch = [pltpu.VMEM((width, size), BF)]
    if final:

        def row(k):
            return (jnp.clip(k - steps, 0, rows // tile - 1), 0)

        line = pl.BlockSpec((1, width), lambda k: (0, 0))
        column = pl.BlockSpec((tile, 1), row)
        wide = pl.BlockSpec((tile, width), row)
        in_specs += [wide, column, line, column, wide]
        args += list(final)
        out_specs = [wide, pl.BlockSpec((8, width), lambda k: (0, 0))]
        out_shape = [
            jax.ShapeDtypeStruct((rows, width), F32),
            jax.ShapeDtypeStruct((8, width), F32),
        ]
        scratch = [pltpu.VMEM((rows, width), F32)] + scratch
    else:
        out_specs = pl.BlockSpec((rows, width), lambda k: (0, 0))
        out_shape = jax.ShapeDtypeStruct((rows, width), F32)
    return pl.pallas_call(
        functools.partial(input_grads_kernel, sizes, part, before is not None, bool(final)),
        grid=(steps + (rows // tile if final else 0),),
        in_specs=in_specs,
        out_specs=out_specs,
        out_shape=out_shape,
        scratch_shapes=scratch,
        compiler_params=params(),
        cost_estimate=cost(1.3e-6 * steps),
        name="input_grads",
    )(*args)


def swap(values, bit, shards):
    return lax.ppermute(values, "shard", [(i, i ^ (1 << bit)) for i in range(shards)])


def border(moving, *values):
    ready = lax.optimization_barrier(tuple(one.got for one in moving) + values)
    for one, got in zip(moving, ready):
        one.got = got
        one.finish()
    rest = ready[len(moving) :]
    return rest[0] if len(rest) == 1 else rest


class Gather:
    def __init__(self, own, order, shards, place):
        self.now, self.order, self.shards, self.place = own, list(order), shards, place
        self.live, self.columns = [], own.shape[-1]

    def start(self):
        self.bit = self.order.pop(0)
        self.got = swap(self.now, self.bit, self.shards)

    def finish(self):
        mine = (self.place >> self.bit) & 1
        axis = len([b for b in self.live if b > self.bit])
        first = jnp.where(mine == 0, self.now, self.got)
        second = jnp.where(mine == 0, self.got, self.now)
        self.now = jnp.stack([first, second], axis=axis)
        self.live.append(self.bit)

    def whole(self):
        while self.order:
            self.start()
            self.finish()
        return self.now


class Core:
    def __init__(self, gather):
        self.now = gather.now.reshape(-1, gather.columns)
        self.got = swap(self.now, 0, gather.shards)

    def finish(self):
        self.pair = (self.now, self.got)


class Sum:
    def __init__(self, pair, order, shards, groups, place, part, group_first=False):
        self.keep, self.give = pair
        self.shards, self.groups, self.place, self.part = shards, groups, place, part
        self.columns, self.dtype = self.keep.shape[-1], self.keep.dtype
        self.group_first = group_first and groups == 2
        self.todo = [0] + (["group"] if self.group_first else []) + list(order) + ["end"]
        self.live = list(range(shards.bit_length() - 2, 0, -1))
        self.now = None

    def start(self):
        self.bit = bit = self.todo.pop(0)
        if bit == "end":
            pairs = [(i, (i + 1) % self.groups) for i in range(self.groups)]
            self.got = lax.ppermute(self.now, "group", pairs)
        elif bit == "group":
            half = self.columns // 2
            mine = lax.axis_index("group")
            axis = self.now.ndim - 1
            self.keep = lax.dynamic_slice_in_dim(self.now, mine * half, half, axis)
            give = lax.dynamic_slice_in_dim(self.now, (1 - mine) * half, half, axis)
            self.got = lax.ppermute(give, "group", [(0, 1), (1, 0)])
        elif bit == 0:
            self.got = swap(self.give, 0, self.shards)
        else:
            axis = self.live.index(bit)
            mine = (self.place >> bit) & 1
            self.keep = lax.dynamic_index_in_dim(self.now, mine, axis, keepdims=False)
            give = lax.dynamic_index_in_dim(self.now, 1 - mine, axis, keepdims=False)
            self.live.remove(bit)
            self.got = swap(give, bit, self.shards)

    def finish(self):
        if self.bit == "end" and self.group_first:
            first = lax.axis_index("group") == 0
            halves = [jnp.where(first, self.now, self.got), jnp.where(first, self.got, self.now)]
            self.now = jnp.concatenate(halves, axis=-1)
        elif self.bit == "end":
            total, got = self.now.astype(F32), self.got
            for step in range(1, self.groups):
                if step > 1:
                    pairs = [(i, (i + 1) % self.groups) for i in range(self.groups)]
                    got = lax.ppermute(got, "group", pairs)
                total = total + got.astype(F32)
            self.now = total
        else:
            now = self.keep.astype(F32) + self.got.astype(F32)
            if self.todo != ["end"] or not self.group_first:
                now = now.astype(self.dtype)
            if self.bit == 0:
                now = now.reshape((2,) * len(self.live) + (self.part, self.columns))
            self.now = now

    def result(self):
        while self.todo:
            self.start()
            self.finish()
        return self.now


def local(
    shards,
    groups,
    hidden_in,
    lengths,
    pre_gain,
    in_proj,
    conv_weight,
    conv_bias,
    head_params,
    gate_gain,
    out_proj,
    cotangent,
):
    micro, own, slot, width = hidden_in.shape
    rows = micro * own * slot
    inner = out_proj.shape[0] * shards
    channels = conv_bias.shape[0] * shards
    heads = head_params.shape[1]
    tail = channels - inner + heads
    part = in_proj.shape[0]
    out_part = out_proj.shape[0]
    own_conv = conv_bias.shape[0]
    taps = conv_weight.shape[0]
    hidden = hidden_in.reshape(rows, width)
    cot = cotangent.reshape(rows, width)
    place = lax.axis_index("shard")
    core = place & 1
    core_word = core.astype(jnp.int32).reshape(1)
    chip_bits = list(range(1, shards.bit_length() - 1))
    up = chip_bits
    down = chip_bits[::-1]

    unit = GROUP_HEADS * 64
    groups_all = inner // unit
    cuts = [(0, groups_all // 3), (groups_all // 3, groups_all - groups_all // 3)]
    begin = cuts[0][1] * unit
    small = jnp.concatenate([pre_gain, gate_gain, conv_bias, conv_weight.reshape(-1)], axis=0)
    small = small.astype(F32)
    small = jnp.pad(small, (0, -small.shape[0] % LANES))[None, :]
    packed = Gather(small, down + [0], shards, place).whole().reshape(shards, -1)
    narrow = 4 * LANES
    first_own = jnp.concatenate(
        [
            in_proj[:, 2 * inner :],
            jnp.zeros((part, narrow - tail), BF),
            in_proj[:, inner : inner + begin],
        ],
        axis=1,
    )
    gather_a = Gather(first_own, down, shards, place)
    gather_b = Gather(in_proj[:, inner + begin : 2 * inner], down, shards, place)
    gather_z = Gather(in_proj[:, :inner], down, shards, place)

    sizes = (part, out_part, own_conv, taps * own_conv)
    ends = [sum(sizes[: i + 1]) for i in range(4)]
    pre_all = packed[:, : ends[0]].reshape(1, width)
    gate_all = packed[:, ends[0] : ends[1]].reshape(1, inner)
    bias_all = packed[:, ends[1] : ends[2]].reshape(1, channels)
    taps_all = packed[:, ends[2] : ends[3]].reshape(shards, taps, -1)
    taps_all = jnp.swapaxes(taps_all, 0, 1).reshape(taps, channels)
    skip_row = jnp.pad(jnp.repeat(head_params[2], inner // heads), (0, channels - inner))
    table = jnp.concatenate(
        [taps_all, bias_all, skip_row[None, :], jnp.zeros((2, channels), F32)], axis=0
    )
    table_x, table_bc = table[:, :inner], table[:, inner:]
    rate = -jnp.exp(head_params[1])
    head_rows = jnp.pad(
        jnp.stack([head_params[0], rate], axis=0), ((0, 6), (0, LANES - heads))
    )

    inv_first = lax.rsqrt(jnp.mean(hidden * hidden, axis=-1, keepdims=True) + EPS)
    normed = (hidden * inv_first * pre_all).astype(BF)
    turned = normed.T.reshape(shards // 2, 2, part, rows)
    mine = lax.dynamic_index_in_dim(turned, core, 1, keepdims=False).reshape(-1, rows)
    other = lax.dynamic_index_in_dim(turned, 1 - core, 1, keepdims=False).reshape(-1, rows)
    positions = jnp.arange(slot, dtype=jnp.int32)
    mask = (positions[None, :] < lengths.reshape(-1)[:, None]).astype(F32).reshape(rows, 1)
    grad_low = (mask * cot).astype(BF)

    def run_down(gather, left):
        while len(gather.order) > left:
            gather.start()
            border([gather])

    run_down(gather_a, 1)
    gather_b.now = border([], gather_b.now, gather_a.now)[0]
    gather_a.start()
    gather_b.start()
    border([gather_a])
    core_a = Core(gather_a)
    border([gather_b])
    run_down(gather_b, 2)
    gather_b.start()
    mine, other, grad_low = border([core_a], mine, other, grad_low)
    wa_mine, wa_other = core_a.pair

    offset = narrow // unit
    pa = project(mine, other, wa_mine, wa_other, 512)
    prep = prepare(pa, table_bc, head_rows, slot)
    pa, gather_z.now, own_out, *prep = border([gather_b], pa, gather_z.now, out_proj, *prep)
    gather_b.start()
    gather_z.start()
    w_out = lax.all_gather(own_out, "shard", axis=0, tiled=True)
    ya = scan_forward(pa, offset, table_x, prep, slot, *cuts[0])
    ya = border([gather_b, gather_z], ya)
    core_b = Core(gather_b)
    run_down(gather_z, 2)
    gather_z.start()
    mine, other = border([core_b], mine, other)
    wb_mine, wb_other = core_b.pair
    pb = project(mine, other, wb_mine, wb_other, 512)
    pb, mine = border([gather_z], pb, mine)
    gather_z.start()
    yb = scan_forward(pb, 0, table_x, prep, slot, *cuts[1])
    yb, grad_low = border([], yb, grad_low)
    grad_gate = dot_nt(grad_low, w_out)
    grad_gate, mine = border([gather_z], grad_gate, mine)
    core_z = Core(gather_z)
    mine, other = border([core_z], mine, other)
    wz_mine, wz_other = core_z.pair
    pz = project(mine, other, wz_mine, wz_other, 512)
    gate_low, inv = gate_forward([ya, yb], pz, gate_all)

    reduce = functools.partial(Sum, shards=shards, groups=groups, place=place, order=up)
    pair_out = out_grads(core_word, gate_low, grad_low, out_part)
    *pair_out, grad_gate = border([], *pair_out, grad_gate)
    s_out = reduce(pair_out, part=out_part, group_first=True)
    s_out.start()
    grad_y, grad_z, gain_sum = gate_backward([ya, yb], pz, grad_gate, inv, gate_all)
    grad_y, grad_z, mine = border([s_out], grad_y, grad_z, mine)
    s_out.start()
    pair_z = weight_grads(mine, other, grad_z, 512, BF)
    *pair_z, grad_y = border([], *pair_z, grad_y)
    s_z = reduce(pair_z, part=part)
    s_z.start()

    first, count = cuts[1]
    parts = [(first, count // 2), (first + count // 2, count - count // 2)]
    outs_b = scan_backward(pb, 0, table_x, yb, 0, grad_y, prep, slot, *parts[0])
    grad_y, *outs_b = border([s_z], grad_y, *outs_b)
    s_z.start()
    at = parts[0][1]
    outs_c = scan_backward(pb, at, table_x, yb, at, grad_y, prep, slot, *parts[1], before=outs_b)
    grad_y, mine, *outs_c = border([s_out], grad_y, mine, *outs_c)
    s_out.start()
    grad_b = outs_c[0]
    pair_b = weight_grads(mine, other, grad_b, 512, BF)
    *pair_b, grad_y = border([], *pair_b, grad_y)
    s_b = reduce(pair_b, part=part)
    s_b.start()
    outs_a = scan_backward(pa, offset, table_x, ya, 0, grad_y, prep, slot, *cuts[0], before=outs_c)
    mine, *outs_a = border([s_z, s_out, s_b], mine, *outs_a)
    s_z.start()
    s_out.start()
    s_b.start()
    grad_a, lines_bc, head_total = finish(
        pa, table_bc, head_rows, prep, outs_a[2:], outs_a[0], narrow, slot
    )
    pair_a = weight_grads(mine, other, grad_a, 512, BF)
    *pair_a, grad_z = border([s_out], *pair_a, grad_z)
    s_a = reduce(pair_a, part=part)
    s_a.start()
    s_out.start()
    part_sum = input_grads(core_word, [grad_z], [wz_mine], [wz_other], part)
    part_sum, grad_a, grad_b = border([s_z, s_b, s_a, s_out], part_sum, grad_a, grad_b)
    s_a.start()
    s_z.start()
    s_b.start()
    grad_input, pre_lines = input_grads(
        core_word,
        [grad_b, grad_a],
        [wb_mine, wa_mine],
        [wb_other, wa_other],
        part,
        before=part_sum,
        final=(hidden, inv_first, pre_all, mask, cot),
    )
    gate_low, pre_lines = border([s_a, s_z, s_b], gate_low, pre_lines)
    for one in (s_a, s_b, s_z, s_out):
        one.start()
    layer_out = mask * (hidden + dot_nn(gate_low, w_out))

    lines = jnp.concatenate([outs_a[1], outs_b[1], outs_c[1], lines_bc], axis=1)
    gain_line = jnp.sum(gain_sum, axis=0, keepdims=True)
    pre_line = jnp.sum(pre_lines, axis=0, keepdims=True)
    head_line = head_total[:3].reshape(1, 3 * LANES)

    def widen(line):
        return jnp.pad(line, ((0, 0), (0, channels - line.shape[1])))

    vector = jnp.concatenate(
        [lines[:5], widen(pre_line), widen(gain_line), widen(head_line)], axis=0
    )
    for bit in [0] + up:
        vector = vector + swap(vector, bit, shards)
    for _ in range(groups - 1):
        vector = vector + lax.ppermute(vector, "group", [(0, 1), (1, 0)])
    g_lines = lax.dynamic_slice(vector, (0, place * own_conv), (5, own_conv))
    g_pre = lax.dynamic_slice(vector, (5, place * part), (1, part))[0]
    g_gate = lax.dynamic_slice(vector, (6, place * out_part), (1, out_part))[0]
    g_heads = vector[7, : 3 * LANES].reshape(3, LANES)[:, :heads]
    layer_out = border([s_a, s_b, s_z, s_out], layer_out)
    sum_a = s_a.result()
    g_in = jnp.concatenate([s_z.result(), sum_a[:, narrow:], s_b.result(), sum_a[:, :tail]], axis=1)
    return (
        layer_out.reshape(hidden_in.shape),
        grad_input.reshape(hidden_in.shape),
        g_pre,
        g_in,
        g_lines[:4],
        g_lines[4],
        g_heads,
        g_gate,
        s_out.result(),
    )


def solution(mesh):
    rows = P(None, ("group", "shard"), None, None)
    in_specs = (
        rows,
        P(None, ("group", "shard")),
        P("shard"),
        P("shard", None),
        P(None, "shard"),
        P("shard"),
        P(),
        P("shard"),
        P("shard", None),
        rows,
    )
    out_specs = (
        rows,
        rows,
        P("shard"),
        P("shard", None),
        P(None, "shard"),
        P("shard"),
        P(),
        P("shard"),
        P("shard", None),
    )
    body = functools.partial(local, mesh.shape["shard"], mesh.shape["group"])
    return jax.shard_map(body, mesh=mesh, in_specs=in_specs, out_specs=out_specs, check_vma=False)
```

```python
import functools

import jax
import jax.numpy as jnp
from jax import lax
from jax.experimental import pallas as pl
from jax.experimental.pallas import tpu as pltpu
from jax.sharding import PartitionSpec as P

STRETCH = 256
HALF = 128
LANES = 128
GROUP_HEADS = 4
EPS = 1e-05
BF = jnp.bfloat16
F32 = jnp.float32
VMEM_BYTES = 56 * 1024 * 1024


def params(**kwargs):
    return pltpu.CompilerParams(vmem_limit_bytes=VMEM_BYTES, **kwargs)


def cost(seconds):
    return pl.CostEstimate(
        flops=int(seconds * 2.0e13), bytes_accessed=int(seconds * 6.0e10), transcendentals=0
    )


def dot_nn(left, right):
    return lax.dot_general(left, right, (((1,), (0,)), ((), ())), preferred_element_type=F32)


def dot_nt(left, right):
    return lax.dot_general(left, right, (((1,), (1,)), ((), ())), preferred_element_type=F32)


def dot_tn(left, right):
    return lax.dot_general(left, right, (((0,), (0,)), ((), ())), preferred_element_type=F32)


def sigmoid(values):
    return 1.0 / (1.0 + jnp.exp(-values))


def row_index(values):
    return lax.broadcasted_iota(jnp.int32, (values.shape[0], 1), 0)


def shift_down(values, count):
    rolled = pltpu.roll(values, count, 0)
    return jnp.where(row_index(values) >= count, rolled, 0.0)


def shift_up(values, count):
    rows = values.shape[0]
    rolled = pltpu.roll(values, rows - count, 0)
    return jnp.where(row_index(values) < rows - count, rolled, 0.0)


def conv_parts(values, taps_ref):
    shifted = [shift_down(values, 3), shift_down(values, 2), shift_down(values, 1), values]
    pre = taps_ref[4:5, :]
    for k in range(4):
        pre = pre + taps_ref[k : k + 1, :] * shifted[k]
    return shifted, pre


def conv_back(grad_pre, taps_ref):
    total = taps_ref[3:4, :] * grad_pre
    for k in range(3):
        total = total + taps_ref[k : k + 1, :] * shift_up(grad_pre, 3 - k)
    return total


def column_sum(values):
    return jnp.sum(values, axis=0, keepdims=True)


def prepare_kernel(head_count, raw_ref, taps_ref, heads_ref, b_ref, c_ref, bt_ref, ct_ref, dt_ref, cum_ref, cumt_ref):
    _, pre = conv_parts(raw_ref[:, : 2 * LANES], taps_ref)
    active = pre * sigmoid(pre)
    b_part, c_part = active[:, :LANES], active[:, LANES:]
    b_ref[...] = b_part.astype(BF)
    c_ref[...] = c_part.astype(BF)
    bt_ref[...] = b_part.T.astype(BF)
    ct_ref[...] = c_part.T.astype(BF)
    lane = lax.broadcasted_iota(jnp.int32, (1, LANES), 1)
    raw = jnp.where(lane < head_count, raw_ref[:, 2 * LANES :], 0.0) + heads_ref[0:1, :]
    dt = jnp.maximum(raw, 0.0) + jnp.log1p(jnp.exp(-jnp.abs(raw)))
    cum = dt * heads_ref[1:2, :]
    place = row_index(cum) % STRETCH
    step = 1
    while step < STRETCH:
        cum = cum + jnp.where(place >= step, pltpu.roll(cum, step, 0), 0.0)
        step *= 2
    dt_ref[...] = dt
    cum_ref[...] = cum
    cumt_ref[...] = cum.T


def prepare(raw, at, taps, heads, head_count, slot):
    rows = raw.shape[0]
    tall = pl.BlockSpec((slot, LANES), lambda q: (q, 0))
    wide = pl.BlockSpec((LANES, slot), lambda q: (0, q))
    return pl.pallas_call(
        functools.partial(prepare_kernel, head_count),
        grid=(rows // slot,),
        in_specs=[
            pl.BlockSpec((slot, 3 * LANES), lambda q: (q, at)),
            pl.BlockSpec((8, 2 * LANES), lambda q: (0, 0)),
            pl.BlockSpec((8, LANES), lambda q: (0, 0)),
        ],
        out_specs=[tall, tall, wide, wide, tall, tall, wide],
        out_shape=[
            jax.ShapeDtypeStruct((rows, LANES), BF),
            jax.ShapeDtypeStruct((rows, LANES), BF),
            jax.ShapeDtypeStruct((LANES, rows), BF),
            jax.ShapeDtypeStruct((LANES, rows), BF),
            jax.ShapeDtypeStruct((rows, LANES), F32),
            jax.ShapeDtypeStruct((rows, LANES), F32),
            jax.ShapeDtypeStruct((LANES, rows), F32),
        ],
        compiler_params=params(),
        name="prepare",
    )(raw, taps, heads)


def head_tables(cum_ref, dt_ref, first_head):
    shift = lax.rem(LANES - first_head, LANES)
    cum = pltpu.roll(cum_ref[...], shift, 1)
    dt = pltpu.roll(dt_ref[...], shift, 1)
    rows = cum.shape[0]
    cum_wide = [jnp.broadcast_to(cum[:, i : i + 1], (rows, LANES)) for i in range(GROUP_HEADS)]
    dt_wide = [jnp.broadcast_to(dt[:, i : i + 1], (rows, LANES)) for i in range(GROUP_HEADS)]
    left = lax.broadcasted_iota(jnp.int32, (1, LANES), 1) < LANES // 2

    def spread(wide):
        return jnp.concatenate(
            [jnp.where(left, wide[i], wide[i + 1]) for i in range(0, GROUP_HEADS, 2)], axis=1
        )

    return cum_wide, spread(cum_wide), spread(dt_wide), left


def decay_tiles(cum_wide, cumt_row, block, lower):
    begin = block * STRETCH
    top = cum_wide[begin : begin + HALF]
    low = cum_wide[begin + HALF : begin + STRETCH]
    row_left = cumt_row[:, begin : begin + HALF]
    row_right = cumt_row[:, begin + HALF : begin + STRETCH]
    first = jnp.where(lower, jnp.exp(top - row_left), 0.0)
    second = jnp.exp(low - row_left)
    third = jnp.where(lower, jnp.exp(low - row_right), 0.0)
    return first, jnp.concatenate([second, third], axis=1)


def join_tiles(first, below):
    return jnp.concatenate(
        [jnp.concatenate([first, jnp.zeros_like(first)], axis=1), below], axis=0
    )


def lower_mask():
    return lax.broadcasted_iota(jnp.int32, (HALF, HALF), 0) >= lax.broadcasted_iota(
        jnp.int32, (HALF, HALF), 1
    )


def forward_kernel(
    group_start, x_ref, taps_ref, b_ref, c_ref, bt_ref, dt_ref, cum_ref, cumt_ref, y_ref
):
    first_head = (pl.program_id(1) + group_start) * GROUP_HEADS
    _, pre = conv_parts(x_ref[...], taps_ref)
    x_low = (pre * sigmoid(pre)).astype(BF).astype(F32)
    cum_wide, cum_x, dt_x, left = head_tables(cum_ref, dt_ref, first_head)
    x_dt = (x_low * dt_x).astype(BF)
    skipped = taps_ref[5:6, :] * x_low
    fade = jnp.exp(cum_x[STRETCH - 1 : STRETCH] - cum_x[:STRETCH])
    scaled = (x_low[:STRETCH] * (fade * dt_x[:STRETCH])).astype(BF)
    state = dot_nn(bt_ref[:, :STRETCH], scaled).astype(BF)
    inter = jnp.exp(cum_x[STRETCH:]) * dot_nn(c_ref[STRETCH:, :], state)
    lower = lower_mask()
    zero = jnp.zeros((STRETCH, LANES), BF)
    for block in range(2):
        rows = slice(block * STRETCH, (block + 1) * STRETCH)
        cb = dot_nt(c_ref[rows, :], b_ref[rows, :])
        for pair in range(GROUP_HEADS // 2):
            lanes = slice(pair * LANES, (pair + 1) * LANES)
            x_pair = x_dt[rows, lanes]
            total = skipped[rows, lanes]
            if block == 1:
                total = total + inter[:, lanes]
            for side in range(2):
                head = 2 * pair + side
                row = cumt_ref[pl.ds(first_head + head, 1), :]
                first, below = decay_tiles(cum_wide[head], row, block, lower)
                mixing = join_tiles(
                    (cb[:HALF, :HALF] * first).astype(BF), (cb[HALF:, :] * below).astype(BF)
                )
                keep = left if side == 0 else jnp.logical_not(left)
                total = total + dot_nn(mixing, jnp.where(keep, x_pair, zero))
            y_ref[rows, lanes] = total


def scan_forward(px, offset, taps, prep, slot, start, count):
    b_low, c_low, b_t, _, dt, cum, cum_t = prep
    rows = px.shape[0]
    width = GROUP_HEADS * 64
    tall = pl.BlockSpec((slot, LANES), lambda q, h: (q, 0))
    wide = pl.BlockSpec((LANES, slot), lambda q, h: (0, q))
    tile = pl.BlockSpec((slot, width), lambda q, h: (q, h))
    return pl.pallas_call(
        functools.partial(forward_kernel, start),
        grid=(rows // slot, count),
        in_specs=[
            pl.BlockSpec((slot, width), lambda q, h: (q, h + offset)),
            pl.BlockSpec((8, width), lambda q, h: (0, h + start)),
            tall,
            tall,
            wide,
            tall,
            tall,
            wide,
        ],
        out_specs=tile,
        out_shape=jax.ShapeDtypeStruct((rows, count * width), F32),
        compiler_params=params(),
        cost_estimate=cost(3.3e-6 * count),
        name="scan_forward",
    )(px, taps, b_low, c_low, b_t, dt, cum, cum_t)


def gate_kernel(count, *refs):
    y_refs = refs[:count]
    z_ref, gain_ref, gate_ref, inv_ref = refs[count:]
    y = jnp.concatenate([ref[...] for ref in y_refs], axis=1)
    z = z_ref[...]
    gated = y * (z * sigmoid(z))
    mean = jnp.sum(gated * gated, axis=1, keepdims=True) * (1.0 / gated.shape[1])
    inv = lax.rsqrt(mean + EPS)
    gate_ref[...] = (gated * inv * gain_ref[...]).astype(BF)
    inv_ref[...] = jnp.broadcast_to(inv, inv_ref.shape)


def row_tile(size, array):
    return pl.BlockSpec((size, array.shape[1]), lambda t: (t, 0))


def gate_forward(y_parts, pz, gain):
    rows, inner = pz.shape
    size = 128
    tile = pl.BlockSpec((size, inner), lambda t: (t, 0))
    return pl.pallas_call(
        functools.partial(gate_kernel, len(y_parts)),
        grid=(rows // size,),
        in_specs=[row_tile(size, y) for y in y_parts]
        + [tile, pl.BlockSpec((1, inner), lambda t: (0, 0))],
        out_specs=[tile, pl.BlockSpec((size, LANES), lambda t: (t, 0))],
        out_shape=[
            jax.ShapeDtypeStruct((rows, inner), BF),
            jax.ShapeDtypeStruct((rows, LANES), F32),
        ],
        compiler_params=params(),
        cost_estimate=cost(15e-6),
        name="gate_forward",
    )(*y_parts, pz, gain)


def gate_back_kernel(count, *refs):
    y_refs = refs[:count]
    z_ref, grad_ref, inv_ref, gain_ref, gy_ref, gz_ref, gain_sum_ref = refs[count:]
    y = jnp.concatenate([ref[...] for ref in y_refs], axis=1)
    z = z_ref[...]
    grad = grad_ref[...]
    inv = inv_ref[:, 0:1]
    sig = sigmoid(z)
    silu = z * sig
    normal = y * silu * inv
    grad_normal = grad * gain_ref[...]
    mean = jnp.sum(grad_normal * normal, axis=1, keepdims=True) * (1.0 / y.shape[1])
    gated = inv * (grad_normal - normal * mean)
    gy_ref[...] = (gated * silu).astype(BF)
    gz_ref[...] = (gated * y * (sig + silu * (1.0 - sig))).astype(BF)
    part = grad * normal
    folded = part[0:8]
    for start in range(8, part.shape[0], 8):
        folded = folded + part[start : start + 8]

    @pl.when(pl.program_id(0) == 0)
    def _():
        gain_sum_ref[...] = folded

    @pl.when(pl.program_id(0) > 0)
    def _():
        gain_sum_ref[...] += folded


def gate_backward(y_parts, pz, grad_gate, inv, gain):
    rows, inner = pz.shape
    size = 128
    tile = pl.BlockSpec((size, inner), lambda t: (t, 0))
    return pl.pallas_call(
        functools.partial(gate_back_kernel, len(y_parts)),
        grid=(rows // size,),
        in_specs=[row_tile(size, y) for y in y_parts]
        + [
            tile,
            tile,
            pl.BlockSpec((size, LANES), lambda t: (t, 0)),
            pl.BlockSpec((1, inner), lambda t: (0, 0)),
        ],
        out_specs=[tile, tile, pl.BlockSpec((8, inner), lambda t: (0, 0))],
        out_shape=[
            jax.ShapeDtypeStruct((rows, inner), BF),
            jax.ShapeDtypeStruct((rows, inner), BF),
            jax.ShapeDtypeStruct((8, inner), F32),
        ],
        compiler_params=params(),
        cost_estimate=cost(24e-6),
        name="gate_backward",
    )(*y_parts, pz, grad_gate, inv, gain)


def head_sums(product, spread):
    high = product.astype(BF)
    low = (product - high.astype(F32)).astype(BF)
    return dot_nn(high, spread) + dot_nn(low, spread)


def backward_kernel(group_start, *refs):
    x_ref, taps_ref, y_ref, gy_ref, b_ref, c_ref, bt_ref, ct_ref = refs[:8]
    dt_ref, cum_ref, cumt_ref = refs[8:11]
    gx_ref, lines_ref, *totals = refs[-8:]
    gb_ref, gc_ref, one_ref, two_ref, cb_ref, heads_ref = totals
    befores = refs[12:-8]
    first_head = (pl.program_id(0) + group_start) * GROUP_HEADS
    seq = pl.program_id(1)
    slot = x_ref.shape[0]

    @pl.when((pl.program_id(0) == 0) & (seq == 0))
    def _():
        for i, total in enumerate(totals):
            total[...] = befores[i][...] if befores else jnp.zeros_like(total)

    at = pl.multiple_of(seq * slot, slot)
    whole_rows = pl.ds(at, slot)
    early_rows = pl.ds(at, STRETCH)
    late_rows = pl.ds(pl.multiple_of(at + STRETCH, STRETCH), STRETCH)
    shifted, pre = conv_parts(x_ref[...], taps_ref)
    sig = sigmoid(pre)
    active = pre * sig
    slope = sig + active * (1.0 - sig)
    x_low = active.astype(BF).astype(F32)
    gy_low = gy_ref[...]
    gy = gy_low.astype(F32)
    cum_wide, cum_x, dt_x, left = head_tables(cum_ref, dt_ref, first_head)
    x_dt = (x_low * dt_x).astype(BF)
    skip = taps_ref[5:6, :]

    grad_inter = (gy[STRETCH:] * jnp.exp(cum_x[STRETCH:])).astype(BF)
    fade = jnp.exp(cum_x[STRETCH - 1 : STRETCH] - cum_x[:STRETCH])
    scaled = (x_low[:STRETCH] * (fade * dt_x[:STRETCH])).astype(BF)
    state = dot_nn(bt_ref[:, :STRETCH], scaled)
    gc_ref[late_rows, :] += dot_nt(grad_inter, state.astype(BF))
    grad_state = dot_nn(ct_ref[:, STRETCH:], grad_inter).astype(BF)
    gb_ref[early_rows, :] += dot_nt(scaled, grad_state)
    grad_scaled = dot_nn(b_ref[:STRETCH, :], grad_state)
    last_sum = column_sum(grad_state.astype(F32) * state)

    lower = lower_mask()
    zero = jnp.zeros((STRETCH, LANES), BF)
    rest = []
    for block in range(2):
        rows = slice(block * STRETCH, (block + 1) * STRETCH)
        cb = dot_nt(c_ref[rows, :], b_ref[rows, :])
        cb_first = cb_below = None
        parts = []
        for pair in range(GROUP_HEADS // 2):
            lanes = slice(pair * LANES, (pair + 1) * LANES)
            x_pair = x_dt[rows, lanes]
            gy_pair = gy_low[rows, lanes]
            total = None
            for side in range(2):
                head = 2 * pair + side
                row = cumt_ref[pl.ds(first_head + head, 1), :]
                first, below = decay_tiles(cum_wide[head], row, block, lower)
                mixing = join_tiles(
                    (cb[:HALF, :HALF] * first).astype(BF), (cb[HALF:, :] * below).astype(BF)
                )
                keep = left if side == 0 else jnp.logical_not(left)
                gy_head = jnp.where(keep, gy_pair, zero)
                mix_first = dot_nt(gy_head[:HALF], x_pair[:HALF]) * first
                mix_below = dot_nt(gy_head[HALF:], x_pair) * below
                cb_first = mix_first if cb_first is None else cb_first + mix_first
                cb_below = mix_below if cb_below is None else cb_below + mix_below
                now = dot_tn(mixing, gy_head)
                total = now if total is None else total + now
            parts.append(total)
        cb_ref[seq, block, :HALF, :HALF] += cb_first
        cb_ref[seq, block, HALF:, :] += cb_below
        rest.append(jnp.concatenate(parts, axis=1))
    moved = x_dt.astype(F32) * jnp.concatenate(rest, axis=0)
    moved = jnp.concatenate(
        [moved[:STRETCH] + scaled.astype(F32) * grad_scaled, moved[STRETCH:]], axis=0
    )
    rest[0] = rest[0] + fade * grad_scaled
    grad_pull = jnp.concatenate(rest, axis=0)

    width = x_low.shape[1]
    spread = (
        lax.broadcasted_iota(jnp.int32, (width, LANES), 1)
        == first_head + lax.broadcasted_iota(jnp.int32, (width, LANES), 0) // 64
    ).astype(F32).astype(BF)
    moved = gy * (y_ref[...] - skip * x_low) - moved
    edge = lax.broadcasted_iota(jnp.int32, (8, 1), 0) == 7
    moved = jnp.concatenate(
        [
            moved[: STRETCH - 8],
            moved[STRETCH - 8 : STRETCH] + jnp.where(edge, last_sum, 0.0),
            moved[STRETCH:],
        ],
        axis=0,
    )
    one_ref[whole_rows, :] += head_sums(moved, spread)
    two_ref[whole_rows, :] += head_sums(x_low * grad_pull, spread)
    third = lax.broadcasted_iota(jnp.int32, (8, 1), 0) == 2
    skip_line = jnp.where(third, column_sum(gy * x_low), 0.0)
    heads_ref[...] += head_sums(skip_line, spread)

    grad_pre = (skip * gy + dt_x * grad_pull) * slope
    gx_ref[...] = conv_back(grad_pre, taps_ref).astype(BF)
    lines = [column_sum(grad_pre * shifted[k]) for k in range(4)] + [column_sum(grad_pre)]
    lines = jnp.concatenate(lines + [jnp.zeros((3, width), F32)], axis=0)

    @pl.when(seq == 0)
    def _():
        lines_ref[...] = lines

    @pl.when(seq > 0)
    def _():
        lines_ref[...] += lines


def scan_backward(px, at, taps, y_rows, y_at, grad_y, prep, slot, start, count, before=None):
    b_low, c_low, b_t, c_t, dt, cum, cum_t = prep
    rows = px.shape[0]
    width = GROUP_HEADS * 64
    seqs = rows // slot
    tall = pl.BlockSpec((slot, LANES), lambda h, q: (q, 0))
    wide = pl.BlockSpec((LANES, slot), lambda h, q: (0, q))
    tile = pl.BlockSpec((slot, width), lambda h, q: (q, h + at))
    flat = jax.ShapeDtypeStruct((rows, LANES), F32)
    whole = pl.BlockSpec((rows, LANES), lambda h, q: (0, 0))
    totals = [whole] * 4 + [
        pl.BlockSpec((seqs, 2, STRETCH, STRETCH), lambda h, q: (0, 0, 0, 0)),
        pl.BlockSpec((8, LANES), lambda h, q: (0, 0)),
    ]
    extra, extra_specs, aliases = [jnp.zeros((8, LANES), BF)], [pl.BlockSpec(memory_space=pl.ANY)], {}
    if before is not None:
        if before[0].shape == px.shape:
            extra = [before[0]]
            aliases[11] = 0
        extra = extra + list(before[2:])
        extra_specs = extra_specs + totals
        aliases.update({12 + i: 2 + i for i in range(6)})
    return pl.pallas_call(
        functools.partial(backward_kernel, start),
        grid=(count, seqs),
        in_specs=[
            tile,
            pl.BlockSpec((8, width), lambda h, q: (0, h + start)),
            pl.BlockSpec((slot, width), lambda h, q: (q, h + y_at)),
            pl.BlockSpec((slot, width), lambda h, q: (q, h + start)),
            tall,
            tall,
            wide,
            wide,
            tall,
            tall,
            wide,
        ]
        + extra_specs,
        out_specs=[tile, pl.BlockSpec((8, width), lambda h, q: (0, h))] + totals,
        out_shape=[
            jax.ShapeDtypeStruct(px.shape, BF),
            jax.ShapeDtypeStruct((8, count * width), F32),
            flat,
            flat,
            flat,
            flat,
            jax.ShapeDtypeStruct((seqs, 2, STRETCH, STRETCH), F32),
            jax.ShapeDtypeStruct((8, LANES), F32),
        ],
        input_output_aliases=aliases,
        compiler_params=params(),
        cost_estimate=cost(3.3e-6 * count),
        name="scan_backward",
    )(px, taps, y_rows, grad_y, b_low, c_low, b_t, c_t, dt, cum, cum_t, *extra)


def finish_kernel(
    head_count,
    raw_ref,
    taps_ref,
    heads_ref,
    b_ref,
    c_ref,
    dt_ref,
    gb_ref,
    gc_ref,
    one_ref,
    two_ref,
    cb_ref,
    head_before_ref,
    before_ref,
    out_ref,
    lines_ref,
    head_total_ref,
):
    @pl.when(pl.program_id(0) == 0)
    def _():
        lines_ref[...] = jnp.zeros_like(lines_ref)
        head_total_ref[...] = head_before_ref[...]

    shifted, pre = conv_parts(raw_ref[:, : 2 * LANES], taps_ref)
    sig = sigmoid(pre)
    slope = sig + pre * sig * (1.0 - sig)
    grad_b, grad_c = [], []
    for block in range(2):
        rows = slice(block * STRETCH, (block + 1) * STRETCH)
        cb = cb_ref[0, block].astype(BF)
        grad_c.append(gc_ref[rows, :] + dot_nn(cb, b_ref[rows, :]))
        grad_b.append(gb_ref[rows, :] + dot_tn(cb, c_ref[rows, :]))
    grad_active = jnp.concatenate(
        [jnp.concatenate(grad_b, axis=0), jnp.concatenate(grad_c, axis=0)], axis=1
    )
    grad_pre = grad_active * slope
    lines = [column_sum(grad_pre * shifted[k]) for k in range(4)] + [column_sum(grad_pre)]
    lines.append(jnp.zeros((3, 2 * LANES), F32))
    lines_ref[...] += jnp.concatenate(lines, axis=0)

    dt = dt_ref[...]
    two = two_ref[...]
    rate = heads_ref[1:2, :]
    place = row_index(dt)
    grad_cum = one_ref[...]
    inside = place % STRETCH
    step = 1
    while step < STRETCH:
        moved = pltpu.roll(grad_cum, grad_cum.shape[0] - step, 0)
        grad_cum = grad_cum + jnp.where(inside < STRETCH - step, moved, 0.0)
        step *= 2
    grad_dt = grad_cum * rate + two
    lane = lax.broadcasted_iota(jnp.int32, (1, LANES), 1)
    raw = jnp.where(lane < head_count, raw_ref[:, 2 * LANES : 3 * LANES], 0.0)
    grad_raw = grad_dt * sigmoid(raw + heads_ref[0:1, :])
    head_total_ref[...] += jnp.concatenate(
        [column_sum(grad_raw), column_sum(grad_cum * dt) * rate, jnp.zeros((6, LANES), F32)], axis=0
    )
    out_ref[:, : 2 * LANES] = conv_back(grad_pre, taps_ref).astype(BF)
    out_ref[:, 2 * LANES : 3 * LANES] = grad_raw.astype(BF)
    out_ref[:, 3 * LANES :] = jnp.zeros_like(out_ref[:, 3 * LANES :])


def finish(raw, at, taps, heads, head_count, prep, totals, grads, narrow, grads_at, slot):
    b_low, c_low, _, _, dt, _, _ = prep
    rows = raw.shape[0]
    seqs = rows // slot
    tall = pl.BlockSpec((slot, LANES), lambda q: (q, 0))
    return pl.pallas_call(
        functools.partial(finish_kernel, head_count),
        grid=(seqs,),
        in_specs=[
            pl.BlockSpec((slot, 3 * LANES), lambda q: (q, at)),
            pl.BlockSpec((8, 2 * LANES), lambda q: (0, 0)),
            pl.BlockSpec((8, LANES), lambda q: (0, 0)),
            tall,
            tall,
            tall,
            tall,
            tall,
            tall,
            tall,
            pl.BlockSpec((1, 2, STRETCH, STRETCH), lambda q: (q, 0, 0, 0)),
            pl.BlockSpec((8, LANES), lambda q: (0, 0)),
            pl.BlockSpec(memory_space=pl.ANY),
        ],
        out_specs=[
            pl.BlockSpec((slot, narrow), lambda q: (q, grads_at)),
            pl.BlockSpec((8, 2 * LANES), lambda q: (0, 0)),
            pl.BlockSpec((8, LANES), lambda q: (0, 0)),
        ],
        out_shape=[
            jax.ShapeDtypeStruct(grads.shape, BF),
            jax.ShapeDtypeStruct((8, 2 * LANES), F32),
            jax.ShapeDtypeStruct((8, LANES), F32),
        ],
        input_output_aliases={12: 0},
        compiler_params=params(),
        cost_estimate=cost(3e-6),
        name="finish",
    )(raw, taps, heads, b_low, c_low, dt, *totals, grads)


def project_kernel(rows_ref, weight_ref, out_ref):
    out_ref[...] = dot_nn(rows_ref[...], weight_ref[...])


def project(normed, weight, at, count, size):
    rows, depth = normed.shape
    return pl.pallas_call(
        project_kernel,
        grid=(count,),
        in_specs=[
            pl.BlockSpec((rows, depth), lambda j: (0, 0)),
            pl.BlockSpec((depth, size), lambda j: (0, j + at)),
        ],
        out_specs=pl.BlockSpec((rows, size), lambda j: (0, j)),
        out_shape=jax.ShapeDtypeStruct((rows, count * size), F32),
        compiler_params=params(),
        cost_estimate=cost(2.5e-6 * count),
        name="project",
    )(normed, weight)


def pair_kernel(mine_ref, other_ref, grad_ref, keep_ref, give_ref):
    grad = grad_ref[...]
    give_ref[...] = dot_nn(other_ref[...], grad).astype(give_ref.dtype)
    keep_ref[...] = dot_nn(mine_ref[...], grad).astype(keep_ref.dtype)


def weight_grads(mine, other, grad, at, count, size):
    depth, rows = mine.shape
    whole = pl.BlockSpec((depth, rows), lambda j: (0, 0))
    tile = pl.BlockSpec((depth, size), lambda j: (0, j))
    shape = jax.ShapeDtypeStruct((depth, count * size), BF)
    return pl.pallas_call(
        pair_kernel,
        grid=(count,),
        in_specs=[whole, whole, pl.BlockSpec((rows, size), lambda j: (0, j + at))],
        out_specs=[tile, tile],
        out_shape=[shape, shape],
        compiler_params=params(),
        cost_estimate=cost(2.5e-6 * count),
        name="weight_grads",
    )(mine, other, grad)


def input_grads_kernel(sizes, ends, has_before, final, *refs):
    pairs = [refs[2 * i : 2 * i + 2] for i in range(len(sizes))]
    refs = refs[2 * len(sizes) :]
    steps = sum(sizes)
    step = pl.program_id(0)
    if has_before:
        before_ref, refs = refs[0], refs[1:]
    if final:
        hidden_ref, inv_ref, gain_ref, mask_ref, cot_ref, out_ref, line_ref, total = refs
    else:
        (total,) = refs

    def add(grad_ref, weight):
        now = dot_nt(grad_ref[...], weight)

        @pl.when(step == 0)
        def _():
            total[...] = now + before_ref[...] if has_before else now

        @pl.when(step > 0)
        def _():
            total[...] += now

    begin = 0
    for (grad_ref, weight_ref), size, end in zip(pairs, sizes, ends):
        full = size if end is None else size - 1

        @pl.when((step >= begin) & (step < begin + full))
        def _(grad_ref=grad_ref, weight_ref=weight_ref):
            add(grad_ref, weight_ref[...])

        if end is not None:

            @pl.when(step == begin + full)
            def _(grad_ref=grad_ref, weight_ref=weight_ref, end=end):
                weight = weight_ref[...]
                lane = lax.broadcasted_iota(jnp.int32, weight.shape, 1)
                add(grad_ref, jnp.where(lane < end, weight, jnp.zeros_like(weight)))

        begin += size
    if final:

        @pl.when(step == 0)
        def _():
            line_ref[...] = jnp.zeros_like(line_ref)

        @pl.when(step >= steps)
        def _():
            tile = hidden_ref.shape[0]
            grad = total[pl.ds(pl.multiple_of((step - steps) * tile, tile), tile), :]
            inv = inv_ref[...]
            normal = hidden_ref[...] * inv
            product = grad * normal
            folded = product[0:8]
            for start in range(8, tile, 8):
                folded = folded + product[start : start + 8]
            line_ref[...] += folded
            inside = jnp.sum(product * gain_ref[...], axis=1, keepdims=True) * (1.0 / grad.shape[1])
            out_ref[...] = inv * (grad * gain_ref[...] - normal * inside) + mask_ref[...] * cot_ref[...]


def input_grads(grads, places, weight, before=None, final=None):
    rows = grads[0].shape[0]
    width = weight.shape[0]
    size, tile = 512, 128
    sizes = [g.shape[1] // size for g in grads]
    steps = sum(sizes)
    in_specs, args, begin = [], [], 0
    for grad, (at, _), count in zip(grads, places, sizes):

        def place(k, begin=begin, count=count, at=0):
            return (0, at + jnp.clip(k - begin, 0, count - 1))

        in_specs += [
            pl.BlockSpec((rows, size), place),
            pl.BlockSpec((width, size), functools.partial(place, at=at)),
        ]
        args += [grad, weight]
        begin += count
    if before is not None:
        in_specs.append(pl.BlockSpec((rows, width), lambda k: (0, 0), pipeline_mode=pl.Buffered(1)))
        args.append(before)
    if final:

        def row(k):
            return (jnp.clip(k - steps, 0, rows // tile - 1), 0)

        line = pl.BlockSpec((1, width), lambda k: (0, 0))
        column = pl.BlockSpec((tile, 1), row)
        wide = pl.BlockSpec((tile, width), row)
        in_specs += [wide, column, line, column, wide]
        args += list(final)
        out_specs = [wide, pl.BlockSpec((8, width), lambda k: (0, 0))]
        out_shape = [
            jax.ShapeDtypeStruct((rows, width), F32),
            jax.ShapeDtypeStruct((8, width), F32),
        ]
        scratch = [pltpu.VMEM((rows, width), F32)]
    else:
        out_specs = pl.BlockSpec((rows, width), lambda k: (0, 0))
        out_shape = jax.ShapeDtypeStruct((rows, width), F32)
        scratch = []
    ends = [end for _, end in places]
    return pl.pallas_call(
        functools.partial(input_grads_kernel, sizes, ends, before is not None, bool(final)),
        grid=(steps + (rows // tile if final else 0),),
        in_specs=in_specs,
        out_specs=out_specs,
        out_shape=out_shape,
        scratch_shapes=scratch,
        compiler_params=params(),
        cost_estimate=cost(2.5e-6 * steps),
        name="input_grads",
    )(*args)


def swap(values, bit, shards):
    return lax.ppermute(values, "shard", [(i, i ^ (1 << bit)) for i in range(shards)])


def border(moving, *values):
    ready = lax.optimization_barrier(tuple(one.got for one in moving) + values)
    for one, got in zip(moving, ready):
        one.got = got
        one.finish()
    rest = ready[len(moving) :]
    return rest[0] if len(rest) == 1 else rest


class Gather:
    def __init__(self, own, order, shards, place):
        self.now, self.order, self.shards, self.place = own, list(order), shards, place
        self.live, self.columns = [], own.shape[-1]

    def start(self):
        self.bit = self.order.pop(0)
        self.got = swap(self.now, self.bit, self.shards)

    def finish(self):
        mine = (self.place >> self.bit) & 1
        axis = len([b for b in self.live if b > self.bit])
        first = jnp.where(mine == 0, self.now, self.got)
        second = jnp.where(mine == 0, self.got, self.now)
        self.now = jnp.stack([first, second], axis=axis)
        self.live.append(self.bit)

    def whole(self):
        while self.order:
            self.start()
            self.finish()
        return self.now


class Sum:
    def __init__(self, pair, order, shards, groups, place, part, group_first=False):
        self.keep, self.give = pair
        self.shards, self.groups, self.place, self.part = shards, groups, place, part
        self.columns, self.dtype = self.keep.shape[-1], self.keep.dtype
        self.group_first = group_first and groups == 2
        self.todo = [0] + (["group"] if self.group_first else []) + list(order) + ["end"]
        self.live = list(range(shards.bit_length() - 2, 0, -1))
        self.now = None

    def start(self):
        self.bit = bit = self.todo.pop(0)
        if bit == "end":
            pairs = [(i, (i + 1) % self.groups) for i in range(self.groups)]
            self.got = lax.ppermute(self.now, "group", pairs)
        elif bit == "group":
            half = self.columns // 2
            mine = lax.axis_index("group")
            axis = self.now.ndim - 1
            self.keep = lax.dynamic_slice_in_dim(self.now, mine * half, half, axis)
            give = lax.dynamic_slice_in_dim(self.now, (1 - mine) * half, half, axis)
            self.got = lax.ppermute(give, "group", [(0, 1), (1, 0)])
        elif bit == 0:
            self.got = swap(self.give, 0, self.shards)
        else:
            axis = self.live.index(bit)
            mine = (self.place >> bit) & 1
            self.keep = lax.dynamic_index_in_dim(self.now, mine, axis, keepdims=False)
            give = lax.dynamic_index_in_dim(self.now, 1 - mine, axis, keepdims=False)
            self.live.remove(bit)
            self.got = swap(give, bit, self.shards)

    def finish(self):
        if self.bit == "end" and self.group_first:
            first = lax.axis_index("group") == 0
            halves = [jnp.where(first, self.now, self.got), jnp.where(first, self.got, self.now)]
            self.now = jnp.concatenate(halves, axis=-1)
        elif self.bit == "end":
            total, got = self.now.astype(F32), self.got
            for step in range(1, self.groups):
                if step > 1:
                    pairs = [(i, (i + 1) % self.groups) for i in range(self.groups)]
                    got = lax.ppermute(got, "group", pairs)
                total = total + got.astype(F32)
            self.now = total
        else:
            now = self.keep.astype(F32) + self.got.astype(F32)
            if self.todo != ["end"] or not self.group_first:
                now = now.astype(self.dtype)
            if self.bit == 0:
                now = now.reshape((2,) * len(self.live) + (self.part, self.columns))
            self.now = now

    def result(self):
        while self.todo:
            self.start()
            self.finish()
        return self.now


def local(
    shards,
    groups,
    hidden_in,
    lengths,
    pre_gain,
    in_proj,
    conv_weight,
    conv_bias,
    head_params,
    gate_gain,
    out_proj,
    cotangent,
):
    micro, own, slot, width = hidden_in.shape
    rows = micro * own * slot
    inner = out_proj.shape[0] * shards
    channels = conv_bias.shape[0] * shards
    heads = head_params.shape[1]
    tail = channels - inner + heads
    part = in_proj.shape[0]
    out_part = out_proj.shape[0]
    own_conv = conv_bias.shape[0]
    taps = conv_weight.shape[0]
    hidden = hidden_in.reshape(rows, width)
    cot = cotangent.reshape(rows, width)
    place = lax.axis_index("shard")
    core = place & 1
    chip_bits = list(range(1, shards.bit_length() - 1))
    up = chip_bits
    down = chip_bits[::-1]

    w_in = lax.all_gather(in_proj, "shard", axis=0, tiled=True)
    w_out = lax.all_gather(out_proj, "shard", axis=0, tiled=True)
    small = jnp.concatenate([pre_gain, gate_gain, conv_bias, conv_weight.reshape(-1)], axis=0)
    small = small.astype(F32)
    small = jnp.pad(small, (0, -small.shape[0] % LANES))[None, :]
    packed = Gather(small, down + [0], shards, place).whole().reshape(shards, -1)
    sizes = (part, out_part, own_conv, taps * own_conv)
    ends = [sum(sizes[: i + 1]) for i in range(4)]
    pre_all = packed[:, : ends[0]].reshape(1, width)
    gate_all = packed[:, ends[0] : ends[1]].reshape(1, inner)
    bias_all = packed[:, ends[1] : ends[2]].reshape(1, channels)
    taps_all = packed[:, ends[2] : ends[3]].reshape(shards, taps, -1)
    taps_all = jnp.swapaxes(taps_all, 0, 1).reshape(taps, channels)
    skip_row = jnp.pad(jnp.repeat(head_params[2], inner // heads), (0, channels - inner))
    table = jnp.concatenate(
        [taps_all, bias_all, skip_row[None, :], jnp.zeros((2, channels), F32)], axis=0
    )
    table_x, table_bc = table[:, :inner], table[:, inner:]
    rate = -jnp.exp(head_params[1])
    head_rows = jnp.pad(
        jnp.stack([head_params[0], rate], axis=0), ((0, 6), (0, LANES - heads))
    )

    inv_first = lax.rsqrt(jnp.mean(hidden * hidden, axis=-1, keepdims=True) + EPS)
    normed = (hidden * inv_first * pre_all).astype(BF)
    turned = normed.T.reshape(shards // 2, 2, part, rows)
    mine = lax.dynamic_index_in_dim(turned, core, 1, keepdims=False).reshape(-1, rows)
    other = lax.dynamic_index_in_dim(turned, 1 - core, 1, keepdims=False).reshape(-1, rows)
    positions = jnp.arange(slot, dtype=jnp.int32)
    mask = (positions[None, :] < lengths.reshape(-1)[:, None]).astype(F32).reshape(rows, 1)
    grad_low = (mask * cot).astype(BF)

    size = 4 * LANES
    blocks = inner // size
    raw_at = inner // (3 * LANES)
    prep_at = (raw_at, table_bc, head_rows, heads)
    px = project(normed, w_in, blocks, blocks + 1, size)
    prep = prepare(px, *prep_at, slot)
    unit = GROUP_HEADS * 64
    y_rows = scan_forward(px, 0, table_x, prep, slot, 0, inner // unit)
    pz = project(normed, w_in, 0, blocks, size)
    gate_low, inv = gate_forward([y_rows], pz, gate_all)

    g_out = dot_tn(gate_low, grad_low).astype(BF)
    g_out, grad_low, mine, other = border([], g_out, grad_low, mine, other)
    sum_out = lax.psum_scatter(g_out, "shard", scatter_dimension=0, tiled=True)
    grad_gate = dot_nt(grad_low, w_out)
    grad_y, grad_z, gain_sum = gate_backward([y_rows], pz, grad_gate, inv, gate_all)
    g_z = dot_nn(turned.reshape(width, rows), grad_z).astype(BF)
    g_z, grad_y = border([], g_z, grad_y)
    sum_z = lax.psum_scatter(g_z, "shard", scatter_dimension=0, tiled=True)

    reduce = functools.partial(Sum, shards=shards, groups=groups, place=place, order=up)
    third = inner // unit // 3
    outs = None
    for start in (0, third):
        outs_now = scan_backward(
            px, start, table_x, y_rows, start, grad_y, prep, slot, start, third, before=outs
        )
        outs_first, outs = outs, outs_now
    lines_x = [outs_first[1], outs[1]]
    b_blocks = 2 * third * unit // size
    pair_b = weight_grads(mine, other, outs[0], 0, b_blocks, size)
    *pair_b, grad_y = border([], *pair_b, grad_y)
    s_b = reduce(pair_b, part=part)
    s_b.start()
    rest = inner // unit - 2 * third
    outs = scan_backward(
        px, 2 * third, table_x, y_rows, 2 * third, grad_y, prep, slot, 2 * third, rest, before=outs
    )
    mine, *outs = border([s_b], mine, *outs)
    s_b.start()
    lines_x.append(outs[1])
    grad_x, lines_bc, head_total = finish(
        px, *prep_at, prep, outs[2:], outs[0], size, blocks, slot
    )
    pair_a = weight_grads(mine, other, grad_x, b_blocks, blocks + 1 - b_blocks, size)
    *pair_a, grad_z, grad_x = border([], *pair_a, grad_z, grad_x)
    s_a = reduce(pair_a, part=part)
    s_a.start()
    part_sum = input_grads([grad_z], [(0, None)], w_in)
    part_sum, grad_x = border([s_b, s_a], part_sum, grad_x)
    s_a.start()
    s_b.start()
    grad_input, pre_lines = input_grads(
        [grad_x],
        [(blocks, tail % size)],
        w_in,
        before=part_sum,
        final=(hidden, inv_first, pre_all, mask, cot),
    )
    gate_low, pre_lines = border([s_a, s_b], gate_low, pre_lines)
    s_a.start()
    s_b.start()
    layer_out = mask * (hidden + dot_nn(gate_low, w_out))

    lines = jnp.concatenate(lines_x + [lines_bc], axis=1)
    gain_line = jnp.sum(gain_sum, axis=0, keepdims=True)
    pre_line = jnp.sum(pre_lines, axis=0, keepdims=True)
    head_line = head_total[:3].reshape(1, 3 * LANES)

    def widen(line):
        return jnp.pad(line, ((0, 0), (0, channels - line.shape[1])))

    vector = jnp.concatenate(
        [lines[:5], widen(pre_line), widen(gain_line), widen(head_line)], axis=0
    )
    for bit in [0] + up:
        vector = vector + swap(vector, bit, shards)
    for _ in range(groups - 1):
        vector = vector + lax.ppermute(vector, "group", [(0, 1), (1, 0)])
    g_lines = lax.dynamic_slice(vector, (0, place * own_conv), (5, own_conv))
    g_pre = lax.dynamic_slice(vector, (5, place * part), (1, part))[0]
    g_gate = lax.dynamic_slice(vector, (6, place * out_part), (1, out_part))[0]
    g_heads = vector[7, : 3 * LANES].reshape(3, LANES)[:, :heads]
    layer_out = border([s_a, s_b], layer_out)

    def both_groups(values):
        total = values.astype(F32)
        for step in range(1, groups):
            pairs = [(i, (i + step) % groups) for i in range(groups)]
            total = total + lax.ppermute(values, "group", pairs).astype(F32)
        return total

    sum_out, sum_z = both_groups(sum_out), both_groups(sum_z)
    s_a.start()
    s_b.start()
    s_a.finish()
    s_b.finish()
    sum_a = s_a.result()
    b_columns = b_blocks * size
    g_in = jnp.concatenate([sum_z, s_b.result(), sum_a[:, : inner - b_columns + tail]], axis=1)
    return (
        layer_out.reshape(hidden_in.shape),
        grad_input.reshape(hidden_in.shape),
        g_pre,
        g_in,
        g_lines[:4],
        g_lines[4],
        g_heads,
        g_gate,
        sum_out,
    )


def solution(mesh):
    rows = P(None, ("group", "shard"), None, None)
    in_specs = (
        rows,
        P(None, ("group", "shard")),
        P("shard"),
        P("shard", None),
        P(None, "shard"),
        P("shard"),
        P(),
        P("shard"),
        P("shard", None),
        rows,
    )
    out_specs = (
        rows,
        rows,
        P("shard"),
        P("shard", None),
        P(None, "shard"),
        P("shard"),
        P(),
        P("shard"),
        P("shard", None),
    )
    body = functools.partial(local, mesh.shape["shard"], mesh.shape["group"])
    return jax.shard_map(body, mesh=mesh, in_specs=in_specs, out_specs=out_specs, check_vma=False)
```

```python
import functools

import jax
import jax.numpy as jnp
from jax import lax
from jax.experimental import pallas as pl
from jax.experimental.pallas import tpu as pltpu
from jax.sharding import PartitionSpec as P

STRETCH = 256
HALF = 128
LANES = 128
GROUP_HEADS = 4
EPS = 1e-05
BF = jnp.bfloat16
F32 = jnp.float32
VMEM_BYTES = 56 * 1024 * 1024


def params(**kwargs):
    return pltpu.CompilerParams(vmem_limit_bytes=VMEM_BYTES, **kwargs)


def cost(seconds):
    return pl.CostEstimate(
        flops=int(seconds * 2.0e13), bytes_accessed=int(seconds * 6.0e10), transcendentals=0
    )


def dot_nn(left, right):
    return lax.dot_general(left, right, (((1,), (0,)), ((), ())), preferred_element_type=F32)


def dot_nt(left, right):
    return lax.dot_general(left, right, (((1,), (1,)), ((), ())), preferred_element_type=F32)


def dot_tn(left, right):
    return lax.dot_general(left, right, (((0,), (0,)), ((), ())), preferred_element_type=F32)


def sigmoid(values):
    return 1.0 / (1.0 + jnp.exp(-values))


def row_index(values):
    return lax.broadcasted_iota(jnp.int32, (values.shape[0], 1), 0)


def shift_down(values, count):
    rolled = pltpu.roll(values, count, 0)
    return jnp.where(row_index(values) >= count, rolled, 0.0)


def shift_up(values, count):
    rows = values.shape[0]
    rolled = pltpu.roll(values, rows - count, 0)
    return jnp.where(row_index(values) < rows - count, rolled, 0.0)


def conv_parts(values, taps_ref):
    shifted = [shift_down(values, 3), shift_down(values, 2), shift_down(values, 1), values]
    pre = taps_ref[4:5, :]
    for k in range(4):
        pre = pre + taps_ref[k : k + 1, :] * shifted[k]
    return shifted, pre


def conv_back(grad_pre, taps_ref):
    total = taps_ref[3:4, :] * grad_pre
    for k in range(3):
        total = total + taps_ref[k : k + 1, :] * shift_up(grad_pre, 3 - k)
    return total


def column_sum(values):
    return jnp.sum(values, axis=0, keepdims=True)


def prepare_kernel(head_count, raw_ref, taps_ref, heads_ref, b_ref, c_ref, bt_ref, ct_ref, dt_ref, cum_ref, cumt_ref):
    _, pre = conv_parts(raw_ref[:, : 2 * LANES], taps_ref)
    active = pre * sigmoid(pre)
    b_part, c_part = active[:, :LANES], active[:, LANES:]
    b_ref[...] = b_part.astype(BF)
    c_ref[...] = c_part.astype(BF)
    bt_ref[...] = b_part.T.astype(BF)
    ct_ref[...] = c_part.T.astype(BF)
    lane = lax.broadcasted_iota(jnp.int32, (1, LANES), 1)
    raw = jnp.where(lane < head_count, raw_ref[:, 2 * LANES :], 0.0) + heads_ref[0:1, :]
    dt = jnp.maximum(raw, 0.0) + jnp.log1p(jnp.exp(-jnp.abs(raw)))
    cum = dt * heads_ref[1:2, :]
    place = row_index(cum) % STRETCH
    step = 1
    while step < STRETCH:
        cum = cum + jnp.where(place >= step, pltpu.roll(cum, step, 0), 0.0)
        step *= 2
    dt_ref[...] = dt
    cum_ref[...] = cum
    cumt_ref[...] = cum.T


def prepare(raw, at, taps, heads, head_count, slot):
    rows = raw.shape[0]
    tall = pl.BlockSpec((slot, LANES), lambda q: (q, 0))
    wide = pl.BlockSpec((LANES, slot), lambda q: (0, q))
    return pl.pallas_call(
        functools.partial(prepare_kernel, head_count),
        grid=(rows // slot,),
        in_specs=[
            pl.BlockSpec((slot, 3 * LANES), lambda q: (q, at)),
            pl.BlockSpec((8, 2 * LANES), lambda q: (0, 0)),
            pl.BlockSpec((8, LANES), lambda q: (0, 0)),
        ],
        out_specs=[tall, tall, wide, wide, tall, tall, wide],
        out_shape=[
            jax.ShapeDtypeStruct((rows, LANES), BF),
            jax.ShapeDtypeStruct((rows, LANES), BF),
            jax.ShapeDtypeStruct((LANES, rows), BF),
            jax.ShapeDtypeStruct((LANES, rows), BF),
            jax.ShapeDtypeStruct((rows, LANES), F32),
            jax.ShapeDtypeStruct((rows, LANES), F32),
            jax.ShapeDtypeStruct((LANES, rows), F32),
        ],
        compiler_params=params(),
        name="prepare",
    )(raw, taps, heads)


def head_tables(cum_ref, dt_ref, first_head):
    shift = lax.rem(LANES - first_head, LANES)
    cum = pltpu.roll(cum_ref[...], shift, 1)
    dt = pltpu.roll(dt_ref[...], shift, 1)
    rows = cum.shape[0]
    cum_wide = [jnp.broadcast_to(cum[:, i : i + 1], (rows, LANES)) for i in range(GROUP_HEADS)]
    dt_wide = [jnp.broadcast_to(dt[:, i : i + 1], (rows, LANES)) for i in range(GROUP_HEADS)]
    left = lax.broadcasted_iota(jnp.int32, (1, LANES), 1) < LANES // 2

    def spread(wide):
        return jnp.concatenate(
            [jnp.where(left, wide[i], wide[i + 1]) for i in range(0, GROUP_HEADS, 2)], axis=1
        )

    return cum_wide, spread(cum_wide), spread(dt_wide), left


def decay_tiles(cum_wide, cumt_row, block, lower):
    begin = block * STRETCH
    top = cum_wide[begin : begin + HALF]
    low = cum_wide[begin + HALF : begin + STRETCH]
    row_left = cumt_row[:, begin : begin + HALF]
    row_right = cumt_row[:, begin + HALF : begin + STRETCH]
    first = jnp.where(lower, jnp.exp(top - row_left), 0.0)
    second = jnp.exp(low - row_left)
    third = jnp.where(lower, jnp.exp(low - row_right), 0.0)
    return first, jnp.concatenate([second, third], axis=1)


def join_tiles(first, below):
    return jnp.concatenate(
        [jnp.concatenate([first, jnp.zeros_like(first)], axis=1), below], axis=0
    )


def lower_mask():
    return lax.broadcasted_iota(jnp.int32, (HALF, HALF), 0) >= lax.broadcasted_iota(
        jnp.int32, (HALF, HALF), 1
    )


def forward_kernel(
    group_start, x_ref, taps_ref, b_ref, c_ref, bt_ref, dt_ref, cum_ref, cumt_ref, y_ref
):
    first_head = (pl.program_id(1) + group_start) * GROUP_HEADS
    _, pre = conv_parts(x_ref[...], taps_ref)
    x_low = (pre * sigmoid(pre)).astype(BF).astype(F32)
    cum_wide, cum_x, dt_x, left = head_tables(cum_ref, dt_ref, first_head)
    x_dt = (x_low * dt_x).astype(BF)
    skipped = taps_ref[5:6, :] * x_low
    fade = jnp.exp(cum_x[STRETCH - 1 : STRETCH] - cum_x[:STRETCH])
    scaled = (x_low[:STRETCH] * (fade * dt_x[:STRETCH])).astype(BF)
    state = dot_nn(bt_ref[:, :STRETCH], scaled).astype(BF)
    inter = jnp.exp(cum_x[STRETCH:]) * dot_nn(c_ref[STRETCH:, :], state)
    lower = lower_mask()
    zero = jnp.zeros((STRETCH, LANES), BF)
    for block in range(2):
        rows = slice(block * STRETCH, (block + 1) * STRETCH)
        cb = dot_nt(c_ref[rows, :], b_ref[rows, :])
        for pair in range(GROUP_HEADS // 2):
            lanes = slice(pair * LANES, (pair + 1) * LANES)
            x_pair = x_dt[rows, lanes]
            total = skipped[rows, lanes]
            if block == 1:
                total = total + inter[:, lanes]
            for side in range(2):
                head = 2 * pair + side
                row = cumt_ref[pl.ds(first_head + head, 1), :]
                first, below = decay_tiles(cum_wide[head], row, block, lower)
                mixing = join_tiles(
                    (cb[:HALF, :HALF] * first).astype(BF), (cb[HALF:, :] * below).astype(BF)
                )
                keep = left if side == 0 else jnp.logical_not(left)
                total = total + dot_nn(mixing, jnp.where(keep, x_pair, zero))
            y_ref[rows, lanes] = total


def scan_forward(px, offset, taps, prep, slot, start, count):
    b_low, c_low, b_t, _, dt, cum, cum_t = prep
    rows = px.shape[0]
    width = GROUP_HEADS * 64
    tall = pl.BlockSpec((slot, LANES), lambda q, h: (q, 0))
    wide = pl.BlockSpec((LANES, slot), lambda q, h: (0, q))
    tile = pl.BlockSpec((slot, width), lambda q, h: (q, h))
    return pl.pallas_call(
        functools.partial(forward_kernel, start),
        grid=(rows // slot, count),
        in_specs=[
            pl.BlockSpec((slot, width), lambda q, h: (q, h + offset)),
            pl.BlockSpec((8, width), lambda q, h: (0, h + start)),
            tall,
            tall,
            wide,
            tall,
            tall,
            wide,
        ],
        out_specs=tile,
        out_shape=jax.ShapeDtypeStruct((rows, count * width), F32),
        compiler_params=params(),
        cost_estimate=cost(3.3e-6 * count),
        name="scan_forward",
    )(px, taps, b_low, c_low, b_t, dt, cum, cum_t)


def gate_kernel(count, *refs):
    y_refs = refs[:count]
    z_ref, gain_ref, gate_ref, inv_ref = refs[count:]
    y = jnp.concatenate([ref[...] for ref in y_refs], axis=1)
    z = z_ref[...]
    gated = y * (z * sigmoid(z))
    mean = jnp.sum(gated * gated, axis=1, keepdims=True) * (1.0 / gated.shape[1])
    inv = lax.rsqrt(mean + EPS)
    gate_ref[...] = (gated * inv * gain_ref[...]).astype(BF)
    inv_ref[...] = jnp.broadcast_to(inv, inv_ref.shape)


def row_tile(size, array):
    return pl.BlockSpec((size, array.shape[1]), lambda t: (t, 0))


def gate_forward(y_parts, pz, gain):
    rows, inner = pz.shape
    size = 128
    tile = pl.BlockSpec((size, inner), lambda t: (t, 0))
    return pl.pallas_call(
        functools.partial(gate_kernel, len(y_parts)),
        grid=(rows // size,),
        in_specs=[row_tile(size, y) for y in y_parts]
        + [tile, pl.BlockSpec((1, inner), lambda t: (0, 0))],
        out_specs=[tile, pl.BlockSpec((size, LANES), lambda t: (t, 0))],
        out_shape=[
            jax.ShapeDtypeStruct((rows, inner), BF),
            jax.ShapeDtypeStruct((rows, LANES), F32),
        ],
        compiler_params=params(),
        cost_estimate=cost(15e-6),
        name="gate_forward",
    )(*y_parts, pz, gain)


def gate_back_kernel(count, *refs):
    y_refs = refs[:count]
    z_ref, grad_ref, inv_ref, gain_ref, gy_ref, gz_ref = refs[count:]
    y = jnp.concatenate([ref[...] for ref in y_refs], axis=1)
    z = z_ref[...]
    grad = grad_ref[...]
    inv = inv_ref[:, 0:1]
    sig = sigmoid(z)
    silu = z * sig
    normal = y * silu * inv
    grad_normal = grad * gain_ref[...]
    mean = jnp.sum(grad_normal * normal, axis=1, keepdims=True) * (1.0 / y.shape[1])
    gated = inv * (grad_normal - normal * mean)
    gy_ref[...] = (gated * silu).astype(BF)
    gz_ref[...] = (gated * y * (sig + silu * (1.0 - sig))).astype(BF)


def gate_backward(y_parts, pz, grad_gate, inv, gain):
    rows, inner = pz.shape
    size = 128
    tile = pl.BlockSpec((size, inner), lambda t: (t, 0))
    return pl.pallas_call(
        functools.partial(gate_back_kernel, len(y_parts)),
        grid=(rows // size,),
        in_specs=[row_tile(size, y) for y in y_parts]
        + [
            tile,
            tile,
            pl.BlockSpec((size, LANES), lambda t: (t, 0)),
            pl.BlockSpec((1, inner), lambda t: (0, 0)),
        ],
        out_specs=[tile, tile],
        out_shape=[
            jax.ShapeDtypeStruct((rows, inner), BF),
            jax.ShapeDtypeStruct((rows, inner), BF),
        ],
        compiler_params=params(),
        cost_estimate=cost(24e-6),
        name="gate_backward",
    )(*y_parts, pz, grad_gate, inv, gain)


def head_sums(product, spread):
    high = product.astype(BF)
    low = (product - high.astype(F32)).astype(BF)
    return dot_nn(high, spread) + dot_nn(low, spread)


def backward_kernel(group_start, *refs):
    x_ref, taps_ref, y_ref, gy_ref, b_ref, c_ref, bt_ref, ct_ref = refs[:8]
    dt_ref, cum_ref, cumt_ref = refs[8:11]
    gx_ref, lines_ref, *totals = refs[-8:]
    gb_ref, gc_ref, one_ref, two_ref, cb_ref, heads_ref = totals
    befores = refs[12:-8]
    first_head = (pl.program_id(0) + group_start) * GROUP_HEADS
    seq = pl.program_id(1)
    slot = x_ref.shape[0]

    @pl.when((pl.program_id(0) == 0) & (seq == 0))
    def _():
        for i, total in enumerate(totals):
            total[...] = befores[i][...] if befores else jnp.zeros_like(total)

    at = pl.multiple_of(seq * slot, slot)
    whole_rows = pl.ds(at, slot)
    early_rows = pl.ds(at, STRETCH)
    late_rows = pl.ds(pl.multiple_of(at + STRETCH, STRETCH), STRETCH)
    shifted, pre = conv_parts(x_ref[...], taps_ref)
    sig = sigmoid(pre)
    active = pre * sig
    slope = sig + active * (1.0 - sig)
    x_low = active.astype(BF).astype(F32)
    gy_low = gy_ref[...]
    gy = gy_low.astype(F32)
    cum_wide, cum_x, dt_x, left = head_tables(cum_ref, dt_ref, first_head)
    x_dt = (x_low * dt_x).astype(BF)
    skip = taps_ref[5:6, :]

    grad_inter = (gy[STRETCH:] * jnp.exp(cum_x[STRETCH:])).astype(BF)
    fade = jnp.exp(cum_x[STRETCH - 1 : STRETCH] - cum_x[:STRETCH])
    scaled = (x_low[:STRETCH] * (fade * dt_x[:STRETCH])).astype(BF)
    state = dot_nn(bt_ref[:, :STRETCH], scaled)
    gc_ref[late_rows, :] += dot_nt(grad_inter, state.astype(BF))
    grad_state = dot_nn(ct_ref[:, STRETCH:], grad_inter).astype(BF)
    gb_ref[early_rows, :] += dot_nt(scaled, grad_state)
    grad_scaled = dot_nn(b_ref[:STRETCH, :], grad_state)
    last_sum = column_sum(grad_state.astype(F32) * state)

    lower = lower_mask()
    zero = jnp.zeros((STRETCH, LANES), BF)
    rest = []
    for block in range(2):
        rows = slice(block * STRETCH, (block + 1) * STRETCH)
        cb = dot_nt(c_ref[rows, :], b_ref[rows, :])
        cb_first = cb_below = None
        parts = []
        for pair in range(GROUP_HEADS // 2):
            lanes = slice(pair * LANES, (pair + 1) * LANES)
            x_pair = x_dt[rows, lanes]
            gy_pair = gy_low[rows, lanes]
            total = None
            for side in range(2):
                head = 2 * pair + side
                row = cumt_ref[pl.ds(first_head + head, 1), :]
                first, below = decay_tiles(cum_wide[head], row, block, lower)
                mixing = join_tiles(
                    (cb[:HALF, :HALF] * first).astype(BF), (cb[HALF:, :] * below).astype(BF)
                )
                keep = left if side == 0 else jnp.logical_not(left)
                gy_head = jnp.where(keep, gy_pair, zero)
                mix_first = dot_nt(gy_head[:HALF], x_pair[:HALF]) * first
                mix_below = dot_nt(gy_head[HALF:], x_pair) * below
                cb_first = mix_first if cb_first is None else cb_first + mix_first
                cb_below = mix_below if cb_below is None else cb_below + mix_below
                now = dot_tn(mixing, gy_head)
                total = now if total is None else total + now
            parts.append(total)
        cb_ref[seq, block, :HALF, :HALF] += cb_first
        cb_ref[seq, block, HALF:, :] += cb_below
        rest.append(jnp.concatenate(parts, axis=1))
    moved = x_dt.astype(F32) * jnp.concatenate(rest, axis=0)
    moved = jnp.concatenate(
        [moved[:STRETCH] + scaled.astype(F32) * grad_scaled, moved[STRETCH:]], axis=0
    )
    rest[0] = rest[0] + fade * grad_scaled
    grad_pull = jnp.concatenate(rest, axis=0)

    width = x_low.shape[1]
    spread = (
        lax.broadcasted_iota(jnp.int32, (width, LANES), 1)
        == first_head + lax.broadcasted_iota(jnp.int32, (width, LANES), 0) // 64
    ).astype(F32).astype(BF)
    moved = gy * (y_ref[...] - skip * x_low) - moved
    edge = lax.broadcasted_iota(jnp.int32, (8, 1), 0) == 7
    moved = jnp.concatenate(
        [
            moved[: STRETCH - 8],
            moved[STRETCH - 8 : STRETCH] + jnp.where(edge, last_sum, 0.0),
            moved[STRETCH:],
        ],
        axis=0,
    )
    one_ref[whole_rows, :] += head_sums(moved, spread)
    two_ref[whole_rows, :] += head_sums(x_low * grad_pull, spread)
    third = lax.broadcasted_iota(jnp.int32, (8, 1), 0) == 2
    skip_line = jnp.where(third, column_sum(gy * x_low), 0.0)
    heads_ref[...] += head_sums(skip_line, spread)

    grad_pre = (skip * gy + dt_x * grad_pull) * slope
    gx_ref[...] = conv_back(grad_pre, taps_ref).astype(BF)
    lines = [column_sum(grad_pre * shifted[k]) for k in range(4)] + [column_sum(grad_pre)]
    lines = jnp.concatenate(lines + [jnp.zeros((3, width), F32)], axis=0)

    @pl.when(seq == 0)
    def _():
        lines_ref[...] = lines

    @pl.when(seq > 0)
    def _():
        lines_ref[...] += lines


def scan_backward(px, at, taps, y_rows, y_at, grad_y, prep, slot, start, count, before=None):
    b_low, c_low, b_t, c_t, dt, cum, cum_t = prep
    rows = px.shape[0]
    width = GROUP_HEADS * 64
    seqs = rows // slot
    tall = pl.BlockSpec((slot, LANES), lambda h, q: (q, 0))
    wide = pl.BlockSpec((LANES, slot), lambda h, q: (0, q))
    tile = pl.BlockSpec((slot, width), lambda h, q: (q, h + at))
    flat = jax.ShapeDtypeStruct((rows, LANES), F32)
    whole = pl.BlockSpec((rows, LANES), lambda h, q: (0, 0))
    totals = [whole] * 4 + [
        pl.BlockSpec((seqs, 2, STRETCH, STRETCH), lambda h, q: (0, 0, 0, 0)),
        pl.BlockSpec((8, LANES), lambda h, q: (0, 0)),
    ]
    extra, extra_specs, aliases = [jnp.zeros((8, LANES), BF)], [pl.BlockSpec(memory_space=pl.ANY)], {}
    if before is not None:
        if before[0].shape == px.shape:
            extra = [before[0]]
            aliases[11] = 0
        extra = extra + list(before[2:])
        extra_specs = extra_specs + totals
        aliases.update({12 + i: 2 + i for i in range(6)})
    return pl.pallas_call(
        functools.partial(backward_kernel, start),
        grid=(count, seqs),
        in_specs=[
            tile,
            pl.BlockSpec((8, width), lambda h, q: (0, h + start)),
            pl.BlockSpec((slot, width), lambda h, q: (q, h + y_at)),
            pl.BlockSpec((slot, width), lambda h, q: (q, h + start)),
            tall,
            tall,
            wide,
            wide,
            tall,
            tall,
            wide,
        ]
        + extra_specs,
        out_specs=[tile, pl.BlockSpec((8, width), lambda h, q: (0, h))] + totals,
        out_shape=[
            jax.ShapeDtypeStruct(px.shape, BF),
            jax.ShapeDtypeStruct((8, count * width), F32),
            flat,
            flat,
            flat,
            flat,
            jax.ShapeDtypeStruct((seqs, 2, STRETCH, STRETCH), F32),
            jax.ShapeDtypeStruct((8, LANES), F32),
        ],
        input_output_aliases=aliases,
        compiler_params=params(),
        cost_estimate=cost(3.3e-6 * count),
        name="scan_backward",
    )(px, taps, y_rows, grad_y, b_low, c_low, b_t, c_t, dt, cum, cum_t, *extra)


def finish_kernel(
    head_count,
    raw_ref,
    taps_ref,
    heads_ref,
    b_ref,
    c_ref,
    dt_ref,
    gb_ref,
    gc_ref,
    one_ref,
    two_ref,
    cb_ref,
    head_before_ref,
    before_ref,
    out_ref,
    lines_ref,
    head_total_ref,
):
    @pl.when(pl.program_id(0) == 0)
    def _():
        lines_ref[...] = jnp.zeros_like(lines_ref)
        head_total_ref[...] = head_before_ref[...]

    shifted, pre = conv_parts(raw_ref[:, : 2 * LANES], taps_ref)
    sig = sigmoid(pre)
    slope = sig + pre * sig * (1.0 - sig)
    grad_b, grad_c = [], []
    for block in range(2):
        rows = slice(block * STRETCH, (block + 1) * STRETCH)
        cb = cb_ref[0, block].astype(BF)
        grad_c.append(gc_ref[rows, :] + dot_nn(cb, b_ref[rows, :]))
        grad_b.append(gb_ref[rows, :] + dot_tn(cb, c_ref[rows, :]))
    grad_active = jnp.concatenate(
        [jnp.concatenate(grad_b, axis=0), jnp.concatenate(grad_c, axis=0)], axis=1
    )
    grad_pre = grad_active * slope
    lines = [column_sum(grad_pre * shifted[k]) for k in range(4)] + [column_sum(grad_pre)]
    lines.append(jnp.zeros((3, 2 * LANES), F32))
    lines_ref[...] += jnp.concatenate(lines, axis=0)

    dt = dt_ref[...]
    two = two_ref[...]
    rate = heads_ref[1:2, :]
    place = row_index(dt)
    grad_cum = one_ref[...]
    inside = place % STRETCH
    step = 1
    while step < STRETCH:
        moved = pltpu.roll(grad_cum, grad_cum.shape[0] - step, 0)
        grad_cum = grad_cum + jnp.where(inside < STRETCH - step, moved, 0.0)
        step *= 2
    grad_dt = grad_cum * rate + two
    lane = lax.broadcasted_iota(jnp.int32, (1, LANES), 1)
    raw = jnp.where(lane < head_count, raw_ref[:, 2 * LANES : 3 * LANES], 0.0)
    grad_raw = grad_dt * sigmoid(raw + heads_ref[0:1, :])
    head_total_ref[...] += jnp.concatenate(
        [column_sum(grad_raw), column_sum(grad_cum * dt) * rate, jnp.zeros((6, LANES), F32)], axis=0
    )
    out_ref[:, : 2 * LANES] = conv_back(grad_pre, taps_ref).astype(BF)
    out_ref[:, 2 * LANES : 3 * LANES] = grad_raw.astype(BF)
    out_ref[:, 3 * LANES :] = jnp.zeros_like(out_ref[:, 3 * LANES :])


def finish(raw, at, taps, heads, head_count, prep, totals, grads, narrow, grads_at, slot):
    b_low, c_low, _, _, dt, _, _ = prep
    rows = raw.shape[0]
    seqs = rows // slot
    tall = pl.BlockSpec((slot, LANES), lambda q: (q, 0))
    return pl.pallas_call(
        functools.partial(finish_kernel, head_count),
        grid=(seqs,),
        in_specs=[
            pl.BlockSpec((slot, 3 * LANES), lambda q: (q, at)),
            pl.BlockSpec((8, 2 * LANES), lambda q: (0, 0)),
            pl.BlockSpec((8, LANES), lambda q: (0, 0)),
            tall,
            tall,
            tall,
            tall,
            tall,
            tall,
            tall,
            pl.BlockSpec((1, 2, STRETCH, STRETCH), lambda q: (q, 0, 0, 0)),
            pl.BlockSpec((8, LANES), lambda q: (0, 0)),
            pl.BlockSpec(memory_space=pl.ANY),
        ],
        out_specs=[
            pl.BlockSpec((slot, narrow), lambda q: (q, grads_at)),
            pl.BlockSpec((8, 2 * LANES), lambda q: (0, 0)),
            pl.BlockSpec((8, LANES), lambda q: (0, 0)),
        ],
        out_shape=[
            jax.ShapeDtypeStruct(grads.shape, BF),
            jax.ShapeDtypeStruct((8, 2 * LANES), F32),
            jax.ShapeDtypeStruct((8, LANES), F32),
        ],
        input_output_aliases={12: 0},
        compiler_params=params(),
        cost_estimate=cost(3e-6),
        name="finish",
    )(raw, taps, heads, b_low, c_low, dt, *totals, grads)


def project_kernel(rows_ref, weight_ref, out_ref):
    out_ref[...] = dot_nn(rows_ref[...], weight_ref[...])


def project(normed, weight, at, count, size):
    rows, depth = normed.shape
    return pl.pallas_call(
        project_kernel,
        grid=(count,),
        in_specs=[
            pl.BlockSpec((rows, depth), lambda j: (0, 0)),
            pl.BlockSpec((depth, size), lambda j: (0, j + at)),
        ],
        out_specs=pl.BlockSpec((rows, size), lambda j: (0, j)),
        out_shape=jax.ShapeDtypeStruct((rows, count * size), F32),
        compiler_params=params(),
        cost_estimate=cost(2.5e-6 * count),
        name="project",
    )(normed, weight)


def pair_kernel(mine_ref, other_ref, grad_ref, keep_ref, give_ref):
    grad = grad_ref[...]
    give_ref[...] = dot_nn(other_ref[...], grad).astype(give_ref.dtype)
    keep_ref[...] = dot_nn(mine_ref[...], grad).astype(keep_ref.dtype)


def weight_grads(mine, other, grad, at, count, size):
    depth, rows = mine.shape
    whole = pl.BlockSpec((depth, rows), lambda j: (0, 0))
    tile = pl.BlockSpec((depth, size), lambda j: (0, j))
    shape = jax.ShapeDtypeStruct((depth, count * size), BF)
    return pl.pallas_call(
        pair_kernel,
        grid=(count,),
        in_specs=[whole, whole, pl.BlockSpec((rows, size), lambda j: (0, j + at))],
        out_specs=[tile, tile],
        out_shape=[shape, shape],
        compiler_params=params(),
        cost_estimate=cost(2.5e-6 * count),
        name="weight_grads",
    )(mine, other, grad)


def input_grads_kernel(sizes, ends, has_before, final, *refs):
    pairs = [refs[2 * i : 2 * i + 2] for i in range(len(sizes))]
    refs = refs[2 * len(sizes) :]
    steps = sum(sizes)
    step = pl.program_id(0)
    if has_before:
        before_ref, refs = refs[0], refs[1:]
    if final:
        hidden_ref, inv_ref, gain_ref, mask_ref, cot_ref, out_ref, total = refs
    else:
        (total,) = refs

    def add(grad_ref, weight):
        now = dot_nt(grad_ref[...], weight)

        @pl.when(step == 0)
        def _():
            total[...] = now + before_ref[...] if has_before else now

        @pl.when(step > 0)
        def _():
            total[...] += now

    begin = 0
    for (grad_ref, weight_ref), size, end in zip(pairs, sizes, ends):
        full = size if end is None else size - 1

        @pl.when((step >= begin) & (step < begin + full))
        def _(grad_ref=grad_ref, weight_ref=weight_ref):
            add(grad_ref, weight_ref[...])

        if end is not None:

            @pl.when(step == begin + full)
            def _(grad_ref=grad_ref, weight_ref=weight_ref, end=end):
                weight = weight_ref[...]
                lane = lax.broadcasted_iota(jnp.int32, weight.shape, 1)
                add(grad_ref, jnp.where(lane < end, weight, jnp.zeros_like(weight)))

        begin += size
    if final:

        @pl.when(step >= steps)
        def _():
            tile = hidden_ref.shape[0]
            grad = total[pl.ds(pl.multiple_of((step - steps) * tile, tile), tile), :]
            inv = inv_ref[...]
            normal = hidden_ref[...] * inv
            grad = grad * gain_ref[...]
            inside = jnp.sum(grad * normal, axis=1, keepdims=True) * (1.0 / grad.shape[1])
            out_ref[...] = inv * (grad - normal * inside) + mask_ref[...] * cot_ref[...]


def input_grads(grads, places, weight, before=None, final=None):
    rows = grads[0].shape[0]
    width = weight.shape[0]
    size, tile = 512, 128
    sizes = [g.shape[1] // size for g in grads]
    steps = sum(sizes)
    in_specs, args, begin = [], [], 0
    for grad, (at, _), count in zip(grads, places, sizes):

        def place(k, begin=begin, count=count, at=0):
            return (0, at + jnp.clip(k - begin, 0, count - 1))

        in_specs += [
            pl.BlockSpec((rows, size), place),
            pl.BlockSpec((width, size), functools.partial(place, at=at)),
        ]
        args += [grad, weight]
        begin += count
    if before is not None:
        in_specs.append(pl.BlockSpec((rows, width), lambda k: (0, 0), pipeline_mode=pl.Buffered(1)))
        args.append(before)
    if final:

        def row(k):
            return (jnp.clip(k - steps, 0, rows // tile - 1), 0)

        line = pl.BlockSpec((1, width), lambda k: (0, 0))
        column = pl.BlockSpec((tile, 1), row)
        wide = pl.BlockSpec((tile, width), row)
        in_specs += [wide, column, line, column, wide]
        args += list(final)
        out_specs = wide
        out_shape = jax.ShapeDtypeStruct((rows, width), F32)
        scratch = [pltpu.VMEM((rows, width), F32)]
    else:
        out_specs = pl.BlockSpec((rows, width), lambda k: (0, 0))
        out_shape = jax.ShapeDtypeStruct((rows, width), F32)
        scratch = []
    ends = [end for _, end in places]
    return pl.pallas_call(
        functools.partial(input_grads_kernel, sizes, ends, before is not None, bool(final)),
        grid=(steps + (rows // tile if final else 0),),
        in_specs=in_specs,
        out_specs=out_specs,
        out_shape=out_shape,
        scratch_shapes=scratch,
        compiler_params=params(),
        cost_estimate=cost(2.5e-6 * steps),
        name="input_grads",
    )(*args)


def swap(values, bit, shards):
    return lax.ppermute(values, "shard", [(i, i ^ (1 << bit)) for i in range(shards)])


def border(moving, *values):
    ready = lax.optimization_barrier(tuple(one.got for one in moving) + values)
    for one, got in zip(moving, ready):
        one.got = got
        one.finish()
    rest = ready[len(moving) :]
    return rest[0] if len(rest) == 1 else rest


class Gather:
    def __init__(self, own, order, shards, place):
        self.now, self.order, self.shards, self.place = own, list(order), shards, place
        self.live, self.columns = [], own.shape[-1]

    def start(self):
        self.bit = self.order.pop(0)
        self.got = swap(self.now, self.bit, self.shards)

    def finish(self):
        mine = (self.place >> self.bit) & 1
        axis = len([b for b in self.live if b > self.bit])
        first = jnp.where(mine == 0, self.now, self.got)
        second = jnp.where(mine == 0, self.got, self.now)
        self.now = jnp.stack([first, second], axis=axis)
        self.live.append(self.bit)

    def whole(self):
        while self.order:
            self.start()
            self.finish()
        return self.now


class Spread:
    def __init__(self, now, bits, shards, groups):
        self.now, self.bits, self.shards, self.groups = now, list(bits), shards, groups

    def start(self):
        if self.bits:
            self.got = swap(self.now, self.bits.pop(0), self.shards)
        else:
            pairs = [(i, (i + 1) % self.groups) for i in range(self.groups)]
            self.got = lax.ppermute(self.now, "group", pairs)

    def finish(self):
        self.now = self.now + self.got

    def result(self):
        while self.bits:
            self.start()
            self.finish()
        return self.now


class Group:
    def __init__(self, now, groups):
        self.now, self.groups = now, groups

    def start(self):
        self.pairs = [(i, (i + 1) % self.groups) for i in range(self.groups)]
        self.got = lax.ppermute(self.now, "group", self.pairs)

    def finish(self):
        total, got = self.now.astype(F32), self.got
        for step in range(1, self.groups):
            if step > 1:
                got = lax.ppermute(got, "group", self.pairs)
            total = total + got.astype(F32)
        self.now = total


class Sum:
    def __init__(self, pair, order, shards, groups, place, part, group_first=False):
        self.keep, self.give = pair
        self.shards, self.groups, self.place, self.part = shards, groups, place, part
        self.columns, self.dtype = self.keep.shape[-1], self.keep.dtype
        self.group_first = group_first and groups == 2
        self.todo = [0] + (["group"] if self.group_first else []) + list(order) + ["end"]
        self.live = list(range(shards.bit_length() - 2, 0, -1))
        self.now = None

    def start(self):
        self.bit = bit = self.todo.pop(0)
        if bit == "end":
            pairs = [(i, (i + 1) % self.groups) for i in range(self.groups)]
            self.got = lax.ppermute(self.now, "group", pairs)
        elif bit == "group":
            half = self.columns // 2
            mine = lax.axis_index("group")
            axis = self.now.ndim - 1
            self.keep = lax.dynamic_slice_in_dim(self.now, mine * half, half, axis)
            give = lax.dynamic_slice_in_dim(self.now, (1 - mine) * half, half, axis)
            self.got = lax.ppermute(give, "group", [(0, 1), (1, 0)])
        elif bit == 0:
            self.got = swap(self.give, 0, self.shards)
        else:
            axis = self.live.index(bit)
            mine = (self.place >> bit) & 1
            self.keep = lax.dynamic_index_in_dim(self.now, mine, axis, keepdims=False)
            give = lax.dynamic_index_in_dim(self.now, 1 - mine, axis, keepdims=False)
            self.live.remove(bit)
            self.got = swap(give, bit, self.shards)

    def finish(self):
        if self.bit == "end" and self.group_first:
            first = lax.axis_index("group") == 0
            halves = [jnp.where(first, self.now, self.got), jnp.where(first, self.got, self.now)]
            self.now = jnp.concatenate(halves, axis=-1)
        elif self.bit == "end":
            total, got = self.now.astype(F32), self.got
            for step in range(1, self.groups):
                if step > 1:
                    pairs = [(i, (i + 1) % self.groups) for i in range(self.groups)]
                    got = lax.ppermute(got, "group", pairs)
                total = total + got.astype(F32)
            self.now = total
        else:
            now = self.keep.astype(F32) + self.got.astype(F32)
            if self.todo != ["end"] or not self.group_first:
                now = now.astype(self.dtype)
            if self.bit == 0:
                now = now.reshape((2,) * len(self.live) + (self.part, self.columns))
            self.now = now

    def result(self):
        while self.todo:
            self.start()
            self.finish()
        return self.now


def local(
    shards,
    groups,
    hidden_in,
    lengths,
    pre_gain,
    in_proj,
    conv_weight,
    conv_bias,
    head_params,
    gate_gain,
    out_proj,
    cotangent,
):
    micro, own, slot, width = hidden_in.shape
    rows = micro * own * slot
    inner = out_proj.shape[0] * shards
    channels = conv_bias.shape[0] * shards
    heads = head_params.shape[1]
    tail = channels - inner + heads
    part = in_proj.shape[0]
    out_part = out_proj.shape[0]
    own_conv = conv_bias.shape[0]
    taps = conv_weight.shape[0]
    hidden = hidden_in.reshape(rows, width)
    cot = cotangent.reshape(rows, width)
    place = lax.axis_index("shard")
    core = place & 1
    chip_bits = list(range(1, shards.bit_length() - 1))
    up = chip_bits
    down = chip_bits[::-1]

    w_in = lax.all_gather(in_proj, "shard", axis=0, tiled=True)
    w_out = lax.all_gather(out_proj, "shard", axis=0, tiled=True)
    small = jnp.concatenate([pre_gain, gate_gain, conv_bias, conv_weight.reshape(-1)], axis=0)
    small = small.astype(F32)
    small = jnp.pad(small, (0, -small.shape[0] % LANES))[None, :]
    packed = Gather(small, down + [0], shards, place).whole().reshape(shards, -1)
    sizes = (part, out_part, own_conv, taps * own_conv)
    ends = [sum(sizes[: i + 1]) for i in range(4)]
    pre_all = packed[:, : ends[0]].reshape(1, width)
    gate_all = packed[:, ends[0] : ends[1]].reshape(1, inner)
    bias_all = packed[:, ends[1] : ends[2]].reshape(1, channels)
    taps_all = packed[:, ends[2] : ends[3]].reshape(shards, taps, -1)
    taps_all = jnp.swapaxes(taps_all, 0, 1).reshape(taps, channels)
    skip_row = jnp.pad(jnp.repeat(head_params[2], inner // heads), (0, channels - inner))
    table = jnp.concatenate(
        [taps_all, bias_all, skip_row[None, :], jnp.zeros((2, channels), F32)], axis=0
    )
    table_x, table_bc = table[:, :inner], table[:, inner:]
    rate = -jnp.exp(head_params[1])
    head_rows = jnp.pad(
        jnp.stack([head_params[0], rate], axis=0), ((0, 6), (0, LANES - heads))
    )

    inv_first = lax.rsqrt(jnp.mean(hidden * hidden, axis=-1, keepdims=True) + EPS)
    normed = (hidden * inv_first * pre_all).astype(BF)
    turned = normed.T.reshape(shards // 2, 2, part, rows)
    mine = lax.dynamic_index_in_dim(turned, core, 1, keepdims=False).reshape(-1, rows)
    other = lax.dynamic_index_in_dim(turned, 1 - core, 1, keepdims=False).reshape(-1, rows)
    positions = jnp.arange(slot, dtype=jnp.int32)
    mask = (positions[None, :] < lengths.reshape(-1)[:, None]).astype(F32).reshape(rows, 1)
    grad_low = (mask * cot).astype(BF)

    size = 4 * LANES
    blocks = inner // size
    raw_at = inner // (3 * LANES)
    prep_at = (raw_at, table_bc, head_rows, heads)
    px = project(normed, w_in, blocks, blocks + 1, size)
    prep = prepare(px, *prep_at, slot)
    unit = GROUP_HEADS * 64
    y_rows = scan_forward(px, 0, table_x, prep, slot, 0, inner // unit)
    pz = project(normed, w_in, 0, blocks, size)
    gate_low, inv = gate_forward([y_rows], pz, gate_all)

    g_out = dot_tn(gate_low, grad_low).astype(BF)
    g_out, grad_low, mine, other = border([], g_out, grad_low, mine, other)
    sum_out = lax.psum_scatter(g_out, "shard", scatter_dimension=0, tiled=True)
    grad_gate = dot_nt(grad_low, w_out)
    grad_y, grad_z = gate_backward([y_rows], pz, grad_gate, inv, gate_all)
    g_z = dot_nn(turned.reshape(width, rows), grad_z).astype(BF)
    g_z, grad_y = border([], g_z, grad_y)
    sum_z = lax.psum_scatter(g_z, "shard", scatter_dimension=0, tiled=True)

    reduce = functools.partial(Sum, shards=shards, groups=groups, place=place, order=up)
    third = inner // unit // 3
    outs = None
    for start in (0, third):
        outs_now = scan_backward(
            px, start, table_x, y_rows, start, grad_y, prep, slot, start, third, before=outs
        )
        outs_first, outs = outs, outs_now
    lines_x = [outs_first[1], outs[1]]
    b_blocks = 2 * third * unit // size
    pair_b = weight_grads(mine, other, outs[0], 0, b_blocks, size)
    *pair_b, grad_y = border([], *pair_b, grad_y)
    s_b = reduce(pair_b, part=part)
    s_b.start()
    grad_y, sum_out = border([], grad_y, sum_out)
    rest = inner // unit - 2 * third
    outs = scan_backward(
        px, 2 * third, table_x, y_rows, 2 * third, grad_y, prep, slot, 2 * third, rest, before=outs
    )
    s_out = Group(sum_out, groups)
    s_out.start()
    mine, *outs = border([s_b, s_out], mine, *outs)
    lines_x.append(outs[1])
    s_b.start()
    outs[0], s_b.keep = border([], outs[0], s_b.keep)
    grad_x, lines_bc, head_total = finish(
        px, *prep_at, prep, outs[2:], outs[0], size, blocks, slot
    )
    pair_a = weight_grads(mine, other, grad_x, b_blocks, blocks + 1 - b_blocks, size)

    lines = jnp.concatenate(lines_x + [lines_bc], axis=1)
    head_line = head_total[:3].reshape(1, 3 * LANES)
    head_line = jnp.pad(head_line, ((0, 0), (0, channels - 3 * LANES)))
    small = jnp.concatenate([lines[:5], head_line, lines[6:]], axis=0)
    s_small = Spread(small, [0] + up, shards, groups)
    s_small.start()
    *pair_a, grad_z, grad_x = border([s_small], *pair_a, grad_z, grad_x)
    s_a = reduce(pair_a, part=part)
    s_a.start()
    s_small.start()
    part_sum = input_grads([grad_z], [(0, None)], w_in)
    part_sum, grad_x = border([s_b, s_a, s_small], part_sum, grad_x)
    s_a.start()
    s_small.start()
    s_b.start()
    grad_input = input_grads(
        [grad_x],
        [(blocks, tail % size)],
        w_in,
        before=part_sum,
        final=(hidden, inv_first, pre_all, mask, cot),
    )
    gate_low, grad_input, sum_z = border([s_a, s_b, s_small], gate_low, grad_input, sum_z)
    s_a.start()
    s_small.start()
    s_b.start()
    s_z = Group(sum_z, groups)
    s_z.start()
    layer_out = mask * (hidden + dot_nn(gate_low, w_out))
    layer_out = border([s_a, s_small, s_b, s_z], layer_out)
    s_a.start()
    s_small.start()
    s_b.start()
    for one in (s_small, s_a, s_b):
        one.finish()
    sum_a, small = s_a.result(), s_small.now
    b_columns = b_blocks * size
    g_in = jnp.concatenate(
        [s_z.now, s_b.result(), sum_a[:, : inner - b_columns + tail]], axis=1
    )
    g_out = s_out.now

    def gain_grads(weight, grads, gain):
        return jnp.sum(weight.astype(F32) * grads, axis=1) / gain.astype(F32)

    g_pre = gain_grads(in_proj, g_in, pre_gain)
    g_gate = gain_grads(out_proj, g_out, gate_gain)
    g_lines = lax.dynamic_slice(small, (0, place * own_conv), (5, own_conv))
    g_heads = small[5, : 3 * LANES].reshape(3, LANES)[:, :heads]
    return (
        layer_out.reshape(hidden_in.shape),
        grad_input.reshape(hidden_in.shape),
        g_pre,
        g_in,
        g_lines[:4],
        g_lines[4],
        g_heads,
        g_gate,
        g_out,
    )


def solution(mesh):
    rows = P(None, ("group", "shard"), None, None)
    in_specs = (
        rows,
        P(None, ("group", "shard")),
        P("shard"),
        P("shard", None),
        P(None, "shard"),
        P("shard"),
        P(),
        P("shard"),
        P("shard", None),
        rows,
    )
    out_specs = (
        rows,
        rows,
        P("shard"),
        P("shard", None),
        P(None, "shard"),
        P("shard"),
        P(),
        P("shard"),
        P("shard", None),
    )
    body = functools.partial(local, mesh.shape["shard"], mesh.shape["group"])
    return jax.shard_map(body, mesh=mesh, in_specs=in_specs, out_specs=out_specs, check_vma=False)
```

```python
import functools

import jax
import jax.numpy as jnp
from jax import lax
from jax.experimental import pallas as pl
from jax.experimental.pallas import tpu as pltpu
from jax.sharding import PartitionSpec as P

STRETCH = 256
HALF = 128
LANES = 128
GROUP_HEADS = 8
EPS = 1e-05
BF = jnp.bfloat16
F32 = jnp.float32
VMEM_BYTES = 56 * 1024 * 1024


def params(**kwargs):
    return pltpu.CompilerParams(vmem_limit_bytes=VMEM_BYTES, **kwargs)


def cost(seconds):
    return pl.CostEstimate(
        flops=int(seconds * 2.0e13), bytes_accessed=int(seconds * 6.0e10), transcendentals=0
    )


def dot_nn(left, right):
    return lax.dot_general(left, right, (((1,), (0,)), ((), ())), preferred_element_type=F32)


def dot_nt(left, right):
    return lax.dot_general(left, right, (((1,), (1,)), ((), ())), preferred_element_type=F32)


def dot_tn(left, right):
    return lax.dot_general(left, right, (((0,), (0,)), ((), ())), preferred_element_type=F32)


def sigmoid(values):
    return 1.0 / (1.0 + jnp.exp(-values))


def row_index(values):
    return lax.broadcasted_iota(jnp.int32, (values.shape[0], 1), 0)


def shift_down(values, count):
    rolled = pltpu.roll(values, count, 0)
    return jnp.where(row_index(values) >= count, rolled, 0.0)


def shift_up(values, count):
    rows = values.shape[0]
    rolled = pltpu.roll(values, rows - count, 0)
    return jnp.where(row_index(values) < rows - count, rolled, 0.0)


def conv_parts(values, taps_ref):
    shifted = [shift_down(values, 3), shift_down(values, 2), shift_down(values, 1), values]
    pre = taps_ref[4:5, :]
    for k in range(4):
        pre = pre + taps_ref[k : k + 1, :] * shifted[k]
    return shifted, pre


def conv_back(grad_pre, taps_ref):
    total = taps_ref[3:4, :] * grad_pre
    for k in range(3):
        total = total + taps_ref[k : k + 1, :] * shift_up(grad_pre, 3 - k)
    return total


def column_sum(values):
    return jnp.sum(values, axis=0, keepdims=True)


def prepare_kernel(head_count, raw_ref, taps_ref, heads_ref, b_ref, c_ref, bt_ref, ct_ref, dt_ref, cum_ref, cumt_ref):
    _, pre = conv_parts(raw_ref[:, : 2 * LANES], taps_ref)
    active = pre * sigmoid(pre)
    b_part, c_part = active[:, :LANES], active[:, LANES:]
    b_ref[...] = b_part.astype(BF)
    c_ref[...] = c_part.astype(BF)
    bt_ref[...] = b_part.T.astype(BF)
    ct_ref[...] = c_part.T.astype(BF)
    lane = lax.broadcasted_iota(jnp.int32, (1, LANES), 1)
    raw = jnp.where(lane < head_count, raw_ref[:, 2 * LANES : 3 * LANES], 0.0) + heads_ref[0:1, :]
    dt = jnp.maximum(raw, 0.0) + jnp.log1p(jnp.exp(-jnp.abs(raw)))
    cum = dt * heads_ref[1:2, :]
    place = row_index(cum) % STRETCH
    step = 1
    while step < STRETCH:
        cum = cum + jnp.where(place >= step, pltpu.roll(cum, step, 0), 0.0)
        step *= 2
    dt_ref[...] = dt
    cum_ref[...] = cum
    cumt_ref[...] = cum.T


def prepare(raw, at, taps, heads, head_count, slot):
    rows = raw.shape[0]
    tall = pl.BlockSpec((slot, LANES), lambda q: (q, 0))
    wide = pl.BlockSpec((LANES, slot), lambda q: (0, q))
    return pl.pallas_call(
        functools.partial(prepare_kernel, head_count),
        grid=(rows // slot,),
        in_specs=[
            pl.BlockSpec((slot, 4 * LANES), lambda q: (q, at)),
            pl.BlockSpec((8, 2 * LANES), lambda q: (0, 0)),
            pl.BlockSpec((8, LANES), lambda q: (0, 0)),
        ],
        out_specs=[tall, tall, wide, wide, tall, tall, wide],
        out_shape=[
            jax.ShapeDtypeStruct((rows, LANES), BF),
            jax.ShapeDtypeStruct((rows, LANES), BF),
            jax.ShapeDtypeStruct((LANES, rows), BF),
            jax.ShapeDtypeStruct((LANES, rows), BF),
            jax.ShapeDtypeStruct((rows, LANES), F32),
            jax.ShapeDtypeStruct((rows, LANES), F32),
            jax.ShapeDtypeStruct((LANES, rows), F32),
        ],
        compiler_params=params(),
        name="prepare",
    )(raw, taps, heads)


def head_tables(cum_ref, dt_ref, first_head):
    shift = lax.rem(LANES - first_head, LANES)
    cum = pltpu.roll(cum_ref[...], shift, 1)
    dt = pltpu.roll(dt_ref[...], shift, 1)
    rows = cum.shape[0]
    cum_wide = [jnp.broadcast_to(cum[:, i : i + 1], (rows, LANES)) for i in range(GROUP_HEADS)]
    dt_wide = [jnp.broadcast_to(dt[:, i : i + 1], (rows, LANES)) for i in range(GROUP_HEADS)]
    left = lax.broadcasted_iota(jnp.int32, (1, LANES), 1) < LANES // 2

    def spread(wide):
        return jnp.concatenate(
            [jnp.where(left, wide[i], wide[i + 1]) for i in range(0, GROUP_HEADS, 2)], axis=1
        )

    return cum_wide, spread(cum_wide), spread(dt_wide), left


def decay_tiles(cum_wide, cumt_row, block, lower):
    begin = block * STRETCH
    top = cum_wide[begin : begin + HALF]
    low = cum_wide[begin + HALF : begin + STRETCH]
    row_left = cumt_row[:, begin : begin + HALF]
    row_right = cumt_row[:, begin + HALF : begin + STRETCH]
    first = jnp.where(lower, jnp.exp(top - row_left), 0.0)
    second = jnp.exp(low - row_left)
    third = jnp.where(lower, jnp.exp(low - row_right), 0.0)
    return first, jnp.concatenate([second, third], axis=1)


def join_tiles(first, below):
    return jnp.concatenate(
        [jnp.concatenate([first, jnp.zeros_like(first)], axis=1), below], axis=0
    )


def lower_mask():
    return lax.broadcasted_iota(jnp.int32, (HALF, HALF), 0) >= lax.broadcasted_iota(
        jnp.int32, (HALF, HALF), 1
    )


def forward_kernel(
    group_start, x_ref, taps_ref, b_ref, c_ref, bt_ref, dt_ref, cum_ref, cumt_ref, y_ref
):
    first_head = (pl.program_id(1) + group_start) * GROUP_HEADS
    _, pre = conv_parts(x_ref[...], taps_ref)
    x_low = (pre * sigmoid(pre)).astype(BF).astype(F32)
    cum_wide, cum_x, dt_x, left = head_tables(cum_ref, dt_ref, first_head)
    x_dt = (x_low * dt_x).astype(BF)
    skipped = taps_ref[5:6, :] * x_low
    fade = jnp.exp(cum_x[STRETCH - 1 : STRETCH] - cum_x[:STRETCH])
    scaled = (x_low[:STRETCH] * (fade * dt_x[:STRETCH])).astype(BF)
    state = dot_nn(bt_ref[:, :STRETCH], scaled).astype(BF)
    inter = jnp.exp(cum_x[STRETCH:]) * dot_nn(c_ref[STRETCH:, :], state)
    lower = lower_mask()
    zero = jnp.zeros((STRETCH, LANES), BF)
    for block in range(2):
        rows = slice(block * STRETCH, (block + 1) * STRETCH)
        cb = dot_nt(c_ref[rows, :], b_ref[rows, :])
        for pair in range(GROUP_HEADS // 2):
            lanes = slice(pair * LANES, (pair + 1) * LANES)
            x_pair = x_dt[rows, lanes]
            total = skipped[rows, lanes]
            if block == 1:
                total = total + inter[:, lanes]
            for side in range(2):
                head = 2 * pair + side
                row = cumt_ref[pl.ds(first_head + head, 1), :]
                first, below = decay_tiles(cum_wide[head], row, block, lower)
                mixing = join_tiles(
                    (cb[:HALF, :HALF] * first).astype(BF), (cb[HALF:, :] * below).astype(BF)
                )
                keep = left if side == 0 else jnp.logical_not(left)
                total = total + dot_nn(mixing, jnp.where(keep, x_pair, zero))
            y_ref[rows, lanes] = total


def scan_forward(px, offset, taps, prep, slot, start, count):
    b_low, c_low, b_t, _, dt, cum, cum_t = prep
    rows = px.shape[0]
    width = GROUP_HEADS * 64
    tall = pl.BlockSpec((slot, LANES), lambda q, h: (q, 0))
    wide = pl.BlockSpec((LANES, slot), lambda q, h: (0, q))
    tile = pl.BlockSpec((slot, width), lambda q, h: (q, h))
    return pl.pallas_call(
        functools.partial(forward_kernel, start),
        grid=(rows // slot, count),
        in_specs=[
            pl.BlockSpec((slot, width), lambda q, h: (q, h + offset)),
            pl.BlockSpec((8, width), lambda q, h: (0, h + start)),
            tall,
            tall,
            wide,
            tall,
            tall,
            wide,
        ],
        out_specs=tile,
        out_shape=jax.ShapeDtypeStruct((rows, count * width), F32),
        compiler_params=params(),
        cost_estimate=cost(3.3e-6 * count),
        name="scan_forward",
    )(px, taps, b_low, c_low, b_t, dt, cum, cum_t)


def gate_kernel(count, *refs):
    y_refs = refs[:count]
    z_ref, gain_ref, gate_ref, inv_ref = refs[count:]
    y = jnp.concatenate([ref[...] for ref in y_refs], axis=1)
    z = z_ref[...]
    gated = y * (z * sigmoid(z))
    mean = jnp.sum(gated * gated, axis=1, keepdims=True) * (1.0 / gated.shape[1])
    inv = lax.rsqrt(mean + EPS)
    gate_ref[...] = (gated * inv * gain_ref[...]).astype(BF)
    inv_ref[...] = jnp.broadcast_to(inv, inv_ref.shape)


def row_tile(size, array):
    return pl.BlockSpec((size, array.shape[1]), lambda t: (t, 0))


def gate_forward(y_parts, pz, gain):
    rows, inner = pz.shape
    size = 128
    tile = pl.BlockSpec((size, inner), lambda t: (t, 0))
    return pl.pallas_call(
        functools.partial(gate_kernel, len(y_parts)),
        grid=(rows // size,),
        in_specs=[row_tile(size, y) for y in y_parts]
        + [tile, pl.BlockSpec((1, inner), lambda t: (0, 0))],
        out_specs=[tile, pl.BlockSpec((size, LANES), lambda t: (t, 0))],
        out_shape=[
            jax.ShapeDtypeStruct((rows, inner), BF),
            jax.ShapeDtypeStruct((rows, LANES), F32),
        ],
        compiler_params=params(),
        cost_estimate=cost(15e-6),
        name="gate_forward",
    )(*y_parts, pz, gain)


def gate_back_kernel(count, *refs):
    y_refs = refs[:count]
    z_ref, grad_ref, inv_ref, gain_ref, gy_ref, gz_ref = refs[count:]
    y = jnp.concatenate([ref[...] for ref in y_refs], axis=1)
    z = z_ref[...]
    grad = grad_ref[...]
    inv = inv_ref[:, 0:1]
    sig = sigmoid(z)
    silu = z * sig
    normal = y * silu * inv
    grad_normal = grad * gain_ref[...]
    mean = jnp.sum(grad_normal * normal, axis=1, keepdims=True) * (1.0 / y.shape[1])
    gated = inv * (grad_normal - normal * mean)
    gy_ref[...] = (gated * silu).astype(BF)
    gz_ref[...] = (gated * y * (sig + silu * (1.0 - sig))).astype(BF)


def gate_backward(y_parts, pz, grad_gate, inv, gain):
    rows, inner = pz.shape
    size = 128
    tile = pl.BlockSpec((size, inner), lambda t: (t, 0))
    return pl.pallas_call(
        functools.partial(gate_back_kernel, len(y_parts)),
        grid=(rows // size,),
        in_specs=[row_tile(size, y) for y in y_parts]
        + [
            tile,
            tile,
            pl.BlockSpec((size, LANES), lambda t: (t, 0)),
            pl.BlockSpec((1, inner), lambda t: (0, 0)),
        ],
        out_specs=[tile, tile],
        out_shape=[
            jax.ShapeDtypeStruct((rows, inner), BF),
            jax.ShapeDtypeStruct((rows, inner), BF),
        ],
        compiler_params=params(),
        cost_estimate=cost(24e-6),
        name="gate_backward",
    )(*y_parts, pz, grad_gate, inv, gain)


def head_sums(product, spread):
    high = product.astype(BF)
    low = (product - high.astype(F32)).astype(BF)
    return dot_nn(high, spread) + dot_nn(low, spread)


def backward_kernel(group_start, *refs):
    x_ref, taps_ref, y_ref, gy_ref, b_ref, c_ref, bt_ref, ct_ref = refs[:8]
    dt_ref, cum_ref, cumt_ref = refs[8:11]
    gx_ref, lines_ref, *totals = refs[-8:]
    gb_ref, gc_ref, one_ref, two_ref, cb_ref, heads_ref = totals
    befores = refs[12:-8]
    first_head = (pl.program_id(0) + group_start) * GROUP_HEADS
    seq = pl.program_id(1)
    slot = x_ref.shape[0]

    @pl.when((pl.program_id(0) == 0) & (seq == 0))
    def _():
        for i, total in enumerate(totals):
            total[...] = befores[i][...] if befores else jnp.zeros_like(total)

    at = pl.multiple_of(seq * slot, slot)
    whole_rows = pl.ds(at, slot)
    early_rows = pl.ds(at, STRETCH)
    late_rows = pl.ds(pl.multiple_of(at + STRETCH, STRETCH), STRETCH)
    shifted, pre = conv_parts(x_ref[...], taps_ref)
    sig = sigmoid(pre)
    active = pre * sig
    slope = sig + active * (1.0 - sig)
    x_low = active.astype(BF).astype(F32)
    gy_low = gy_ref[...]
    gy = gy_low.astype(F32)
    cum_wide, cum_x, dt_x, left = head_tables(cum_ref, dt_ref, first_head)
    x_dt = (x_low * dt_x).astype(BF)
    skip = taps_ref[5:6, :]

    grad_inter = (gy[STRETCH:] * jnp.exp(cum_x[STRETCH:])).astype(BF)
    fade = jnp.exp(cum_x[STRETCH - 1 : STRETCH] - cum_x[:STRETCH])
    scaled = (x_low[:STRETCH] * (fade * dt_x[:STRETCH])).astype(BF)
    state = dot_nn(bt_ref[:, :STRETCH], scaled)
    gc_ref[late_rows, :] += dot_nt(grad_inter, state.astype(BF))
    grad_state = dot_nn(ct_ref[:, STRETCH:], grad_inter).astype(BF)
    gb_ref[early_rows, :] += dot_nt(scaled, grad_state)
    grad_scaled = dot_nn(b_ref[:STRETCH, :], grad_state)
    last_sum = column_sum(grad_state.astype(F32) * state)

    lower = lower_mask()
    zero = jnp.zeros((STRETCH, LANES), BF)
    rest = []
    for block in range(2):
        rows = slice(block * STRETCH, (block + 1) * STRETCH)
        cb = dot_nt(c_ref[rows, :], b_ref[rows, :])
        cb_first = cb_below = None
        parts = []
        for pair in range(GROUP_HEADS // 2):
            lanes = slice(pair * LANES, (pair + 1) * LANES)
            x_pair = x_dt[rows, lanes]
            gy_pair = gy_low[rows, lanes]
            total = None
            for side in range(2):
                head = 2 * pair + side
                row = cumt_ref[pl.ds(first_head + head, 1), :]
                first, below = decay_tiles(cum_wide[head], row, block, lower)
                mixing = join_tiles(
                    (cb[:HALF, :HALF] * first).astype(BF), (cb[HALF:, :] * below).astype(BF)
                )
                keep = left if side == 0 else jnp.logical_not(left)
                gy_head = jnp.where(keep, gy_pair, zero)
                mix_first = dot_nt(gy_head[:HALF], x_pair[:HALF]) * first
                mix_below = dot_nt(gy_head[HALF:], x_pair) * below
                cb_first = mix_first if cb_first is None else cb_first + mix_first
                cb_below = mix_below if cb_below is None else cb_below + mix_below
                now = dot_tn(mixing, gy_head)
                total = now if total is None else total + now
            parts.append(total)
        cb_ref[seq, block, :HALF, :HALF] += cb_first
        cb_ref[seq, block, HALF:, :] += cb_below
        rest.append(jnp.concatenate(parts, axis=1))
    moved = x_dt.astype(F32) * jnp.concatenate(rest, axis=0)
    moved = jnp.concatenate(
        [moved[:STRETCH] + scaled.astype(F32) * grad_scaled, moved[STRETCH:]], axis=0
    )
    rest[0] = rest[0] + fade * grad_scaled
    grad_pull = jnp.concatenate(rest, axis=0)

    width = x_low.shape[1]
    spread = (
        lax.broadcasted_iota(jnp.int32, (width, LANES), 1)
        == first_head + lax.broadcasted_iota(jnp.int32, (width, LANES), 0) // 64
    ).astype(F32).astype(BF)
    moved = gy * (y_ref[...] - skip * x_low) - moved
    edge = lax.broadcasted_iota(jnp.int32, (8, 1), 0) == 7
    moved = jnp.concatenate(
        [
            moved[: STRETCH - 8],
            moved[STRETCH - 8 : STRETCH] + jnp.where(edge, last_sum, 0.0),
            moved[STRETCH:],
        ],
        axis=0,
    )
    one_ref[whole_rows, :] += head_sums(moved, spread)
    two_ref[whole_rows, :] += head_sums(x_low * grad_pull, spread)
    third = lax.broadcasted_iota(jnp.int32, (8, 1), 0) == 2
    skip_line = jnp.where(third, column_sum(gy * x_low), 0.0)
    heads_ref[...] += head_sums(skip_line, spread)

    grad_pre = (skip * gy + dt_x * grad_pull) * slope
    gx_ref[...] = conv_back(grad_pre, taps_ref).astype(BF)
    lines = [column_sum(grad_pre * shifted[k]) for k in range(4)] + [column_sum(grad_pre)]
    lines = jnp.concatenate(lines + [jnp.zeros((3, width), F32)], axis=0)

    @pl.when(seq == 0)
    def _():
        lines_ref[...] = lines

    @pl.when(seq > 0)
    def _():
        lines_ref[...] += lines


def scan_backward(px, at, taps, y_rows, y_at, grad_y, prep, slot, start, count, before=None):
    b_low, c_low, b_t, c_t, dt, cum, cum_t = prep
    rows = px.shape[0]
    width = GROUP_HEADS * 64
    seqs = rows // slot
    tall = pl.BlockSpec((slot, LANES), lambda h, q: (q, 0))
    wide = pl.BlockSpec((LANES, slot), lambda h, q: (0, q))
    tile = pl.BlockSpec((slot, width), lambda h, q: (q, h + at))
    flat = jax.ShapeDtypeStruct((rows, LANES), F32)
    whole = pl.BlockSpec((rows, LANES), lambda h, q: (0, 0))
    totals = [whole] * 4 + [
        pl.BlockSpec((seqs, 2, STRETCH, STRETCH), lambda h, q: (0, 0, 0, 0)),
        pl.BlockSpec((8, LANES), lambda h, q: (0, 0)),
    ]
    extra, extra_specs, aliases = [jnp.zeros((8, LANES), BF)], [pl.BlockSpec(memory_space=pl.ANY)], {}
    if before is not None:
        if before[0].shape == px.shape:
            extra = [before[0]]
            aliases[11] = 0
        extra = extra + list(before[2:])
        extra_specs = extra_specs + totals
        aliases.update({12 + i: 2 + i for i in range(6)})
    return pl.pallas_call(
        functools.partial(backward_kernel, start),
        grid=(count, seqs),
        in_specs=[
            tile,
            pl.BlockSpec((8, width), lambda h, q: (0, h + start)),
            pl.BlockSpec((slot, width), lambda h, q: (q, h + y_at)),
            pl.BlockSpec((slot, width), lambda h, q: (q, h + start)),
            tall,
            tall,
            wide,
            wide,
            tall,
            tall,
            wide,
        ]
        + extra_specs,
        out_specs=[tile, pl.BlockSpec((8, width), lambda h, q: (0, h))] + totals,
        out_shape=[
            jax.ShapeDtypeStruct(px.shape, BF),
            jax.ShapeDtypeStruct((8, count * width), F32),
            flat,
            flat,
            flat,
            flat,
            jax.ShapeDtypeStruct((seqs, 2, STRETCH, STRETCH), F32),
            jax.ShapeDtypeStruct((8, LANES), F32),
        ],
        input_output_aliases=aliases,
        compiler_params=params(),
        cost_estimate=cost(3.3e-6 * count),
        name="scan_backward",
    )(px, taps, y_rows, grad_y, b_low, c_low, b_t, c_t, dt, cum, cum_t, *extra)


def finish_kernel(
    head_count,
    raw_ref,
    taps_ref,
    heads_ref,
    b_ref,
    c_ref,
    dt_ref,
    gb_ref,
    gc_ref,
    one_ref,
    two_ref,
    cb_ref,
    head_before_ref,
    before_ref,
    out_ref,
    lines_ref,
    head_total_ref,
):
    @pl.when(pl.program_id(0) == 0)
    def _():
        lines_ref[...] = jnp.zeros_like(lines_ref)
        head_total_ref[...] = head_before_ref[...]

    shifted, pre = conv_parts(raw_ref[:, : 2 * LANES], taps_ref)
    sig = sigmoid(pre)
    slope = sig + pre * sig * (1.0 - sig)
    grad_b, grad_c = [], []
    for block in range(2):
        rows = slice(block * STRETCH, (block + 1) * STRETCH)
        cb = cb_ref[0, block].astype(BF)
        grad_c.append(gc_ref[rows, :] + dot_nn(cb, b_ref[rows, :]))
        grad_b.append(gb_ref[rows, :] + dot_tn(cb, c_ref[rows, :]))
    grad_active = jnp.concatenate(
        [jnp.concatenate(grad_b, axis=0), jnp.concatenate(grad_c, axis=0)], axis=1
    )
    grad_pre = grad_active * slope
    lines = [column_sum(grad_pre * shifted[k]) for k in range(4)] + [column_sum(grad_pre)]
    lines.append(jnp.zeros((3, 2 * LANES), F32))
    lines_ref[...] += jnp.concatenate(lines, axis=0)

    dt = dt_ref[...]
    two = two_ref[...]
    rate = heads_ref[1:2, :]
    place = row_index(dt)
    grad_cum = one_ref[...]
    inside = place % STRETCH
    step = 1
    while step < STRETCH:
        moved = pltpu.roll(grad_cum, grad_cum.shape[0] - step, 0)
        grad_cum = grad_cum + jnp.where(inside < STRETCH - step, moved, 0.0)
        step *= 2
    grad_dt = grad_cum * rate + two
    lane = lax.broadcasted_iota(jnp.int32, (1, LANES), 1)
    raw = jnp.where(lane < head_count, raw_ref[:, 2 * LANES : 3 * LANES], 0.0)
    grad_raw = grad_dt * sigmoid(raw + heads_ref[0:1, :])
    head_total_ref[...] += jnp.concatenate(
        [column_sum(grad_raw), column_sum(grad_cum * dt) * rate, jnp.zeros((6, LANES), F32)], axis=0
    )
    out_ref[:, : 2 * LANES] = conv_back(grad_pre, taps_ref).astype(BF)
    out_ref[:, 2 * LANES : 3 * LANES] = grad_raw.astype(BF)
    out_ref[:, 3 * LANES :] = jnp.zeros_like(out_ref[:, 3 * LANES :])


def finish(raw, at, taps, heads, head_count, prep, totals, grads, narrow, grads_at, slot):
    b_low, c_low, _, _, dt, _, _ = prep
    rows = raw.shape[0]
    seqs = rows // slot
    tall = pl.BlockSpec((slot, LANES), lambda q: (q, 0))
    return pl.pallas_call(
        functools.partial(finish_kernel, head_count),
        grid=(seqs,),
        in_specs=[
            pl.BlockSpec((slot, 4 * LANES), lambda q: (q, at)),
            pl.BlockSpec((8, 2 * LANES), lambda q: (0, 0)),
            pl.BlockSpec((8, LANES), lambda q: (0, 0)),
            tall,
            tall,
            tall,
            tall,
            tall,
            tall,
            tall,
            pl.BlockSpec((1, 2, STRETCH, STRETCH), lambda q: (q, 0, 0, 0)),
            pl.BlockSpec((8, LANES), lambda q: (0, 0)),
            pl.BlockSpec(memory_space=pl.ANY),
        ],
        out_specs=[
            pl.BlockSpec((slot, narrow), lambda q: (q, grads_at)),
            pl.BlockSpec((8, 2 * LANES), lambda q: (0, 0)),
            pl.BlockSpec((8, LANES), lambda q: (0, 0)),
        ],
        out_shape=[
            jax.ShapeDtypeStruct(grads.shape, BF),
            jax.ShapeDtypeStruct((8, 2 * LANES), F32),
            jax.ShapeDtypeStruct((8, LANES), F32),
        ],
        input_output_aliases={12: 0},
        compiler_params=params(),
        cost_estimate=cost(3e-6),
        name="finish",
    )(raw, taps, heads, b_low, c_low, dt, *totals, grads)


def project_kernel(rows_ref, weight_ref, out_ref):
    out_ref[...] = dot_nn(rows_ref[...], weight_ref[...])


def project(normed, weight, at, count, size):
    rows, depth = normed.shape
    return pl.pallas_call(
        project_kernel,
        grid=(count,),
        in_specs=[
            pl.BlockSpec((rows, depth), lambda j: (0, 0)),
            pl.BlockSpec((depth, size), lambda j: (0, j + at)),
        ],
        out_specs=pl.BlockSpec((rows, size), lambda j: (0, j)),
        out_shape=jax.ShapeDtypeStruct((rows, count * size), F32),
        compiler_params=params(),
        cost_estimate=cost(2.5e-6 * count),
        name="project",
    )(normed, weight)


def pair_kernel(mine_ref, other_ref, grad_ref, keep_ref, give_ref):
    grad = grad_ref[...]
    give_ref[...] = dot_nn(other_ref[...], grad).astype(give_ref.dtype)
    keep_ref[...] = dot_nn(mine_ref[...], grad).astype(keep_ref.dtype)


def weight_grads(mine, other, grad, at, count, size):
    depth, rows = mine.shape
    whole = pl.BlockSpec((depth, rows), lambda j: (0, 0))
    tile = pl.BlockSpec((depth, size), lambda j: (0, j))
    shape = jax.ShapeDtypeStruct((depth, count * size), BF)
    return pl.pallas_call(
        pair_kernel,
        grid=(count,),
        in_specs=[whole, whole, pl.BlockSpec((rows, size), lambda j: (0, j + at))],
        out_specs=[tile, tile],
        out_shape=[shape, shape],
        compiler_params=params(),
        cost_estimate=cost(2.5e-6 * count),
        name="weight_grads",
    )(mine, other, grad)


def input_grads_kernel(sizes, ends, has_before, final, *refs):
    pairs = [refs[2 * i : 2 * i + 2] for i in range(len(sizes))]
    refs = refs[2 * len(sizes) :]
    steps = sum(sizes)
    step = pl.program_id(0)
    if has_before:
        before_ref, refs = refs[0], refs[1:]
    if final:
        hidden_ref, inv_ref, gain_ref, mask_ref, cot_ref, out_ref, total = refs
    else:
        (total,) = refs

    def add(grad_ref, weight):
        now = dot_nt(grad_ref[...], weight)

        @pl.when(step == 0)
        def _():
            total[...] = now + before_ref[...] if has_before else now

        @pl.when(step > 0)
        def _():
            total[...] += now

    begin = 0
    for (grad_ref, weight_ref), size, end in zip(pairs, sizes, ends):
        full = size if end is None else size - 1

        @pl.when((step >= begin) & (step < begin + full))
        def _(grad_ref=grad_ref, weight_ref=weight_ref):
            add(grad_ref, weight_ref[...])

        if end is not None:

            @pl.when(step == begin + full)
            def _(grad_ref=grad_ref, weight_ref=weight_ref, end=end):
                weight = weight_ref[...]
                lane = lax.broadcasted_iota(jnp.int32, weight.shape, 1)
                add(grad_ref, jnp.where(lane < end, weight, jnp.zeros_like(weight)))

        begin += size
    if final:

        @pl.when(step >= steps)
        def _():
            tile = hidden_ref.shape[0]
            grad = total[pl.ds(pl.multiple_of((step - steps) * tile, tile), tile), :]
            inv = inv_ref[...]
            normal = hidden_ref[...] * inv
            grad = grad * gain_ref[...]
            inside = jnp.sum(grad * normal, axis=1, keepdims=True) * (1.0 / grad.shape[1])
            out_ref[...] = inv * (grad - normal * inside) + mask_ref[...] * cot_ref[...]


def input_grads(grads, weights, places, before=None, final=None):
    rows = grads[0].shape[0]
    width = weights[0].shape[0]
    size, tile = 512, 128
    sizes = [g.shape[1] // size for g in grads]
    steps = sum(sizes)
    in_specs, args, begin = [], [], 0
    for grad, weight, (at, _), count in zip(grads, weights, places, sizes):

        def place(k, begin=begin, count=count, at=0):
            return (0, at + jnp.clip(k - begin, 0, count - 1))

        in_specs += [
            pl.BlockSpec((rows, size), place),
            pl.BlockSpec((width, size), functools.partial(place, at=at)),
        ]
        args += [grad, weight]
        begin += count
    if before is not None:
        in_specs.append(pl.BlockSpec((rows, width), lambda k: (0, 0), pipeline_mode=pl.Buffered(1)))
        args.append(before)
    if final:

        def row(k):
            return (jnp.clip(k - steps, 0, rows // tile - 1), 0)

        line = pl.BlockSpec((1, width), lambda k: (0, 0))
        column = pl.BlockSpec((tile, 1), row)
        wide = pl.BlockSpec((tile, width), row)
        in_specs += [wide, column, line, column, wide]
        args += list(final)
        out_specs = wide
        out_shape = jax.ShapeDtypeStruct((rows, width), F32)
        scratch = [pltpu.VMEM((rows, width), F32)]
    else:
        out_specs = pl.BlockSpec((rows, width), lambda k: (0, 0))
        out_shape = jax.ShapeDtypeStruct((rows, width), F32)
        scratch = []
    ends = [end for _, end in places]
    return pl.pallas_call(
        functools.partial(input_grads_kernel, sizes, ends, before is not None, bool(final)),
        grid=(steps + (rows // tile if final else 0),),
        in_specs=in_specs,
        out_specs=out_specs,
        out_shape=out_shape,
        scratch_shapes=scratch,
        compiler_params=params(),
        cost_estimate=cost(2.5e-6 * steps),
        name="input_grads",
    )(*args)


def swap(values, bit, shards):
    return lax.ppermute(values, "shard", [(i, i ^ (1 << bit)) for i in range(shards)])


def border(moving, *values):
    ready = lax.optimization_barrier(tuple(one.got for one in moving) + values)
    for one, got in zip(moving, ready):
        one.got = got
        one.finish()
    rest = ready[len(moving) :]
    return rest[0] if len(rest) == 1 else rest


class Gather:
    def __init__(self, own, order, shards, place):
        self.now, self.order, self.shards, self.place = own, list(order), shards, place
        self.live, self.columns = [], own.shape[-1]

    def start(self):
        self.bit = self.order.pop(0)
        self.got = swap(self.now, self.bit, self.shards)

    def finish(self):
        mine = (self.place >> self.bit) & 1
        axis = len([b for b in self.live if b > self.bit])
        first = jnp.where(mine == 0, self.now, self.got)
        second = jnp.where(mine == 0, self.got, self.now)
        self.now = jnp.stack([first, second], axis=axis)
        self.live.append(self.bit)

    def whole(self):
        while self.order:
            self.start()
            self.finish()
        return self.now


class Spread:
    def __init__(self, now, bits, shards, groups):
        self.now, self.bits, self.shards, self.groups = now, list(bits), shards, groups

    def start(self):
        if self.bits:
            self.got = swap(self.now, self.bits.pop(0), self.shards)
        else:
            pairs = [(i, (i + 1) % self.groups) for i in range(self.groups)]
            self.got = lax.ppermute(self.now, "group", pairs)

    def finish(self):
        self.now = self.now + self.got

    def result(self):
        while self.bits:
            self.start()
            self.finish()
        return self.now


class Group:
    def __init__(self, now, groups):
        self.now, self.groups = now, groups

    def start(self):
        self.pairs = [(i, (i + 1) % self.groups) for i in range(self.groups)]
        self.got = lax.ppermute(self.now, "group", self.pairs)

    def finish(self):
        total, got = self.now.astype(F32), self.got
        for step in range(1, self.groups):
            if step > 1:
                got = lax.ppermute(got, "group", self.pairs)
            total = total + got.astype(F32)
        self.now = total


class Sum:
    def __init__(self, pair, order, shards, groups, place, part, group_first=False):
        self.keep, self.give = pair
        self.shards, self.groups, self.place, self.part = shards, groups, place, part
        self.columns, self.dtype = self.keep.shape[-1], self.keep.dtype
        self.group_first = group_first and groups == 2
        self.todo = [0] + (["group"] if self.group_first else []) + list(order) + ["end"]
        self.live = list(range(shards.bit_length() - 2, 0, -1))
        self.now = None

    def start(self):
        self.bit = bit = self.todo.pop(0)
        if bit == "end":
            pairs = [(i, (i + 1) % self.groups) for i in range(self.groups)]
            self.got = lax.ppermute(self.now, "group", pairs)
        elif bit == "group":
            half = self.columns // 2
            mine = lax.axis_index("group")
            axis = self.now.ndim - 1
            self.keep = lax.dynamic_slice_in_dim(self.now, mine * half, half, axis)
            give = lax.dynamic_slice_in_dim(self.now, (1 - mine) * half, half, axis)
            self.got = lax.ppermute(give, "group", [(0, 1), (1, 0)])
        elif bit == 0:
            self.got = swap(self.give, 0, self.shards)
        else:
            axis = self.live.index(bit)
            mine = (self.place >> bit) & 1
            self.keep = lax.dynamic_index_in_dim(self.now, mine, axis, keepdims=False)
            give = lax.dynamic_index_in_dim(self.now, 1 - mine, axis, keepdims=False)
            self.live.remove(bit)
            self.got = swap(give, bit, self.shards)

    def finish(self):
        if self.bit == "end" and self.group_first:
            first = lax.axis_index("group") == 0
            halves = [jnp.where(first, self.now, self.got), jnp.where(first, self.got, self.now)]
            self.now = jnp.concatenate(halves, axis=-1)
        elif self.bit == "end":
            total, got = self.now.astype(F32), self.got
            for step in range(1, self.groups):
                if step > 1:
                    pairs = [(i, (i + 1) % self.groups) for i in range(self.groups)]
                    got = lax.ppermute(got, "group", pairs)
                total = total + got.astype(F32)
            self.now = total
        else:
            now = self.keep.astype(F32) + self.got.astype(F32)
            if self.todo != ["end"] or not self.group_first:
                now = now.astype(self.dtype)
            if self.bit == 0:
                now = now.reshape((2,) * len(self.live) + (self.part, self.columns))
            self.now = now

    def result(self):
        while self.todo:
            self.start()
            self.finish()
        return self.now


def local(
    shards,
    groups,
    hidden_in,
    lengths,
    pre_gain,
    in_proj,
    conv_weight,
    conv_bias,
    head_params,
    gate_gain,
    out_proj,
    cotangent,
):
    micro, own, slot, width = hidden_in.shape
    rows = micro * own * slot
    inner = out_proj.shape[0] * shards
    channels = conv_bias.shape[0] * shards
    heads = head_params.shape[1]
    tail = channels - inner + heads
    part = in_proj.shape[0]
    out_part = out_proj.shape[0]
    own_conv = conv_bias.shape[0]
    taps = conv_weight.shape[0]
    hidden = hidden_in.reshape(rows, width)
    cot = cotangent.reshape(rows, width)
    place = lax.axis_index("shard")
    core = place & 1
    chip_bits = list(range(1, shards.bit_length() - 1))
    up = chip_bits
    down = chip_bits[::-1]

    unit = GROUP_HEADS * 64
    units = inner // unit
    late = units // 3
    b_columns = (units - late) * unit
    w_rest = lax.all_gather(in_proj[:, : inner + b_columns], "shard", axis=0, tiled=True)
    first_own = in_proj[:, inner + b_columns :]
    w_out = lax.all_gather(out_proj, "shard", axis=0, tiled=True)
    small = jnp.concatenate([pre_gain, gate_gain, conv_bias, conv_weight.reshape(-1)], axis=0)
    small = small.astype(F32)
    small = jnp.pad(small, (0, -small.shape[0] % LANES))[None, :]
    packed = Gather(small, down + [0], shards, place).whole().reshape(shards, -1)
    sizes = (part, out_part, own_conv, taps * own_conv)
    ends = [sum(sizes[: i + 1]) for i in range(4)]
    pre_all = packed[:, : ends[0]].reshape(1, width)
    gate_all = packed[:, ends[0] : ends[1]].reshape(1, inner)
    bias_all = packed[:, ends[1] : ends[2]].reshape(1, channels)
    taps_all = packed[:, ends[2] : ends[3]].reshape(shards, taps, -1)
    taps_all = jnp.swapaxes(taps_all, 0, 1).reshape(taps, channels)
    skip_row = jnp.pad(jnp.repeat(head_params[2], inner // heads), (0, channels - inner))
    table = jnp.concatenate(
        [taps_all, bias_all, skip_row[None, :], jnp.zeros((2, channels), F32)], axis=0
    )
    table_x, table_bc = table[:, :inner], table[:, inner:]
    rate = -jnp.exp(head_params[1])
    head_rows = jnp.pad(
        jnp.stack([head_params[0], rate], axis=0), ((0, 6), (0, LANES - heads))
    )

    inv_first = lax.rsqrt(jnp.mean(hidden * hidden, axis=-1, keepdims=True) + EPS)
    normed = (hidden * inv_first * pre_all).astype(BF)
    turned = normed.T.reshape(shards // 2, 2, part, rows)
    mine = lax.dynamic_index_in_dim(turned, core, 1, keepdims=False).reshape(-1, rows)
    other = lax.dynamic_index_in_dim(turned, 1 - core, 1, keepdims=False).reshape(-1, rows)
    positions = jnp.arange(slot, dtype=jnp.int32)
    mask = (positions[None, :] < lengths.reshape(-1)[:, None]).astype(F32).reshape(rows, 1)
    grad_low = (mask * cot).astype(BF)

    gather_a = Gather(first_own, down + [0], shards, place)
    while gather_a.order:
        gather_a.start()
        border([gather_a])
    w_a = gather_a.now.reshape(width, -1)
    normed = border([], normed, w_a)[0]

    size = 4 * LANES
    blocks, b_blocks = inner // size, b_columns // size
    a_blocks = blocks - b_blocks
    raw_at = (inner - b_columns) // (4 * LANES)
    pa = project(normed, w_a, 0, a_blocks + 1, size)
    prep = prepare(pa, raw_at, table_bc, head_rows, heads, slot)
    ya = scan_forward(pa, 0, table_x, prep, slot, units - late, late)
    ya, normed = border([], ya, normed)
    pb = project(normed, w_rest, blocks, b_blocks, size)
    yb = scan_forward(pb, 0, table_x, prep, slot, 0, units - late)
    pz = project(normed, w_rest, 0, blocks, size)
    gate_low, inv = gate_forward([yb, ya], pz, gate_all)

    g_out = dot_tn(gate_low, grad_low).astype(BF)
    g_out, grad_low, mine, other = border([], g_out, grad_low, mine, other)
    sum_out = lax.psum_scatter(g_out, "shard", scatter_dimension=0, tiled=True)
    grad_gate = dot_nt(grad_low, w_out)
    grad_y, grad_z = gate_backward([yb, ya], pz, grad_gate, inv, gate_all)
    g_z = dot_nn(turned.reshape(width, rows), grad_z).astype(BF)
    g_z, grad_y = border([], g_z, grad_y)
    sum_z = lax.psum_scatter(g_z, "shard", scatter_dimension=0, tiled=True)

    reduce = functools.partial(Sum, shards=shards, groups=groups, place=place, order=up)
    half = (units - late) // 2
    outs_first = scan_backward(pb, 0, table_x, yb, 0, grad_y, prep, slot, 0, half)
    outs = scan_backward(
        pb, half, table_x, yb, half, grad_y, prep, slot, half, units - late - half, before=outs_first
    )
    lines_x = [outs_first[1], outs[1]]
    grad_b = outs[0]
    pair_b = weight_grads(mine, other, grad_b, 0, b_blocks, size)
    *pair_b, grad_y = border([], *pair_b, grad_y)
    s_b = reduce(pair_b, part=part, group_first=True)
    s_b.start()
    grad_y, sum_out = border([], grad_y, sum_out)
    outs = scan_backward(
        pa, 0, table_x, ya, 0, grad_y, prep, slot, units - late, late, before=outs
    )
    s_out = Group(sum_out, groups)
    s_out.start()
    mine, *outs = border([s_b, s_out], mine, *outs)
    lines_x.append(outs[1])
    s_b.start()
    outs[0], s_b.keep = border([], outs[0], s_b.keep)
    grad_a, lines_bc, head_total = finish(
        pa,
        raw_at,
        table_bc,
        head_rows,
        heads,
        prep,
        outs[2:],
        outs[0],
        size,
        a_blocks,
        slot,
    )
    pair_a = weight_grads(mine, other, grad_a, 0, a_blocks + 1, size)

    lines = jnp.concatenate(lines_x + [lines_bc], axis=1)
    head_line = head_total[:3].reshape(1, 3 * LANES)
    head_line = jnp.pad(head_line, ((0, 0), (0, channels - 3 * LANES)))
    small = jnp.concatenate([lines[:5], head_line, lines[6:]], axis=0)
    s_small = Spread(small, [0] + up, shards, groups)
    s_small.start()
    *pair_a, grad_z, grad_a = border([s_small], *pair_a, grad_z, grad_a)
    s_a = reduce(pair_a, part=part)
    s_a.start()
    s_small.start()
    part_sum = input_grads([grad_z], [w_rest], [(0, None)])
    part_sum, grad_a = border([s_b, s_a, s_small], part_sum, grad_a)
    s_a.start()
    s_small.start()
    s_b.start()
    grad_input = input_grads(
        [grad_b, grad_a],
        [w_rest, w_a],
        [(blocks, None), (0, tail)],
        before=part_sum,
        final=(hidden, inv_first, pre_all, mask, cot),
    )
    gate_low, grad_input, sum_z = border([s_a, s_b, s_small], gate_low, grad_input, sum_z)
    s_a.start()
    s_small.start()
    s_b.start()
    s_z = Group(sum_z, groups)
    s_z.start()
    layer_out = mask * (hidden + dot_nn(gate_low, w_out))
    layer_out = border([s_a, s_small, s_b, s_z], layer_out)
    s_a.start()
    s_small.start()
    s_b.start()
    for one in (s_small, s_a, s_b):
        one.finish()
    sum_a, small = s_a.result(), s_small.now
    g_in = jnp.concatenate(
        [s_z.now, s_b.result(), sum_a[:, : inner - b_columns + tail]], axis=1
    )
    g_out = s_out.now

    def gain_grads(weight, grads, gain):
        return jnp.sum(weight.astype(F32) * grads, axis=1) / gain.astype(F32)

    g_pre = gain_grads(in_proj, g_in, pre_gain)
    g_gate = gain_grads(out_proj, g_out, gate_gain)
    g_lines = lax.dynamic_slice(small, (0, place * own_conv), (5, own_conv))
    g_heads = small[5, : 3 * LANES].reshape(3, LANES)[:, :heads]
    return (
        layer_out.reshape(hidden_in.shape),
        grad_input.reshape(hidden_in.shape),
        g_pre,
        g_in,
        g_lines[:4],
        g_lines[4],
        g_heads,
        g_gate,
        g_out,
    )


def solution(mesh):
    rows = P(None, ("group", "shard"), None, None)
    in_specs = (
        rows,
        P(None, ("group", "shard")),
        P("shard"),
        P("shard", None),
        P(None, "shard"),
        P("shard"),
        P(),
        P("shard"),
        P("shard", None),
        rows,
    )
    out_specs = (
        rows,
        rows,
        P("shard"),
        P("shard", None),
        P(None, "shard"),
        P("shard"),
        P(),
        P("shard"),
        P("shard", None),
    )
    body = functools.partial(local, mesh.shape["shard"], mesh.shape["group"])
    return jax.shard_map(body, mesh=mesh, in_specs=in_specs, out_specs=out_specs, check_vma=False)
```

```python
import functools

import jax
import jax.numpy as jnp
from jax import lax
from jax.experimental import pallas as pl
from jax.experimental.pallas import tpu as pltpu
from jax.sharding import PartitionSpec as P

STRETCH = 256
HALF = 128
LANES = 128
GROUP_HEADS = 8
EPS = 1e-05
BF = jnp.bfloat16
F32 = jnp.float32
VMEM_BYTES = 56 * 1024 * 1024


def params(**kwargs):
    return pltpu.CompilerParams(vmem_limit_bytes=VMEM_BYTES, **kwargs)


def cost(seconds):
    return pl.CostEstimate(
        flops=int(seconds * 2.0e13), bytes_accessed=int(seconds * 6.0e10), transcendentals=0
    )


def dot_nn(left, right):
    return lax.dot_general(left, right, (((1,), (0,)), ((), ())), preferred_element_type=F32)


def dot_nt(left, right):
    return lax.dot_general(left, right, (((1,), (1,)), ((), ())), preferred_element_type=F32)


def dot_tn(left, right):
    return lax.dot_general(left, right, (((0,), (0,)), ((), ())), preferred_element_type=F32)


def sigmoid(values):
    return 1.0 / (1.0 + jnp.exp(-values))


def row_index(values):
    return lax.broadcasted_iota(jnp.int32, (values.shape[0], 1), 0)


def shift_down(values, count):
    rolled = pltpu.roll(values, count, 0)
    return jnp.where(row_index(values) >= count, rolled, 0.0)


def shift_up(values, count):
    rows = values.shape[0]
    rolled = pltpu.roll(values, rows - count, 0)
    return jnp.where(row_index(values) < rows - count, rolled, 0.0)


def conv_parts(values, taps_ref):
    shifted = [shift_down(values, 3), shift_down(values, 2), shift_down(values, 1), values]
    pre = taps_ref[4:5, :]
    for k in range(4):
        pre = pre + taps_ref[k : k + 1, :] * shifted[k]
    return shifted, pre


def conv_back(grad_pre, taps_ref):
    total = taps_ref[3:4, :] * grad_pre
    for k in range(3):
        total = total + taps_ref[k : k + 1, :] * shift_up(grad_pre, 3 - k)
    return total


def column_sum(values):
    return jnp.sum(values, axis=0, keepdims=True)


def prepare_kernel(head_count, raw_ref, taps_ref, heads_ref, b_ref, c_ref, bt_ref, ct_ref, dt_ref, cum_ref, cumt_ref):
    _, pre = conv_parts(raw_ref[:, : 2 * LANES], taps_ref)
    active = pre * sigmoid(pre)
    b_part, c_part = active[:, :LANES], active[:, LANES:]
    b_ref[...] = b_part.astype(BF)
    c_ref[...] = c_part.astype(BF)
    bt_ref[...] = b_part.T.astype(BF)
    ct_ref[...] = c_part.T.astype(BF)
    lane = lax.broadcasted_iota(jnp.int32, (1, LANES), 1)
    raw = jnp.where(lane < head_count, raw_ref[:, 2 * LANES :], 0.0) + heads_ref[0:1, :]
    dt = jnp.maximum(raw, 0.0) + jnp.log1p(jnp.exp(-jnp.abs(raw)))
    cum = dt * heads_ref[1:2, :]
    place = row_index(cum) % STRETCH
    step = 1
    while step < STRETCH:
        cum = cum + jnp.where(place >= step, pltpu.roll(cum, step, 0), 0.0)
        step *= 2
    dt_ref[...] = dt
    cum_ref[...] = cum
    cumt_ref[...] = cum.T


def prepare(raw, at, taps, heads, head_count, slot):
    rows = raw.shape[0]
    tall = pl.BlockSpec((slot, LANES), lambda q: (q, 0))
    wide = pl.BlockSpec((LANES, slot), lambda q: (0, q))
    return pl.pallas_call(
        functools.partial(prepare_kernel, head_count),
        grid=(rows // slot,),
        in_specs=[
            pl.BlockSpec((slot, 3 * LANES), lambda q: (q, at)),
            pl.BlockSpec((8, 2 * LANES), lambda q: (0, 0)),
            pl.BlockSpec((8, LANES), lambda q: (0, 0)),
        ],
        out_specs=[tall, tall, wide, wide, tall, tall, wide],
        out_shape=[
            jax.ShapeDtypeStruct((rows, LANES), BF),
            jax.ShapeDtypeStruct((rows, LANES), BF),
            jax.ShapeDtypeStruct((LANES, rows), BF),
            jax.ShapeDtypeStruct((LANES, rows), BF),
            jax.ShapeDtypeStruct((rows, LANES), F32),
            jax.ShapeDtypeStruct((rows, LANES), F32),
            jax.ShapeDtypeStruct((LANES, rows), F32),
        ],
        compiler_params=params(),
        name="prepare",
    )(raw, taps, heads)


def head_tables(cum_ref, dt_ref, first_head):
    shift = lax.rem(LANES - first_head, LANES)
    cum = pltpu.roll(cum_ref[...], shift, 1)
    dt = pltpu.roll(dt_ref[...], shift, 1)
    rows = cum.shape[0]
    cum_wide = [jnp.broadcast_to(cum[:, i : i + 1], (rows, LANES)) for i in range(GROUP_HEADS)]
    dt_wide = [jnp.broadcast_to(dt[:, i : i + 1], (rows, LANES)) for i in range(GROUP_HEADS)]
    left = lax.broadcasted_iota(jnp.int32, (1, LANES), 1) < LANES // 2

    def spread(wide):
        return jnp.concatenate(
            [jnp.where(left, wide[i], wide[i + 1]) for i in range(0, GROUP_HEADS, 2)], axis=1
        )

    return cum_wide, spread(cum_wide), spread(dt_wide), left


def decay_tiles(cum_wide, cumt_row, block, lower):
    begin = block * STRETCH
    top = cum_wide[begin : begin + HALF]
    low = cum_wide[begin + HALF : begin + STRETCH]
    row_left = cumt_row[:, begin : begin + HALF]
    row_right = cumt_row[:, begin + HALF : begin + STRETCH]
    first = jnp.where(lower, jnp.exp(top - row_left), 0.0)
    second = jnp.exp(low - row_left)
    third = jnp.where(lower, jnp.exp(low - row_right), 0.0)
    return first, jnp.concatenate([second, third], axis=1)


def join_tiles(first, below):
    return jnp.concatenate(
        [jnp.concatenate([first, jnp.zeros_like(first)], axis=1), below], axis=0
    )


def lower_mask():
    return lax.broadcasted_iota(jnp.int32, (HALF, HALF), 0) >= lax.broadcasted_iota(
        jnp.int32, (HALF, HALF), 1
    )


def forward_kernel(
    group_start, x_ref, taps_ref, b_ref, c_ref, bt_ref, dt_ref, cum_ref, cumt_ref, y_ref
):
    first_head = (pl.program_id(1) + group_start) * GROUP_HEADS
    _, pre = conv_parts(x_ref[...], taps_ref)
    x_low = (pre * sigmoid(pre)).astype(BF).astype(F32)
    cum_wide, cum_x, dt_x, left = head_tables(cum_ref, dt_ref, first_head)
    x_dt = (x_low * dt_x).astype(BF)
    skipped = taps_ref[5:6, :] * x_low
    fade = jnp.exp(cum_x[STRETCH - 1 : STRETCH] - cum_x[:STRETCH])
    scaled = (x_low[:STRETCH] * (fade * dt_x[:STRETCH])).astype(BF)
    state = dot_nn(bt_ref[:, :STRETCH], scaled).astype(BF)
    inter = jnp.exp(cum_x[STRETCH:]) * dot_nn(c_ref[STRETCH:, :], state)
    lower = lower_mask()
    zero = jnp.zeros((STRETCH, LANES), BF)
    for block in range(2):
        rows = slice(block * STRETCH, (block + 1) * STRETCH)
        cb = dot_nt(c_ref[rows, :], b_ref[rows, :])
        for pair in range(GROUP_HEADS // 2):
            lanes = slice(pair * LANES, (pair + 1) * LANES)
            x_pair = x_dt[rows, lanes]
            total = skipped[rows, lanes]
            if block == 1:
                total = total + inter[:, lanes]
            for side in range(2):
                head = 2 * pair + side
                row = cumt_ref[pl.ds(first_head + head, 1), :]
                first, below = decay_tiles(cum_wide[head], row, block, lower)
                mixing = join_tiles(
                    (cb[:HALF, :HALF] * first).astype(BF), (cb[HALF:, :] * below).astype(BF)
                )
                keep = left if side == 0 else jnp.logical_not(left)
                total = total + dot_nn(mixing, jnp.where(keep, x_pair, zero))
            y_ref[rows, lanes] = total


def scan_forward(px, offset, taps, prep, slot, start, count):
    b_low, c_low, b_t, _, dt, cum, cum_t = prep
    rows = px.shape[0]
    width = GROUP_HEADS * 64
    tall = pl.BlockSpec((slot, LANES), lambda q, h: (q, 0))
    wide = pl.BlockSpec((LANES, slot), lambda q, h: (0, q))
    tile = pl.BlockSpec((slot, width), lambda q, h: (q, h))
    return pl.pallas_call(
        functools.partial(forward_kernel, start),
        grid=(rows // slot, count),
        in_specs=[
            pl.BlockSpec((slot, width), lambda q, h: (q, h + offset)),
            pl.BlockSpec((8, width), lambda q, h: (0, h + start)),
            tall,
            tall,
            wide,
            tall,
            tall,
            wide,
        ],
        out_specs=tile,
        out_shape=jax.ShapeDtypeStruct((rows, count * width), F32),
        compiler_params=params(),
        cost_estimate=cost(3.3e-6 * count),
        name="scan_forward",
    )(px, taps, b_low, c_low, b_t, dt, cum, cum_t)


def gate_kernel(count, *refs):
    y_refs = refs[:count]
    z_ref, gain_ref, gate_ref, inv_ref = refs[count:]
    y = jnp.concatenate([ref[...] for ref in y_refs], axis=1)
    z = z_ref[...]
    gated = y * (z * sigmoid(z))
    mean = jnp.sum(gated * gated, axis=1, keepdims=True) * (1.0 / gated.shape[1])
    inv = lax.rsqrt(mean + EPS)
    gate_ref[...] = (gated * inv * gain_ref[...]).astype(BF)
    inv_ref[...] = jnp.broadcast_to(inv, inv_ref.shape)


def row_tile(size, array):
    return pl.BlockSpec((size, array.shape[1]), lambda t: (t, 0))


def gate_forward(y_parts, pz, gain):
    rows, inner = pz.shape
    size = 128
    tile = pl.BlockSpec((size, inner), lambda t: (t, 0))
    return pl.pallas_call(
        functools.partial(gate_kernel, len(y_parts)),
        grid=(rows // size,),
        in_specs=[row_tile(size, y) for y in y_parts]
        + [tile, pl.BlockSpec((1, inner), lambda t: (0, 0))],
        out_specs=[tile, pl.BlockSpec((size, LANES), lambda t: (t, 0))],
        out_shape=[
            jax.ShapeDtypeStruct((rows, inner), BF),
            jax.ShapeDtypeStruct((rows, LANES), F32),
        ],
        compiler_params=params(),
        cost_estimate=cost(15e-6),
        name="gate_forward",
    )(*y_parts, pz, gain)


def gate_back_kernel(count, *refs):
    y_refs = refs[:count]
    z_ref, grad_ref, inv_ref, gain_ref, gy_ref, gz_ref = refs[count:]
    y = jnp.concatenate([ref[...] for ref in y_refs], axis=1)
    z = z_ref[...]
    grad = grad_ref[...]
    inv = inv_ref[:, 0:1]
    sig = sigmoid(z)
    silu = z * sig
    normal = y * silu * inv
    grad_normal = grad * gain_ref[...]
    mean = jnp.sum(grad_normal * normal, axis=1, keepdims=True) * (1.0 / y.shape[1])
    gated = inv * (grad_normal - normal * mean)
    gy_ref[...] = (gated * silu).astype(BF)
    gz_ref[...] = (gated * y * (sig + silu * (1.0 - sig))).astype(BF)


def gate_backward(y_parts, pz, grad_gate, inv, gain):
    rows, inner = pz.shape
    size = 128
    tile = pl.BlockSpec((size, inner), lambda t: (t, 0))
    return pl.pallas_call(
        functools.partial(gate_back_kernel, len(y_parts)),
        grid=(rows // size,),
        in_specs=[row_tile(size, y) for y in y_parts]
        + [
            tile,
            tile,
            pl.BlockSpec((size, LANES), lambda t: (t, 0)),
            pl.BlockSpec((1, inner), lambda t: (0, 0)),
        ],
        out_specs=[tile, tile],
        out_shape=[
            jax.ShapeDtypeStruct((rows, inner), BF),
            jax.ShapeDtypeStruct((rows, inner), BF),
        ],
        compiler_params=params(),
        cost_estimate=cost(24e-6),
        name="gate_backward",
    )(*y_parts, pz, grad_gate, inv, gain)


def head_sums(product, spread):
    high = product.astype(BF)
    low = (product - high.astype(F32)).astype(BF)
    return dot_nn(high, spread) + dot_nn(low, spread)


def backward_kernel(group_start, *refs):
    x_ref, taps_ref, y_ref, gy_ref, b_ref, c_ref, bt_ref, ct_ref = refs[:8]
    dt_ref, cum_ref, cumt_ref = refs[8:11]
    gx_ref, lines_ref, *totals = refs[-8:]
    gb_ref, gc_ref, one_ref, two_ref, cb_ref, heads_ref = totals
    befores = refs[12:-8]
    first_head = (pl.program_id(0) + group_start) * GROUP_HEADS
    seq = pl.program_id(1)
    slot = x_ref.shape[0]

    @pl.when((pl.program_id(0) == 0) & (seq == 0))
    def _():
        for i, total in enumerate(totals):
            total[...] = befores[i][...] if befores else jnp.zeros_like(total)

    at = pl.multiple_of(seq * slot, slot)
    whole_rows = pl.ds(at, slot)
    early_rows = pl.ds(at, STRETCH)
    late_rows = pl.ds(pl.multiple_of(at + STRETCH, STRETCH), STRETCH)
    shifted, pre = conv_parts(x_ref[...], taps_ref)
    sig = sigmoid(pre)
    active = pre * sig
    slope = sig + active * (1.0 - sig)
    x_low = active.astype(BF).astype(F32)
    gy_low = gy_ref[...]
    gy = gy_low.astype(F32)
    cum_wide, cum_x, dt_x, left = head_tables(cum_ref, dt_ref, first_head)
    x_dt = (x_low * dt_x).astype(BF)
    skip = taps_ref[5:6, :]

    grad_inter = (gy[STRETCH:] * jnp.exp(cum_x[STRETCH:])).astype(BF)
    fade = jnp.exp(cum_x[STRETCH - 1 : STRETCH] - cum_x[:STRETCH])
    scaled = (x_low[:STRETCH] * (fade * dt_x[:STRETCH])).astype(BF)
    state = dot_nn(bt_ref[:, :STRETCH], scaled)
    gc_ref[late_rows, :] += dot_nt(grad_inter, state.astype(BF))
    grad_state = dot_nn(ct_ref[:, STRETCH:], grad_inter).astype(BF)
    gb_ref[early_rows, :] += dot_nt(scaled, grad_state)
    grad_scaled = dot_nn(b_ref[:STRETCH, :], grad_state)
    last_sum = column_sum(grad_state.astype(F32) * state)

    lower = lower_mask()
    zero = jnp.zeros((STRETCH, LANES), BF)
    rest = []
    for block in range(2):
        rows = slice(block * STRETCH, (block + 1) * STRETCH)
        cb = dot_nt(c_ref[rows, :], b_ref[rows, :])
        cb_first = cb_below = None
        parts = []
        for pair in range(GROUP_HEADS // 2):
            lanes = slice(pair * LANES, (pair + 1) * LANES)
            x_pair = x_dt[rows, lanes]
            gy_pair = gy_low[rows, lanes]
            total = None
            for side in range(2):
                head = 2 * pair + side
                row = cumt_ref[pl.ds(first_head + head, 1), :]
                first, below = decay_tiles(cum_wide[head], row, block, lower)
                mixing = join_tiles(
                    (cb[:HALF, :HALF] * first).astype(BF), (cb[HALF:, :] * below).astype(BF)
                )
                keep = left if side == 0 else jnp.logical_not(left)
                gy_head = jnp.where(keep, gy_pair, zero)
                mix_first = dot_nt(gy_head[:HALF], x_pair[:HALF]) * first
                mix_below = dot_nt(gy_head[HALF:], x_pair) * below
                cb_first = mix_first if cb_first is None else cb_first + mix_first
                cb_below = mix_below if cb_below is None else cb_below + mix_below
                now = dot_tn(mixing, gy_head)
                total = now if total is None else total + now
            parts.append(total)
        cb_ref[seq, block, :HALF, :HALF] += cb_first
        cb_ref[seq, block, HALF:, :] += cb_below
        rest.append(jnp.concatenate(parts, axis=1))
    moved = x_dt.astype(F32) * jnp.concatenate(rest, axis=0)
    moved = jnp.concatenate(
        [moved[:STRETCH] + scaled.astype(F32) * grad_scaled, moved[STRETCH:]], axis=0
    )
    rest[0] = rest[0] + fade * grad_scaled
    grad_pull = jnp.concatenate(rest, axis=0)

    width = x_low.shape[1]
    spread = (
        lax.broadcasted_iota(jnp.int32, (width, LANES), 1)
        == first_head + lax.broadcasted_iota(jnp.int32, (width, LANES), 0) // 64
    ).astype(F32).astype(BF)
    moved = gy * (y_ref[...] - skip * x_low) - moved
    edge = lax.broadcasted_iota(jnp.int32, (8, 1), 0) == 7
    moved = jnp.concatenate(
        [
            moved[: STRETCH - 8],
            moved[STRETCH - 8 : STRETCH] + jnp.where(edge, last_sum, 0.0),
            moved[STRETCH:],
        ],
        axis=0,
    )
    one_ref[whole_rows, :] += head_sums(moved, spread)
    two_ref[whole_rows, :] += head_sums(x_low * grad_pull, spread)
    third = lax.broadcasted_iota(jnp.int32, (8, 1), 0) == 2
    skip_line = jnp.where(third, column_sum(gy * x_low), 0.0)
    heads_ref[...] += head_sums(skip_line, spread)

    grad_pre = (skip * gy + dt_x * grad_pull) * slope
    gx_ref[...] = conv_back(grad_pre, taps_ref).astype(BF)
    lines = [column_sum(grad_pre * shifted[k]) for k in range(4)] + [column_sum(grad_pre)]
    lines = jnp.concatenate(lines + [jnp.zeros((3, width), F32)], axis=0)

    @pl.when(seq == 0)
    def _():
        lines_ref[...] = lines

    @pl.when(seq > 0)
    def _():
        lines_ref[...] += lines


def scan_backward(px, at, taps, y_rows, y_at, grad_y, prep, slot, start, count, before=None):
    b_low, c_low, b_t, c_t, dt, cum, cum_t = prep
    rows = px.shape[0]
    width = GROUP_HEADS * 64
    seqs = rows // slot
    tall = pl.BlockSpec((slot, LANES), lambda h, q: (q, 0))
    wide = pl.BlockSpec((LANES, slot), lambda h, q: (0, q))
    tile = pl.BlockSpec((slot, width), lambda h, q: (q, h + at))
    flat = jax.ShapeDtypeStruct((rows, LANES), F32)
    whole = pl.BlockSpec((rows, LANES), lambda h, q: (0, 0))
    totals = [whole] * 4 + [
        pl.BlockSpec((seqs, 2, STRETCH, STRETCH), lambda h, q: (0, 0, 0, 0)),
        pl.BlockSpec((8, LANES), lambda h, q: (0, 0)),
    ]
    extra, extra_specs, aliases = [jnp.zeros((8, LANES), BF)], [pl.BlockSpec(memory_space=pl.ANY)], {}
    if before is not None:
        if before[0].shape == px.shape:
            extra = [before[0]]
            aliases[11] = 0
        extra = extra + list(before[2:])
        extra_specs = extra_specs + totals
        aliases.update({12 + i: 2 + i for i in range(6)})
    return pl.pallas_call(
        functools.partial(backward_kernel, start),
        grid=(count, seqs),
        in_specs=[
            tile,
            pl.BlockSpec((8, width), lambda h, q: (0, h + start)),
            pl.BlockSpec((slot, width), lambda h, q: (q, h + y_at)),
            pl.BlockSpec((slot, width), lambda h, q: (q, h + start)),
            tall,
            tall,
            wide,
            wide,
            tall,
            tall,
            wide,
        ]
        + extra_specs,
        out_specs=[tile, pl.BlockSpec((8, width), lambda h, q: (0, h))] + totals,
        out_shape=[
            jax.ShapeDtypeStruct(px.shape, BF),
            jax.ShapeDtypeStruct((8, count * width), F32),
            flat,
            flat,
            flat,
            flat,
            jax.ShapeDtypeStruct((seqs, 2, STRETCH, STRETCH), F32),
            jax.ShapeDtypeStruct((8, LANES), F32),
        ],
        input_output_aliases=aliases,
        compiler_params=params(),
        cost_estimate=cost(3.3e-6 * count),
        name="scan_backward",
    )(px, taps, y_rows, grad_y, b_low, c_low, b_t, c_t, dt, cum, cum_t, *extra)


def finish_kernel(
    head_count,
    raw_ref,
    taps_ref,
    heads_ref,
    b_ref,
    c_ref,
    dt_ref,
    gb_ref,
    gc_ref,
    one_ref,
    two_ref,
    cb_ref,
    head_before_ref,
    before_ref,
    out_ref,
    lines_ref,
    head_total_ref,
):
    @pl.when(pl.program_id(0) == 0)
    def _():
        lines_ref[...] = jnp.zeros_like(lines_ref)
        head_total_ref[...] = head_before_ref[...]

    shifted, pre = conv_parts(raw_ref[:, : 2 * LANES], taps_ref)
    sig = sigmoid(pre)
    slope = sig + pre * sig * (1.0 - sig)
    grad_b, grad_c = [], []
    for block in range(2):
        rows = slice(block * STRETCH, (block + 1) * STRETCH)
        cb = cb_ref[0, block].astype(BF)
        grad_c.append(gc_ref[rows, :] + dot_nn(cb, b_ref[rows, :]))
        grad_b.append(gb_ref[rows, :] + dot_tn(cb, c_ref[rows, :]))
    grad_active = jnp.concatenate(
        [jnp.concatenate(grad_b, axis=0), jnp.concatenate(grad_c, axis=0)], axis=1
    )
    grad_pre = grad_active * slope
    lines = [column_sum(grad_pre * shifted[k]) for k in range(4)] + [column_sum(grad_pre)]
    lines.append(jnp.zeros((3, 2 * LANES), F32))
    lines_ref[...] += jnp.concatenate(lines, axis=0)

    dt = dt_ref[...]
    two = two_ref[...]
    rate = heads_ref[1:2, :]
    place = row_index(dt)
    grad_cum = one_ref[...]
    inside = place % STRETCH
    step = 1
    while step < STRETCH:
        moved = pltpu.roll(grad_cum, grad_cum.shape[0] - step, 0)
        grad_cum = grad_cum + jnp.where(inside < STRETCH - step, moved, 0.0)
        step *= 2
    grad_dt = grad_cum * rate + two
    lane = lax.broadcasted_iota(jnp.int32, (1, LANES), 1)
    raw = jnp.where(lane < head_count, raw_ref[:, 2 * LANES : 3 * LANES], 0.0)
    grad_raw = grad_dt * sigmoid(raw + heads_ref[0:1, :])
    head_total_ref[...] += jnp.concatenate(
        [column_sum(grad_raw), column_sum(grad_cum * dt) * rate, jnp.zeros((6, LANES), F32)], axis=0
    )
    out_ref[:, : 2 * LANES] = conv_back(grad_pre, taps_ref).astype(BF)
    out_ref[:, 2 * LANES : 3 * LANES] = grad_raw.astype(BF)
    out_ref[:, 3 * LANES :] = jnp.zeros_like(out_ref[:, 3 * LANES :])


def finish(raw, at, taps, heads, head_count, prep, totals, grads, narrow, grads_at, slot):
    b_low, c_low, _, _, dt, _, _ = prep
    rows = raw.shape[0]
    seqs = rows // slot
    tall = pl.BlockSpec((slot, LANES), lambda q: (q, 0))
    return pl.pallas_call(
        functools.partial(finish_kernel, head_count),
        grid=(seqs,),
        in_specs=[
            pl.BlockSpec((slot, 3 * LANES), lambda q: (q, at)),
            pl.BlockSpec((8, 2 * LANES), lambda q: (0, 0)),
            pl.BlockSpec((8, LANES), lambda q: (0, 0)),
            tall,
            tall,
            tall,
            tall,
            tall,
            tall,
            tall,
            pl.BlockSpec((1, 2, STRETCH, STRETCH), lambda q: (q, 0, 0, 0)),
            pl.BlockSpec((8, LANES), lambda q: (0, 0)),
            pl.BlockSpec(memory_space=pl.ANY),
        ],
        out_specs=[
            pl.BlockSpec((slot, narrow), lambda q: (q, grads_at)),
            pl.BlockSpec((8, 2 * LANES), lambda q: (0, 0)),
            pl.BlockSpec((8, LANES), lambda q: (0, 0)),
        ],
        out_shape=[
            jax.ShapeDtypeStruct(grads.shape, BF),
            jax.ShapeDtypeStruct((8, 2 * LANES), F32),
            jax.ShapeDtypeStruct((8, LANES), F32),
        ],
        input_output_aliases={12: 0},
        compiler_params=params(),
        cost_estimate=cost(3e-6),
        name="finish",
    )(raw, taps, heads, b_low, c_low, dt, *totals, grads)


def project_kernel(rows_ref, weight_ref, out_ref):
    out_ref[...] = dot_nn(rows_ref[...], weight_ref[...])


def project(normed, weight, at, count, size):
    rows, depth = normed.shape
    return pl.pallas_call(
        project_kernel,
        grid=(count,),
        in_specs=[
            pl.BlockSpec((rows, depth), lambda j: (0, 0)),
            pl.BlockSpec((depth, size), lambda j: (0, j + at)),
        ],
        out_specs=pl.BlockSpec((rows, size), lambda j: (0, j)),
        out_shape=jax.ShapeDtypeStruct((rows, count * size), F32),
        compiler_params=params(),
        cost_estimate=cost(2.5e-6 * count),
        name="project",
    )(normed, weight)


def pair_kernel(mine_ref, other_ref, grad_ref, keep_ref, give_ref):
    grad = grad_ref[...]
    give_ref[...] = dot_nn(other_ref[...], grad).astype(give_ref.dtype)
    keep_ref[...] = dot_nn(mine_ref[...], grad).astype(keep_ref.dtype)


def weight_grads(mine, other, grad, at, count, size):
    depth, rows = mine.shape
    whole = pl.BlockSpec((depth, rows), lambda j: (0, 0))
    tile = pl.BlockSpec((depth, size), lambda j: (0, j))
    shape = jax.ShapeDtypeStruct((depth, count * size), BF)
    return pl.pallas_call(
        pair_kernel,
        grid=(count,),
        in_specs=[whole, whole, pl.BlockSpec((rows, size), lambda j: (0, j + at))],
        out_specs=[tile, tile],
        out_shape=[shape, shape],
        compiler_params=params(),
        cost_estimate=cost(2.5e-6 * count),
        name="weight_grads",
    )(mine, other, grad)


def input_grads_kernel(sizes, ends, has_before, final, *refs):
    pairs = [refs[2 * i : 2 * i + 2] for i in range(len(sizes))]
    refs = refs[2 * len(sizes) :]
    steps = sum(sizes)
    step = pl.program_id(0)
    if has_before:
        before_ref, refs = refs[0], refs[1:]
    if final:
        hidden_ref, inv_ref, gain_ref, mask_ref, cot_ref, out_ref, total = refs
    else:
        (total,) = refs

    def add(grad_ref, weight):
        now = dot_nt(grad_ref[...], weight)

        @pl.when(step == 0)
        def _():
            total[...] = now + before_ref[...] if has_before else now

        @pl.when(step > 0)
        def _():
            total[...] += now

    begin = 0
    for (grad_ref, weight_ref), size, end in zip(pairs, sizes, ends):
        full = size if end is None else size - 1

        @pl.when((step >= begin) & (step < begin + full))
        def _(grad_ref=grad_ref, weight_ref=weight_ref):
            add(grad_ref, weight_ref[...])

        if end is not None:

            @pl.when(step == begin + full)
            def _(grad_ref=grad_ref, weight_ref=weight_ref, end=end):
                weight = weight_ref[...]
                lane = lax.broadcasted_iota(jnp.int32, weight.shape, 1)
                add(grad_ref, jnp.where(lane < end, weight, jnp.zeros_like(weight)))

        begin += size
    if final:

        @pl.when(step >= steps)
        def _():
            tile = hidden_ref.shape[0]
            grad = total[pl.ds(pl.multiple_of((step - steps) * tile, tile), tile), :]
            inv = inv_ref[...]
            normal = hidden_ref[...] * inv
            grad = grad * gain_ref[...]
            inside = jnp.sum(grad * normal, axis=1, keepdims=True) * (1.0 / grad.shape[1])
            out_ref[...] = inv * (grad - normal * inside) + mask_ref[...] * cot_ref[...]


def input_grads(grads, places, weight, before=None, final=None):
    rows = grads[0].shape[0]
    width = weight.shape[0]
    size, tile = 512, 128
    sizes = [g.shape[1] // size for g in grads]
    steps = sum(sizes)
    in_specs, args, begin = [], [], 0
    for grad, (at, _), count in zip(grads, places, sizes):

        def place(k, begin=begin, count=count, at=0):
            return (0, at + jnp.clip(k - begin, 0, count - 1))

        in_specs += [
            pl.BlockSpec((rows, size), place),
            pl.BlockSpec((width, size), functools.partial(place, at=at)),
        ]
        args += [grad, weight]
        begin += count
    if before is not None:
        in_specs.append(pl.BlockSpec((rows, width), lambda k: (0, 0), pipeline_mode=pl.Buffered(1)))
        args.append(before)
    if final:

        def row(k):
            return (jnp.clip(k - steps, 0, rows // tile - 1), 0)

        line = pl.BlockSpec((1, width), lambda k: (0, 0))
        column = pl.BlockSpec((tile, 1), row)
        wide = pl.BlockSpec((tile, width), row)
        in_specs += [wide, column, line, column, wide]
        args += list(final)
        out_specs = wide
        out_shape = jax.ShapeDtypeStruct((rows, width), F32)
        scratch = [pltpu.VMEM((rows, width), F32)]
    else:
        out_specs = pl.BlockSpec((rows, width), lambda k: (0, 0))
        out_shape = jax.ShapeDtypeStruct((rows, width), F32)
        scratch = []
    ends = [end for _, end in places]
    return pl.pallas_call(
        functools.partial(input_grads_kernel, sizes, ends, before is not None, bool(final)),
        grid=(steps + (rows // tile if final else 0),),
        in_specs=in_specs,
        out_specs=out_specs,
        out_shape=out_shape,
        scratch_shapes=scratch,
        compiler_params=params(),
        cost_estimate=cost(2.5e-6 * steps),
        name="input_grads",
    )(*args)


def swap(values, bit, shards):
    return lax.ppermute(values, "shard", [(i, i ^ (1 << bit)) for i in range(shards)])


def border(moving, *values):
    ready = lax.optimization_barrier(tuple(one.got for one in moving) + values)
    for one, got in zip(moving, ready):
        one.got = got
        one.finish()
    rest = ready[len(moving) :]
    return rest[0] if len(rest) == 1 else rest


class Gather:
    def __init__(self, own, order, shards, place):
        self.now, self.order, self.shards, self.place = own, list(order), shards, place
        self.live, self.columns = [], own.shape[-1]

    def start(self):
        self.bit = self.order.pop(0)
        self.got = swap(self.now, self.bit, self.shards)

    def finish(self):
        mine = (self.place >> self.bit) & 1
        axis = len([b for b in self.live if b > self.bit])
        first = jnp.where(mine == 0, self.now, self.got)
        second = jnp.where(mine == 0, self.got, self.now)
        self.now = jnp.stack([first, second], axis=axis)
        self.live.append(self.bit)

    def whole(self):
        while self.order:
            self.start()
            self.finish()
        return self.now


class Spread:
    def __init__(self, now, bits, shards, groups):
        self.now, self.bits, self.shards, self.groups = now, list(bits), shards, groups

    def start(self):
        if self.bits:
            self.got = swap(self.now, self.bits.pop(0), self.shards)
        else:
            pairs = [(i, (i + 1) % self.groups) for i in range(self.groups)]
            self.got = lax.ppermute(self.now, "group", pairs)

    def finish(self):
        self.now = self.now + self.got

    def result(self):
        while self.bits:
            self.start()
            self.finish()
        return self.now


class Group:
    def __init__(self, now, groups):
        self.now, self.groups = now, groups

    def start(self):
        self.pairs = [(i, (i + 1) % self.groups) for i in range(self.groups)]
        self.got = lax.ppermute(self.now, "group", self.pairs)

    def finish(self):
        total, got = self.now.astype(F32), self.got
        for step in range(1, self.groups):
            if step > 1:
                got = lax.ppermute(got, "group", self.pairs)
            total = total + got.astype(F32)
        self.now = total


class Sum:
    def __init__(self, pair, order, shards, groups, place, part, group_first=False):
        self.keep, self.give = pair
        self.shards, self.groups, self.place, self.part = shards, groups, place, part
        self.columns, self.dtype = self.keep.shape[-1], self.keep.dtype
        self.group_first = group_first and groups == 2
        self.todo = [0] + (["group"] if self.group_first else []) + list(order) + ["end"]
        self.live = list(range(shards.bit_length() - 2, 0, -1))
        self.now = None

    def start(self):
        self.bit = bit = self.todo.pop(0)
        if bit == "end":
            pairs = [(i, (i + 1) % self.groups) for i in range(self.groups)]
            self.got = lax.ppermute(self.now, "group", pairs)
        elif bit == "group":
            half = self.columns // 2
            mine = lax.axis_index("group")
            axis = self.now.ndim - 1
            self.keep = lax.dynamic_slice_in_dim(self.now, mine * half, half, axis)
            give = lax.dynamic_slice_in_dim(self.now, (1 - mine) * half, half, axis)
            self.got = lax.ppermute(give, "group", [(0, 1), (1, 0)])
        elif bit == 0:
            self.got = swap(self.give, 0, self.shards)
        else:
            axis = self.live.index(bit)
            mine = (self.place >> bit) & 1
            self.keep = lax.dynamic_index_in_dim(self.now, mine, axis, keepdims=False)
            give = lax.dynamic_index_in_dim(self.now, 1 - mine, axis, keepdims=False)
            self.live.remove(bit)
            self.got = swap(give, bit, self.shards)

    def finish(self):
        if self.bit == "end" and self.group_first:
            first = lax.axis_index("group") == 0
            halves = [jnp.where(first, self.now, self.got), jnp.where(first, self.got, self.now)]
            self.now = jnp.concatenate(halves, axis=-1)
        elif self.bit == "end":
            total, got = self.now.astype(F32), self.got
            for step in range(1, self.groups):
                if step > 1:
                    pairs = [(i, (i + 1) % self.groups) for i in range(self.groups)]
                    got = lax.ppermute(got, "group", pairs)
                total = total + got.astype(F32)
            self.now = total
        else:
            now = self.keep.astype(F32) + self.got.astype(F32)
            if self.todo != ["end"] or not self.group_first:
                now = now.astype(self.dtype)
            if self.bit == 0:
                now = now.reshape((2,) * len(self.live) + (self.part, self.columns))
            self.now = now

    def result(self):
        while self.todo:
            self.start()
            self.finish()
        return self.now


def local(
    shards,
    groups,
    hidden_in,
    lengths,
    pre_gain,
    in_proj,
    conv_weight,
    conv_bias,
    head_params,
    gate_gain,
    out_proj,
    cotangent,
):
    micro, own, slot, width = hidden_in.shape
    rows = micro * own * slot
    inner = out_proj.shape[0] * shards
    channels = conv_bias.shape[0] * shards
    heads = head_params.shape[1]
    tail = channels - inner + heads
    part = in_proj.shape[0]
    out_part = out_proj.shape[0]
    own_conv = conv_bias.shape[0]
    taps = conv_weight.shape[0]
    hidden = hidden_in.reshape(rows, width)
    cot = cotangent.reshape(rows, width)
    place = lax.axis_index("shard")
    core = place & 1
    chip_bits = list(range(1, shards.bit_length() - 1))
    up = chip_bits
    down = chip_bits[::-1]

    w_in = lax.all_gather(in_proj, "shard", axis=0, tiled=True)
    w_out = lax.all_gather(out_proj, "shard", axis=0, tiled=True)
    small = jnp.concatenate([pre_gain, gate_gain, conv_bias, conv_weight.reshape(-1)], axis=0)
    small = small.astype(F32)
    small = jnp.pad(small, (0, -small.shape[0] % LANES))[None, :]
    packed = Gather(small, down + [0], shards, place).whole().reshape(shards, -1)
    sizes = (part, out_part, own_conv, taps * own_conv)
    ends = [sum(sizes[: i + 1]) for i in range(4)]
    pre_all = packed[:, : ends[0]].reshape(1, width)
    gate_all = packed[:, ends[0] : ends[1]].reshape(1, inner)
    bias_all = packed[:, ends[1] : ends[2]].reshape(1, channels)
    taps_all = packed[:, ends[2] : ends[3]].reshape(shards, taps, -1)
    taps_all = jnp.swapaxes(taps_all, 0, 1).reshape(taps, channels)
    skip_row = jnp.pad(jnp.repeat(head_params[2], inner // heads), (0, channels - inner))
    table = jnp.concatenate(
        [taps_all, bias_all, skip_row[None, :], jnp.zeros((2, channels), F32)], axis=0
    )
    table_x, table_bc = table[:, :inner], table[:, inner:]
    rate = -jnp.exp(head_params[1])
    head_rows = jnp.pad(
        jnp.stack([head_params[0], rate], axis=0), ((0, 6), (0, LANES - heads))
    )

    inv_first = lax.rsqrt(jnp.mean(hidden * hidden, axis=-1, keepdims=True) + EPS)
    normed = (hidden * inv_first * pre_all).astype(BF)
    turned = normed.T.reshape(shards // 2, 2, part, rows)
    mine = lax.dynamic_index_in_dim(turned, core, 1, keepdims=False).reshape(-1, rows)
    other = lax.dynamic_index_in_dim(turned, 1 - core, 1, keepdims=False).reshape(-1, rows)
    positions = jnp.arange(slot, dtype=jnp.int32)
    mask = (positions[None, :] < lengths.reshape(-1)[:, None]).astype(F32).reshape(rows, 1)
    grad_low = (mask * cot).astype(BF)

    size = 4 * LANES
    blocks = inner // size
    raw_at = inner // (3 * LANES)
    prep_at = (raw_at, table_bc, head_rows, heads)
    px = project(normed, w_in, blocks, blocks + 1, size)
    prep = prepare(px, *prep_at, slot)
    unit = GROUP_HEADS * 64
    y_rows = scan_forward(px, 0, table_x, prep, slot, 0, inner // unit)
    pz = project(normed, w_in, 0, blocks, size)
    gate_low, inv = gate_forward([y_rows], pz, gate_all)

    g_out = dot_tn(gate_low, grad_low).astype(BF)
    g_out, grad_low, mine, other = border([], g_out, grad_low, mine, other)
    sum_out = lax.psum_scatter(g_out, "shard", scatter_dimension=0, tiled=True)
    grad_gate = dot_nt(grad_low, w_out)
    grad_y, grad_z = gate_backward([y_rows], pz, grad_gate, inv, gate_all)
    reduce = functools.partial(Sum, shards=shards, groups=groups, place=place, order=up)
    third = inner // unit // 3
    outs = None
    for start in (0, third):
        outs_now = scan_backward(
            px, start, table_x, y_rows, start, grad_y, prep, slot, start, third, before=outs
        )
        outs_first, outs = outs, outs_now
    lines_x = [outs_first[1], outs[1]]
    b_blocks = 2 * third * unit // size
    pair_b = weight_grads(mine, other, outs[0], 0, b_blocks, size)
    *pair_b, grad_z = border([], *pair_b, grad_z)
    s_b = reduce(pair_b, part=part, group_first=True)
    s_b.start()
    g_z = dot_nn(turned.reshape(width, rows), grad_z).astype(BF)
    g_z, grad_y, sum_out = border([s_b], g_z, grad_y, sum_out)
    sum_z = lax.psum_scatter(g_z, "shard", scatter_dimension=0, tiled=True)
    s_b.start()
    rest = inner // unit - 2 * third
    outs = scan_backward(
        px, 2 * third, table_x, y_rows, 2 * third, grad_y, prep, slot, 2 * third, rest, before=outs
    )
    mine, *outs = border([s_b], mine, *outs)
    s_out = Group(sum_out, groups)
    lines_x.append(outs[1])
    grad_x, lines_bc, head_total = finish(
        px, *prep_at, prep, outs[2:], outs[0], size, blocks, slot
    )
    pair_a = weight_grads(mine, other, grad_x, b_blocks, blocks + 1 - b_blocks, size)

    lines = jnp.concatenate(lines_x + [lines_bc], axis=1)
    head_line = head_total[:3].reshape(1, 3 * LANES)
    head_line = jnp.pad(head_line, ((0, 0), (0, channels - 3 * LANES)))
    small = jnp.concatenate([lines[:5], head_line, lines[6:]], axis=0)
    s_small = Spread(small, [0] + up, shards, groups)
    s_small.start()
    *pair_a, grad_z, grad_x = border([s_small], *pair_a, grad_z, grad_x)
    s_a = reduce(pair_a, part=part)
    s_a.start()
    s_b.start()
    s_small.start()
    part_sum = input_grads([grad_z], [(0, None)], w_in)
    part_sum, grad_x = border([s_b, s_a, s_small], part_sum, grad_x)
    s_a.start()
    s_small.start()
    s_b.start()
    s_out.start()
    grad_input = input_grads(
        [grad_x],
        [(blocks, tail % size)],
        w_in,
        before=part_sum,
        final=(hidden, inv_first, pre_all, mask, cot),
    )
    gate_low, grad_input, sum_z = border([s_a, s_b, s_small, s_out], gate_low, grad_input, sum_z)
    s_a.start()
    s_small.start()
    s_b.start()
    s_z = Group(sum_z, groups)
    s_z.start()
    layer_out = mask * (hidden + dot_nn(gate_low, w_out))
    layer_out = border([s_a, s_small, s_b, s_z], layer_out)
    s_a.start()
    s_small.start()
    s_b.start()
    for one in (s_small, s_a, s_b):
        one.finish()
    sum_a, small = s_a.result(), s_small.now
    b_columns = b_blocks * size
    g_in = jnp.concatenate(
        [s_z.now, s_b.result(), sum_a[:, : inner - b_columns + tail]], axis=1
    )
    g_out = s_out.now

    def gain_grads(weight, grads, gain):
        return jnp.sum(weight.astype(F32) * grads, axis=1) / gain.astype(F32)

    g_pre = gain_grads(in_proj, g_in, pre_gain)
    g_gate = gain_grads(out_proj, g_out, gate_gain)
    g_lines = lax.dynamic_slice(small, (0, place * own_conv), (5, own_conv))
    g_heads = small[5, : 3 * LANES].reshape(3, LANES)[:, :heads]
    return (
        layer_out.reshape(hidden_in.shape),
        grad_input.reshape(hidden_in.shape),
        g_pre,
        g_in,
        g_lines[:4],
        g_lines[4],
        g_heads,
        g_gate,
        g_out,
    )


def solution(mesh):
    rows = P(None, ("group", "shard"), None, None)
    in_specs = (
        rows,
        P(None, ("group", "shard")),
        P("shard"),
        P("shard", None),
        P(None, "shard"),
        P("shard"),
        P(),
        P("shard"),
        P("shard", None),
        rows,
    )
    out_specs = (
        rows,
        rows,
        P("shard"),
        P("shard", None),
        P(None, "shard"),
        P("shard"),
        P(),
        P("shard"),
        P("shard", None),
    )
    body = functools.partial(local, mesh.shape["shard"], mesh.shape["group"])
    return jax.shard_map(body, mesh=mesh, in_specs=in_specs, out_specs=out_specs, check_vma=False)
```

```python
import functools

import jax
import jax.numpy as jnp
from jax import lax
from jax.experimental import pallas as pl
from jax.experimental.pallas import tpu as pltpu
from jax.sharding import PartitionSpec as P

STRETCH = 256
HALF = 128
LANES = 128
GROUP_HEADS = 8
EPS = 1e-05
BF = jnp.bfloat16
F32 = jnp.float32
VMEM_BYTES = 56 * 1024 * 1024


def params(**kwargs):
    return pltpu.CompilerParams(vmem_limit_bytes=VMEM_BYTES, **kwargs)


def cost(seconds):
    return pl.CostEstimate(
        flops=int(seconds * 2.0e13), bytes_accessed=int(seconds * 6.0e10), transcendentals=0
    )


def dot_nn(left, right):
    return lax.dot_general(left, right, (((1,), (0,)), ((), ())), preferred_element_type=F32)


def dot_nt(left, right):
    return lax.dot_general(left, right, (((1,), (1,)), ((), ())), preferred_element_type=F32)


def dot_tn(left, right):
    return lax.dot_general(left, right, (((0,), (0,)), ((), ())), preferred_element_type=F32)


def sigmoid(values):
    return 1.0 / (1.0 + jnp.exp(-values))


def row_index(values):
    return lax.broadcasted_iota(jnp.int32, (values.shape[0], 1), 0)


def shift_down(values, count):
    rolled = pltpu.roll(values, count, 0)
    place = lax.broadcasted_iota(jnp.int32, (8, 1), 0)
    return jnp.concatenate([jnp.where(place >= count, rolled[:8], 0.0), rolled[8:]], axis=0)


def shift_up(values, count):
    rows = values.shape[0]
    rolled = pltpu.roll(values, rows - count, 0)
    place = lax.broadcasted_iota(jnp.int32, (8, 1), 0)
    last = jnp.where(place < 8 - count, rolled[rows - 8 :], 0.0)
    return jnp.concatenate([rolled[: rows - 8], last], axis=0)


def conv_sum(values, taps_ref):
    pre = taps_ref[4:5, :]
    for k in range(3):
        pre = pre + taps_ref[k : k + 1, :] * shift_down(values, 3 - k)
    return pre + taps_ref[3:4, :] * values


def conv_back(grad_pre, values, taps_ref):
    total = taps_ref[3:4, :] * grad_pre
    lines = []
    for k in range(3):
        moved = shift_up(grad_pre, 3 - k)
        total = total + taps_ref[k : k + 1, :] * moved
        lines.append(column_sum(moved * values))
    lines += [column_sum(grad_pre * values), column_sum(grad_pre)]
    lines.append(jnp.zeros((3, values.shape[1]), F32))
    return total, jnp.concatenate(lines, axis=0)


def column_sum(values):
    return jnp.sum(values, axis=0, keepdims=True)


def prepare_kernel(head_count, raw_ref, taps_ref, heads_ref, b_ref, c_ref, bt_ref, ct_ref, dt_ref, cum_ref, cumt_ref):
    pre = conv_sum(raw_ref[:, : 2 * LANES], taps_ref)
    active = pre * sigmoid(pre)
    b_part, c_part = active[:, :LANES], active[:, LANES:]
    b_ref[...] = b_part.astype(BF)
    c_ref[...] = c_part.astype(BF)
    bt_ref[...] = b_part.T.astype(BF)
    ct_ref[...] = c_part.T.astype(BF)
    lane = lax.broadcasted_iota(jnp.int32, (1, LANES), 1)
    raw = jnp.where(lane < head_count, raw_ref[:, 2 * LANES :], 0.0) + heads_ref[0:1, :]
    dt = jnp.maximum(raw, 0.0) + jnp.log1p(jnp.exp(-jnp.abs(raw)))
    cum = dt * heads_ref[1:2, :]
    place = row_index(cum) % STRETCH
    step = 1
    while step < STRETCH:
        cum = cum + jnp.where(place >= step, pltpu.roll(cum, step, 0), 0.0)
        step *= 2
    dt_ref[...] = dt
    cum_ref[...] = cum
    cumt_ref[...] = cum.T


def prepare(raw, at, taps, heads, head_count, slot):
    rows = raw.shape[0]
    tall = pl.BlockSpec((slot, LANES), lambda q: (q, 0))
    wide = pl.BlockSpec((LANES, slot), lambda q: (0, q))
    return pl.pallas_call(
        functools.partial(prepare_kernel, head_count),
        grid=(rows // slot,),
        in_specs=[
            pl.BlockSpec((slot, 3 * LANES), lambda q: (q, at)),
            pl.BlockSpec((8, 2 * LANES), lambda q: (0, 0)),
            pl.BlockSpec((8, LANES), lambda q: (0, 0)),
        ],
        out_specs=[tall, tall, wide, wide, tall, tall, wide],
        out_shape=[
            jax.ShapeDtypeStruct((rows, LANES), BF),
            jax.ShapeDtypeStruct((rows, LANES), BF),
            jax.ShapeDtypeStruct((LANES, rows), BF),
            jax.ShapeDtypeStruct((LANES, rows), BF),
            jax.ShapeDtypeStruct((rows, LANES), F32),
            jax.ShapeDtypeStruct((rows, LANES), F32),
            jax.ShapeDtypeStruct((LANES, rows), F32),
        ],
        compiler_params=params(),
        name="prepare",
    )(raw, taps, heads)


def head_tables(cum_ref, dt_ref, first_head):
    shift = lax.rem(LANES - first_head, LANES)
    cum = pltpu.roll(cum_ref[...], shift, 1)
    dt = pltpu.roll(dt_ref[...], shift, 1)
    rows = cum.shape[0]
    cum_wide = [jnp.broadcast_to(cum[:, i : i + 1], (rows, LANES)) for i in range(GROUP_HEADS)]
    dt_wide = [jnp.broadcast_to(dt[:, i : i + 1], (rows, LANES)) for i in range(GROUP_HEADS)]
    left = lax.broadcasted_iota(jnp.int32, (1, LANES), 1) < LANES // 2

    def spread(wide):
        return jnp.concatenate(
            [jnp.where(left, wide[i], wide[i + 1]) for i in range(0, GROUP_HEADS, 2)], axis=1
        )

    return cum_wide, spread(cum_wide), spread(dt_wide), left


def decay_tiles(cum_wide, cumt_row, block, lower):
    begin = block * STRETCH
    top = cum_wide[begin : begin + HALF]
    low = cum_wide[begin + HALF : begin + STRETCH]
    row_left = cumt_row[:, begin : begin + HALF]
    row_right = cumt_row[:, begin + HALF : begin + STRETCH]
    first = jnp.where(lower, jnp.exp(top - row_left), 0.0)
    second = jnp.exp(low - row_left)
    third = jnp.where(lower, jnp.exp(low - row_right), 0.0)
    return first, jnp.concatenate([second, third], axis=1)


def join_tiles(first, below):
    return jnp.concatenate(
        [jnp.concatenate([first, jnp.zeros_like(first)], axis=1), below], axis=0
    )


def lower_mask():
    return lax.broadcasted_iota(jnp.int32, (HALF, HALF), 0) >= lax.broadcasted_iota(
        jnp.int32, (HALF, HALF), 1
    )


def forward_kernel(
    group_start, x_ref, taps_ref, b_ref, c_ref, bt_ref, dt_ref, cum_ref, cumt_ref, y_ref
):
    first_head = (pl.program_id(1) + group_start) * GROUP_HEADS
    pre = conv_sum(x_ref[...], taps_ref)
    x_low = (pre * sigmoid(pre)).astype(BF).astype(F32)
    cum_wide, cum_x, dt_x, left = head_tables(cum_ref, dt_ref, first_head)
    x_dt = (x_low * dt_x).astype(BF)
    skipped = taps_ref[5:6, :] * x_low
    fade = jnp.exp(cum_x[STRETCH - 1 : STRETCH] - cum_x[:STRETCH])
    scaled = (x_low[:STRETCH] * (fade * dt_x[:STRETCH])).astype(BF)
    state = dot_nn(bt_ref[:, :STRETCH], scaled).astype(BF)
    lower = lower_mask()
    zero = jnp.zeros((STRETCH, LANES), BF)
    for block in range(2):
        rows = slice(block * STRETCH, (block + 1) * STRETCH)
        cb = dot_nt(c_ref[rows, :], b_ref[rows, :])
        if block == 1:
            inter = dot_nn(c_ref[rows, :], state)
        for pair in range(GROUP_HEADS // 2):
            lanes = slice(pair * LANES, (pair + 1) * LANES)
            x_pair = x_dt[rows, lanes]
            total = None
            for side in range(2):
                head = 2 * pair + side
                row = cumt_ref[pl.ds(first_head + head, 1), :]
                first, below = decay_tiles(cum_wide[head], row, block, lower)
                mixing = join_tiles(
                    (cb[:HALF, :HALF] * first).astype(BF), (cb[HALF:, :] * below).astype(BF)
                )
                keep = left if side == 0 else jnp.logical_not(left)
                now = dot_nn(mixing, jnp.where(keep, x_pair, zero))
                total = now if total is None else total + now
            if block == 1:
                total = total + jnp.exp(cum_x[rows, lanes]) * inter[:, lanes]
            y_ref[rows, lanes] = total + skipped[rows, lanes]


def scan_forward(px, offset, taps, prep, slot, start, count):
    b_low, c_low, b_t, _, dt, cum, cum_t = prep
    rows = px.shape[0]
    width = GROUP_HEADS * 64
    tall = pl.BlockSpec((slot, LANES), lambda q, h: (q, 0))
    wide = pl.BlockSpec((LANES, slot), lambda q, h: (0, q))
    tile = pl.BlockSpec((slot, width), lambda q, h: (q, h))
    return pl.pallas_call(
        functools.partial(forward_kernel, start),
        grid=(rows // slot, count),
        in_specs=[
            pl.BlockSpec((slot, width), lambda q, h: (q, h + offset)),
            pl.BlockSpec((8, width), lambda q, h: (0, h + start)),
            tall,
            tall,
            wide,
            tall,
            tall,
            wide,
        ],
        out_specs=tile,
        out_shape=jax.ShapeDtypeStruct((rows, count * width), F32),
        compiler_params=params(),
        cost_estimate=cost(3.3e-6 * count),
        name="scan_forward",
    )(px, taps, b_low, c_low, b_t, dt, cum, cum_t)


def gate_kernel(count, *refs):
    y_refs = refs[:count]
    z_ref, gain_ref, gate_ref, inv_ref = refs[count:]
    y = jnp.concatenate([ref[...] for ref in y_refs], axis=1)
    z = z_ref[...].astype(F32)
    gated = y * (z * sigmoid(z))
    mean = jnp.sum(gated * gated, axis=1, keepdims=True) * (1.0 / gated.shape[1])
    inv = lax.rsqrt(mean + EPS)
    gate_ref[...] = (gated * inv * gain_ref[...]).astype(BF)
    inv_ref[...] = jnp.broadcast_to(inv, inv_ref.shape)


def row_tile(size, array):
    return pl.BlockSpec((size, array.shape[1]), lambda t: (t, 0))


def gate_forward(y_parts, pz, gain):
    rows, inner = pz.shape
    size = 128
    tile = pl.BlockSpec((size, inner), lambda t: (t, 0))
    return pl.pallas_call(
        functools.partial(gate_kernel, len(y_parts)),
        grid=(rows // size,),
        in_specs=[row_tile(size, y) for y in y_parts]
        + [tile, pl.BlockSpec((1, inner), lambda t: (0, 0))],
        out_specs=[tile, pl.BlockSpec((size, LANES), lambda t: (t, 0))],
        out_shape=[
            jax.ShapeDtypeStruct((rows, inner), BF),
            jax.ShapeDtypeStruct((rows, LANES), F32),
        ],
        compiler_params=params(),
        cost_estimate=cost(15e-6),
        name="gate_forward",
    )(*y_parts, pz, gain)


def gate_back_kernel(count, *refs):
    y_refs = refs[:count]
    z_ref, grad_ref, inv_ref, gain_ref, gy_ref, gz_ref = refs[count:]
    y = jnp.concatenate([ref[...] for ref in y_refs], axis=1)
    z = z_ref[...].astype(F32)
    grad = grad_ref[...].astype(F32)
    inv = inv_ref[:, 0:1]
    sig = sigmoid(z)
    silu = z * sig
    normal = y * silu * inv
    grad_normal = grad * gain_ref[...]
    mean = jnp.sum(grad_normal * normal, axis=1, keepdims=True) * (1.0 / y.shape[1])
    gated = inv * (grad_normal - normal * mean)
    gy_ref[...] = (gated * silu).astype(BF)
    gz_ref[...] = (gated * y * (sig + silu * (1.0 - sig))).astype(BF)


def gate_backward(y_parts, pz, grad_gate, inv, gain):
    rows, inner = pz.shape
    size = 128
    tile = pl.BlockSpec((size, inner), lambda t: (t, 0))
    return pl.pallas_call(
        functools.partial(gate_back_kernel, len(y_parts)),
        grid=(rows // size,),
        in_specs=[row_tile(size, y) for y in y_parts]
        + [
            tile,
            tile,
            pl.BlockSpec((size, LANES), lambda t: (t, 0)),
            pl.BlockSpec((1, inner), lambda t: (0, 0)),
        ],
        out_specs=[tile, tile],
        out_shape=[
            jax.ShapeDtypeStruct((rows, inner), BF),
            jax.ShapeDtypeStruct((rows, inner), BF),
        ],
        compiler_params=params(),
        cost_estimate=cost(24e-6),
        name="gate_backward",
    )(*y_parts, pz, grad_gate, inv, gain)


def head_sums(product, spread):
    high = product.astype(BF)
    low = (product - high.astype(F32)).astype(BF)
    return dot_nn(high, spread) + dot_nn(low, spread)


def backward_kernel(group_start, *refs):
    x_ref, taps_ref, y_ref, gy_ref, b_ref, c_ref, bt_ref, ct_ref = refs[:8]
    dt_ref, cum_ref, cumt_ref = refs[8:11]
    gx_ref, lines_ref, *totals = refs[-8:]
    gb_ref, gc_ref, one_ref, two_ref, cb_ref, heads_ref = totals
    befores = refs[12:-8]
    first_head = (pl.program_id(0) + group_start) * GROUP_HEADS
    seq = pl.program_id(1)
    slot = x_ref.shape[0]

    @pl.when((pl.program_id(0) == 0) & (seq == 0))
    def _():
        for i, total in enumerate(totals):
            total[...] = befores[i][...] if befores else jnp.zeros_like(total)

    at = pl.multiple_of(seq * slot, slot)
    whole_rows = pl.ds(at, slot)
    early_rows = pl.ds(at, STRETCH)
    late_rows = pl.ds(pl.multiple_of(at + STRETCH, STRETCH), STRETCH)
    pre = conv_sum(x_ref[...], taps_ref)
    sig = sigmoid(pre)
    active = pre * sig
    slope = sig + active * (1.0 - sig)
    x_low = active.astype(BF).astype(F32)
    gy_low = gy_ref[...]
    gy = gy_low.astype(F32)
    cum_wide, cum_x, dt_x, left = head_tables(cum_ref, dt_ref, first_head)
    x_dt = (x_low * dt_x).astype(BF)
    skip = taps_ref[5:6, :]

    grad_inter = (gy[STRETCH:] * jnp.exp(cum_x[STRETCH:])).astype(BF)
    fade = jnp.exp(cum_x[STRETCH - 1 : STRETCH] - cum_x[:STRETCH])
    scaled = (x_low[:STRETCH] * (fade * dt_x[:STRETCH])).astype(BF)
    state = dot_nn(bt_ref[:, :STRETCH], scaled)
    grad_state = dot_nn(ct_ref[:, STRETCH:], grad_inter).astype(BF)

    lower = lower_mask()
    zero = jnp.zeros((STRETCH, LANES), BF)
    rest = [None, None]
    for block in (1, 0):
        rows = slice(block * STRETCH, (block + 1) * STRETCH)
        cb = dot_nt(c_ref[rows, :], b_ref[rows, :])
        cb_first = cb_below = None
        parts = []
        for pair in range(GROUP_HEADS // 2):
            lanes = slice(pair * LANES, (pair + 1) * LANES)
            x_pair = x_dt[rows, lanes]
            gy_pair = gy_low[rows, lanes]
            total = None
            for side in range(2):
                head = 2 * pair + side
                row = cumt_ref[pl.ds(first_head + head, 1), :]
                first, below = decay_tiles(cum_wide[head], row, block, lower)
                mixing = join_tiles(
                    (cb[:HALF, :HALF] * first).astype(BF), (cb[HALF:, :] * below).astype(BF)
                )
                keep = left if side == 0 else jnp.logical_not(left)
                gy_head = jnp.where(keep, gy_pair, zero)
                mix_first = dot_nt(gy_head[:HALF], x_pair[:HALF]) * first
                mix_below = dot_nt(gy_head[HALF:], x_pair) * below
                cb_first = mix_first if cb_first is None else cb_first + mix_first
                cb_below = mix_below if cb_below is None else cb_below + mix_below
                now = dot_tn(mixing, gy_head)
                total = now if total is None else total + now
            parts.append(total)
        cb_ref[seq, block, :HALF, :HALF] += cb_first
        cb_ref[seq, block, HALF:, :] += cb_below
        rest[block] = jnp.concatenate(parts, axis=1)
        if block == 1:
            grad_scaled = dot_nn(b_ref[:STRETCH, :], grad_state)
            gc_ref[late_rows, :] += dot_nt(grad_inter, state.astype(BF))
            gb_ref[early_rows, :] += dot_nt(scaled, grad_state)
            last_sum = column_sum(grad_state.astype(F32) * state)
    moved = x_dt.astype(F32) * jnp.concatenate(rest, axis=0)
    moved = jnp.concatenate(
        [moved[:STRETCH] + scaled.astype(F32) * grad_scaled, moved[STRETCH:]], axis=0
    )
    rest[0] = rest[0] + fade * grad_scaled
    grad_pull = jnp.concatenate(rest, axis=0)

    width = x_low.shape[1]
    spread = (
        lax.broadcasted_iota(jnp.int32, (width, LANES), 1)
        == first_head + lax.broadcasted_iota(jnp.int32, (width, LANES), 0) // 64
    ).astype(F32).astype(BF)
    moved = gy * (y_ref[...] - skip * x_low) - moved
    edge = lax.broadcasted_iota(jnp.int32, (8, 1), 0) == 7
    moved = jnp.concatenate(
        [
            moved[: STRETCH - 8],
            moved[STRETCH - 8 : STRETCH] + jnp.where(edge, last_sum, 0.0),
            moved[STRETCH:],
        ],
        axis=0,
    )
    one_ref[whole_rows, :] += head_sums(moved, spread)
    two_ref[whole_rows, :] += dot_nn((x_low * grad_pull).astype(BF), spread)
    third = lax.broadcasted_iota(jnp.int32, (8, 1), 0) == 2
    skip_line = jnp.where(third, column_sum(gy * x_low), 0.0)
    heads_ref[...] += head_sums(skip_line, spread)

    grad_pre = (skip * gy + dt_x * grad_pull) * slope
    grad_in, lines = conv_back(grad_pre, x_ref[...], taps_ref)
    gx_ref[...] = grad_in.astype(BF)

    @pl.when(seq == 0)
    def _():
        lines_ref[...] = lines

    @pl.when(seq > 0)
    def _():
        lines_ref[...] += lines


def scan_backward(px, at, taps, y_rows, y_at, grad_y, prep, slot, start, count, before=None):
    b_low, c_low, b_t, c_t, dt, cum, cum_t = prep
    rows = px.shape[0]
    width = GROUP_HEADS * 64
    seqs = rows // slot
    tall = pl.BlockSpec((slot, LANES), lambda h, q: (q, 0))
    wide = pl.BlockSpec((LANES, slot), lambda h, q: (0, q))
    tile = pl.BlockSpec((slot, width), lambda h, q: (q, h + at))
    flat = jax.ShapeDtypeStruct((rows, LANES), F32)
    whole = pl.BlockSpec((rows, LANES), lambda h, q: (0, 0))
    totals = [whole] * 4 + [
        pl.BlockSpec((seqs, 2, STRETCH, STRETCH), lambda h, q: (0, 0, 0, 0)),
        pl.BlockSpec((8, LANES), lambda h, q: (0, 0)),
    ]
    extra, extra_specs, aliases = [jnp.zeros((8, LANES), BF)], [pl.BlockSpec(memory_space=pl.ANY)], {}
    if before is not None:
        if before[0].shape == px.shape:
            extra = [before[0]]
            aliases[11] = 0
        extra = extra + list(before[2:])
        extra_specs = extra_specs + totals
        aliases.update({12 + i: 2 + i for i in range(6)})
    return pl.pallas_call(
        functools.partial(backward_kernel, start),
        grid=(count, seqs),
        in_specs=[
            tile,
            pl.BlockSpec((8, width), lambda h, q: (0, h + start)),
            pl.BlockSpec((slot, width), lambda h, q: (q, h + y_at)),
            pl.BlockSpec((slot, width), lambda h, q: (q, h + start)),
            tall,
            tall,
            wide,
            wide,
            tall,
            tall,
            wide,
        ]
        + extra_specs,
        out_specs=[tile, pl.BlockSpec((8, width), lambda h, q: (0, h))] + totals,
        out_shape=[
            jax.ShapeDtypeStruct(px.shape, BF),
            jax.ShapeDtypeStruct((8, count * width), F32),
            flat,
            flat,
            flat,
            flat,
            jax.ShapeDtypeStruct((seqs, 2, STRETCH, STRETCH), F32),
            jax.ShapeDtypeStruct((8, LANES), F32),
        ],
        input_output_aliases=aliases,
        compiler_params=params(),
        cost_estimate=cost(3.3e-6 * count),
        name="scan_backward",
    )(px, taps, y_rows, grad_y, b_low, c_low, b_t, c_t, dt, cum, cum_t, *extra)


def finish_kernel(
    head_count,
    raw_ref,
    taps_ref,
    heads_ref,
    b_ref,
    c_ref,
    dt_ref,
    gb_ref,
    gc_ref,
    one_ref,
    two_ref,
    cb_ref,
    head_before_ref,
    before_ref,
    out_ref,
    lines_ref,
    head_total_ref,
):
    @pl.when(pl.program_id(0) == 0)
    def _():
        lines_ref[...] = jnp.zeros_like(lines_ref)
        head_total_ref[...] = head_before_ref[...]

    pre = conv_sum(raw_ref[:, : 2 * LANES], taps_ref)
    sig = sigmoid(pre)
    slope = sig + pre * sig * (1.0 - sig)
    grad_b, grad_c = [], []
    for block in range(2):
        rows = slice(block * STRETCH, (block + 1) * STRETCH)
        cb = cb_ref[0, block].astype(BF)
        grad_c.append(gc_ref[rows, :] + dot_nn(cb, b_ref[rows, :]))
        grad_b.append(gb_ref[rows, :] + dot_tn(cb, c_ref[rows, :]))
    grad_active = jnp.concatenate(
        [jnp.concatenate(grad_b, axis=0), jnp.concatenate(grad_c, axis=0)], axis=1
    )
    grad_pre = grad_active * slope
    grad_in, lines = conv_back(grad_pre, raw_ref[:, : 2 * LANES], taps_ref)
    lines_ref[...] += lines

    dt = dt_ref[...]
    two = two_ref[...]
    rate = heads_ref[1:2, :]
    place = row_index(dt)
    grad_cum = one_ref[...]
    inside = place % STRETCH
    step = 1
    while step < STRETCH:
        moved = pltpu.roll(grad_cum, grad_cum.shape[0] - step, 0)
        grad_cum = grad_cum + jnp.where(inside < STRETCH - step, moved, 0.0)
        step *= 2
    grad_dt = grad_cum * rate + two
    lane = lax.broadcasted_iota(jnp.int32, (1, LANES), 1)
    raw = jnp.where(lane < head_count, raw_ref[:, 2 * LANES : 3 * LANES], 0.0)
    grad_raw = grad_dt * sigmoid(raw + heads_ref[0:1, :])
    head_total_ref[...] += jnp.concatenate(
        [column_sum(grad_raw), column_sum(grad_cum * dt) * rate, jnp.zeros((6, LANES), F32)], axis=0
    )
    out_ref[:, : 2 * LANES] = grad_in.astype(BF)
    out_ref[:, 2 * LANES : 3 * LANES] = grad_raw.astype(BF)
    out_ref[:, 3 * LANES :] = jnp.zeros_like(out_ref[:, 3 * LANES :])


def finish(raw, at, taps, heads, head_count, prep, totals, grads, narrow, grads_at, slot):
    b_low, c_low, _, _, dt, _, _ = prep
    rows = raw.shape[0]
    seqs = rows // slot
    tall = pl.BlockSpec((slot, LANES), lambda q: (q, 0))
    return pl.pallas_call(
        functools.partial(finish_kernel, head_count),
        grid=(seqs,),
        in_specs=[
            pl.BlockSpec((slot, 3 * LANES), lambda q: (q, at)),
            pl.BlockSpec((8, 2 * LANES), lambda q: (0, 0)),
            pl.BlockSpec((8, LANES), lambda q: (0, 0)),
            tall,
            tall,
            tall,
            tall,
            tall,
            tall,
            tall,
            pl.BlockSpec((1, 2, STRETCH, STRETCH), lambda q: (q, 0, 0, 0)),
            pl.BlockSpec((8, LANES), lambda q: (0, 0)),
            pl.BlockSpec(memory_space=pl.ANY),
        ],
        out_specs=[
            pl.BlockSpec((slot, narrow), lambda q: (q, grads_at)),
            pl.BlockSpec((8, 2 * LANES), lambda q: (0, 0)),
            pl.BlockSpec((8, LANES), lambda q: (0, 0)),
        ],
        out_shape=[
            jax.ShapeDtypeStruct(grads.shape, BF),
            jax.ShapeDtypeStruct((8, 2 * LANES), F32),
            jax.ShapeDtypeStruct((8, LANES), F32),
        ],
        input_output_aliases={12: 0},
        compiler_params=params(),
        cost_estimate=cost(3e-6),
        name="finish",
    )(raw, taps, heads, b_low, c_low, dt, *totals, grads)


def project_kernel(rows_ref, weight_ref, out_ref):
    out_ref[...] = dot_nn(rows_ref[...], weight_ref[...]).astype(out_ref.dtype)


def project(normed, weight, at, count, size, dtype=F32):
    rows, depth = normed.shape
    return pl.pallas_call(
        project_kernel,
        grid=(count,),
        in_specs=[
            pl.BlockSpec((rows, depth), lambda j: (0, 0)),
            pl.BlockSpec((depth, size), lambda j: (0, j + at)),
        ],
        out_specs=pl.BlockSpec((rows, size), lambda j: (0, j)),
        out_shape=jax.ShapeDtypeStruct((rows, count * size), dtype),
        compiler_params=params(),
        cost_estimate=cost(2.5e-6 * count),
        name="project",
    )(normed, weight)


def pair_kernel(mine_ref, other_ref, grad_ref, keep_ref, give_ref):
    grad = grad_ref[...]
    give_ref[...] = dot_nn(other_ref[...], grad).astype(give_ref.dtype)
    keep_ref[...] = dot_nn(mine_ref[...], grad).astype(keep_ref.dtype)


def weight_grads(mine, other, grad, at, count, size):
    depth, rows = mine.shape
    whole = pl.BlockSpec((depth, rows), lambda j: (0, 0))
    tile = pl.BlockSpec((depth, size), lambda j: (0, j))
    shape = jax.ShapeDtypeStruct((depth, count * size), BF)
    return pl.pallas_call(
        pair_kernel,
        grid=(count,),
        in_specs=[whole, whole, pl.BlockSpec((rows, size), lambda j: (0, j + at))],
        out_specs=[tile, tile],
        out_shape=[shape, shape],
        compiler_params=params(),
        cost_estimate=cost(2.5e-6 * count),
        name="weight_grads",
    )(mine, other, grad)


def input_grads_kernel(sizes, ends, has_before, final, *refs):
    pairs = [refs[2 * i : 2 * i + 2] for i in range(len(sizes))]
    refs = refs[2 * len(sizes) :]
    steps = sum(sizes)
    step = pl.program_id(0)
    if has_before:
        before_ref, refs = refs[0], refs[1:]
    if final:
        hidden_ref, inv_ref, gain_ref, mask_ref, cot_ref, out_ref, total = refs
    else:
        (total,) = refs

    def add(grad_ref, weight):
        now = dot_nt(grad_ref[...], weight)

        @pl.when(step == 0)
        def _():
            total[...] = now + before_ref[...] if has_before else now

        @pl.when(step > 0)
        def _():
            total[...] += now

    begin = 0
    for (grad_ref, weight_ref), size, end in zip(pairs, sizes, ends):
        full = size if end is None else size - 1

        @pl.when((step >= begin) & (step < begin + full))
        def _(grad_ref=grad_ref, weight_ref=weight_ref):
            add(grad_ref, weight_ref[...])

        if end is not None:

            @pl.when(step == begin + full)
            def _(grad_ref=grad_ref, weight_ref=weight_ref, end=end):
                weight = weight_ref[...]
                lane = lax.broadcasted_iota(jnp.int32, weight.shape, 1)
                add(grad_ref, jnp.where(lane < end, weight, jnp.zeros_like(weight)))

        begin += size
    if final:

        @pl.when(step >= steps)
        def _():
            tile = hidden_ref.shape[0]
            grad = total[pl.ds(pl.multiple_of((step - steps) * tile, tile), tile), :]
            inv = inv_ref[...]
            normal = hidden_ref[...] * inv
            grad = grad * gain_ref[...]
            inside = jnp.sum(grad * normal, axis=1, keepdims=True) * (1.0 / grad.shape[1])
            out_ref[...] = inv * (grad - normal * inside) + mask_ref[...] * cot_ref[...]


def input_grads(grads, places, weight, before=None, final=None):
    rows = grads[0].shape[0]
    width = weight.shape[0]
    size, tile = 512, 128
    sizes = [g.shape[1] // size for g in grads]
    steps = sum(sizes)
    in_specs, args, begin = [], [], 0
    for grad, (at, _), count in zip(grads, places, sizes):

        def place(k, begin=begin, count=count, at=0):
            return (0, at + jnp.clip(k - begin, 0, count - 1))

        in_specs += [
            pl.BlockSpec((rows, size), place),
            pl.BlockSpec((width, size), functools.partial(place, at=at)),
        ]
        args += [grad, weight]
        begin += count
    if before is not None:
        in_specs.append(pl.BlockSpec((rows, width), lambda k: (0, 0), pipeline_mode=pl.Buffered(1)))
        args.append(before)
    if final:

        def row(k):
            return (jnp.clip(k - steps, 0, rows // tile - 1), 0)

        line = pl.BlockSpec((1, width), lambda k: (0, 0))
        column = pl.BlockSpec((tile, 1), row)
        wide = pl.BlockSpec((tile, width), row)
        in_specs += [wide, column, line, column, wide]
        args += list(final)
        out_specs = wide
        out_shape = jax.ShapeDtypeStruct((rows, width), F32)
        scratch = [pltpu.VMEM((rows, width), F32)]
    else:
        out_specs = pl.BlockSpec((rows, width), lambda k: (0, 0))
        out_shape = jax.ShapeDtypeStruct((rows, width), F32)
        scratch = []
    ends = [end for _, end in places]
    return pl.pallas_call(
        functools.partial(input_grads_kernel, sizes, ends, before is not None, bool(final)),
        grid=(steps + (rows // tile if final else 0),),
        in_specs=in_specs,
        out_specs=out_specs,
        out_shape=out_shape,
        scratch_shapes=scratch,
        compiler_params=params(),
        cost_estimate=cost(2.5e-6 * steps),
        name="input_grads",
    )(*args)


def swap(values, bit, shards):
    return lax.ppermute(values, "shard", [(i, i ^ (1 << bit)) for i in range(shards)])


def border(moving, *values):
    ready = lax.optimization_barrier(tuple(one.got for one in moving) + values)
    for one, got in zip(moving, ready):
        one.got = got
        one.finish()
    rest = ready[len(moving) :]
    return rest[0] if len(rest) == 1 else rest


class Gather:
    def __init__(self, own, order, shards, place):
        self.now, self.order, self.shards, self.place = own, list(order), shards, place
        self.live, self.columns = [], own.shape[-1]

    def start(self):
        self.bit = self.order.pop(0)
        self.got = swap(self.now, self.bit, self.shards)

    def finish(self):
        mine = (self.place >> self.bit) & 1
        axis = len([b for b in self.live if b > self.bit])
        first = jnp.where(mine == 0, self.now, self.got)
        second = jnp.where(mine == 0, self.got, self.now)
        self.now = jnp.stack([first, second], axis=axis)
        self.live.append(self.bit)

    def whole(self):
        while self.order:
            self.start()
            self.finish()
        return self.now


class Group:
    def __init__(self, now, groups):
        self.now, self.groups = now, groups

    def start(self):
        self.pairs = [(i, (i + 1) % self.groups) for i in range(self.groups)]
        self.got = lax.ppermute(self.now, "group", self.pairs)

    def finish(self):
        total, got = self.now.astype(F32), self.got
        for step in range(1, self.groups):
            if step > 1:
                got = lax.ppermute(got, "group", self.pairs)
            total = total + got.astype(F32)
        self.now = total


class Sum:
    def __init__(self, pair, order, shards, groups, place, part, group_first=False):
        self.keep, self.give = pair
        self.shards, self.groups, self.place, self.part = shards, groups, place, part
        self.columns, self.dtype = self.keep.shape[-1], self.keep.dtype
        self.group_first = group_first and groups == 2
        self.todo = [0] + (["group"] if self.group_first else []) + list(order) + ["end"]
        self.live = list(range(shards.bit_length() - 2, 0, -1))
        self.now = None

    def start(self):
        self.bit = bit = self.todo.pop(0)
        if bit == "end":
            pairs = [(i, (i + 1) % self.groups) for i in range(self.groups)]
            self.got = lax.ppermute(self.now, "group", pairs)
        elif bit == "group":
            half = self.columns // 2
            mine = lax.axis_index("group")
            axis = self.now.ndim - 1
            self.keep = lax.dynamic_slice_in_dim(self.now, mine * half, half, axis)
            give = lax.dynamic_slice_in_dim(self.now, (1 - mine) * half, half, axis)
            self.got = lax.ppermute(give, "group", [(0, 1), (1, 0)])
        elif bit == 0:
            self.got = swap(self.give, 0, self.shards)
        else:
            axis = self.live.index(bit)
            mine = (self.place >> bit) & 1
            self.keep = lax.dynamic_index_in_dim(self.now, mine, axis, keepdims=False)
            give = lax.dynamic_index_in_dim(self.now, 1 - mine, axis, keepdims=False)
            self.live.remove(bit)
            self.got = swap(give, bit, self.shards)

    def finish(self):
        if self.bit == "end" and self.group_first:
            first = lax.axis_index("group") == 0
            halves = [jnp.where(first, self.now, self.got), jnp.where(first, self.got, self.now)]
            self.now = jnp.concatenate(halves, axis=-1)
        elif self.bit == "end":
            total, got = self.now.astype(F32), self.got
            for step in range(1, self.groups):
                if step > 1:
                    pairs = [(i, (i + 1) % self.groups) for i in range(self.groups)]
                    got = lax.ppermute(got, "group", pairs)
                total = total + got.astype(F32)
            self.now = total
        else:
            now = self.keep.astype(F32) + self.got.astype(F32)
            if self.todo != ["end"] or not self.group_first:
                now = now.astype(self.dtype)
            if self.bit == 0:
                now = now.reshape((2,) * len(self.live) + (self.part, self.columns))
            self.now = now

    def result(self):
        while self.todo:
            self.start()
            self.finish()
        return self.now


def local(
    shards,
    groups,
    hidden_in,
    lengths,
    pre_gain,
    in_proj,
    conv_weight,
    conv_bias,
    head_params,
    gate_gain,
    out_proj,
    cotangent,
):
    micro, own, slot, width = hidden_in.shape
    rows = micro * own * slot
    inner = out_proj.shape[0] * shards
    channels = conv_bias.shape[0] * shards
    heads = head_params.shape[1]
    tail = channels - inner + heads
    part = in_proj.shape[0]
    out_part = out_proj.shape[0]
    own_conv = conv_bias.shape[0]
    taps = conv_weight.shape[0]
    hidden = hidden_in.reshape(rows, width)
    cot = cotangent.reshape(rows, width)
    place = lax.axis_index("shard")
    core = place & 1
    chip_bits = list(range(1, shards.bit_length() - 1))
    up = chip_bits
    down = chip_bits[::-1]

    w_in = lax.all_gather(in_proj, "shard", axis=0, tiled=True)
    w_out = lax.all_gather(out_proj, "shard", axis=0, tiled=True)
    small = jnp.concatenate([pre_gain, gate_gain, conv_bias, conv_weight.reshape(-1)], axis=0)
    small = small.astype(F32)
    small = jnp.pad(small, (0, -small.shape[0] % LANES))[None, :]
    packed = Gather(small, down + [0], shards, place).whole().reshape(shards, -1)
    sizes = (part, out_part, own_conv, taps * own_conv)
    ends = [sum(sizes[: i + 1]) for i in range(4)]
    pre_all = packed[:, : ends[0]].reshape(1, width)
    gate_all = packed[:, ends[0] : ends[1]].reshape(1, inner)
    bias_all = packed[:, ends[1] : ends[2]].reshape(1, channels)
    taps_all = packed[:, ends[2] : ends[3]].reshape(shards, taps, -1)
    taps_all = jnp.swapaxes(taps_all, 0, 1).reshape(taps, channels)
    skip_row = jnp.pad(jnp.repeat(head_params[2], inner // heads), (0, channels - inner))
    table = jnp.concatenate(
        [taps_all, bias_all, skip_row[None, :], jnp.zeros((2, channels), F32)], axis=0
    )
    table_x, table_bc = table[:, :inner], table[:, inner:]
    rate = -jnp.exp(head_params[1])
    head_rows = jnp.pad(
        jnp.stack([head_params[0], rate], axis=0), ((0, 6), (0, LANES - heads))
    )

    inv_first = lax.rsqrt(jnp.mean(hidden * hidden, axis=-1, keepdims=True) + EPS)
    normed = (hidden * inv_first * pre_all).astype(BF)
    turned = normed.T.reshape(shards // 2, 2, part, rows)
    mine = lax.dynamic_index_in_dim(turned, core, 1, keepdims=False).reshape(-1, rows)
    other = lax.dynamic_index_in_dim(turned, 1 - core, 1, keepdims=False).reshape(-1, rows)
    positions = jnp.arange(slot, dtype=jnp.int32)
    mask = (positions[None, :] < lengths.reshape(-1)[:, None]).astype(F32).reshape(rows, 1)
    grad_low = (mask * cot).astype(BF)

    size = 4 * LANES
    blocks = inner // size
    raw_at = inner // (3 * LANES)
    prep_at = (raw_at, table_bc, head_rows, heads)
    px = project(normed, w_in, blocks, blocks + 1, size)
    prep = prepare(px, *prep_at, slot)
    unit = GROUP_HEADS * 64
    y_rows = scan_forward(px, 0, table_x, prep, slot, 0, inner // unit)
    pz = project(normed, w_in, 0, blocks, size, BF)
    gate_low, inv = gate_forward([y_rows], pz, gate_all)

    g_out = dot_tn(gate_low, grad_low).astype(BF)
    g_out, grad_low, mine, other = border([], g_out, grad_low, mine, other)
    sum_out = lax.psum_scatter(g_out, "shard", scatter_dimension=0, tiled=True)
    grad_gate = dot_nt(grad_low, w_out).astype(BF)
    grad_y, grad_z = gate_backward([y_rows], pz, grad_gate, inv, gate_all)
    reduce = functools.partial(Sum, shards=shards, groups=groups, place=place, order=up)
    third = inner // unit // 3
    outs = None
    for start in (0, third):
        outs_now = scan_backward(
            px, start, table_x, y_rows, start, grad_y, prep, slot, start, third, before=outs
        )
        outs_first, outs = outs, outs_now
    lines_x = [outs_first[1], outs[1]]
    b_blocks = 2 * third * unit // size
    pair_b = weight_grads(mine, other, outs[0], 0, b_blocks, size)
    *pair_b, grad_z = border([], *pair_b, grad_z)
    s_b = reduce(pair_b, part=part, group_first=True)
    s_b.start()
    g_z = dot_nn(turned.reshape(width, rows), grad_z).astype(BF)
    g_z, grad_y, sum_out = border([s_b], g_z, grad_y, sum_out)
    sum_z = lax.psum_scatter(g_z, "shard", scatter_dimension=0, tiled=True)
    s_b.start()
    rest = inner // unit - 2 * third
    outs = scan_backward(
        px, 2 * third, table_x, y_rows, 2 * third, grad_y, prep, slot, 2 * third, rest, before=outs
    )
    mine, *outs = border([s_b], mine, *outs)
    s_out = Group(sum_out, groups)
    lines_x.append(outs[1])
    grad_x, lines_bc, head_total = finish(
        px, *prep_at, prep, outs[2:], outs[0], size, blocks, slot
    )
    pair_a = weight_grads(mine, other, grad_x, b_blocks, blocks + 1 - b_blocks, size)

    free = size - tail
    lines = jnp.concatenate(lines_x + [lines_bc], axis=1)[:5].reshape(5, shards, own_conv)
    lines = jnp.pad(lines, ((0, 0), (0, 0), (0, free - own_conv)))
    head_line = head_total[:3, :heads].reshape(1, 1, 3 * heads)
    head_line = jnp.pad(head_line, ((0, 0), (0, 0), (0, free - 3 * heads)))
    small = jnp.concatenate([lines, jnp.broadcast_to(head_line, (1, shards, free))], axis=0)
    small = jnp.swapaxes(small.astype(BF), 0, 1).reshape(shards // 2, 2, 6, free)

    def with_small(grads, index):
        picked = lax.dynamic_index_in_dim(small, index, 1, keepdims=False)
        grads = grads.reshape(shards // 2, part, -1)
        at = grads.shape[2] - free
        return lax.dynamic_update_slice(grads, picked, (0, 0, at)).reshape(shards // 2 * part, -1)

    pair_a = [with_small(pair_a[0], core), with_small(pair_a[1], 1 - core)]
    *pair_a, grad_z, grad_x = border([], *pair_a, grad_z, grad_x)
    s_a = reduce(pair_a, part=part)
    s_a.start()
    s_b.start()
    part_sum = input_grads([grad_z], [(0, None)], w_in)
    part_sum, grad_x = border([s_b, s_a], part_sum, grad_x)
    s_a.start()
    s_b.start()
    s_out.start()
    grad_input = input_grads(
        [grad_x],
        [(blocks, tail % size)],
        w_in,
        before=part_sum,
        final=(hidden, inv_first, pre_all, mask, cot),
    )
    gate_low, grad_input, sum_z = border([s_a, s_b, s_out], gate_low, grad_input, sum_z)
    s_a.start()
    s_b.start()
    s_z = Group(sum_z, groups)
    s_z.start()
    layer_out = mask * (hidden + dot_nn(gate_low, w_out))
    layer_out = border([s_a, s_b, s_z], layer_out)
    s_a.start()
    s_b.start()
    for one in (s_a, s_b):
        one.finish()
    sum_a = s_a.result()
    b_columns = b_blocks * size
    g_in = jnp.concatenate(
        [s_z.now, s_b.result(), sum_a[:, : inner - b_columns + tail]], axis=1
    )
    g_out = s_out.now

    def gain_grads(weight, grads, gain):
        return jnp.sum(weight.astype(F32) * grads, axis=1) / gain.astype(F32)

    g_pre = gain_grads(in_proj, g_in, pre_gain)
    g_gate = gain_grads(out_proj, g_out, gate_gain)
    small = sum_a[:6, inner - b_columns + tail :]
    g_lines = small[:5, :own_conv]
    g_heads = small[5, : 3 * heads].reshape(3, heads)
    return (
        layer_out.reshape(hidden_in.shape),
        grad_input.reshape(hidden_in.shape),
        g_pre,
        g_in,
        g_lines[:4],
        g_lines[4],
        g_heads,
        g_gate,
        g_out,
    )


def solution(mesh):
    rows = P(None, ("group", "shard"), None, None)
    in_specs = (
        rows,
        P(None, ("group", "shard")),
        P("shard"),
        P("shard", None),
        P(None, "shard"),
        P("shard"),
        P(),
        P("shard"),
        P("shard", None),
        rows,
    )
    out_specs = (
        rows,
        rows,
        P("shard"),
        P("shard", None),
        P(None, "shard"),
        P("shard"),
        P(),
        P("shard"),
        P("shard", None),
    )
    body = functools.partial(local, mesh.shape["shard"], mesh.shape["group"])
    return jax.shard_map(body, mesh=mesh, in_specs=in_specs, out_specs=out_specs, check_vma=False)
```

```python
import functools

import jax
import jax.numpy as jnp
from jax import lax
from jax.experimental import pallas as pl
from jax.experimental.pallas import tpu as pltpu
from jax.sharding import PartitionSpec as P

STRETCH = 256
HALF = 128
LANES = 128
GROUP_HEADS = 8
EPS = 1e-05
BF = jnp.bfloat16
F32 = jnp.float32
VMEM_BYTES = 56 * 1024 * 1024


def params(**kwargs):
    return pltpu.CompilerParams(vmem_limit_bytes=VMEM_BYTES, **kwargs)


def cost(seconds):
    return pl.CostEstimate(
        flops=int(seconds * 2.0e13), bytes_accessed=int(seconds * 6.0e10), transcendentals=0
    )


def dot_nn(left, right):
    return lax.dot_general(left, right, (((1,), (0,)), ((), ())), preferred_element_type=F32)


def dot_nt(left, right):
    return lax.dot_general(left, right, (((1,), (1,)), ((), ())), preferred_element_type=F32)


def dot_tn(left, right):
    return lax.dot_general(left, right, (((0,), (0,)), ((), ())), preferred_element_type=F32)


def sigmoid(values):
    return 1.0 / (1.0 + jnp.exp(-values))


def row_index(values):
    return lax.broadcasted_iota(jnp.int32, (values.shape[0], 1), 0)


def shift_down(values, count):
    rolled = pltpu.roll(values, count, 0)
    place = lax.broadcasted_iota(jnp.int32, (8, 1), 0)
    return jnp.concatenate([jnp.where(place >= count, rolled[:8], 0.0), rolled[8:]], axis=0)


def shift_up(values, count):
    rows = values.shape[0]
    rolled = pltpu.roll(values, rows - count, 0)
    place = lax.broadcasted_iota(jnp.int32, (8, 1), 0)
    last = jnp.where(place < 8 - count, rolled[rows - 8 :], 0.0)
    return jnp.concatenate([rolled[: rows - 8], last], axis=0)


def conv_sum(values, taps_ref):
    pre = taps_ref[4:5, :]
    for k in range(3):
        pre = pre + taps_ref[k : k + 1, :] * shift_down(values, 3 - k)
    return pre + taps_ref[3:4, :] * values


def conv_back(grad_pre, values, taps_ref):
    total = taps_ref[3:4, :] * grad_pre
    lines = []
    for k in range(3):
        moved = shift_up(grad_pre, 3 - k)
        total = total + taps_ref[k : k + 1, :] * moved
        lines.append(column_sum(moved * values))
    lines += [column_sum(grad_pre * values), column_sum(grad_pre)]
    lines.append(jnp.zeros((3, values.shape[1]), F32))
    return total, jnp.concatenate(lines, axis=0)


def column_sum(values):
    return jnp.sum(values, axis=0, keepdims=True)


def prepare_kernel(head_count, raw_ref, taps_ref, heads_ref, b_ref, c_ref, bt_ref, ct_ref, dt_ref, cum_ref, cumt_ref):
    pre = conv_sum(raw_ref[:, : 2 * LANES], taps_ref)
    active = pre * sigmoid(pre)
    b_part, c_part = active[:, :LANES], active[:, LANES:]
    b_ref[...] = b_part.astype(BF)
    c_ref[...] = c_part.astype(BF)
    bt_ref[...] = b_part.T.astype(BF)
    ct_ref[...] = c_part.T.astype(BF)
    lane = lax.broadcasted_iota(jnp.int32, (1, LANES), 1)
    raw = jnp.where(lane < head_count, raw_ref[:, 2 * LANES :], 0.0) + heads_ref[0:1, :]
    dt = jnp.maximum(raw, 0.0) + jnp.log1p(jnp.exp(-jnp.abs(raw)))
    cum = dt * heads_ref[1:2, :]
    place = row_index(cum) % STRETCH
    step = 1
    while step < STRETCH:
        cum = cum + jnp.where(place >= step, pltpu.roll(cum, step, 0), 0.0)
        step *= 2
    dt_ref[...] = dt
    cum_ref[...] = cum
    cumt_ref[...] = cum.T


def prepare(raw, at, taps, heads, head_count, slot):
    rows = raw.shape[0]
    tall = pl.BlockSpec((slot, LANES), lambda q: (q, 0))
    wide = pl.BlockSpec((LANES, slot), lambda q: (0, q))
    return pl.pallas_call(
        functools.partial(prepare_kernel, head_count),
        grid=(rows // slot,),
        in_specs=[
            pl.BlockSpec((slot, 3 * LANES), lambda q: (q, at)),
            pl.BlockSpec((8, 2 * LANES), lambda q: (0, 0)),
            pl.BlockSpec((8, LANES), lambda q: (0, 0)),
        ],
        out_specs=[tall, tall, wide, wide, tall, tall, wide],
        out_shape=[
            jax.ShapeDtypeStruct((rows, LANES), BF),
            jax.ShapeDtypeStruct((rows, LANES), BF),
            jax.ShapeDtypeStruct((LANES, rows), BF),
            jax.ShapeDtypeStruct((LANES, rows), BF),
            jax.ShapeDtypeStruct((rows, LANES), F32),
            jax.ShapeDtypeStruct((rows, LANES), F32),
            jax.ShapeDtypeStruct((LANES, rows), F32),
        ],
        compiler_params=params(),
        name="prepare",
    )(raw, taps, heads)


def head_tables(cum_ref, dt_ref, first_head):
    shift = lax.rem(LANES - first_head, LANES)
    cum = pltpu.roll(cum_ref[...], shift, 1)
    dt = pltpu.roll(dt_ref[...], shift, 1)
    rows = cum.shape[0]
    cum_wide = [jnp.broadcast_to(cum[:, i : i + 1], (rows, LANES)) for i in range(GROUP_HEADS)]
    dt_wide = [jnp.broadcast_to(dt[:, i : i + 1], (rows, LANES)) for i in range(GROUP_HEADS)]
    left = lax.broadcasted_iota(jnp.int32, (1, LANES), 1) < LANES // 2

    def spread(wide):
        return jnp.concatenate(
            [jnp.where(left, wide[i], wide[i + 1]) for i in range(0, GROUP_HEADS, 2)], axis=1
        )

    return cum_wide, spread(cum_wide), spread(dt_wide), left


def decay_tiles(cum_wide, cumt_row, block, lower):
    begin = block * STRETCH
    top = cum_wide[begin : begin + HALF]
    low = cum_wide[begin + HALF : begin + STRETCH]
    row_left = cumt_row[:, begin : begin + HALF]
    row_right = cumt_row[:, begin + HALF : begin + STRETCH]
    first = jnp.where(lower, jnp.exp(top - row_left), 0.0)
    second = jnp.exp(low - row_left)
    third = jnp.where(lower, jnp.exp(low - row_right), 0.0)
    return first, jnp.concatenate([second, third], axis=1)


def join_tiles(first, below):
    return jnp.concatenate(
        [jnp.concatenate([first, jnp.zeros_like(first)], axis=1), below], axis=0
    )


def lower_mask():
    return lax.broadcasted_iota(jnp.int32, (HALF, HALF), 0) >= lax.broadcasted_iota(
        jnp.int32, (HALF, HALF), 1
    )


def forward_kernel(
    group_start, x_ref, taps_ref, b_ref, c_ref, bt_ref, dt_ref, cum_ref, cumt_ref, y_ref
):
    first_head = (pl.program_id(1) + group_start) * GROUP_HEADS
    pre = conv_sum(x_ref[...], taps_ref)
    x_low = (pre * sigmoid(pre)).astype(BF).astype(F32)
    cum_wide, cum_x, dt_x, left = head_tables(cum_ref, dt_ref, first_head)
    x_dt = (x_low * dt_x).astype(BF)
    skipped = taps_ref[5:6, :] * x_low
    fade = jnp.exp(cum_x[STRETCH - 1 : STRETCH] - cum_x[:STRETCH])
    scaled = (x_low[:STRETCH] * (fade * dt_x[:STRETCH])).astype(BF)
    state = dot_nn(bt_ref[:, :STRETCH], scaled).astype(BF)
    lower = lower_mask()
    zero = jnp.zeros((STRETCH, LANES), BF)
    for block in range(2):
        rows = slice(block * STRETCH, (block + 1) * STRETCH)
        cb = dot_nt(c_ref[rows, :], b_ref[rows, :])
        if block == 1:
            inter = dot_nn(c_ref[rows, :], state)
        for pair in range(GROUP_HEADS // 2):
            lanes = slice(pair * LANES, (pair + 1) * LANES)
            x_pair = x_dt[rows, lanes]
            total = None
            for side in range(2):
                head = 2 * pair + side
                row = cumt_ref[pl.ds(first_head + head, 1), :]
                first, below = decay_tiles(cum_wide[head], row, block, lower)
                mixing = join_tiles(
                    (cb[:HALF, :HALF] * first).astype(BF), (cb[HALF:, :] * below).astype(BF)
                )
                keep = left if side == 0 else jnp.logical_not(left)
                now = dot_nn(mixing, jnp.where(keep, x_pair, zero))
                total = now if total is None else total + now
            if block == 1:
                total = total + jnp.exp(cum_x[rows, lanes]) * inter[:, lanes]
            y_ref[rows, lanes] = total + skipped[rows, lanes]


def scan_forward(px, offset, taps, prep, slot, start, count):
    b_low, c_low, b_t, _, dt, cum, cum_t = prep
    rows = px.shape[0]
    width = GROUP_HEADS * 64
    tall = pl.BlockSpec((slot, LANES), lambda q, h: (q, 0))
    wide = pl.BlockSpec((LANES, slot), lambda q, h: (0, q))
    tile = pl.BlockSpec((slot, width), lambda q, h: (q, h))
    return pl.pallas_call(
        functools.partial(forward_kernel, start),
        grid=(rows // slot, count),
        in_specs=[
            pl.BlockSpec((slot, width), lambda q, h: (q, h + offset)),
            pl.BlockSpec((8, width), lambda q, h: (0, h + start)),
            tall,
            tall,
            wide,
            tall,
            tall,
            wide,
        ],
        out_specs=tile,
        out_shape=jax.ShapeDtypeStruct((rows, count * width), F32),
        compiler_params=params(),
        cost_estimate=cost(3.3e-6 * count),
        name="scan_forward",
    )(px, taps, b_low, c_low, b_t, dt, cum, cum_t)


def gate_kernel(count, *refs):
    y_refs = refs[:count]
    z_ref, gain_ref, gate_ref, inv_ref = refs[count:]
    y = jnp.concatenate([ref[...] for ref in y_refs], axis=1)
    z = z_ref[...].astype(F32)
    gated = y * (z * sigmoid(z))
    mean = jnp.sum(gated * gated, axis=1, keepdims=True) * (1.0 / gated.shape[1])
    inv = lax.rsqrt(mean + EPS)
    gate_ref[...] = (gated * inv * gain_ref[...]).astype(BF)
    inv_ref[...] = jnp.broadcast_to(inv, inv_ref.shape)


def row_tile(size, array):
    return pl.BlockSpec((size, array.shape[1]), lambda t: (t, 0))


def gate_forward(y_parts, pz, gain):
    rows, inner = pz.shape
    size = 128
    tile = pl.BlockSpec((size, inner), lambda t: (t, 0))
    return pl.pallas_call(
        functools.partial(gate_kernel, len(y_parts)),
        grid=(rows // size,),
        in_specs=[row_tile(size, y) for y in y_parts]
        + [tile, pl.BlockSpec((1, inner), lambda t: (0, 0))],
        out_specs=[tile, pl.BlockSpec((size, LANES), lambda t: (t, 0))],
        out_shape=[
            jax.ShapeDtypeStruct((rows, inner), BF),
            jax.ShapeDtypeStruct((rows, LANES), F32),
        ],
        compiler_params=params(),
        cost_estimate=cost(15e-6),
        name="gate_forward",
    )(*y_parts, pz, gain)


def gate_back_kernel(count, *refs):
    y_refs = refs[:count]
    z_ref, grad_ref, inv_ref, gain_ref, gy_ref, gz_ref = refs[count:]
    y = jnp.concatenate([ref[...] for ref in y_refs], axis=1)
    z = z_ref[...].astype(F32)
    grad = grad_ref[...].astype(F32)
    inv = inv_ref[:, 0:1]
    sig = sigmoid(z)
    silu = z * sig
    normal = y * silu * inv
    grad_normal = grad * gain_ref[...]
    mean = jnp.sum(grad_normal * normal, axis=1, keepdims=True) * (1.0 / y.shape[1])
    gated = inv * (grad_normal - normal * mean)
    gy_ref[...] = (gated * silu).astype(BF)
    gz_ref[...] = (gated * y * (sig + silu * (1.0 - sig))).astype(BF)


def gate_backward(y_parts, pz, grad_gate, inv, gain):
    rows, inner = pz.shape
    size = 128
    tile = pl.BlockSpec((size, inner), lambda t: (t, 0))
    return pl.pallas_call(
        functools.partial(gate_back_kernel, len(y_parts)),
        grid=(rows // size,),
        in_specs=[row_tile(size, y) for y in y_parts]
        + [
            tile,
            tile,
            pl.BlockSpec((size, LANES), lambda t: (t, 0)),
            pl.BlockSpec((1, inner), lambda t: (0, 0)),
        ],
        out_specs=[tile, tile],
        out_shape=[
            jax.ShapeDtypeStruct((rows, inner), BF),
            jax.ShapeDtypeStruct((rows, inner), BF),
        ],
        compiler_params=params(),
        cost_estimate=cost(24e-6),
        name="gate_backward",
    )(*y_parts, pz, grad_gate, inv, gain)


def head_sums(product, spread):
    high = product.astype(BF)
    low = (product - high.astype(F32)).astype(BF)
    return dot_nn(high, spread) + dot_nn(low, spread)


def backward_kernel(group_start, *refs):
    x_ref, taps_ref, y_ref, gy_ref, b_ref, c_ref, bt_ref, ct_ref = refs[:8]
    dt_ref, cum_ref, cumt_ref = refs[8:11]
    gx_ref, lines_ref, *totals = refs[-8:]
    gb_ref, gc_ref, one_ref, two_ref, cb_ref, heads_ref = totals
    befores = refs[12:-8]
    first_head = (pl.program_id(0) + group_start) * GROUP_HEADS
    seq = pl.program_id(1)
    slot = x_ref.shape[0]

    @pl.when((pl.program_id(0) == 0) & (seq == 0))
    def _():
        for i, total in enumerate(totals):
            total[...] = befores[i][...] if befores else jnp.zeros_like(total)

    at = pl.multiple_of(seq * slot, slot)
    whole_rows = pl.ds(at, slot)
    early_rows = pl.ds(at, STRETCH)
    late_rows = pl.ds(pl.multiple_of(at + STRETCH, STRETCH), STRETCH)
    pre = conv_sum(x_ref[...], taps_ref)
    sig = sigmoid(pre)
    active = pre * sig
    slope = sig + active * (1.0 - sig)
    x_low = active.astype(BF).astype(F32)
    gy_low = gy_ref[...]
    gy = gy_low.astype(F32)
    cum_wide, cum_x, dt_x, left = head_tables(cum_ref, dt_ref, first_head)
    x_dt = (x_low * dt_x).astype(BF)
    skip = taps_ref[5:6, :]

    grad_inter = (gy[STRETCH:] * jnp.exp(cum_x[STRETCH:])).astype(BF)
    fade = jnp.exp(cum_x[STRETCH - 1 : STRETCH] - cum_x[:STRETCH])
    scaled = (x_low[:STRETCH] * (fade * dt_x[:STRETCH])).astype(BF)
    state = dot_nn(bt_ref[:, :STRETCH], scaled)
    grad_state = dot_nn(ct_ref[:, STRETCH:], grad_inter).astype(BF)

    lower = lower_mask()
    zero = jnp.zeros((STRETCH, LANES), BF)
    rest = [None, None]
    for block in (1, 0):
        rows = slice(block * STRETCH, (block + 1) * STRETCH)
        cb = dot_nt(c_ref[rows, :], b_ref[rows, :])
        cb_first = cb_below = None
        parts = []
        for pair in range(GROUP_HEADS // 2):
            lanes = slice(pair * LANES, (pair + 1) * LANES)
            x_pair = x_dt[rows, lanes]
            gy_pair = gy_low[rows, lanes]
            total = None
            for side in range(2):
                head = 2 * pair + side
                row = cumt_ref[pl.ds(first_head + head, 1), :]
                first, below = decay_tiles(cum_wide[head], row, block, lower)
                mixing = join_tiles(
                    (cb[:HALF, :HALF] * first).astype(BF), (cb[HALF:, :] * below).astype(BF)
                )
                keep = left if side == 0 else jnp.logical_not(left)
                gy_head = jnp.where(keep, gy_pair, zero)
                mix_first = dot_nt(gy_head[:HALF], x_pair[:HALF]) * first
                mix_below = dot_nt(gy_head[HALF:], x_pair) * below
                cb_first = mix_first if cb_first is None else cb_first + mix_first
                cb_below = mix_below if cb_below is None else cb_below + mix_below
                now = dot_tn(mixing, gy_head)
                total = now if total is None else total + now
            parts.append(total)
        cb_ref[seq, block, :HALF, :HALF] += cb_first
        cb_ref[seq, block, HALF:, :] += cb_below
        rest[block] = jnp.concatenate(parts, axis=1)
        if block == 1:
            grad_scaled = dot_nn(b_ref[:STRETCH, :], grad_state)
            gc_ref[late_rows, :] += dot_nt(grad_inter, state.astype(BF))
            gb_ref[early_rows, :] += dot_nt(scaled, grad_state)
            last_sum = column_sum(grad_state.astype(F32) * state)
    moved = x_dt.astype(F32) * jnp.concatenate(rest, axis=0)
    moved = jnp.concatenate(
        [moved[:STRETCH] + scaled.astype(F32) * grad_scaled, moved[STRETCH:]], axis=0
    )
    rest[0] = rest[0] + fade * grad_scaled
    grad_pull = jnp.concatenate(rest, axis=0)

    width = x_low.shape[1]
    spread = (
        lax.broadcasted_iota(jnp.int32, (width, LANES), 1)
        == first_head + lax.broadcasted_iota(jnp.int32, (width, LANES), 0) // 64
    ).astype(F32).astype(BF)
    moved = gy * (y_ref[...] - skip * x_low) - moved
    edge = lax.broadcasted_iota(jnp.int32, (8, 1), 0) == 7
    moved = jnp.concatenate(
        [
            moved[: STRETCH - 8],
            moved[STRETCH - 8 : STRETCH] + jnp.where(edge, last_sum, 0.0),
            moved[STRETCH:],
        ],
        axis=0,
    )
    one_ref[whole_rows, :] += head_sums(moved, spread)
    two_ref[whole_rows, :] += dot_nn((x_low * grad_pull).astype(BF), spread)
    third = lax.broadcasted_iota(jnp.int32, (8, 1), 0) == 2
    skip_line = jnp.where(third, column_sum(gy * x_low), 0.0)
    heads_ref[...] += head_sums(skip_line, spread)

    grad_pre = (skip * gy + dt_x * grad_pull) * slope
    grad_in, lines = conv_back(grad_pre, x_ref[...], taps_ref)
    gx_ref[...] = grad_in.astype(BF)

    @pl.when(seq == 0)
    def _():
        lines_ref[...] = lines

    @pl.when(seq > 0)
    def _():
        lines_ref[...] += lines


def scan_backward(px, at, taps, y_rows, y_at, grad_y, prep, slot, start, count, before=None):
    b_low, c_low, b_t, c_t, dt, cum, cum_t = prep
    rows = px.shape[0]
    width = GROUP_HEADS * 64
    seqs = rows // slot
    tall = pl.BlockSpec((slot, LANES), lambda h, q: (q, 0))
    wide = pl.BlockSpec((LANES, slot), lambda h, q: (0, q))
    tile = pl.BlockSpec((slot, width), lambda h, q: (q, h + at))
    flat = jax.ShapeDtypeStruct((rows, LANES), F32)
    whole = pl.BlockSpec((rows, LANES), lambda h, q: (0, 0))
    totals = [whole] * 4 + [
        pl.BlockSpec((seqs, 2, STRETCH, STRETCH), lambda h, q: (0, 0, 0, 0)),
        pl.BlockSpec((8, LANES), lambda h, q: (0, 0)),
    ]
    extra, extra_specs, aliases = [jnp.zeros((8, LANES), BF)], [pl.BlockSpec(memory_space=pl.ANY)], {}
    if before is not None:
        if before[0].shape == px.shape:
            extra = [before[0]]
            aliases[11] = 0
        extra = extra + list(before[2:])
        extra_specs = extra_specs + totals
        aliases.update({12 + i: 2 + i for i in range(6)})
    return pl.pallas_call(
        functools.partial(backward_kernel, start),
        grid=(count, seqs),
        in_specs=[
            tile,
            pl.BlockSpec((8, width), lambda h, q: (0, h + start)),
            pl.BlockSpec((slot, width), lambda h, q: (q, h + y_at)),
            pl.BlockSpec((slot, width), lambda h, q: (q, h + start)),
            tall,
            tall,
            wide,
            wide,
            tall,
            tall,
            wide,
        ]
        + extra_specs,
        out_specs=[tile, pl.BlockSpec((8, width), lambda h, q: (0, h))] + totals,
        out_shape=[
            jax.ShapeDtypeStruct(px.shape, BF),
            jax.ShapeDtypeStruct((8, count * width), F32),
            flat,
            flat,
            flat,
            flat,
            jax.ShapeDtypeStruct((seqs, 2, STRETCH, STRETCH), F32),
            jax.ShapeDtypeStruct((8, LANES), F32),
        ],
        input_output_aliases=aliases,
        compiler_params=params(),
        cost_estimate=cost(3.3e-6 * count),
        name="scan_backward",
    )(px, taps, y_rows, grad_y, b_low, c_low, b_t, c_t, dt, cum, cum_t, *extra)


def finish_kernel(
    head_count,
    raw_ref,
    taps_ref,
    heads_ref,
    b_ref,
    c_ref,
    dt_ref,
    gb_ref,
    gc_ref,
    one_ref,
    two_ref,
    cb_ref,
    head_before_ref,
    before_ref,
    out_ref,
    lines_ref,
    head_total_ref,
):
    @pl.when(pl.program_id(0) == 0)
    def _():
        lines_ref[...] = jnp.zeros_like(lines_ref)
        head_total_ref[...] = head_before_ref[...]

    pre = conv_sum(raw_ref[:, : 2 * LANES], taps_ref)
    sig = sigmoid(pre)
    slope = sig + pre * sig * (1.0 - sig)
    grad_b, grad_c = [], []
    for block in range(2):
        rows = slice(block * STRETCH, (block + 1) * STRETCH)
        cb = cb_ref[0, block].astype(BF)
        grad_c.append(gc_ref[rows, :] + dot_nn(cb, b_ref[rows, :]))
        grad_b.append(gb_ref[rows, :] + dot_tn(cb, c_ref[rows, :]))
    grad_active = jnp.concatenate(
        [jnp.concatenate(grad_b, axis=0), jnp.concatenate(grad_c, axis=0)], axis=1
    )
    grad_pre = grad_active * slope
    grad_in, lines = conv_back(grad_pre, raw_ref[:, : 2 * LANES], taps_ref)
    lines_ref[...] += lines

    dt = dt_ref[...]
    two = two_ref[...]
    rate = heads_ref[1:2, :]
    place = row_index(dt)
    grad_cum = one_ref[...]
    inside = place % STRETCH
    step = 1
    while step < STRETCH:
        moved = pltpu.roll(grad_cum, grad_cum.shape[0] - step, 0)
        grad_cum = grad_cum + jnp.where(inside < STRETCH - step, moved, 0.0)
        step *= 2
    grad_dt = grad_cum * rate + two
    lane = lax.broadcasted_iota(jnp.int32, (1, LANES), 1)
    raw = jnp.where(lane < head_count, raw_ref[:, 2 * LANES : 3 * LANES], 0.0)
    grad_raw = grad_dt * sigmoid(raw + heads_ref[0:1, :])
    head_total_ref[...] += jnp.concatenate(
        [column_sum(grad_raw), column_sum(grad_cum * dt) * rate, jnp.zeros((6, LANES), F32)], axis=0
    )
    out_ref[:, : 2 * LANES] = grad_in.astype(BF)
    out_ref[:, 2 * LANES : 3 * LANES] = grad_raw.astype(BF)
    out_ref[:, 3 * LANES :] = jnp.zeros_like(out_ref[:, 3 * LANES :])


def finish(raw, at, taps, heads, head_count, prep, totals, grads, narrow, grads_at, slot):
    b_low, c_low, _, _, dt, _, _ = prep
    rows = raw.shape[0]
    seqs = rows // slot
    tall = pl.BlockSpec((slot, LANES), lambda q: (q, 0))
    return pl.pallas_call(
        functools.partial(finish_kernel, head_count),
        grid=(seqs,),
        in_specs=[
            pl.BlockSpec((slot, 3 * LANES), lambda q: (q, at)),
            pl.BlockSpec((8, 2 * LANES), lambda q: (0, 0)),
            pl.BlockSpec((8, LANES), lambda q: (0, 0)),
            tall,
            tall,
            tall,
            tall,
            tall,
            tall,
            tall,
            pl.BlockSpec((1, 2, STRETCH, STRETCH), lambda q: (q, 0, 0, 0)),
            pl.BlockSpec((8, LANES), lambda q: (0, 0)),
            pl.BlockSpec(memory_space=pl.ANY),
        ],
        out_specs=[
            pl.BlockSpec((slot, narrow), lambda q: (q, grads_at)),
            pl.BlockSpec((8, 2 * LANES), lambda q: (0, 0)),
            pl.BlockSpec((8, LANES), lambda q: (0, 0)),
        ],
        out_shape=[
            jax.ShapeDtypeStruct(grads.shape, BF),
            jax.ShapeDtypeStruct((8, 2 * LANES), F32),
            jax.ShapeDtypeStruct((8, LANES), F32),
        ],
        input_output_aliases={12: 0},
        compiler_params=params(),
        cost_estimate=cost(3e-6),
        name="finish",
    )(raw, taps, heads, b_low, c_low, dt, *totals, grads)


def project_kernel(rows_ref, weight_ref, out_ref):
    out_ref[...] = dot_nn(rows_ref[...], weight_ref[...]).astype(out_ref.dtype)


def project(normed, weight, at, count, size, dtype=F32):
    rows, depth = normed.shape
    return pl.pallas_call(
        project_kernel,
        grid=(count,),
        in_specs=[
            pl.BlockSpec((rows, depth), lambda j: (0, 0)),
            pl.BlockSpec((depth, size), lambda j: (0, j + at)),
        ],
        out_specs=pl.BlockSpec((rows, size), lambda j: (0, j)),
        out_shape=jax.ShapeDtypeStruct((rows, count * size), dtype),
        compiler_params=params(),
        cost_estimate=cost(2.5e-6 * count),
        name="project",
    )(normed, weight)


def pair_kernel(part, mine_ref, other_ref, grad_ref, *refs):
    keep_ref, give_ref = refs[-2:]
    grad = grad_ref[...]
    for rows_ref, out_ref, extra_ref in zip(
        (other_ref, mine_ref), (give_ref, keep_ref), refs[:-2] or (None, None)
    ):
        product = dot_nn(rows_ref[...], grad)
        out_ref[...] = product.astype(out_ref.dtype)
        if extra_ref is not None:

            @pl.when(pl.program_id(0) == pl.num_programs(0) - 1)
            def _(product=product, out_ref=out_ref, extra_ref=extra_ref):
                chips, high, wide = extra_ref.shape
                lanes = slice(product.shape[1] - wide, product.shape[1])
                for chip in range(chips):
                    rows = slice(chip * part, chip * part + high)
                    out_ref[rows, lanes] = (
                        product[rows, lanes] + extra_ref[chip].astype(F32)
                    ).astype(out_ref.dtype)


def weight_grads(mine, other, grad, at, count, size, part, extra=()):
    depth, rows = mine.shape
    whole = pl.BlockSpec((depth, rows), lambda j: (0, 0))
    tile = pl.BlockSpec((depth, size), lambda j: (0, j))
    shape = jax.ShapeDtypeStruct((depth, count * size), BF)
    return pl.pallas_call(
        functools.partial(pair_kernel, part),
        grid=(count,),
        in_specs=[whole, whole, pl.BlockSpec((rows, size), lambda j: (0, j + at))]
        + [pl.BlockSpec(e.shape, lambda j: (0, 0, 0)) for e in extra],
        out_specs=[tile, tile],
        out_shape=[shape, shape],
        compiler_params=params(),
        cost_estimate=cost(2.5e-6 * count),
        name="weight_grads",
    )(mine, other, grad, *extra)


def input_grads_kernel(sizes, ends, has_before, final, *refs):
    pairs = [refs[2 * i : 2 * i + 2] for i in range(len(sizes))]
    refs = refs[2 * len(sizes) :]
    steps = sum(sizes)
    step = pl.program_id(0)
    if has_before:
        before_ref, refs = refs[0], refs[1:]
    if final:
        hidden_ref, inv_ref, gain_ref, mask_ref, cot_ref, out_ref, total = refs
    else:
        (total,) = refs

    def add(grad_ref, weight):
        now = dot_nt(grad_ref[...], weight)

        @pl.when(step == 0)
        def _():
            total[...] = now + before_ref[...] if has_before else now

        @pl.when(step > 0)
        def _():
            total[...] += now

    begin = 0
    for (grad_ref, weight_ref), size, end in zip(pairs, sizes, ends):
        full = size if end is None else size - 1

        @pl.when((step >= begin) & (step < begin + full))
        def _(grad_ref=grad_ref, weight_ref=weight_ref):
            add(grad_ref, weight_ref[...])

        if end is not None:

            @pl.when(step == begin + full)
            def _(grad_ref=grad_ref, weight_ref=weight_ref, end=end):
                weight = weight_ref[...]
                lane = lax.broadcasted_iota(jnp.int32, weight.shape, 1)
                add(grad_ref, jnp.where(lane < end, weight, jnp.zeros_like(weight)))

        begin += size
    if final:

        @pl.when(step >= steps)
        def _():
            tile = hidden_ref.shape[0]
            grad = total[pl.ds(pl.multiple_of((step - steps) * tile, tile), tile), :]
            inv = inv_ref[...]
            normal = hidden_ref[...] * inv
            grad = grad * gain_ref[...]
            inside = jnp.sum(grad * normal, axis=1, keepdims=True) * (1.0 / grad.shape[1])
            out_ref[...] = inv * (grad - normal * inside) + mask_ref[...] * cot_ref[...]


def input_grads(grads, places, weight, before=None, final=None):
    rows = grads[0].shape[0]
    width = weight.shape[0]
    size, tile = 512, 256
    sizes = [g.shape[1] // size for g in grads]
    steps = sum(sizes)
    in_specs, args, begin = [], [], 0
    for grad, (at, _), count in zip(grads, places, sizes):

        def place(k, begin=begin, count=count, at=0):
            return (0, at + jnp.clip(k - begin, 0, count - 1))

        in_specs += [
            pl.BlockSpec((rows, size), place),
            pl.BlockSpec((width, size), functools.partial(place, at=at)),
        ]
        args += [grad, weight]
        begin += count
    if before is not None:
        in_specs.append(pl.BlockSpec((rows, width), lambda k: (0, 0), pipeline_mode=pl.Buffered(1)))
        args.append(before)
    if final:

        def row(k):
            return (jnp.clip(k - steps, 0, rows // tile - 1), 0)

        line = pl.BlockSpec((1, width), lambda k: (0, 0))
        column = pl.BlockSpec((tile, 1), row)
        wide = pl.BlockSpec((tile, width), row)
        in_specs += [wide, column, line, column, wide]
        args += list(final)
        out_specs = wide
        out_shape = jax.ShapeDtypeStruct((rows, width), F32)
        scratch = [pltpu.VMEM((rows, width), F32)]
    else:
        out_specs = pl.BlockSpec((rows, width), lambda k: (0, 0))
        out_shape = jax.ShapeDtypeStruct((rows, width), F32)
        scratch = []
    ends = [end for _, end in places]
    return pl.pallas_call(
        functools.partial(input_grads_kernel, sizes, ends, before is not None, bool(final)),
        grid=(steps + (rows // tile if final else 0),),
        in_specs=in_specs,
        out_specs=out_specs,
        out_shape=out_shape,
        scratch_shapes=scratch,
        compiler_params=params(),
        cost_estimate=cost(2.5e-6 * steps),
        name="input_grads",
    )(*args)


def swap(values, bit, shards):
    return lax.ppermute(values, "shard", [(i, i ^ (1 << bit)) for i in range(shards)])


def border(moving, *values):
    ready = lax.optimization_barrier(tuple(one.got for one in moving) + values)
    for one, got in zip(moving, ready):
        one.got = got
        one.finish()
    rest = ready[len(moving) :]
    return rest[0] if len(rest) == 1 else rest


class Gather:
    def __init__(self, own, order, shards, place):
        self.now, self.order, self.shards, self.place = own, list(order), shards, place
        self.live, self.columns = [], own.shape[-1]

    def start(self):
        self.bit = self.order.pop(0)
        self.got = swap(self.now, self.bit, self.shards)

    def finish(self):
        mine = (self.place >> self.bit) & 1
        axis = len([b for b in self.live if b > self.bit])
        first = jnp.where(mine == 0, self.now, self.got)
        second = jnp.where(mine == 0, self.got, self.now)
        self.now = jnp.stack([first, second], axis=axis)
        self.live.append(self.bit)

    def whole(self):
        while self.order:
            self.start()
            self.finish()
        return self.now


class Group:
    def __init__(self, now, groups):
        self.now, self.groups = now, groups

    def start(self):
        self.pairs = [(i, (i + 1) % self.groups) for i in range(self.groups)]
        self.got = lax.ppermute(self.now, "group", self.pairs)

    def finish(self):
        total, got = self.now.astype(F32), self.got
        for step in range(1, self.groups):
            if step > 1:
                got = lax.ppermute(got, "group", self.pairs)
            total = total + got.astype(F32)
        self.now = total


class Sum:
    def __init__(self, pair, order, shards, groups, place, part, group_first=False):
        self.keep, self.give = pair
        self.shards, self.groups, self.place, self.part = shards, groups, place, part
        self.columns, self.dtype = self.keep.shape[-1], self.keep.dtype
        self.group_first = group_first and groups == 2
        self.todo = [0] + (["group"] if self.group_first else []) + list(order) + ["end"]
        self.live = list(range(shards.bit_length() - 2, 0, -1))
        self.now = None

    def start(self):
        self.bit = bit = self.todo.pop(0)
        if bit == "end":
            pairs = [(i, (i + 1) % self.groups) for i in range(self.groups)]
            self.got = lax.ppermute(self.now, "group", pairs)
        elif bit == "group":
            half = self.columns // 2
            mine = lax.axis_index("group")
            axis = self.now.ndim - 1
            self.keep = lax.dynamic_slice_in_dim(self.now, mine * half, half, axis)
            give = lax.dynamic_slice_in_dim(self.now, (1 - mine) * half, half, axis)
            self.got = lax.ppermute(give, "group", [(0, 1), (1, 0)])
        elif bit == 0:
            self.got = swap(self.give, 0, self.shards)
        else:
            axis = self.live.index(bit)
            mine = (self.place >> bit) & 1
            self.keep = lax.dynamic_index_in_dim(self.now, mine, axis, keepdims=False)
            give = lax.dynamic_index_in_dim(self.now, 1 - mine, axis, keepdims=False)
            self.live.remove(bit)
            self.got = swap(give, bit, self.shards)

    def finish(self):
        if self.bit == "end" and self.group_first:
            first = lax.axis_index("group") == 0
            halves = [jnp.where(first, self.now, self.got), jnp.where(first, self.got, self.now)]
            self.now = jnp.concatenate(halves, axis=-1)
        elif self.bit == "end":
            total, got = self.now.astype(F32), self.got
            for step in range(1, self.groups):
                if step > 1:
                    pairs = [(i, (i + 1) % self.groups) for i in range(self.groups)]
                    got = lax.ppermute(got, "group", pairs)
                total = total + got.astype(F32)
            self.now = total
        else:
            now = self.keep.astype(F32) + self.got.astype(F32)
            if self.todo != ["end"] or not self.group_first:
                now = now.astype(self.dtype)
            if self.bit == 0:
                now = now.reshape((2,) * len(self.live) + (self.part, self.columns))
            self.now = now

    def result(self):
        while self.todo:
            self.start()
            self.finish()
        return self.now


def local(
    shards,
    groups,
    hidden_in,
    lengths,
    pre_gain,
    in_proj,
    conv_weight,
    conv_bias,
    head_params,
    gate_gain,
    out_proj,
    cotangent,
):
    micro, own, slot, width = hidden_in.shape
    rows = micro * own * slot
    inner = out_proj.shape[0] * shards
    channels = conv_bias.shape[0] * shards
    heads = head_params.shape[1]
    tail = channels - inner + heads
    part = in_proj.shape[0]
    out_part = out_proj.shape[0]
    own_conv = conv_bias.shape[0]
    taps = conv_weight.shape[0]
    hidden = hidden_in.reshape(rows, width)
    cot = cotangent.reshape(rows, width)
    place = lax.axis_index("shard")
    core = place & 1
    chip_bits = list(range(1, shards.bit_length() - 1))
    up = chip_bits
    down = chip_bits[::-1]

    w_in = lax.all_gather(in_proj, "shard", axis=0, tiled=True)
    w_out = lax.all_gather(out_proj, "shard", axis=0, tiled=True)
    small = jnp.concatenate([pre_gain, gate_gain, conv_bias, conv_weight.reshape(-1)], axis=0)
    small = small.astype(F32)
    small = jnp.pad(small, (0, -small.shape[0] % LANES))[None, :]
    packed = Gather(small, down + [0], shards, place).whole().reshape(shards, -1)
    sizes = (part, out_part, own_conv, taps * own_conv)
    ends = [sum(sizes[: i + 1]) for i in range(4)]
    pre_all = packed[:, : ends[0]].reshape(1, width)
    gate_all = packed[:, ends[0] : ends[1]].reshape(1, inner)
    bias_all = packed[:, ends[1] : ends[2]].reshape(1, channels)
    taps_all = packed[:, ends[2] : ends[3]].reshape(shards, taps, -1)
    taps_all = jnp.swapaxes(taps_all, 0, 1).reshape(taps, channels)
    skip_row = jnp.pad(jnp.repeat(head_params[2], inner // heads), (0, channels - inner))
    table = jnp.concatenate(
        [taps_all, bias_all, skip_row[None, :], jnp.zeros((2, channels), F32)], axis=0
    )
    table_x, table_bc = table[:, :inner], table[:, inner:]
    rate = -jnp.exp(head_params[1])
    head_rows = jnp.pad(
        jnp.stack([head_params[0], rate], axis=0), ((0, 6), (0, LANES - heads))
    )

    inv_first = lax.rsqrt(jnp.mean(hidden * hidden, axis=-1, keepdims=True) + EPS)
    normed = (hidden * inv_first * pre_all).astype(BF)
    turned = normed.T.reshape(shards // 2, 2, part, rows)
    mine = lax.dynamic_index_in_dim(turned, core, 1, keepdims=False).reshape(-1, rows)
    other = lax.dynamic_index_in_dim(turned, 1 - core, 1, keepdims=False).reshape(-1, rows)
    positions = jnp.arange(slot, dtype=jnp.int32)
    mask = (positions[None, :] < lengths.reshape(-1)[:, None]).astype(F32).reshape(rows, 1)
    grad_low = (mask * cot).astype(BF)

    size = 4 * LANES
    blocks = inner // size
    raw_at = inner // (3 * LANES)
    prep_at = (raw_at, table_bc, head_rows, heads)
    px = project(normed, w_in, blocks, blocks + 1, size)
    prep = prepare(px, *prep_at, slot)
    unit = GROUP_HEADS * 64
    y_rows = scan_forward(px, 0, table_x, prep, slot, 0, inner // unit)
    pz = project(normed, w_in, 0, blocks, size, BF)
    gate_low, inv = gate_forward([y_rows], pz, gate_all)

    g_out = dot_tn(gate_low, grad_low).astype(BF)
    g_out, grad_low, mine, other = border([], g_out, grad_low, mine, other)
    sum_out = lax.psum_scatter(g_out, "shard", scatter_dimension=0, tiled=True)
    grad_gate = dot_nt(grad_low, w_out).astype(BF)
    grad_y, grad_z = gate_backward([y_rows], pz, grad_gate, inv, gate_all)
    reduce = functools.partial(Sum, shards=shards, groups=groups, place=place, order=up)
    third = inner // unit // 3
    outs = scan_backward(px, 0, table_x, y_rows, 0, grad_y, prep, slot, 0, 2 * third)
    lines_x = [outs[1]]
    b_blocks = 2 * third * unit // size
    pair_b = weight_grads(mine, other, outs[0], 0, b_blocks, size, part)
    *pair_b, grad_z = border([], *pair_b, grad_z)
    s_b = reduce(pair_b, part=part, group_first=True)
    s_b.start()
    g_z = dot_nn(turned.reshape(width, rows), grad_z).astype(BF)
    g_z, grad_y, sum_out = border([s_b], g_z, grad_y, sum_out)
    sum_z = lax.psum_scatter(g_z, "shard", scatter_dimension=0, tiled=True)
    s_b.start()
    rest = inner // unit - 2 * third
    outs = scan_backward(
        px, 2 * third, table_x, y_rows, 2 * third, grad_y, prep, slot, 2 * third, rest, before=outs
    )
    mine, *outs = border([s_b], mine, *outs)
    s_out = Group(sum_out, groups)
    lines_x.append(outs[1])
    grad_x, lines_bc, head_total = finish(
        px, *prep_at, prep, outs[2:], outs[0], size, blocks, slot
    )

    free = size - tail
    lines = jnp.concatenate(lines_x + [lines_bc], axis=1)[:5].reshape(5, shards, own_conv)
    lines = jnp.pad(lines, ((0, 0), (0, 0), (0, free - own_conv)))
    head_line = head_total[:3, :heads].reshape(1, 1, 3 * heads)
    head_line = jnp.pad(head_line, ((0, 0), (0, 0), (0, free - 3 * heads)))
    small = jnp.concatenate([lines, jnp.broadcast_to(head_line, (1, shards, free))], axis=0)
    small = jnp.swapaxes(small.astype(BF), 0, 1).reshape(shards // 2, 2, 6, free)
    small = jnp.pad(small, ((0, 0), (0, 0), (0, 10), (2 * LANES - free, 0)))
    extra = [
        lax.dynamic_index_in_dim(small, index, 1, keepdims=False) for index in (1 - core, core)
    ]
    pair_a = weight_grads(
        mine, other, grad_x, b_blocks, blocks + 1 - b_blocks, size, part, extra
    )
    *pair_a, grad_z, grad_x = border([], *pair_a, grad_z, grad_x)
    s_a = reduce(pair_a, part=part)
    s_a.start()
    s_b.start()
    part_sum = dot_nt(grad_z, w_in[:, :inner])
    part_sum, grad_x = border([s_b, s_a], part_sum, grad_x)
    s_a.start()
    s_b.start()
    s_out.start()
    grad_input = input_grads(
        [grad_x],
        [(blocks, tail % size)],
        w_in,
        before=part_sum,
        final=(hidden, inv_first, pre_all, mask, cot),
    )
    gate_low, grad_input, sum_z = border([s_a, s_b, s_out], gate_low, grad_input, sum_z)
    s_a.start()
    s_b.start()
    s_z = Group(sum_z, groups)
    s_z.start()
    layer_out = mask * (hidden + dot_nn(gate_low, w_out))
    layer_out = border([s_a, s_b, s_z], layer_out)
    s_a.start()
    s_b.start()
    for one in (s_a, s_b):
        one.finish()
    sum_a = s_a.result()
    b_columns = b_blocks * size
    g_in = jnp.concatenate(
        [s_z.now, s_b.result(), sum_a[:, : inner - b_columns + tail]], axis=1
    )
    g_out = s_out.now

    def gain_grads(weight, grads, gain):
        return jnp.sum(weight.astype(F32) * grads, axis=1) / gain.astype(F32)

    g_pre = gain_grads(in_proj, g_in, pre_gain)
    g_gate = gain_grads(out_proj, g_out, gate_gain)
    small = sum_a[:6, inner - b_columns + tail :]
    g_lines = small[:5, :own_conv]
    g_heads = small[5, : 3 * heads].reshape(3, heads)
    return (
        layer_out.reshape(hidden_in.shape),
        grad_input.reshape(hidden_in.shape),
        g_pre,
        g_in,
        g_lines[:4],
        g_lines[4],
        g_heads,
        g_gate,
        g_out,
    )


def solution(mesh):
    rows = P(None, ("group", "shard"), None, None)
    in_specs = (
        rows,
        P(None, ("group", "shard")),
        P("shard"),
        P("shard", None),
        P(None, "shard"),
        P("shard"),
        P(),
        P("shard"),
        P("shard", None),
        rows,
    )
    out_specs = (
        rows,
        rows,
        P("shard"),
        P("shard", None),
        P(None, "shard"),
        P("shard"),
        P(),
        P("shard"),
        P("shard", None),
    )
    body = functools.partial(local, mesh.shape["shard"], mesh.shape["group"])
    return jax.shard_map(body, mesh=mesh, in_specs=in_specs, out_specs=out_specs, check_vma=False)
```

```python
import functools

import jax
import jax.numpy as jnp
from jax import lax
from jax.experimental import pallas as pl
from jax.experimental.pallas import tpu as pltpu
from jax.sharding import PartitionSpec as P

STRETCH = 256
HALF = 128
LANES = 128
GROUP_HEADS = 8
CHUNK = 16
EPS = 1e-05
BF = jnp.bfloat16
F32 = jnp.float32
VMEM_BYTES = 56 * 1024 * 1024


def params(**kwargs):
    return pltpu.CompilerParams(vmem_limit_bytes=VMEM_BYTES, **kwargs)


def cost(seconds):
    return pl.CostEstimate(
        flops=int(seconds * 2.0e13), bytes_accessed=int(seconds * 6.0e10), transcendentals=0
    )


def dot_nn(left, right):
    return lax.dot_general(left, right, (((1,), (0,)), ((), ())), preferred_element_type=F32)


def dot_nt(left, right):
    return lax.dot_general(left, right, (((1,), (1,)), ((), ())), preferred_element_type=F32)


def dot_tn(left, right):
    return lax.dot_general(left, right, (((0,), (0,)), ((), ())), preferred_element_type=F32)


def sigmoid(values):
    return 1.0 / (1.0 + jnp.exp(-values))


def row_index(values):
    return lax.broadcasted_iota(jnp.int32, (values.shape[0], 1), 0)


def shift_down(values, count):
    rolled = pltpu.roll(values, count, 0)
    place = lax.broadcasted_iota(jnp.int32, (8, 1), 0)
    return jnp.concatenate([jnp.where(place >= count, rolled[:8], 0.0), rolled[8:]], axis=0)


def shift_up(values, count):
    rows = values.shape[0]
    rolled = pltpu.roll(values, rows - count, 0)
    place = lax.broadcasted_iota(jnp.int32, (8, 1), 0)
    last = jnp.where(place < 8 - count, rolled[rows - 8 :], 0.0)
    return jnp.concatenate([rolled[: rows - 8], last], axis=0)


def conv_sum(values, taps_ref):
    pre = taps_ref[4:5, :]
    for k in range(3):
        pre = pre + taps_ref[k : k + 1, :] * shift_down(values, 3 - k)
    return pre + taps_ref[3:4, :] * values


def conv_back(grad_pre, values, taps_ref):
    total = taps_ref[3:4, :] * grad_pre
    lines = []
    for k in range(3):
        moved = shift_up(grad_pre, 3 - k)
        total = total + taps_ref[k : k + 1, :] * moved
        lines.append(column_sum(moved * values))
    lines += [column_sum(grad_pre * values), column_sum(grad_pre)]
    lines.append(jnp.zeros((3, values.shape[1]), F32))
    return total, jnp.concatenate(lines, axis=0)


def column_sum(values):
    return jnp.sum(values, axis=0, keepdims=True)


def prepare_kernel(head_count, raw_ref, taps_ref, heads_ref, b_ref, c_ref, bt_ref, ct_ref, dt_ref, cum_ref, cumt_ref):
    pre = conv_sum(raw_ref[:, : 2 * LANES], taps_ref)
    active = pre * sigmoid(pre)
    b_part, c_part = active[:, :LANES], active[:, LANES:]
    b_ref[...] = b_part.astype(BF)
    c_ref[...] = c_part.astype(BF)
    bt_ref[...] = b_part.T.astype(BF)
    ct_ref[...] = c_part.T.astype(BF)
    lane = lax.broadcasted_iota(jnp.int32, (1, LANES), 1)
    raw = jnp.where(lane < head_count, raw_ref[:, 2 * LANES :], 0.0) + heads_ref[0:1, :]
    dt = jnp.maximum(raw, 0.0) + jnp.log1p(jnp.exp(-jnp.abs(raw)))
    cum = dt * heads_ref[1:2, :]
    place = row_index(cum) % STRETCH
    step = 1
    while step < STRETCH:
        cum = cum + jnp.where(place >= step, pltpu.roll(cum, step, 0), 0.0)
        step *= 2
    dt_ref[...] = dt
    cum_ref[...] = cum
    cumt_ref[...] = cum.T


def prepare(raw, at, taps, heads, head_count, slot):
    rows = raw.shape[0]
    tall = pl.BlockSpec((slot, LANES), lambda q: (q, 0))
    wide = pl.BlockSpec((LANES, slot), lambda q: (0, q))
    return pl.pallas_call(
        functools.partial(prepare_kernel, head_count),
        grid=(rows // slot,),
        in_specs=[
            pl.BlockSpec((slot, 3 * LANES), lambda q: (q, at)),
            pl.BlockSpec((8, 2 * LANES), lambda q: (0, 0)),
            pl.BlockSpec((8, LANES), lambda q: (0, 0)),
        ],
        out_specs=[tall, tall, wide, wide, tall, tall, wide],
        out_shape=[
            jax.ShapeDtypeStruct((rows, LANES), BF),
            jax.ShapeDtypeStruct((rows, LANES), BF),
            jax.ShapeDtypeStruct((LANES, rows), BF),
            jax.ShapeDtypeStruct((LANES, rows), BF),
            jax.ShapeDtypeStruct((rows, LANES), F32),
            jax.ShapeDtypeStruct((rows, LANES), F32),
            jax.ShapeDtypeStruct((LANES, rows), F32),
        ],
        compiler_params=params(),
        name="prepare",
    )(raw, taps, heads)


def head_tables(cum_ref, dt_ref, first_head):
    shift = lax.rem(LANES - first_head, LANES)
    cum = pltpu.roll(cum_ref[...], shift, 1)
    dt = pltpu.roll(dt_ref[...], shift, 1)
    rows = cum.shape[0]
    cum_wide = [jnp.broadcast_to(cum[:, i : i + 1], (rows, LANES)) for i in range(GROUP_HEADS)]
    dt_wide = [jnp.broadcast_to(dt[:, i : i + 1], (rows, LANES)) for i in range(GROUP_HEADS)]
    left = lax.broadcasted_iota(jnp.int32, (1, LANES), 1) < LANES // 2

    def spread(wide):
        return jnp.concatenate(
            [jnp.where(left, wide[i], wide[i + 1]) for i in range(0, GROUP_HEADS, 2)], axis=1
        )

    return cum_wide, spread(cum_wide), spread(dt_wide), left


def decay_tiles(cum_wide, cumt_row, block, lower):
    begin = block * STRETCH
    top = cum_wide[begin : begin + HALF]
    low = cum_wide[begin + HALF : begin + STRETCH]
    row_left = cumt_row[:, begin : begin + HALF]
    row_right = cumt_row[:, begin + HALF : begin + STRETCH]
    first = jnp.where(lower, jnp.exp(top - row_left), 0.0)
    second = jnp.exp(low - row_left)
    third = jnp.where(lower, jnp.exp(low - row_right), 0.0)
    return first, jnp.concatenate([second, third], axis=1)


def join_tiles(first, below):
    return jnp.concatenate(
        [jnp.concatenate([first, jnp.zeros_like(first)], axis=1), below], axis=0
    )


def lower_mask():
    return lax.broadcasted_iota(jnp.int32, (HALF, HALF), 0) >= lax.broadcasted_iota(
        jnp.int32, (HALF, HALF), 1
    )


def forward_kernel(
    group_start, x_ref, taps_ref, b_ref, c_ref, bt_ref, dt_ref, cum_ref, cumt_ref, y_ref
):
    first_head = (pl.program_id(1) + group_start) * GROUP_HEADS
    pre = conv_sum(x_ref[...], taps_ref)
    x_low = (pre * sigmoid(pre)).astype(BF).astype(F32)
    cum_wide, cum_x, dt_x, left = head_tables(cum_ref, dt_ref, first_head)
    x_dt = (x_low * dt_x).astype(BF)
    skipped = taps_ref[5:6, :] * x_low
    fade = jnp.exp(cum_x[STRETCH - 1 : STRETCH] - cum_x[:STRETCH])
    scaled = (x_low[:STRETCH] * (fade * dt_x[:STRETCH])).astype(BF)
    state = dot_nn(bt_ref[:, :STRETCH], scaled).astype(BF)
    lower = lower_mask()
    zero = jnp.zeros((STRETCH, LANES), BF)
    for block in range(2):
        rows = slice(block * STRETCH, (block + 1) * STRETCH)
        cb = dot_nt(c_ref[rows, :], b_ref[rows, :])
        if block == 1:
            inter = dot_nn(c_ref[rows, :], state)
        for pair in range(GROUP_HEADS // 2):
            lanes = slice(pair * LANES, (pair + 1) * LANES)
            x_pair = x_dt[rows, lanes]
            total = None
            for side in range(2):
                head = 2 * pair + side
                row = cumt_ref[pl.ds(first_head + head, 1), :]
                first, below = decay_tiles(cum_wide[head], row, block, lower)
                mixing = join_tiles(
                    (cb[:HALF, :HALF] * first).astype(BF), (cb[HALF:, :] * below).astype(BF)
                )
                keep = left if side == 0 else jnp.logical_not(left)
                now = dot_nn(mixing, jnp.where(keep, x_pair, zero))
                total = now if total is None else total + now
            if block == 1:
                total = total + jnp.exp(cum_x[rows, lanes]) * inter[:, lanes]
            y_ref[rows, lanes] = total + skipped[rows, lanes]


def scan_forward(px, offset, taps, prep, slot, start, count):
    b_low, c_low, b_t, _, dt, cum, cum_t = prep
    rows = px.shape[0]
    width = GROUP_HEADS * 64
    tall = pl.BlockSpec((slot, LANES), lambda q, h: (q, 0))
    wide = pl.BlockSpec((LANES, slot), lambda q, h: (0, q))
    tile = pl.BlockSpec((slot, width), lambda q, h: (q, h))
    return pl.pallas_call(
        functools.partial(forward_kernel, start),
        grid=(rows // slot, count),
        in_specs=[
            pl.BlockSpec((slot, width), lambda q, h: (q, h + offset)),
            pl.BlockSpec((8, width), lambda q, h: (0, h + start)),
            tall,
            tall,
            wide,
            tall,
            tall,
            wide,
        ],
        out_specs=tile,
        out_shape=jax.ShapeDtypeStruct((rows, count * width), F32),
        compiler_params=params(),
        cost_estimate=cost(3.3e-6 * count),
        name="scan_forward",
    )(px, taps, b_low, c_low, b_t, dt, cum, cum_t)


def gate_kernel(count, *refs):
    y_refs = refs[:count]
    z_ref, gain_ref, gate_ref, inv_ref = refs[count:]

    def chunk(i, carry):
        rows = pl.ds(pl.multiple_of(i * CHUNK, CHUNK), CHUNK)
        y = jnp.concatenate([ref[rows, :] for ref in y_refs], axis=1)
        z = z_ref[rows, :].astype(F32)
        gated = y * (z * sigmoid(z))
        mean = jnp.sum(gated * gated, axis=1, keepdims=True) * (1.0 / gated.shape[1])
        inv = lax.rsqrt(mean + EPS)
        gate_ref[rows, :] = (gated * inv * gain_ref[...]).astype(BF)
        inv_ref[rows, :] = jnp.broadcast_to(inv, (CHUNK, LANES))
        return carry

    lax.fori_loop(0, z_ref.shape[0] // CHUNK, chunk, 0, unroll=4)


def row_tile(size, array):
    return pl.BlockSpec((size, array.shape[1]), lambda t: (t, 0))


def gate_forward(y_parts, pz, gain):
    rows, inner = pz.shape
    size = 256
    tile = pl.BlockSpec((size, inner), lambda t: (t, 0))
    return pl.pallas_call(
        functools.partial(gate_kernel, len(y_parts)),
        grid=(rows // size,),
        in_specs=[row_tile(size, y) for y in y_parts]
        + [tile, pl.BlockSpec((1, inner), lambda t: (0, 0))],
        out_specs=[tile, pl.BlockSpec((size, LANES), lambda t: (t, 0))],
        out_shape=[
            jax.ShapeDtypeStruct((rows, inner), BF),
            jax.ShapeDtypeStruct((rows, LANES), F32),
        ],
        compiler_params=params(),
        cost_estimate=cost(15e-6),
        name="gate_forward",
    )(*y_parts, pz, gain)


def gate_back_kernel(count, *refs):
    y_refs = refs[:count]
    z_ref, grad_ref, inv_ref, gain_ref, gy_ref, gz_ref = refs[count:]

    def chunk(i, carry):
        rows = pl.ds(pl.multiple_of(i * CHUNK, CHUNK), CHUNK)
        y = jnp.concatenate([ref[rows, :] for ref in y_refs], axis=1)
        z = z_ref[rows, :].astype(F32)
        inv = inv_ref[rows, 0:1]
        sig = sigmoid(z)
        silu = z * sig
        normal = y * silu * inv
        grad_normal = grad_ref[rows, :].astype(F32) * gain_ref[...]
        mean = jnp.sum(grad_normal * normal, axis=1, keepdims=True) * (1.0 / y.shape[1])
        gated = inv * (grad_normal - normal * mean)
        gy_ref[rows, :] = (gated * silu).astype(BF)
        gz_ref[rows, :] = (gated * y * (sig + silu * (1.0 - sig))).astype(BF)
        return carry

    lax.fori_loop(0, z_ref.shape[0] // CHUNK, chunk, 0, unroll=4)


def gate_backward(y_parts, pz, grad_gate, inv, gain):
    rows, inner = pz.shape
    size = 256
    tile = pl.BlockSpec((size, inner), lambda t: (t, 0))
    return pl.pallas_call(
        functools.partial(gate_back_kernel, len(y_parts)),
        grid=(rows // size,),
        in_specs=[row_tile(size, y) for y in y_parts]
        + [
            tile,
            tile,
            pl.BlockSpec((size, LANES), lambda t: (t, 0)),
            pl.BlockSpec((1, inner), lambda t: (0, 0)),
        ],
        out_specs=[tile, tile],
        out_shape=[
            jax.ShapeDtypeStruct((rows, inner), BF),
            jax.ShapeDtypeStruct((rows, inner), BF),
        ],
        compiler_params=params(),
        cost_estimate=cost(24e-6),
        name="gate_backward",
    )(*y_parts, pz, grad_gate, inv, gain)


def head_sums(product, spread):
    high = product.astype(BF)
    low = (product - high.astype(F32)).astype(BF)
    return dot_nn(high, spread) + dot_nn(low, spread)


def backward_kernel(group_start, *refs):
    x_ref, taps_ref, y_ref, gy_ref, b_ref, c_ref, bt_ref, ct_ref = refs[:8]
    dt_ref, cum_ref, cumt_ref = refs[8:11]
    gx_ref, lines_ref, *totals = refs[-8:]
    gb_ref, gc_ref, one_ref, two_ref, cb_ref, heads_ref = totals
    befores = refs[12:-8]
    first_head = (pl.program_id(0) + group_start) * GROUP_HEADS
    seq = pl.program_id(1)
    slot = x_ref.shape[0]

    @pl.when((pl.program_id(0) == 0) & (seq == 0))
    def _():
        for i, total in enumerate(totals):
            total[...] = befores[i][...] if befores else jnp.zeros_like(total)

    at = pl.multiple_of(seq * slot, slot)
    whole_rows = pl.ds(at, slot)
    early_rows = pl.ds(at, STRETCH)
    late_rows = pl.ds(pl.multiple_of(at + STRETCH, STRETCH), STRETCH)
    pre = conv_sum(x_ref[...], taps_ref)
    sig = sigmoid(pre)
    active = pre * sig
    slope = sig + active * (1.0 - sig)
    x_low = active.astype(BF).astype(F32)
    gy_low = gy_ref[...]
    gy = gy_low.astype(F32)
    cum_wide, cum_x, dt_x, left = head_tables(cum_ref, dt_ref, first_head)
    x_dt = (x_low * dt_x).astype(BF)
    skip = taps_ref[5:6, :]

    grad_inter = (gy[STRETCH:] * jnp.exp(cum_x[STRETCH:])).astype(BF)
    fade = jnp.exp(cum_x[STRETCH - 1 : STRETCH] - cum_x[:STRETCH])
    scaled = (x_low[:STRETCH] * (fade * dt_x[:STRETCH])).astype(BF)
    state = dot_nn(bt_ref[:, :STRETCH], scaled)
    grad_state = dot_nn(ct_ref[:, STRETCH:], grad_inter).astype(BF)

    lower = lower_mask()
    zero = jnp.zeros((STRETCH, LANES), BF)
    rest = [None, None]
    for block in (1, 0):
        rows = slice(block * STRETCH, (block + 1) * STRETCH)
        cb = dot_nt(c_ref[rows, :], b_ref[rows, :])
        cb_first = cb_below = None
        parts = []
        for pair in range(GROUP_HEADS // 2):
            lanes = slice(pair * LANES, (pair + 1) * LANES)
            x_pair = x_dt[rows, lanes]
            gy_pair = gy_low[rows, lanes]
            total = None
            for side in range(2):
                head = 2 * pair + side
                row = cumt_ref[pl.ds(first_head + head, 1), :]
                first, below = decay_tiles(cum_wide[head], row, block, lower)
                mixing = join_tiles(
                    (cb[:HALF, :HALF] * first).astype(BF), (cb[HALF:, :] * below).astype(BF)
                )
                keep = left if side == 0 else jnp.logical_not(left)
                gy_head = jnp.where(keep, gy_pair, zero)
                mix_first = dot_nt(gy_head[:HALF], x_pair[:HALF]) * first
                mix_below = dot_nt(gy_head[HALF:], x_pair) * below
                cb_first = mix_first if cb_first is None else cb_first + mix_first
                cb_below = mix_below if cb_below is None else cb_below + mix_below
                now = dot_tn(mixing, gy_head)
                total = now if total is None else total + now
            parts.append(total)
        cb_ref[seq, block, :HALF, :HALF] += cb_first
        cb_ref[seq, block, HALF:, :] += cb_below
        rest[block] = jnp.concatenate(parts, axis=1)
        if block == 1:
            grad_scaled = dot_nn(b_ref[:STRETCH, :], grad_state)
            gc_ref[late_rows, :] += dot_nt(grad_inter, state.astype(BF))
            gb_ref[early_rows, :] += dot_nt(scaled, grad_state)
            last_sum = column_sum(grad_state.astype(F32) * state)
    moved = x_dt.astype(F32) * jnp.concatenate(rest, axis=0)
    moved = jnp.concatenate(
        [moved[:STRETCH] + scaled.astype(F32) * grad_scaled, moved[STRETCH:]], axis=0
    )
    rest[0] = rest[0] + fade * grad_scaled
    grad_pull = jnp.concatenate(rest, axis=0)

    width = x_low.shape[1]
    spread = (
        lax.broadcasted_iota(jnp.int32, (width, LANES), 1)
        == first_head + lax.broadcasted_iota(jnp.int32, (width, LANES), 0) // 64
    ).astype(F32).astype(BF)
    moved = gy * (y_ref[...] - skip * x_low) - moved
    edge = lax.broadcasted_iota(jnp.int32, (8, 1), 0) == 7
    moved = jnp.concatenate(
        [
            moved[: STRETCH - 8],
            moved[STRETCH - 8 : STRETCH] + jnp.where(edge, last_sum, 0.0),
            moved[STRETCH:],
        ],
        axis=0,
    )
    one_ref[whole_rows, :] += head_sums(moved, spread)
    two_ref[whole_rows, :] += dot_nn((x_low * grad_pull).astype(BF), spread)
    third = lax.broadcasted_iota(jnp.int32, (8, 1), 0) == 2
    skip_line = jnp.where(third, column_sum(gy * x_low), 0.0)
    heads_ref[...] += head_sums(skip_line, spread)

    grad_pre = (skip * gy + dt_x * grad_pull) * slope
    grad_in, lines = conv_back(grad_pre, x_ref[...], taps_ref)
    gx_ref[...] = grad_in.astype(BF)

    @pl.when(seq == 0)
    def _():
        lines_ref[...] = lines

    @pl.when(seq > 0)
    def _():
        lines_ref[...] += lines


def scan_backward(px, at, taps, y_rows, y_at, grad_y, prep, slot, start, count, before=None):
    b_low, c_low, b_t, c_t, dt, cum, cum_t = prep
    rows = px.shape[0]
    width = GROUP_HEADS * 64
    seqs = rows // slot
    tall = pl.BlockSpec((slot, LANES), lambda h, q: (q, 0))
    wide = pl.BlockSpec((LANES, slot), lambda h, q: (0, q))
    tile = pl.BlockSpec((slot, width), lambda h, q: (q, h + at))
    flat = jax.ShapeDtypeStruct((rows, LANES), F32)
    whole = pl.BlockSpec((rows, LANES), lambda h, q: (0, 0))
    totals = [whole] * 4 + [
        pl.BlockSpec((seqs, 2, STRETCH, STRETCH), lambda h, q: (0, 0, 0, 0)),
        pl.BlockSpec((8, LANES), lambda h, q: (0, 0)),
    ]
    extra, extra_specs, aliases = [jnp.zeros((8, LANES), BF)], [pl.BlockSpec(memory_space=pl.ANY)], {}
    if before is not None:
        if before[0].shape == px.shape:
            extra = [before[0]]
            aliases[11] = 0
        extra = extra + list(before[2:])
        extra_specs = extra_specs + totals
        aliases.update({12 + i: 2 + i for i in range(6)})
    return pl.pallas_call(
        functools.partial(backward_kernel, start),
        grid=(count, seqs),
        in_specs=[
            tile,
            pl.BlockSpec((8, width), lambda h, q: (0, h + start)),
            pl.BlockSpec((slot, width), lambda h, q: (q, h + y_at)),
            pl.BlockSpec((slot, width), lambda h, q: (q, h + start)),
            tall,
            tall,
            wide,
            wide,
            tall,
            tall,
            wide,
        ]
        + extra_specs,
        out_specs=[tile, pl.BlockSpec((8, width), lambda h, q: (0, h))] + totals,
        out_shape=[
            jax.ShapeDtypeStruct(px.shape, BF),
            jax.ShapeDtypeStruct((8, count * width), F32),
            flat,
            flat,
            flat,
            flat,
            jax.ShapeDtypeStruct((seqs, 2, STRETCH, STRETCH), F32),
            jax.ShapeDtypeStruct((8, LANES), F32),
        ],
        input_output_aliases=aliases,
        compiler_params=params(),
        cost_estimate=cost(3.3e-6 * count),
        name="scan_backward",
    )(px, taps, y_rows, grad_y, b_low, c_low, b_t, c_t, dt, cum, cum_t, *extra)


def finish_kernel(
    head_count,
    raw_ref,
    taps_ref,
    heads_ref,
    b_ref,
    c_ref,
    dt_ref,
    gb_ref,
    gc_ref,
    one_ref,
    two_ref,
    cb_ref,
    head_before_ref,
    before_ref,
    out_ref,
    lines_ref,
    head_total_ref,
):
    @pl.when(pl.program_id(0) == 0)
    def _():
        lines_ref[...] = jnp.zeros_like(lines_ref)
        head_total_ref[...] = head_before_ref[...]

    pre = conv_sum(raw_ref[:, : 2 * LANES], taps_ref)
    sig = sigmoid(pre)
    slope = sig + pre * sig * (1.0 - sig)
    grad_b, grad_c = [], []
    for block in range(2):
        rows = slice(block * STRETCH, (block + 1) * STRETCH)
        cb = cb_ref[0, block].astype(BF)
        grad_c.append(gc_ref[rows, :] + dot_nn(cb, b_ref[rows, :]))
        grad_b.append(gb_ref[rows, :] + dot_tn(cb, c_ref[rows, :]))
    grad_active = jnp.concatenate(
        [jnp.concatenate(grad_b, axis=0), jnp.concatenate(grad_c, axis=0)], axis=1
    )
    grad_pre = grad_active * slope
    grad_in, lines = conv_back(grad_pre, raw_ref[:, : 2 * LANES], taps_ref)
    lines_ref[...] += lines

    dt = dt_ref[...]
    two = two_ref[...]
    rate = heads_ref[1:2, :]
    place = row_index(dt)
    grad_cum = one_ref[...]
    inside = place % STRETCH
    step = 1
    while step < STRETCH:
        moved = pltpu.roll(grad_cum, grad_cum.shape[0] - step, 0)
        grad_cum = grad_cum + jnp.where(inside < STRETCH - step, moved, 0.0)
        step *= 2
    grad_dt = grad_cum * rate + two
    lane = lax.broadcasted_iota(jnp.int32, (1, LANES), 1)
    raw = jnp.where(lane < head_count, raw_ref[:, 2 * LANES : 3 * LANES], 0.0)
    grad_raw = grad_dt * sigmoid(raw + heads_ref[0:1, :])
    head_total_ref[...] += jnp.concatenate(
        [column_sum(grad_raw), column_sum(grad_cum * dt) * rate, jnp.zeros((6, LANES), F32)], axis=0
    )
    out_ref[:, : 2 * LANES] = grad_in.astype(BF)
    out_ref[:, 2 * LANES : 3 * LANES] = grad_raw.astype(BF)
    out_ref[:, 3 * LANES :] = jnp.zeros_like(out_ref[:, 3 * LANES :])


def finish(raw, at, taps, heads, head_count, prep, totals, grads, narrow, grads_at, slot):
    b_low, c_low, _, _, dt, _, _ = prep
    rows = raw.shape[0]
    seqs = rows // slot
    tall = pl.BlockSpec((slot, LANES), lambda q: (q, 0))
    return pl.pallas_call(
        functools.partial(finish_kernel, head_count),
        grid=(seqs,),
        in_specs=[
            pl.BlockSpec((slot, 3 * LANES), lambda q: (q, at)),
            pl.BlockSpec((8, 2 * LANES), lambda q: (0, 0)),
            pl.BlockSpec((8, LANES), lambda q: (0, 0)),
            tall,
            tall,
            tall,
            tall,
            tall,
            tall,
            tall,
            pl.BlockSpec((1, 2, STRETCH, STRETCH), lambda q: (q, 0, 0, 0)),
            pl.BlockSpec((8, LANES), lambda q: (0, 0)),
            pl.BlockSpec(memory_space=pl.ANY),
        ],
        out_specs=[
            pl.BlockSpec((slot, narrow), lambda q: (q, grads_at)),
            pl.BlockSpec((8, 2 * LANES), lambda q: (0, 0)),
            pl.BlockSpec((8, LANES), lambda q: (0, 0)),
        ],
        out_shape=[
            jax.ShapeDtypeStruct(grads.shape, BF),
            jax.ShapeDtypeStruct((8, 2 * LANES), F32),
            jax.ShapeDtypeStruct((8, LANES), F32),
        ],
        input_output_aliases={12: 0},
        compiler_params=params(),
        cost_estimate=cost(3e-6),
        name="finish",
    )(raw, taps, heads, b_low, c_low, dt, *totals, grads)


def project_kernel(rows_ref, weight_ref, out_ref):
    out_ref[...] = dot_nn(rows_ref[...], weight_ref[...]).astype(out_ref.dtype)


def project(normed, weight, at, count, size, dtype=F32):
    rows, depth = normed.shape
    return pl.pallas_call(
        project_kernel,
        grid=(count,),
        in_specs=[
            pl.BlockSpec((rows, depth), lambda j: (0, 0)),
            pl.BlockSpec((depth, size), lambda j: (0, j + at)),
        ],
        out_specs=pl.BlockSpec((rows, size), lambda j: (0, j)),
        out_shape=jax.ShapeDtypeStruct((rows, count * size), dtype),
        compiler_params=params(),
        cost_estimate=cost(2.5e-6 * count),
        name="project",
    )(normed, weight)


def pair_kernel(part, mine_ref, other_ref, grad_ref, *refs):
    keep_ref, give_ref = refs[-2:]
    grad = grad_ref[...]
    for rows_ref, out_ref, extra_ref in zip(
        (other_ref, mine_ref), (give_ref, keep_ref), refs[:-2] or (None, None)
    ):
        product = dot_nn(rows_ref[...], grad)
        out_ref[...] = product.astype(out_ref.dtype)
        if extra_ref is not None:

            @pl.when(pl.program_id(0) == pl.num_programs(0) - 1)
            def _(product=product, out_ref=out_ref, extra_ref=extra_ref):
                chips, high, wide = extra_ref.shape
                lanes = slice(product.shape[1] - wide, product.shape[1])
                for chip in range(chips):
                    rows = slice(chip * part, chip * part + high)
                    out_ref[rows, lanes] = (
                        product[rows, lanes] + extra_ref[chip].astype(F32)
                    ).astype(out_ref.dtype)


def weight_grads(mine, other, grad, at, count, size, part, extra=()):
    depth, rows = mine.shape
    whole = pl.BlockSpec((depth, rows), lambda j: (0, 0))
    tile = pl.BlockSpec((depth, size), lambda j: (0, j))
    shape = jax.ShapeDtypeStruct((depth, count * size), BF)
    return pl.pallas_call(
        functools.partial(pair_kernel, part),
        grid=(count,),
        in_specs=[whole, whole, pl.BlockSpec((rows, size), lambda j: (0, j + at))]
        + [pl.BlockSpec(e.shape, lambda j: (0, 0, 0)) for e in extra],
        out_specs=[tile, tile],
        out_shape=[shape, shape],
        compiler_params=params(),
        cost_estimate=cost(2.5e-6 * count),
        name="weight_grads",
    )(mine, other, grad, *extra)


def input_grads_kernel(sizes, ends, has_before, final, *refs):
    pairs = [refs[2 * i : 2 * i + 2] for i in range(len(sizes))]
    refs = refs[2 * len(sizes) :]
    steps = sum(sizes)
    step = pl.program_id(0)
    if has_before:
        before_ref, refs = refs[0], refs[1:]
    if final:
        hidden_ref, inv_ref, gain_ref, mask_ref, cot_ref, out_ref, total = refs
    else:
        (total,) = refs

    def add(grad_ref, weight):
        now = dot_nt(grad_ref[...], weight)

        @pl.when(step == 0)
        def _():
            total[...] = now + before_ref[...] if has_before else now

        @pl.when(step > 0)
        def _():
            total[...] += now

    begin = 0
    for (grad_ref, weight_ref), size, end in zip(pairs, sizes, ends):
        full = size if end is None else size - 1

        @pl.when((step >= begin) & (step < begin + full))
        def _(grad_ref=grad_ref, weight_ref=weight_ref):
            add(grad_ref, weight_ref[...])

        if end is not None:

            @pl.when(step == begin + full)
            def _(grad_ref=grad_ref, weight_ref=weight_ref, end=end):
                weight = weight_ref[...]
                lane = lax.broadcasted_iota(jnp.int32, weight.shape, 1)
                add(grad_ref, jnp.where(lane < end, weight, jnp.zeros_like(weight)))

        begin += size
    if final:

        @pl.when(step >= steps)
        def _():
            tile = hidden_ref.shape[0]
            grad = total[pl.ds(pl.multiple_of((step - steps) * tile, tile), tile), :]
            inv = inv_ref[:, 0:1]
            normal = hidden_ref[...] * inv
            grad = grad * gain_ref[...]
            inside = jnp.sum(grad * normal, axis=1, keepdims=True) * (1.0 / grad.shape[1])
            out_ref[...] = inv * (grad - normal * inside) + mask_ref[:, 0:1] * cot_ref[...]


def input_grads(grads, places, weight, before=None, final=None):
    rows = grads[0].shape[0]
    width = weight.shape[0]
    size, tile = 512, 256
    sizes = [g.shape[1] // size for g in grads]
    steps = sum(sizes)
    in_specs, args, begin = [], [], 0
    for grad, (at, _), count in zip(grads, places, sizes):

        def place(k, begin=begin, count=count, at=0):
            return (0, at + jnp.clip(k - begin, 0, count - 1))

        in_specs += [
            pl.BlockSpec((rows, size), place),
            pl.BlockSpec((width, size), functools.partial(place, at=at)),
        ]
        args += [grad, weight]
        begin += count
    if before is not None:
        in_specs.append(pl.BlockSpec((rows, width), lambda k: (0, 0), pipeline_mode=pl.Buffered(1)))
        args.append(before)
    if final:

        def row(k):
            return (jnp.clip(k - steps, 0, rows // tile - 1), 0)

        line = pl.BlockSpec((1, width), lambda k: (0, 0))
        column = pl.BlockSpec((tile, LANES), row)
        wide = pl.BlockSpec((tile, width), row)
        in_specs += [wide, column, line, column, wide]
        args += list(final)
        out_specs = wide
        out_shape = jax.ShapeDtypeStruct((rows, width), F32)
        scratch = [pltpu.VMEM((rows, width), F32)]
    else:
        out_specs = pl.BlockSpec((rows, width), lambda k: (0, 0))
        out_shape = jax.ShapeDtypeStruct((rows, width), F32)
        scratch = []
    ends = [end for _, end in places]
    return pl.pallas_call(
        functools.partial(input_grads_kernel, sizes, ends, before is not None, bool(final)),
        grid=(steps + (rows // tile if final else 0),),
        in_specs=in_specs,
        out_specs=out_specs,
        out_shape=out_shape,
        scratch_shapes=scratch,
        compiler_params=params(),
        cost_estimate=cost(2.5e-6 * steps),
        name="input_grads",
    )(*args)


def swap(values, bit, shards):
    return lax.ppermute(values, "shard", [(i, i ^ (1 << bit)) for i in range(shards)])


def border(moving, *values):
    ready = lax.optimization_barrier(tuple(one.got for one in moving) + values)
    for one, got in zip(moving, ready):
        one.got = got
        one.finish()
    rest = ready[len(moving) :]
    return rest[0] if len(rest) == 1 else rest


class Gather:
    def __init__(self, own, order, shards, place):
        self.now, self.order, self.shards, self.place = own, list(order), shards, place
        self.live, self.columns = [], own.shape[-1]

    def start(self):
        self.bit = self.order.pop(0)
        self.got = swap(self.now, self.bit, self.shards)

    def finish(self):
        mine = (self.place >> self.bit) & 1
        axis = len([b for b in self.live if b > self.bit])
        first = jnp.where(mine == 0, self.now, self.got)
        second = jnp.where(mine == 0, self.got, self.now)
        self.now = jnp.stack([first, second], axis=axis)
        self.live.append(self.bit)

    def whole(self):
        while self.order:
            self.start()
            self.finish()
        return self.now


class Group:
    def __init__(self, now, groups):
        self.now, self.groups = now, groups

    def start(self):
        self.pairs = [(i, (i + 1) % self.groups) for i in range(self.groups)]
        self.got = lax.ppermute(self.now, "group", self.pairs)

    def finish(self):
        total, got = self.now.astype(F32), self.got
        for step in range(1, self.groups):
            if step > 1:
                got = lax.ppermute(got, "group", self.pairs)
            total = total + got.astype(F32)
        self.now = total


class Sum:
    def __init__(self, pair, order, shards, groups, place, part, group_first=False):
        self.keep, self.give = pair
        self.shards, self.groups, self.place, self.part = shards, groups, place, part
        self.columns, self.dtype = self.keep.shape[-1], self.keep.dtype
        self.group_first = group_first and groups == 2
        self.todo = [0] + (["group"] if self.group_first else []) + list(order) + ["end"]
        self.live = list(range(shards.bit_length() - 2, 0, -1))
        self.now = None

    def start(self):
        self.bit = bit = self.todo.pop(0)
        if bit == "end":
            pairs = [(i, (i + 1) % self.groups) for i in range(self.groups)]
            self.got = lax.ppermute(self.now, "group", pairs)
        elif bit == "group":
            half = self.columns // 2
            mine = lax.axis_index("group")
            axis = self.now.ndim - 1
            self.keep = lax.dynamic_slice_in_dim(self.now, mine * half, half, axis)
            give = lax.dynamic_slice_in_dim(self.now, (1 - mine) * half, half, axis)
            self.got = lax.ppermute(give, "group", [(0, 1), (1, 0)])
        elif bit == 0:
            self.got = swap(self.give, 0, self.shards)
        else:
            axis = self.live.index(bit)
            mine = (self.place >> bit) & 1
            self.keep = lax.dynamic_index_in_dim(self.now, mine, axis, keepdims=False)
            give = lax.dynamic_index_in_dim(self.now, 1 - mine, axis, keepdims=False)
            self.live.remove(bit)
            self.got = swap(give, bit, self.shards)

    def finish(self):
        if self.bit == "end" and self.group_first:
            first = lax.axis_index("group") == 0
            halves = [jnp.where(first, self.now, self.got), jnp.where(first, self.got, self.now)]
            self.now = jnp.concatenate(halves, axis=-1)
        elif self.bit == "end":
            total, got = self.now.astype(F32), self.got
            for step in range(1, self.groups):
                if step > 1:
                    pairs = [(i, (i + 1) % self.groups) for i in range(self.groups)]
                    got = lax.ppermute(got, "group", pairs)
                total = total + got.astype(F32)
            self.now = total
        else:
            now = self.keep.astype(F32) + self.got.astype(F32)
            if self.todo != ["end"] or not self.group_first:
                now = now.astype(self.dtype)
            if self.bit == 0:
                now = now.reshape((2,) * len(self.live) + (self.part, self.columns))
            self.now = now

    def result(self):
        while self.todo:
            self.start()
            self.finish()
        return self.now


def local(
    shards,
    groups,
    hidden_in,
    lengths,
    pre_gain,
    in_proj,
    conv_weight,
    conv_bias,
    head_params,
    gate_gain,
    out_proj,
    cotangent,
):
    micro, own, slot, width = hidden_in.shape
    rows = micro * own * slot
    inner = out_proj.shape[0] * shards
    channels = conv_bias.shape[0] * shards
    heads = head_params.shape[1]
    tail = channels - inner + heads
    part = in_proj.shape[0]
    out_part = out_proj.shape[0]
    own_conv = conv_bias.shape[0]
    taps = conv_weight.shape[0]
    hidden = hidden_in.reshape(rows, width)
    cot = cotangent.reshape(rows, width)
    place = lax.axis_index("shard")
    core = place & 1
    chip_bits = list(range(1, shards.bit_length() - 1))
    up = chip_bits
    down = chip_bits[::-1]

    w_in = lax.all_gather(in_proj, "shard", axis=0, tiled=True)
    w_out = lax.all_gather(out_proj, "shard", axis=0, tiled=True)
    small = jnp.concatenate([pre_gain, gate_gain, conv_bias, conv_weight.reshape(-1)], axis=0)
    small = small.astype(F32)
    small = jnp.pad(small, (0, -small.shape[0] % LANES))[None, :]
    packed = Gather(small, down + [0], shards, place).whole().reshape(shards, -1)
    sizes = (part, out_part, own_conv, taps * own_conv)
    ends = [sum(sizes[: i + 1]) for i in range(4)]
    pre_all = packed[:, : ends[0]].reshape(1, width)
    gate_all = packed[:, ends[0] : ends[1]].reshape(1, inner)
    bias_all = packed[:, ends[1] : ends[2]].reshape(1, channels)
    taps_all = packed[:, ends[2] : ends[3]].reshape(shards, taps, -1)
    taps_all = jnp.swapaxes(taps_all, 0, 1).reshape(taps, channels)
    skip_row = jnp.pad(jnp.repeat(head_params[2], inner // heads), (0, channels - inner))
    table = jnp.concatenate(
        [taps_all, bias_all, skip_row[None, :], jnp.zeros((2, channels), F32)], axis=0
    )
    table_x, table_bc = table[:, :inner], table[:, inner:]
    rate = -jnp.exp(head_params[1])
    head_rows = jnp.pad(
        jnp.stack([head_params[0], rate], axis=0), ((0, 6), (0, LANES - heads))
    )

    inv_first = lax.rsqrt(jnp.mean(hidden * hidden, axis=-1, keepdims=True) + EPS)
    normed = (hidden * inv_first * pre_all).astype(BF)
    turned = normed.T.reshape(shards // 2, 2, part, rows)
    mine = lax.dynamic_index_in_dim(turned, core, 1, keepdims=False).reshape(-1, rows)
    other = lax.dynamic_index_in_dim(turned, 1 - core, 1, keepdims=False).reshape(-1, rows)
    positions = jnp.arange(slot, dtype=jnp.int32)
    mask = (positions[None, :] < lengths.reshape(-1)[:, None]).astype(F32).reshape(rows, 1)
    grad_low = (mask * cot).astype(BF)

    inv_wide = jnp.broadcast_to(inv_first, (rows, LANES))
    mask_wide = jnp.broadcast_to(mask, (rows, LANES))
    normed, mine, other, inv_wide, mask_wide, grad_low = border(
        [], normed, mine, other, inv_wide, mask_wide, grad_low
    )

    size = 4 * LANES
    blocks = inner // size
    raw_at = inner // (3 * LANES)
    prep_at = (raw_at, table_bc, head_rows, heads)
    px = project(normed, w_in, blocks, blocks + 1, size)
    prep = prepare(px, *prep_at, slot)
    unit = GROUP_HEADS * 64
    y_rows = scan_forward(px, 0, table_x, prep, slot, 0, inner // unit)
    pz = project(normed, w_in, 0, blocks, size, BF)
    gate_low, inv = gate_forward([y_rows], pz, gate_all)

    g_out = dot_tn(gate_low, grad_low).astype(BF)
    g_out, grad_low, mine, other = border([], g_out, grad_low, mine, other)
    sum_out = lax.psum_scatter(g_out, "shard", scatter_dimension=0, tiled=True)
    grad_gate = dot_nt(grad_low, w_out).astype(BF)
    grad_y, grad_z = gate_backward([y_rows], pz, grad_gate, inv, gate_all)
    reduce = functools.partial(Sum, shards=shards, groups=groups, place=place, order=up)
    third = inner // unit // 3
    outs = scan_backward(px, 0, table_x, y_rows, 0, grad_y, prep, slot, 0, 2 * third)
    lines_x = [outs[1]]
    b_blocks = 2 * third * unit // size
    pair_b = weight_grads(mine, other, outs[0], 0, b_blocks, size, part)
    *pair_b, grad_z = border([], *pair_b, grad_z)
    s_b = reduce(pair_b, part=part, group_first=True)
    s_b.start()
    g_z = dot_nn(turned.reshape(width, rows), grad_z).astype(BF)
    g_z, grad_y, sum_out = border([s_b], g_z, grad_y, sum_out)
    sum_z = lax.psum_scatter(g_z, "shard", scatter_dimension=0, tiled=True)
    s_b.start()
    rest = inner // unit - 2 * third
    outs = scan_backward(
        px, 2 * third, table_x, y_rows, 2 * third, grad_y, prep, slot, 2 * third, rest, before=outs
    )
    mine, *outs = border([s_b], mine, *outs)
    s_out = Group(sum_out, groups)
    lines_x.append(outs[1])
    grad_x, lines_bc, head_total = finish(
        px, *prep_at, prep, outs[2:], outs[0], size, blocks, slot
    )

    free = size - tail
    lines = jnp.concatenate(lines_x + [lines_bc], axis=1)[:5].reshape(5, shards, own_conv)
    lines = jnp.pad(lines, ((0, 0), (0, 0), (0, free - own_conv)))
    head_line = head_total[:3, :heads].reshape(1, 1, 3 * heads)
    head_line = jnp.pad(head_line, ((0, 0), (0, 0), (0, free - 3 * heads)))
    small = jnp.concatenate([lines, jnp.broadcast_to(head_line, (1, shards, free))], axis=0)
    small = jnp.swapaxes(small.astype(BF), 0, 1).reshape(shards // 2, 2, 6, free)
    small = jnp.pad(small, ((0, 0), (0, 0), (0, 10), (2 * LANES - free, 0)))
    extra = [
        lax.dynamic_index_in_dim(small, index, 1, keepdims=False) for index in (1 - core, core)
    ]
    pair_a = weight_grads(
        mine, other, grad_x, b_blocks, blocks + 1 - b_blocks, size, part, extra
    )
    *pair_a, grad_z, grad_x = border([], *pair_a, grad_z, grad_x)
    s_a = reduce(pair_a, part=part)
    s_a.start()
    s_b.start()
    part_sum = dot_nt(grad_z, w_in[:, :inner])
    part_sum, grad_x = border([s_b, s_a], part_sum, grad_x)
    s_a.start()
    s_b.start()
    s_out.start()
    grad_input = input_grads(
        [grad_x],
        [(blocks, tail % size)],
        w_in,
        before=part_sum,
        final=(hidden, inv_wide, pre_all, mask_wide, cot),
    )
    gate_low, grad_input, sum_z = border([s_a, s_b, s_out], gate_low, grad_input, sum_z)
    s_a.start()
    s_b.start()
    s_z = Group(sum_z, groups)
    s_z.start()
    layer_out = mask * (hidden + dot_nn(gate_low, w_out))
    layer_out = border([s_a, s_b, s_z], layer_out)
    s_a.start()
    s_b.start()
    for one in (s_a, s_b):
        one.finish()
    sum_a = s_a.result()
    b_columns = b_blocks * size
    g_in = jnp.concatenate(
        [s_z.now, s_b.result(), sum_a[:, : inner - b_columns + tail]], axis=1
    )
    g_out = s_out.now

    def paired(weight, grads):
        return jnp.sum(weight.astype(F32) * grads, axis=1)

    sum_b, late_at = s_b.result(), inner + b_columns
    g_pre = paired(in_proj[:, :inner], s_z.now) + paired(in_proj[:, inner:late_at], sum_b)
    g_pre = g_pre + paired(in_proj[:, late_at:], sum_a[:, : inner - b_columns + tail])
    g_pre = g_pre / pre_gain.astype(F32)
    g_gate = paired(out_proj, g_out) / gate_gain.astype(F32)
    small = sum_a[:6, inner - b_columns + tail :]
    g_lines = small[:5, :own_conv]
    g_heads = small[5, : 3 * heads].reshape(3, heads)
    return (
        layer_out.reshape(hidden_in.shape),
        grad_input.reshape(hidden_in.shape),
        g_pre,
        g_in,
        g_lines[:4],
        g_lines[4],
        g_heads,
        g_gate,
        g_out,
    )


def solution(mesh):
    rows = P(None, ("group", "shard"), None, None)
    in_specs = (
        rows,
        P(None, ("group", "shard")),
        P("shard"),
        P("shard", None),
        P(None, "shard"),
        P("shard"),
        P(),
        P("shard"),
        P("shard", None),
        rows,
    )
    out_specs = (
        rows,
        rows,
        P("shard"),
        P("shard", None),
        P(None, "shard"),
        P("shard"),
        P(),
        P("shard"),
        P("shard", None),
    )
    body = functools.partial(local, mesh.shape["shard"], mesh.shape["group"])
    return jax.shard_map(body, mesh=mesh, in_specs=in_specs, out_specs=out_specs, check_vma=False)
```
